32 devices in a mesh: wide: 8 (over z, x), narrow: 4 (over y, core).
Axes of the slice: x: 2, y: 2, z: 4, core: 2. Of those that a mesh axis runs over, the one named last changes fastest.
Arguments:
- patches: bfloat16 [40960, 512], P(('wide', 'narrow')), may hold values from -6 to 6
- text_tokens: bfloat16 [4, 77, 512], P('narrow', None, 'wide'), may hold values from -6 to 6
- view_counts: int32 [32, 5], P(('wide', 'narrow')), may hold values from 64 to 256, as said below
- out_grad: bfloat16 [40960, 512], P(('wide', 'narrow')), may hold values from -6 to 6
- owners: int32 [12], replicated, may hold values from 0 to 3, as said below
- masters: float32 [4, 4, 512, 512], P('narrow', None, 'wide'), may hold values from -1.41421356 to 1.41421356, as said below
- first_moment: float32 [4, 4, 512, 512], P('narrow', None, 'wide'), may hold values from -541.84987 to 541.84987
- second_moment: float32 [4, 4, 512, 512], P('narrow', None, 'wide'), may hold values from 286.72 to 73728
- average: float32 [4, 4, 512, 512], P('narrow', None, 'wide'), may hold values from -1.41421356 to 1.41421356
- vec_value: float32 [4608], replicated, may hold values from -0.8 to 1.5
- vec_first: float32 [4608], replicated, may hold values from -677.3123 to 677.3123
- vec_second: float32 [4608], replicated, may hold values from 2580.48 to 114688
- vec_average: float32 [4608], replicated, may hold values from -0.8 to 1.5
Outputs:
- layer_out: bfloat16 [40960, 512], P(('wide', 'narrow'))
- patch_grad: float32 [40960, 512], P(('wide', 'narrow'))
- text_grad: float32 [4, 77, 512], P('narrow', None, 'wide')
- new_masters: float32 [4, 4, 512, 512], P('narrow', None, 'wide')
- new_first: float32 [4, 4, 512, 512], P('narrow', None, 'wide')
- new_second: float32 [4, 4, 512, 512], P('narrow', None, 'wide')
- new_average: float32 [4, 4, 512, 512], P('narrow', None, 'wide')
- new_copies: bfloat16 [4, 4, 512, 512], P('narrow', None, 'wide')
- vec_new_value: float32 [4608], replicated
- vec_new_first: float32 [4608], replicated
- vec_new_second: float32 [4608], replicated
- vec_new_average: float32 [4608], replicated
The draws below stay inside these ranges and needn't reach their ends.
Inputs may be any that keep to these rules, and one draw needn't show every extreme that they name: `owners`: unit u is one of: query, key, value, output projection, then the 4 column blocks of the up projection, then the row blocks of the down projection. Each owner holds at most 4 units, and some owner exactly 4. `view_counts`: A view's live patches fill its first slots; every sample has a view with 256 live patches. `masters`: empty slots hold values that no output reads.
All inputs are finite; a program needn't handle non-finite values.
Results may differ from the reference program's by a relative error of at most 0.012.
The reference program's roundings to bfloat16 on the way count: a program that leaves them out, or rounds other values in their place, can miss the bound.
Values may be sent and summed in bfloat16 or wider, within the bound.
A program may use at most 192 MiB of HBM per device.

```python
import jax
import jax.numpy as jnp
from jax import lax

D = 512
HEADS = 8
HEAD_DIM = 64
FF = 2048
LANG = 77
VIEWS = 5
VIEW_ROWS = 256
SLOTS = 4
STEP = 5
UNITS = 12
ROWS_DEV = 1280
SAMPLES = 32
TOTAL_ROWS = 40960
VEC = 4608
N_NARROW = 4


def owner_list(key):
    subkeys = jax.random.split(jax.random.fold_in(key, 101), 4)
    spare_units = 2 * SLOTS
    load_one = jax.random.randint(subkeys[0], (), 0, SLOTS + 1)
    lower_end = jnp.maximum(0, SLOTS - load_one)
    upper_end = jnp.minimum(SLOTS, spare_units - load_one) + 1
    load_two = jax.random.randint(subkeys[1], (), lower_end, upper_end)
    unit_loads = jnp.stack([jnp.int32(SLOTS), load_one, load_two, spare_units - load_one - load_two]).astype(jnp.int32)
    owner_order = jax.random.permutation(subkeys[2], N_NARROW).astype(jnp.int32)
    bounds = jnp.cumsum(unit_loads).astype(jnp.int32)
    places = jnp.arange(UNITS, dtype=jnp.int32)
    block_ids = jnp.sum((places[:, None] >= bounds[None, :]).astype(jnp.int32), axis=1)
    owner_at = owner_order[block_ids]
    unit_order = jax.random.permutation(subkeys[3], UNITS)
    return jnp.zeros((UNITS,), jnp.int32).at[unit_order].set(owner_at)


def slot_factor(key, unit_values):
    owners = owner_list(key)
    unit_ids = jnp.arange(UNITS, dtype=jnp.int32)
    same_owner = owners[:, None] == owners[None, :]
    earlier = unit_ids[None, :] < unit_ids[:, None]
    unit_rank = jnp.sum((same_owner & earlier).astype(jnp.int32), axis=1)
    owner_ids = jnp.arange(N_NARROW, dtype=jnp.int32)
    slot_ids = jnp.arange(SLOTS, dtype=jnp.int32)
    slot_pick = ((owners[None, None, :] == owner_ids[:, None, None]) & (unit_rank[None, None, :] == slot_ids[None, :, None])).astype(jnp.float32)
    filled = jnp.sum(slot_pick, axis=2)
    return jnp.sum(slot_pick * unit_values[None, None, :], axis=2) + (1.0 - filled) * unit_values[0]


def unit_spread():
    blocks = FF // D
    fans = [2 * D // 3, 2 * D // 3, D, D // 64] + [D] * blocks + [FF] * blocks
    return jnp.array(fans, dtype=jnp.float32) ** (-0.5)


def unit_grad_size():
    blocks = FF // D
    factors = [0.3, 0.3, 0.8, 0.1] + [0.3] * blocks + [0.6] * blocks
    return jnp.array(factors, dtype=jnp.float32) * (0.7 * TOTAL_ROWS) ** 0.5


def vector_grad_size():
    pieces = [jnp.full((D,), 1.0), jnp.full((D,), 1.0), jnp.full((D,), 0.6), jnp.full((D,), 0.6), jnp.full((FF,), 0.3), jnp.full((D,), 1.0)]
    return jnp.concatenate(pieces).astype(jnp.float32) * (0.7 * TOTAL_ROWS) ** 0.5


def gain_places():
    positions = jnp.arange(VEC, dtype=jnp.int32)
    return (positions < D) | (positions >= 2 * D) & (positions < 3 * D)


def draw_owners(key, part):
    return owner_list(key)


def draw_view_counts(key, part):
    key = jax.random.fold_in(key, 7)
    first_key, second_key = jax.random.split(key)
    counts = jax.random.randint(first_key, (SAMPLES, VIEWS), VIEW_ROWS // 4, VIEW_ROWS + 1)
    full_view = jax.random.randint(second_key, (SAMPLES, 1), 0, VIEWS)
    view_ids = jnp.arange(VIEWS, dtype=jnp.int32)[None, :]
    return jnp.where(view_ids == full_view, VIEW_ROWS, counts).astype(jnp.int32)


def draw_masters(key, part):
    factor = slot_factor(key, unit_spread())
    key = jax.random.fold_in(key, 11)
    shape = (N_NARROW, SLOTS, D, D)
    base_draw = jax.random.truncated_normal(key, -4.0, 4.0, shape, jnp.float32)
    return base_draw * factor[:, :, None, None]


def draw_average(key, part):
    factor = slot_factor(key, unit_spread())
    key = jax.random.fold_in(key, 13)
    shape = (N_NARROW, SLOTS, D, D)
    base_draw = jax.random.truncated_normal(key, -4.0, 4.0, shape, jnp.float32)
    return base_draw * factor[:, :, None, None]


def draw_first_moment(key, part):
    factor = slot_factor(key, unit_grad_size())
    key = jax.random.fold_in(key, 17)
    shape = (N_NARROW, SLOTS, D, D)
    base_draw = jax.random.truncated_normal(key, -4.0, 4.0, shape, jnp.float32)
    return base_draw * factor[:, :, None, None]


def draw_second_moment(key, part):
    factor = slot_factor(key, unit_grad_size())
    key = jax.random.fold_in(key, 19)
    shape = (N_NARROW, SLOTS, D, D)
    base_draw = jnp.exp(jax.random.uniform(key, shape, jnp.float32, 0.0, 1.3862944))
    return base_draw * (factor * factor)[:, :, None, None]


def draw_vec_value(key, part):
    key = jax.random.fold_in(key, 23)
    first_key, second_key = jax.random.split(key)
    gains = jax.random.uniform(first_key, (VEC,), jnp.float32, 0.6, 1.4)
    biases = 0.2 * jax.random.truncated_normal(second_key, -4.0, 4.0, (VEC,), jnp.float32)
    return jnp.where(gain_places(), gains, biases)


def draw_vec_average(key, part):
    key = jax.random.fold_in(key, 29)
    first_key, second_key = jax.random.split(key)
    gains = jax.random.uniform(first_key, (VEC,), jnp.float32, 0.6, 1.4)
    biases = 0.2 * jax.random.truncated_normal(second_key, -4.0, 4.0, (VEC,), jnp.float32)
    return jnp.where(gain_places(), gains, biases)


def draw_vec_first(key, part):
    key = jax.random.fold_in(key, 31)
    base_draw = jax.random.truncated_normal(key, -4.0, 4.0, (VEC,), jnp.float32)
    return base_draw * vector_grad_size()


def draw_vec_second(key, part):
    key = jax.random.fold_in(key, 37)
    base_draw = jnp.exp(jax.random.uniform(key, (VEC,), jnp.float32, 0.0, 1.3862944))
    scale_vec = vector_grad_size()
    return base_draw * scale_vec * scale_vec


def levels(rng, extent, shards, low, top_value):
    factor_of, own = 1.0, jax.random.fold_in(rng, 6)
    for position, shards_of in shards:
        draws = jnp.exp(jax.random.uniform(jax.random.fold_in(own, position), (shards_of,), jnp.float32, low / len(shards), top_value / len(shards)))
        factor_of = factor_of * jnp.repeat(draws, extent[position] // shards_of).reshape([-1 if axis == position else 1 for axis in range(len(extent))])
    return factor_of


def scatter_about(rng, shape, deviation, most, cuts=(), kind=jnp.bfloat16):
    entries = deviation * jax.random.normal(rng, shape, jnp.float32)
    if cuts:
        entries = entries * levels(rng, shape, cuts, -0.22, 0.18)
    return jnp.clip(entries, -most, most).astype(kind)


def setup_inputs(seed: int = 0) -> dict:
    keys = jax.random.split(jax.random.key(seed), 14)
    return {
        "patches": scatter_about(keys[0], (TOTAL_ROWS, D), 1.0, 6.0, ((0, 32),)),
        "text_tokens": scatter_about(keys[1], (N_NARROW, LANG, D), 1.0, 6.0, ((0, 4), (2, 8))),
        "view_counts": draw_view_counts(jax.random.fold_in(keys[13], 71), 0),
        "out_grad": scatter_about(keys[3], (TOTAL_ROWS, D), 1.0, 6.0, ((0, 32),)),
        "owners": draw_owners(jax.random.fold_in(keys[13], 71), 0),
        "masters": draw_masters(jax.random.fold_in(keys[13], 71), 0),
        "first_moment": draw_first_moment(jax.random.fold_in(keys[13], 71), 0),
        "second_moment": draw_second_moment(jax.random.fold_in(keys[13], 71), 0),
        "average": draw_average(jax.random.fold_in(keys[13], 71), 0),
        "vec_value": draw_vec_value(jax.random.fold_in(keys[13], 71), 0),
        "vec_first": draw_vec_first(jax.random.fold_in(keys[13], 71), 0),
        "vec_second": draw_vec_second(jax.random.fold_in(keys[13], 71), 0),
        "vec_average": draw_vec_average(jax.random.fold_in(keys[13], 71), 0),
    }


@jax.custom_vjp
def low(v):
    return lax.optimization_barrier(v.astype(jnp.bfloat16)).astype(jnp.float32)

@jax.custom_vjp
def low_back(v):
    return v

def low_keep(v):
    return (low(v), None)

def low_pass(kept, grad):
    return (grad,)

def back_keep(v):
    return (v, None)

def back_low(kept, grad):
    return (low(grad),)
low.defvjp(low_keep, low_pass)
low_back.defvjp(back_keep, back_low)
HIGHEST = lax.Precision.HIGHEST
norm_eps = 1e-05
beta_one = 0.5
beta_two = 0.5
adam_eps = 1e-08
weight_decay = 0.1
average_keep = 0.75
vector_rate = 0.25

def matmul(left_side, right_side):
    return jnp.dot(left_side, right_side, precision=HIGHEST, preferred_element_type=jnp.float32)

def layer_norm(inputs, gain_vec, bias_vec):
    center = inputs - lax.optimization_barrier(jnp.mean(inputs, axis=-1, keepdims=True))
    spread = lax.optimization_barrier(jnp.mean(center * center, axis=-1, keepdims=True))
    return center * lax.rsqrt(spread + norm_eps) * gain_vec + bias_vec

def unit_slots(owners, narrow_count, slot_count):
    unit_ids = jnp.arange(owners.shape[0], dtype=jnp.int32)
    same_owner = owners[:, None] == owners[None, :]
    earlier = unit_ids[None, :] < unit_ids[:, None]
    unit_rank = lax.optimization_barrier(jnp.sum((same_owner & earlier).astype(jnp.int32), axis=1)).astype(jnp.int32)
    owner_ids = jnp.arange(narrow_count, dtype=jnp.int32)
    slot_ids = jnp.arange(slot_count, dtype=jnp.int32)
    slot_pick = (owners[None, None, :] == owner_ids[:, None, None]) & (unit_rank[None, None, :] == slot_ids[None, :, None])
    return (unit_rank, slot_pick.astype(jnp.float32))

def unit_rates():
    blocks = FF // D
    fans = [2 * D // 3, 2 * D // 3, D, D // 64] + [D] * blocks + [FF] * blocks
    return jnp.array(fans, dtype=jnp.float32) ** (-0.5)

def split_vector(vector):
    return (vector[0:D], vector[D:2 * D], vector[2 * D:3 * D], vector[3 * D:4 * D], vector[4 * D:4 * D + FF], vector[4 * D + FF:5 * D + FF])

def assemble(unit_mats):
    blocks = FF // D
    w_up = jnp.concatenate([unit_mats[4 + block_id] for block_id in range(blocks)], axis=1)
    w_down = jnp.concatenate([unit_mats[4 + blocks + block_id] for block_id in range(blocks)], axis=0)
    return (unit_mats[0], unit_mats[1], unit_mats[2], unit_mats[3], w_up, w_down)

def adam_update(master, moment_one, moment_two, averaged, gradient, rate_value):
    moment_one = beta_one * moment_one + (1.0 - beta_one) * gradient
    moment_two = beta_two * moment_two + (1.0 - beta_two) * gradient * gradient
    mean_hat = moment_one / (1.0 - beta_one ** STEP)
    second_hat = moment_two / (1.0 - beta_two ** STEP)
    master = master - rate_value * (mean_hat / (jnp.sqrt(second_hat) + adam_eps) + weight_decay * master)
    averaged = average_keep * averaged + (1.0 - average_keep) * master
    return (master, moment_one, moment_two, averaged)

def block_forward(inputs, text_rows, unit_mats, vector, live_mask):
    w_query, w_key, w_value, w_out, w_up, w_down = assemble(unit_mats)
    gain_one, bias_one, gain_two, bias_two, up_bias, down_bias = split_vector(vector)
    normed_one = low(layer_norm(inputs, gain_one, bias_one))
    text_normed = low(layer_norm(text_rows, gain_one, bias_one))

    def project(source, weight):
        return low_back(low(matmul(source, weight)))
    query = project(normed_one, w_query).reshape(-1, HEADS, HEAD_DIM)
    keyed = jnp.concatenate([project(normed_one, w_key), project(text_normed, w_key)], axis=0).reshape(-1, HEADS, HEAD_DIM)
    valued = jnp.concatenate([project(normed_one, w_value), project(text_normed, w_value)], axis=0).reshape(-1, HEADS, HEAD_DIM)
    scores = low_back(jnp.einsum('qhd,khd->hqk', query, keyed, precision=HIGHEST) * HEAD_DIM ** (-0.5))
    key_live = jnp.concatenate([live_mask > 0.5, jnp.ones((text_rows.shape[0],), dtype=bool)])
    scores = jnp.where(key_live[None, None, :], scores, -jnp.inf)
    row_peak = lax.optimization_barrier(jnp.max(scores, axis=2, keepdims=True))
    exp_scores = jnp.exp(scores - row_peak)
    attn_probs = exp_scores / lax.optimization_barrier(jnp.sum(exp_scores, axis=2, keepdims=True))
    attended = jnp.einsum('hqk,khd->qhd', low(attn_probs), valued, precision=HIGHEST).reshape(-1, D)
    attended = low_back(low(attended))
    middle = inputs + low_back(matmul(attended, w_out))
    normed_two = low(layer_norm(middle, gain_two, bias_two))
    preact = low_back(matmul(normed_two, w_up) + up_bias)
    active = low(jax.nn.gelu(preact, approximate=False))
    outputs = middle + matmul(active, w_down) + down_bias
    return outputs * live_mask[:, None]

def reference(patches, text_tokens, view_counts, out_grad, owners, masters, first_moment, second_moment, average, vec_value, vec_first, vec_second, vec_average):
    unit_rank, slot_pick = unit_slots(owners, N_NARROW, SLOTS)
    flat_index = (owners * SLOTS + unit_rank).astype(jnp.int32)
    unit_mats = low(masters.reshape(N_NARROW * SLOTS, D, D)[flat_index])
    positions = jnp.arange(ROWS_DEV, dtype=jnp.int32)
    view_ids = positions // VIEW_ROWS
    within = positions % VIEW_ROWS
    view_match = view_ids[:, None] == jnp.arange(VIEWS, dtype=jnp.int32)[None, :]
    live_rows = jnp.any(view_match[None, :, :] & (within[None, :, None] < view_counts[:, None, :]), axis=2).astype(jnp.float32)
    inputs_all = patches.astype(jnp.float32).reshape(SAMPLES, ROWS_DEV, D)
    cotangent = out_grad.astype(jnp.float32).reshape(SAMPLES, ROWS_DEV, D)
    text_all = text_tokens.astype(jnp.float32)
    groups = (jnp.arange(SAMPLES, dtype=jnp.int32) % N_NARROW).astype(jnp.int32)

    def per_sample(totals, payload):
        unit_total, vector_total, text_total = totals
        inputs, cot_rows, live_mask, group_id = payload
        text_rows = lax.dynamic_index_in_dim(text_all, group_id, 0, keepdims=False)

        def forward(inputs_in, text_in, mats_in, vector_in):
            return block_forward(inputs_in, text_in, mats_in, vector_in, live_mask)
        outputs, pullback = jax.vjp(forward, inputs, text_rows, unit_mats, vec_value)
        input_grad, text_part, unit_part, vector_part = pullback(cot_rows)
        text_total = text_total.at[group_id].add(text_part)
        return ((unit_total + unit_part, vector_total + vector_part, text_total), (outputs.astype(jnp.bfloat16), input_grad))
    start_totals = (jnp.zeros((UNITS, D, D), jnp.float32), jnp.zeros((VEC,), jnp.float32), jnp.zeros((N_NARROW, LANG, D), jnp.float32))
    totals, stacked = lax.scan(per_sample, start_totals, (inputs_all, cotangent, live_rows, groups))
    unit_total, vector_total, text_total = totals
    layer_out, patch_grad = stacked
    slot_grad = jnp.einsum('nsu,uij->nsij', slot_pick, unit_total, precision=HIGHEST)
    filled = (lax.optimization_barrier(jnp.sum(slot_pick, axis=2)) > 0.5)[:, :, None, None]
    slot_rate = jnp.einsum('nsu,u->ns', slot_pick, unit_rates(), precision=HIGHEST)[:, :, None, None]
    new_state = adam_update(masters, first_moment, second_moment, average, slot_grad, slot_rate)
    new_masters, new_first, new_second, new_average = [jnp.where(filled, state_part, 0.0) for state_part in new_state]
    vec_new_value, vec_new_first, vec_new_second, vec_new_average = adam_update(vec_value, vec_first, vec_second, vec_average, vector_total, vector_rate)
    return (layer_out.reshape(TOTAL_ROWS, D), patch_grad.reshape(TOTAL_ROWS, D), text_total, new_masters, new_first, new_second, new_average, new_masters.astype(jnp.bfloat16), vec_new_value, vec_new_first, vec_new_second, vec_new_average)
```

```python
import functools

import jax
import jax.numpy as jnp
from jax import lax
from jax.experimental import pallas as pl
from jax.experimental.pallas import tpu as pltpu
from jax.sharding import PartitionSpec as P

D = 512
HEADS = 8
FF = 2048
VIEWS = 5
VIEW_ROWS = 256
ROWS = VIEWS * VIEW_ROWS
LANG = 77
TEXT = 128
KEYS = ROWS + TEXT
STEP = 5
UNITS = 12
SLOTS = 4
VEC = 5 * D + FF
F32 = jnp.float32
BF16 = jnp.bfloat16
MESH = pl.DeviceIdType.MESH
NEG = -1e30

norm_eps = 1e-05
beta_one = 0.5
beta_two = 0.5
adam_eps = 1e-08
weight_decay = 0.1
average_keep = 0.75
vector_rate = 0.25
VMEM_LIMIT = 60 * 2**20


def dot(left, right, left_dim=1, right_dim=0):
    return lax.dot_general(
        left, right, (((left_dim,), (right_dim,)), ((), ())), preferred_element_type=F32
    )


def vmem():
    return pl.BlockSpec(memory_space=pltpu.VMEM)


def smem():
    return pl.BlockSpec(memory_space=pltpu.SMEM)


def unit_ranks(owners_ref):
    owner = [owners_ref[u] for u in range(UNITS)]
    rank = []
    for u in range(UNITS):
        total = jnp.int32(0)
        for v in range(u):
            total = total + (owner[v] == owner[u]).astype(jnp.int32)
        rank.append(jnp.minimum(total, SLOTS - 1))
    return owner, rank


def normalize(values):
    center = values - jnp.mean(values, axis=-1, keepdims=True)
    spread = jnp.mean(center * center, axis=-1, keepdims=True)
    scale = lax.rsqrt(spread + norm_eps)
    return center * scale, scale


def norm_back(grads, gain, normed, scale):
    e = grads * gain
    return scale * (
        e
        - jnp.mean(e, axis=-1, keepdims=True)
        - normed * jnp.mean(e * normed, axis=-1, keepdims=True)
    )


def place():
    w = lax.axis_index("wide")
    n = lax.axis_index("narrow")
    return w, n, w // 2, w % 2, n // 2, n % 2


def greet(peers):
    barrier = pltpu.get_barrier_semaphore()
    for peer in peers:
        pl.semaphore_signal(barrier, inc=1, device_id=peer, device_id_type=MESH)
    pl.semaphore_wait(barrier, len(peers))


def all_peers(w, n, z, x):
    peers = [(w, lax.rem(n + k, 4)) for k in range(1, 4)]
    peers += [(lax.rem(z + k, 4) * 2 + x, n) for k in range(1, 4)]
    peers.append((z * 2 + 1 - x, n))
    return peers


class Sender:
    def __init__(self, send, recv):
        self.send, self.recv, self.count = send, recv, 0

    def __call__(self, src, dst, device):
        i = self.count
        self.count += 1
        copy = pltpu.make_async_remote_copy(
            src_ref=src,
            dst_ref=dst,
            send_sem=self.send.at[i],
            recv_sem=self.recv.at[i],
            device_id=device,
            device_id_type=MESH,
        )
        copy.start()
        return copy


def pipeline(groups, stages):
    flying = {}
    for step in range(groups + len(stages)):
        for s in reversed(range(len(stages) + 1)):
            g = step - s
            if not 0 <= g < groups:
                continue
            if s > 0:
                copies, after = flying.pop((g, s - 1))
                for copy in copies:
                    copy.wait()
                if after is not None:
                    after()
            if s < len(stages):
                flying[(g, s)] = stages[s](g)


def gather_kernel(owners, masters, text, w_out, t_out, send_buf, slot_buf, text_buf, send, recv):
    w, n, z, x, y, c = place()
    for q in range(4):
        send_buf[q] = masters[0, :, :, q * 128 : (q + 1) * 128].astype(BF16)
    text_buf[...] = jnp.zeros_like(text_buf)
    text_buf[0:LANG, 0:64] = text[0].astype(F32)
    t_out[z, x] = text_buf[...].T[0:64].astype(BF16)
    greet(all_peers(w, n, z, x))
    go = Sender(send, recv)
    first = []
    for k in range(1, 4):
        q = lax.rem(n + k, 4)
        first.append(go(send_buf.at[q], slot_buf.at[n], (w, q)))
    text_copies = [
        go(t_out.at[z, x], t_out.at[z, x], (lax.rem(z + k, 4) * 2 + x, n)) for k in range(1, 4)
    ]
    slot_buf[n] = send_buf[n]
    owner, rank = unit_ranks(owners)
    for copy in first:
        copy.wait()
    quarter = pl.ds(pl.multiple_of(n * 128, 128), 128)
    for u in range(UNITS):
        w_out[u, z, x, :, quarter] = slot_buf[owner[u], rank[u]]
    for copy in text_copies:
        copy.wait()
    text_last = go(t_out.at[:, x], t_out.at[:, x], (z * 2 + 1 - x, n))

    def cols(q):
        return pl.ds(pl.multiple_of(q * 128, 128), 128)

    def share(ref, device):
        return go(ref, ref, device)

    to_x = (z * 2 + 1 - x, n)
    to_y = (w, (1 - y) * 2 + c)
    to_c = (w, y * 2 + 1 - c)

    def stage_z(g):
        piece = w_out.at[pl.ds(3 * g, 3), z, x, :, cols(n)]
        return [share(piece, (lax.rem(z + k, 4) * 2 + x, n)) for k in range(1, 4)], None

    def stage_one(g):
        u = pl.ds(3 * g, 3)
        return [
            share(w_out.at[u, pl.ds(0, 2), x, :, cols(n)], to_x),
            share(w_out.at[u, pl.ds(2, 2), x, :, cols(n)], to_y),
        ], None

    def stage_two(g):
        u = pl.ds(3 * g, 3)
        return [
            share(w_out.at[u, pl.ds(0, 2), :, :, cols(n)], to_y),
            share(w_out.at[u, pl.ds(2, 2), x, :, cols(c)], to_x),
            share(w_out.at[u, pl.ds(2, 2), x, :, cols(2 + c)], to_x),
        ], None

    def stage_core(g):
        u = pl.ds(3 * g, 3)
        return [
            share(w_out.at[u, :, :, :, cols(c)], to_c),
            share(w_out.at[u, :, :, :, cols(2 + c)], to_c),
        ], None

    pipeline(4, [stage_z, stage_one, stage_two, stage_core])
    text_last.wait()


def gather(owners, masters, text):
    if lax.axis_size("wide") != 8 or lax.axis_size("narrow") != 4:
        packed = lax.all_gather(masters.astype(BF16), "wide", axis=2, tiled=True)
        packed = lax.all_gather(packed, "narrow", axis=0, tiled=True)
        same = owners[:, None] == owners[None, :]
        ids = jnp.arange(UNITS)
        rank = jnp.sum((same & (ids[None, :] < ids[:, None])).astype(jnp.int32), axis=1)
        units = jnp.take(packed.reshape(-1, D, D), owners * SLOTS + rank, axis=0)
        rows = lax.all_gather(text, "wide", axis=2, tiled=True)[0]
        return units, jnp.pad(rows.T, ((0, 0), (0, TEXT - LANG)))
    copies = 3 + 3 + 1 + 4 * 10
    units, text_t = pl.pallas_call(
        gather_kernel,
        out_shape=[
            jax.ShapeDtypeStruct((UNITS, 4, 2, 64, D), BF16),
            jax.ShapeDtypeStruct((4, 2, 64, TEXT), BF16),
        ],
        in_specs=[smem(), vmem(), vmem()],
        out_specs=[vmem(), vmem()],
        scratch_shapes=[
            pltpu.VMEM((4, SLOTS, 64, 128), BF16),
            pltpu.VMEM((4, SLOTS, 64, 128), BF16),
            pltpu.VMEM((128, 128), F32),
            pltpu.SemaphoreType.DMA((copies,)),
            pltpu.SemaphoreType.DMA((copies,)),
        ],
        compiler_params=pltpu.CompilerParams(
            collective_id=1, has_side_effects=True, vmem_limit_bytes=VMEM_LIMIT
        ),
    )(owners, masters, text)
    return units.reshape(UNITS, D, D), text_t.reshape(D, TEXT)


def live_column(counts, rows):
    index = lax.broadcasted_iota(jnp.int32, (VIEW_ROWS, 1), 0)
    return [(index < counts[0, v]) for v in range(rows // VIEW_ROWS)]


def forward_kernel(
    counts, x, text_t, vec, w, att_t, probs, inverse, q_t, keyed, v_t, normed, text_normed
):
    i = pl.program_id(0)

    @pl.when(i == 0)
    def _():
        gain, bias = vec[:, 0:D], vec[:, D : 2 * D]
        normed[...] = (normalize(x[...].astype(F32))[0] * gain + bias).astype(BF16)
        rows = text_t[...].astype(F32).T
        live_text = lax.broadcasted_iota(jnp.int32, (TEXT, 1), 0) < LANG
        text_normed[...] = jnp.where(
            live_text, normalize(rows)[0] * gain + bias, 0.0
        ).astype(BF16)
        q_t[...] = dot(w[0], normed[...], 0, 1).astype(BF16) * BF16(0.125)
        v_t[:, 0:ROWS] = dot(w[2], normed[...], 0, 1).astype(BF16)
        v_t[:, ROWS:KEYS] = dot(w[2], text_normed[...], 0, 1).astype(BF16)
        for p in range(4):
            pair = slice(p * 128, (p + 1) * 128)
            keyed[p, 0:ROWS, 0:128] = dot(normed[...], w[1, :, pair]).astype(BF16)
            keyed[p, ROWS:KEYS, 0:128] = dot(text_normed[...], w[1, :, pair]).astype(BF16)
            for v, live in enumerate(live_column(counts, ROWS)):
                keyed[p, v * VIEW_ROWS : (v + 1) * VIEW_ROWS, 128:256] = jnp.broadcast_to(
                    jnp.where(live, 0.0, NEG), (VIEW_ROWS, 128)
                ).astype(BF16)
            keyed[p, ROWS:KEYS, 128:256] = jnp.broadcast_to(
                jnp.where(live_text, 0.0, NEG), (TEXT, 128)
            ).astype(BF16)

    row = lax.broadcasted_iota(jnp.int32, (128, ROWS), 0)
    one = jnp.where(row == 0, 1.0, 0.0).astype(BF16)
    pair_q = q_t[pl.ds(pl.multiple_of(i * 128, 128), 128), :]
    for h in range(2):
        mine = (row >= 64 * h) & (row < 64 * h + 64)
        q = jnp.where(mine, pair_q, jnp.zeros_like(pair_q))
        scores = dot(keyed[i], jnp.concatenate([q, one], axis=0))
        peak = jnp.max(scores, axis=0, keepdims=True)
        e = jnp.exp(scores - peak)
        total = jnp.sum(e, axis=0, keepdims=True)
        low = e.astype(BF16)
        probs[h] = low
        mixed = dot(v_t[pl.ds(pl.multiple_of(i * 128 + h * 64, 64), 64), :], low)
        inv = 1.0 / total
        att_t[h * 64 : (h + 1) * 64, :] = (mixed * inv).astype(BF16)
        inverse[0, h : h + 1, :] = inv


def attention_forward(counts, x, text_t, vec, units):
    return pl.pallas_call(
        forward_kernel,
        grid=(4,),
        in_specs=[smem(), vmem(), vmem(), vmem(), pl.BlockSpec((3, D, D), lambda i: (0, 0, 0))],
        out_specs=[
            pl.BlockSpec((128, ROWS), lambda i: (i, 0)),
            pl.BlockSpec((2, KEYS, ROWS), lambda i: (i, 0, 0)),
            pl.BlockSpec((1, 2, ROWS), lambda i: (i, 0, 0)),
            pl.BlockSpec((D, ROWS), lambda i: (0, 0)),
            pl.BlockSpec((4, KEYS, 256), lambda i: (0, 0, 0)),
            pl.BlockSpec((D, KEYS), lambda i: (0, 0)),
        ],
        out_shape=[
            jax.ShapeDtypeStruct((D, ROWS), BF16),
            jax.ShapeDtypeStruct((HEADS, KEYS, ROWS), BF16),
            jax.ShapeDtypeStruct((4, 2, ROWS), F32),
            jax.ShapeDtypeStruct((D, ROWS), BF16),
            jax.ShapeDtypeStruct((4, KEYS, 256), BF16),
            jax.ShapeDtypeStruct((D, KEYS), BF16),
        ],
        scratch_shapes=[pltpu.VMEM((ROWS, D), BF16), pltpu.VMEM((TEXT, D), BF16)],
        compiler_params=pltpu.CompilerParams(vmem_limit_bytes=VMEM_LIMIT),
    )(counts, x, text_t, vec, units)


def dense_kernel(
    counts, att_t, x, g, vec, w,
    layer_out, middle_back, back_t, grads, gain_grad, bias_grad, up_grad, down_grad,
    total, *, tile
):
    i = pl.program_id(0)
    steps = pl.num_programs(0)
    gain, bias = vec[:, 2 * D : 3 * D], vec[:, 3 * D : 4 * D]
    a = att_t[...]
    index = lax.broadcasted_iota(jnp.int32, (tile, 1), 0) + i * tile
    live = jnp.zeros((tile, 1), jnp.bool_)
    for v in range(VIEWS):
        live = live | ((index >= v * VIEW_ROWS) & (index < v * VIEW_ROWS + counts[0, v]))
    middle = x[...].astype(F32) + dot(a, w[3], 0, 0)
    normed, scale = normalize(middle)
    low = (normed * gain + bias).astype(BF16)
    out_back = jnp.where(live, g[...].astype(F32), 0.0)
    out_low = out_back.astype(BF16)

    @pl.when(i == 0)
    def _():
        total[...] = jnp.zeros_like(total)
        gain_grad[...] = jnp.zeros_like(gain_grad)
        bias_grad[...] = jnp.zeros_like(bias_grad)
        up_grad[...] = jnp.zeros_like(up_grad)
        down_grad[...] = jnp.zeros_like(down_grad)

    out = middle + vec[:, 4 * D + FF :]
    normed_back = jnp.zeros((tile, D), F32)
    for j in range(4):
        block = slice(j * D, (j + 1) * D)
        preact = dot(low, w[4 + j]) + vec[:, 4 * D + j * D : 5 * D + j * D]
        phi = 0.5 + 0.5 * lax.erf(preact * 0.7071067811865476)
        active = (preact * phi).astype(BF16)
        slope = phi + preact * (jnp.exp(-0.5 * preact * preact) * 0.3989422804014327)
        out = out + dot(active, w[8 + j])
        preact_back = (dot(out_low, w[8 + j], 1, 1) * slope).astype(BF16)
        normed_back = normed_back + dot(preact_back, w[4 + j], 1, 1)
        total[1 + j] += dot(low, preact_back, 0, 0)
        total[5 + j] += dot(active, out_low, 0, 0)
        up_grad[:, block] += jnp.sum(preact_back.astype(F32), axis=0, keepdims=True)
    layer_out[...] = jnp.where(live, out, 0.0).astype(BF16)
    back = out_back + norm_back(normed_back, gain, normed, scale)
    middle_back[...] = back
    branch = back.astype(BF16)
    back_t[...] = dot(w[3], branch, 1, 1).astype(BF16)
    total[0] += dot(a, branch)
    gain_grad[...] += jnp.sum(normed_back * normed, axis=0, keepdims=True)
    bias_grad[...] += jnp.sum(normed_back, axis=0, keepdims=True)
    down_grad[...] += jnp.sum(out_back, axis=0, keepdims=True)

    @pl.when(i == steps - 1)
    def _():
        grads[...] = total[...].astype(BF16)


def dense(counts, att_t, x, g, vec, units, tile=640):
    rows = pl.BlockSpec((tile, D), lambda i: (i, 0))
    columns = pl.BlockSpec((D, tile), lambda i: (0, i))
    return pl.pallas_call(
        functools.partial(dense_kernel, tile=tile),
        grid=(ROWS // tile,),
        in_specs=[smem(), columns, rows, rows, vmem(), vmem()],
        out_specs=[
            rows,
            rows,
            columns,
            pl.BlockSpec((9, D, D), lambda i: (0, 0, 0)),
            pl.BlockSpec((1, D), lambda i: (0, 0)),
            pl.BlockSpec((1, D), lambda i: (0, 0)),
            pl.BlockSpec((1, FF), lambda i: (0, 0)),
            pl.BlockSpec((1, D), lambda i: (0, 0)),
        ],
        out_shape=[
            jax.ShapeDtypeStruct((ROWS, D), BF16),
            jax.ShapeDtypeStruct((ROWS, D), F32),
            jax.ShapeDtypeStruct((D, ROWS), BF16),
            jax.ShapeDtypeStruct((9, D, D), BF16),
            jax.ShapeDtypeStruct((1, D), F32),
            jax.ShapeDtypeStruct((1, D), F32),
            jax.ShapeDtypeStruct((1, FF), F32),
            jax.ShapeDtypeStruct((1, D), F32),
        ],
        scratch_shapes=[pltpu.VMEM((9, D, D), F32)],
        compiler_params=pltpu.CompilerParams(vmem_limit_bytes=VMEM_LIMIT),
    )(counts, att_t, x, g, vec, units)


def backward_kernel(probs, inverse, keyed, v_t, back_t, q_t, att_t, query_back, key_back, value_back):
    row = lax.broadcasted_iota(jnp.int32, (128, ROWS), 0)
    lane = lax.broadcasted_iota(jnp.int32, (KEYS, 128), 1)
    ones = jnp.where(lane < 2, 1.0, 0.0).astype(BF16)
    value = jnp.concatenate([v_t[...].astype(F32).T.astype(BF16), ones], axis=1)
    key_t = keyed[:, 0:128].astype(F32).T.astype(BF16)
    back = back_t[...].astype(F32)
    product = back * att_t[...].astype(F32)
    query = q_t[...].astype(F32)
    key_total = jnp.zeros((KEYS, 128), F32)
    value_total = jnp.zeros((KEYS, 128), F32)
    for h in range(2):
        half = slice(h * 64, (h + 1) * 64)
        inv = inverse[0, h : h + 1, :]
        delta = jnp.sum(product[half], axis=0, keepdims=True) * inv
        high = delta.astype(BF16).astype(F32)
        mine = (row >= 64 * h) & (row < 64 * h + 64)
        scaled = jnp.where(mine, back * inv, 0.0)
        tail = jnp.where(row == 0, -high, jnp.where(row == 1, high - delta, 0.0))
        right = jnp.concatenate([scaled.astype(BF16), tail.astype(BF16)], axis=0)
        low = probs[h]
        score_back = low * dot(value, right).astype(BF16)
        query_back[half, :] = (dot(key_t[half], score_back) * 0.125).astype(BF16)
        key_total += dot(score_back, jnp.where(mine, query, 0.0).T.astype(BF16))
        value_total += dot(low, scaled.T.astype(BF16))
    key_back[...] = key_total.astype(BF16)
    value_back[...] = value_total.astype(BF16)


def attention_backward(probs, inverse, keyed, v_t, back_t, q_t, att_t):
    return pl.pallas_call(
        backward_kernel,
        grid=(4,),
        in_specs=[
            pl.BlockSpec((2, KEYS, ROWS), lambda i: (i, 0, 0)),
            pl.BlockSpec((1, 2, ROWS), lambda i: (i, 0, 0)),
            pl.BlockSpec((None, KEYS, 256), lambda i: (i, 0, 0)),
            pl.BlockSpec((128, KEYS), lambda i: (i, 0)),
            pl.BlockSpec((128, ROWS), lambda i: (i, 0)),
            pl.BlockSpec((128, ROWS), lambda i: (i, 0)),
            pl.BlockSpec((128, ROWS), lambda i: (i, 0)),
        ],
        out_specs=[
            pl.BlockSpec((128, ROWS), lambda i: (i, 0)),
            pl.BlockSpec((KEYS, 128), lambda i: (0, i)),
            pl.BlockSpec((KEYS, 128), lambda i: (0, i)),
        ],
        out_shape=[
            jax.ShapeDtypeStruct((D, ROWS), BF16),
            jax.ShapeDtypeStruct((KEYS, D), BF16),
            jax.ShapeDtypeStruct((KEYS, D), BF16),
        ],
        compiler_params=pltpu.CompilerParams(vmem_limit_bytes=VMEM_LIMIT),
    )(probs, inverse, keyed, v_t, back_t, q_t, att_t)


def project_kernel(
    x, text_t, vec, w, middle_back, query_back, key_back, value_back, text_key, text_value,
    patch_grad, grads, gain_grad, bias_grad, text_grad_t, total
):
    i = pl.program_id(0)
    steps = pl.num_programs(0)
    gain, bias = vec[:, 0:D], vec[:, D : 2 * D]

    @pl.when(i == 0)
    def _():
        live = lax.broadcasted_iota(jnp.int32, (TEXT, 1), 0) < LANG
        normed, scale = normalize(text_t[...].astype(F32).T)
        low_t = jnp.where(live, normed * gain + bias, 0.0).T.astype(BF16)
        k, v = text_key[...], text_value[...]
        back = dot(k, w[1], 1, 1) + dot(v, w[2], 1, 1)
        text_grad_t[...] = norm_back(back, gain, normed, scale).T.astype(BF16)
        gain_grad[...] = jnp.sum(back * normed, axis=0, keepdims=True)
        bias_grad[...] = jnp.sum(back, axis=0, keepdims=True)
        total[0] = jnp.zeros((D, D), F32)
        total[1] = dot(low_t, k)
        total[2] = dot(low_t, v)

    normed, scale = normalize(x[...].astype(F32))
    low_t = (normed * gain + bias).T.astype(BF16)
    q, k, v = query_back[...], key_back[...], value_back[...]
    back = dot(q, w[0], 0, 1) + dot(k, w[1], 1, 1) + dot(v, w[2], 1, 1)
    patch_grad[...] = middle_back[...] + norm_back(back, gain, normed, scale)
    total[0] += dot(low_t, q, 1, 1)
    total[1] += dot(low_t, k)
    total[2] += dot(low_t, v)
    gain_grad[...] += jnp.sum(back * normed, axis=0, keepdims=True)
    bias_grad[...] += jnp.sum(back, axis=0, keepdims=True)

    @pl.when(i == steps - 1)
    def _():
        grads[...] = total[...].astype(BF16)


def project_back(x, text_t, vec, units, middle_back, query_back, key_back, value_back, tile=640):
    rows = pl.BlockSpec((tile, D), lambda i: (i, 0))
    text_rows = pl.BlockSpec((TEXT, D), lambda i: (ROWS // TEXT, 0))
    return pl.pallas_call(
        project_kernel,
        grid=(ROWS // tile,),
        in_specs=[
            rows,
            vmem(),
            vmem(),
            pl.BlockSpec((3, D, D), lambda i: (0, 0, 0)),
            rows,
            pl.BlockSpec((D, tile), lambda i: (0, i)),
            rows,
            rows,
            text_rows,
            text_rows,
        ],
        out_specs=[
            rows,
            pl.BlockSpec((3, D, D), lambda i: (0, 0, 0)),
            pl.BlockSpec((1, D), lambda i: (0, 0)),
            pl.BlockSpec((1, D), lambda i: (0, 0)),
            pl.BlockSpec((D, TEXT), lambda i: (0, 0)),
        ],
        out_shape=[
            jax.ShapeDtypeStruct((ROWS, D), F32),
            jax.ShapeDtypeStruct((3, D, D), BF16),
            jax.ShapeDtypeStruct((1, D), F32),
            jax.ShapeDtypeStruct((1, D), F32),
            jax.ShapeDtypeStruct((D, TEXT), BF16),
        ],
        scratch_shapes=[pltpu.VMEM((3, D, D), F32)],
        compiler_params=pltpu.CompilerParams(vmem_limit_bytes=VMEM_LIMIT),
    )(
        x, text_t, vec, units, middle_back, query_back, key_back, value_back, key_back, value_back
    )


def add(a, b):
    return (a.astype(F32) + b.astype(F32)).astype(BF16)


def reduce_kernel(
    owners, rest, first, text, gain_one, bias_one, gain_two, bias_two, up, down,
    slot_grad, text_out, vec_out,
    c_buf, c_sum, ya_buf, ya_sum, xb_buf, xb_sum, xa_buf, yb_buf, z_sum, z_buf, red, s_buf, r_buf,
    tx_buf, t_sum, tz_buf, v_own, v_buf, vz_buf, send, recv
):
    w, n, z, x, y, c = place()
    offset = 0
    for piece in (gain_one, bias_one, gain_two, bias_two, up, down):
        size = piece.shape[1]
        v_own[:, offset : offset + size] = piece[...]
        offset += size
    greet(all_peers(w, n, z, x))
    go = Sender(send, recv)
    to_x = (z * 2 + 1 - x, n)
    to_y = (w, (1 - y) * 2 + c)
    to_c = (w, y * 2 + 1 - c)

    def to_z(k):
        return (lax.rem(z + k, 4) * 2 + x, n)

    def cols(q):
        return pl.ds(pl.multiple_of(q * 128, 128), 128)

    def source(g):
        return (first, 0) if g == 3 else (rest, 3 * g)

    def units_of(g):
        return pl.ds(0, 3) if g == 3 else pl.ds(3 * (g + 1), 3)

    def vector_stage(s, device):
        if s == 0:
            sent = v_own
        else:
            sent = v_buf.at[s + 2]
        return go(sent, v_buf.at[s], device)

    vc = vector_stage(0, to_c)
    tx = go(text.at[:, 1 - x], tx_buf, to_x)

    def stage_core(g):
        ref, base = source(g)
        u, at = units_of(g), pl.ds(base, 3)
        copies = [
            go(ref.at[at, :, :, :, cols(2 * k + 1 - c)], c_buf.at[k, u], to_c) for k in range(2)
        ]

        def after():
            for k in range(2):
                c_sum[k, u] = add(ref[at, :, :, :, cols(2 * k + c)], c_buf[k, u])

        return copies, after

    def stage_one(g):
        u = units_of(g)
        copies = [
            go(c_sum.at[1 - y, u, pl.ds(0, 2)], ya_buf.at[u], to_y),
            go(c_sum.at[0, u, pl.ds(2, 2), 1 - x], xb_buf.at[0, u], to_x),
            go(c_sum.at[1, u, pl.ds(2, 2), 1 - x], xb_buf.at[1, u], to_x),
        ]

        def after():
            ya_sum[u] = add(c_sum[y, u, 0:2], ya_buf[u])
            for k in range(2):
                xb_sum[k, u] = add(c_sum[k, u, 2:4, x], xb_buf[k, u])

        return copies, after

    def stage_two(g):
        u = units_of(g)
        copies = [
            go(ya_sum.at[u, :, 1 - x], xa_buf.at[u], to_x),
            go(xb_sum.at[1 - y, u], yb_buf.at[u], to_y),
        ]

        def after():
            z_sum[u, 0:2] = add(ya_sum[u, :, x], xa_buf[u])
            z_sum[u, 2:4] = add(xb_sum[y, u], yb_buf[u])

        return copies, after

    def stage_z(g):
        u = units_of(g)
        copies = [
            go(z_sum.at[u, lax.rem(z + k, 4)], z_buf.at[k - 1, u], to_z(k)) for k in range(1, 4)
        ]

        def after():
            total = z_sum[u, z].astype(F32)
            for k in range(3):
                total = total + z_buf[k, u].astype(F32)
            red[u] = total.astype(BF16)

        return copies, after

    pipeline(4, [stage_core, stage_one, stage_two, stage_z])

    owner, rank = unit_ranks(owners)
    for q in range(4):
        for s in range(SLOTS):
            unit = jnp.int32(0)
            for u in range(UNITS):
                unit = unit + jnp.where((owner[u] == q) & (rank[u] == s), u, 0)
            s_buf[q, s] = red[jnp.minimum(unit, UNITS - 1)]
    last = []
    for k in range(1, 4):
        q = lax.rem(n + k, 4)
        last.append(go(s_buf.at[q], r_buf.at[n], (w, q)))
    r_buf[n] = s_buf[n]

    vc.wait()
    v_buf[3] = v_own[...] + v_buf[0]
    vy = vector_stage(1, to_y)
    tx.wait()
    t_sum[...] = add(text[:, x], tx_buf[...])
    tz = [go(t_sum.at[lax.rem(z + k, 4)], tz_buf.at[k - 1], to_z(k)) for k in range(1, 4)]
    vy.wait()
    v_buf[4] = v_buf[3] + v_buf[1]
    vx = vector_stage(2, to_x)
    vx.wait()
    vz_buf[z] = v_buf[4] + v_buf[2]
    vz = [go(vz_buf.at[z], vz_buf.at[z], to_z(k)) for k in range(1, 4)]
    for copy in tz:
        copy.wait()
    total = t_sum[z].astype(F32)
    for k in range(3):
        total = total + tz_buf[k].astype(F32)
    text_out[...] = total
    for copy in last:
        copy.wait()
    for q in range(4):
        for s in range(SLOTS):
            slot_grad[s, :, q * 128 : (q + 1) * 128] = r_buf[q, s].astype(F32)
    for copy in vz:
        copy.wait()
    vec_out[...] = (vz_buf[0] + vz_buf[1]) + (vz_buf[2] + vz_buf[3])


def reduce_all(owners, rest, first, text, vecs):
    wide = lax.axis_size("wide")
    if wide != 8 or lax.axis_size("narrow") != 4:
        vec = lax.psum(jnp.concatenate(vecs, axis=1), ("wide", "narrow"))
        text_sum = lax.psum_scatter(text.astype(F32), "wide", scatter_dimension=0, tiled=True)
        all_units = jnp.concatenate([first, rest], axis=0).astype(F32)
        rows = lax.psum_scatter(all_units, "wide", scatter_dimension=1, tiled=True)
        same = owners[:, None] == owners[None, :]
        ids = jnp.arange(UNITS)
        rank = jnp.sum((same & (ids[None, :] < ids[:, None])).astype(jnp.int32), axis=1)
        pick = (owners[None, None, :] == jnp.arange(lax.axis_size("narrow"))[:, None, None]) & (
            rank[None, None, :] == jnp.arange(SLOTS)[None, :, None]
        )
        terms = jnp.einsum("nsu,urc->nsrc", pick.astype(F32), rows, precision=lax.Precision.HIGHEST)
        slots = lax.psum_scatter(terms, "narrow", scatter_dimension=0, tiled=True)
        return slots[0], text_sum, vec
    copies = 1 + 1 + 4 * 10 + 3 + 1 + 3 + 1 + 3
    bf = lambda *s: pltpu.VMEM(s, BF16)
    return pl.pallas_call(
        reduce_kernel,
        out_shape=[
            jax.ShapeDtypeStruct((SLOTS, 64, D), F32),
            jax.ShapeDtypeStruct((64, TEXT), F32),
            jax.ShapeDtypeStruct((1, VEC), F32),
        ],
        in_specs=[smem()] + [vmem()] * 9,
        out_specs=[vmem()] * 3,
        scratch_shapes=[
            bf(2, UNITS, 4, 2, 64, 128),
            bf(2, UNITS, 4, 2, 64, 128),
            bf(UNITS, 2, 2, 64, 128),
            bf(UNITS, 2, 2, 64, 128),
            bf(2, UNITS, 2, 64, 128),
            bf(2, UNITS, 2, 64, 128),
            bf(UNITS, 2, 64, 128),
            bf(UNITS, 2, 64, 128),
            bf(UNITS, 4, 64, 128),
            bf(3, UNITS, 64, 128),
            bf(UNITS, 64, 128),
            bf(4, SLOTS, 64, 128),
            bf(4, SLOTS, 64, 128),
            bf(4, 64, TEXT),
            bf(4, 64, TEXT),
            bf(3, 64, TEXT),
            pltpu.VMEM((1, VEC), F32),
            pltpu.VMEM((5, 1, VEC), F32),
            pltpu.VMEM((4, 1, VEC), F32),
            pltpu.SemaphoreType.DMA((copies,)),
            pltpu.SemaphoreType.DMA((copies,)),
        ],
        compiler_params=pltpu.CompilerParams(
            collective_id=2, has_side_effects=True, vmem_limit_bytes=VMEM_LIMIT
        ),
    )(
        owners,
        rest.reshape(9, 4, 2, 64, D),
        first.reshape(3, 4, 2, 64, D),
        text.reshape(4, 2, 64, TEXT),
        *vecs,
    )


def adam(master, moment_one, moment_two, averaged, gradient, rate):
    moment_one = beta_one * moment_one + (1.0 - beta_one) * gradient
    moment_two = beta_two * moment_two + (1.0 - beta_two) * gradient * gradient
    mean_hat = moment_one / (1.0 - beta_one**STEP)
    second_hat = moment_two / (1.0 - beta_two**STEP)
    master = master - rate * (
        mean_hat / (jnp.sqrt(second_hat) + adam_eps) + weight_decay * master
    )
    averaged = average_keep * averaged + (1.0 - average_keep) * master
    return master, moment_one, moment_two, averaged


def unit_rates():
    blocks = FF // D
    fans = [2 * D // 3, 2 * D // 3, D, D // 64] + [D] * blocks + [FF] * blocks
    return [float(fan) ** -0.5 for fan in fans]


def update_kernel(
    owners, grad, masters, first, second, average, text_t, vec_grad, vec, vec_first, vec_second,
    vec_average,
    new_masters, new_first, new_second, new_average, new_copies, text_grad,
    vec_new_value, vec_new_first, vec_new_second, vec_new_average,
):
    n = lax.axis_index("narrow")
    owner, rank = unit_ranks(owners)
    for s in range(SLOTS):
        rate, filled = jnp.float32(0.0), jnp.int32(0)
        for u, value in enumerate(unit_rates()):
            match = (owner[u] == n) & (rank[u] == s)
            rate = rate + jnp.where(match, jnp.float32(value), jnp.float32(0.0))
            filled = filled + match.astype(jnp.int32)
        state = adam(
            masters[0, s], first[0, s], second[0, s], average[0, s], grad[s], rate
        )
        keep = jnp.broadcast_to(filled, state[0].shape) > 0
        state = [jnp.where(keep, part, 0.0) for part in state]
        for ref, part in zip((new_masters, new_first, new_second, new_average), state):
            ref[0, s] = part
        new_copies[0, s] = state[0].astype(BF16)
    text_grad[0] = text_t[...].T[0:LANG]
    state = adam(
        vec[...], vec_first[...], vec_second[...], vec_average[...], vec_grad[...], vector_rate
    )
    for ref, part in zip(
        (vec_new_value, vec_new_first, vec_new_second, vec_new_average), state
    ):
        ref[...] = part


def update(owners, grad, masters, first, second, average, text_t, vec_grad, vec, v1, v2, va):
    state = jax.ShapeDtypeStruct(masters.shape, F32)
    vector = jax.ShapeDtypeStruct((1, VEC), F32)
    return pl.pallas_call(
        update_kernel,
        out_shape=[state] * 4
        + [
            jax.ShapeDtypeStruct(masters.shape, BF16),
            jax.ShapeDtypeStruct((1, LANG, text_t.shape[0]), F32),
        ]
        + [vector] * 4,
        in_specs=[smem()] + [vmem()] * 11,
        out_specs=[vmem()] * 10,
        compiler_params=pltpu.CompilerParams(vmem_limit_bytes=VMEM_LIMIT),
    )(owners, grad, masters, first, second, average, text_t, vec_grad, vec, v1, v2, va)


def local(
    patches, text_tokens, view_counts, out_grad, owners, masters, first_moment, second_moment,
    average, vec_value, vec_first, vec_second, vec_average,
):
    vec = vec_value.reshape(1, VEC)
    units, text_t = gather(owners, masters, text_tokens)
    att_t, probs, inverse, q_t, keyed, v_t = attention_forward(
        view_counts, patches, text_t, vec, units
    )
    layer_out, middle_back, back_t, rest, gain_two, bias_two, up, down = dense(
        view_counts, att_t, patches, out_grad, vec, units
    )
    query_back, key_back, value_back = attention_backward(
        probs, inverse, keyed, v_t, back_t, q_t, att_t
    )
    patch_grad, first, gain_one, bias_one, text_part = project_back(
        patches, text_t, vec, units, middle_back, query_back, key_back, value_back
    )
    slot_grad, text_sum, vec_grad = reduce_all(
        owners, rest, first, text_part, (gain_one, bias_one, gain_two, bias_two, up, down)
    )
    outs = update(
        owners, slot_grad, masters, first_moment, second_moment, average, text_sum, vec_grad, vec,
        vec_first.reshape(1, VEC), vec_second.reshape(1, VEC), vec_average.reshape(1, VEC),
    )
    new_masters, new_first, new_second, new_average, new_copies, text_grad = outs[:6]
    vectors = [part.reshape(VEC) for part in outs[6:]]
    return (
        layer_out, patch_grad, text_grad, new_masters, new_first, new_second, new_average,
        new_copies, *vectors,
    )


def solution(mesh):
    rows = P(("wide", "narrow"), None)
    state = P("narrow", None, "wide", None)
    text = P("narrow", None, "wide")
    in_specs = (rows, text, rows, rows, P(), state, state, state, state, P(), P(), P(), P())
    out_specs = (rows, rows, text, state, state, state, state, state, P(), P(), P(), P())
    return jax.shard_map(local, mesh=mesh, in_specs=in_specs, out_specs=out_specs, check_vma=False)
```

```python
import functools

import jax
import jax.numpy as jnp
from jax import lax
from jax.experimental import pallas as pl
from jax.experimental.pallas import tpu as pltpu
from jax.sharding import PartitionSpec as P

D = 512
HEADS = 8
FF = 2048
VIEWS = 5
VIEW_ROWS = 256
ROWS = VIEWS * VIEW_ROWS
LANG = 77
TEXT = 128
KEYS = ROWS + TEXT
STEP = 5
UNITS = 12
SLOTS = 4
VEC = 5 * D + FF
F32 = jnp.float32
BF16 = jnp.bfloat16
MESH = pl.DeviceIdType.MESH
NEG = -1e30

norm_eps = 1e-05
beta_one = 0.5
beta_two = 0.5
adam_eps = 1e-08
weight_decay = 0.1
average_keep = 0.75
vector_rate = 0.25
VMEM_LIMIT = 60 * 2**20


def dot(left, right, left_dim=1, right_dim=0):
    return lax.dot_general(
        left, right, (((left_dim,), (right_dim,)), ((), ())), preferred_element_type=F32
    )


def vmem():
    return pl.BlockSpec(memory_space=pltpu.VMEM)


def smem():
    return pl.BlockSpec(memory_space=pltpu.SMEM)


def vec_row(vec, start, size):
    first = start // 128
    return jnp.concatenate([vec[first + r : first + r + 1, :] for r in range(size // 128)], axis=1)


def unit_ranks(owners_ref):
    owner = [owners_ref[u] for u in range(UNITS)]
    rank = []
    for u in range(UNITS):
        total = jnp.int32(0)
        for v in range(u):
            total = total + (owner[v] == owner[u]).astype(jnp.int32)
        rank.append(jnp.minimum(total, SLOTS - 1))
    return owner, rank


def normalize(values):
    center = values - jnp.mean(values, axis=-1, keepdims=True)
    spread = jnp.mean(center * center, axis=-1, keepdims=True)
    scale = lax.rsqrt(spread + norm_eps)
    return center * scale, scale


def norm_back(grads, gain, normed, scale):
    e = grads * gain
    return scale * (
        e
        - jnp.mean(e, axis=-1, keepdims=True)
        - normed * jnp.mean(e * normed, axis=-1, keepdims=True)
    )


def place():
    w = lax.axis_index("wide")
    n = lax.axis_index("narrow")
    return w, n, w // 2, w % 2, n // 2, n % 2


def narrow_peers(w, n):
    return [(w, lax.rem(n + k, 4)) for k in range(1, 4)]


def wide_peers(w, n):
    return [(lax.rem(w + k, 8), n) for k in range(1, 8)]


def greet(peers):
    barrier = pltpu.get_barrier_semaphore()
    for peer in peers:
        pl.semaphore_signal(barrier, inc=1, device_id=peer, device_id_type=MESH)


def greeted(peers):
    pl.semaphore_wait(pltpu.get_barrier_semaphore(), len(peers))


class Links:
    def __init__(self, send, recv):
        self.send, self.recv, self.slots = send, recv, {}

    def copies(self, key, parts):
        made = []
        for k, (src, dst, device) in enumerate(parts()):
            slot = self.slots.setdefault((key, k), len(self.slots))
            made.append(
                pltpu.make_async_remote_copy(
                    src_ref=src,
                    dst_ref=dst,
                    send_sem=self.send.at[slot],
                    recv_sem=self.recv.at[slot],
                    device_id=device,
                    device_id_type=MESH,
                )
            )
        return made

    def start(self, key, parts):
        for copy in self.copies(key, parts):
            copy.start()

    def wait(self, key, parts):
        for copy in self.copies(key, parts):
            copy.wait()


def partners(w, n, z, x, y, c):
    to_z = [(lax.rem(z + k, 4) * 2 + x, n) for k in range(1, 4)]
    return to_z, (z * 2 + 1 - x, n), (w, (1 - y) * 2 + c), (w, y * 2 + 1 - c)


def spread(ref, head, own, stage, at):
    w, n, z, x, y, c = at
    to_z, to_x, to_y, to_c = partners(*at)
    if stage == 0:
        return [(own, ref.at[(*head, z, x, y, c)], peer) for peer in to_z]
    if stage == 1:
        parts = [((pl.ds(0, 2), x, y, c), to_x), ((pl.ds(2, 2), x, y, c), to_y)]
    elif stage == 2:
        whole = slice(None)
        parts = [((pl.ds(0, 2), whole, y, c), to_y), ((pl.ds(2, 2), x, whole, c), to_x)]
    else:
        whole = slice(None)
        parts = [((whole, whole, whole, c), to_c)]
    return [(ref.at[(*head, *part)], ref.at[(*head, *part)], peer) for part, peer in parts]


def front_kernel(
    owners, counts, masters, text, x, vec,
    att_t, probs, inverse, q_out, key_out, v_out, normed_out, w_first_out, w_rest, text_out,
    send_buf, slot_buf, own, w_first, text_buf, q_t, keyed, v_t, normed, normed_t, text_normed,
    send, recv, local
):
    i = pl.program_id(0)
    at = place()
    w, n, z, sx, y, c = at
    links = Links(send, recv)
    rest_own = pltpu.make_async_copy(
        own.at[pl.ds(3, 9)], w_rest.at[:, z, sx, y, c], local.at[0]
    )
    written = [
        pltpu.make_async_copy(q_t, q_out, local.at[1]),
        pltpu.make_async_copy(keyed.at[:, :, pl.ds(0, 128)], key_out, local.at[2]),
        pltpu.make_async_copy(v_t, v_out, local.at[3]),
        pltpu.make_async_copy(normed_t, normed_out, local.at[4]),
        pltpu.make_async_copy(w_first, w_first_out, local.at[5]),
        pltpu.make_async_copy(text_buf, text_out, local.at[6]),
    ]

    def rest(g, stage):
        head = (pl.ds(3 * g, 3),)
        return ("rest", g, stage), lambda: spread(
            w_rest, head, own.at[pl.ds(3 + 3 * g, 3)], stage, at
        )

    @pl.when(i == 0)
    def _():
        peers = narrow_peers(w, n) + wide_peers(w, n)
        greet(peers)
        send_buf[...] = masters[0].reshape(SLOTS, 4, 16, D).astype(BF16)
        text_buf[z, sx] = jnp.zeros((64, TEXT), BF16)
        text_buf[z, sx, :, 0:LANG] = text[0]
        greeted(peers)
        slots = "slots", lambda: [
            (send_buf.at[:, q], slot_buf.at[n], (w, q)) for _, q in narrow_peers(w, n)
        ]
        links.start(*slots)
        piece = text_buf.at[z, sx]
        texts = "text", lambda: [(piece, piece, peer) for peer in wide_peers(w, n)]
        links.start(*texts)
        slot_buf[n] = send_buf[:, n]
        gain, bias = vec_row(vec, 0, D), vec_row(vec, D, D)
        low = (normalize(x[...].astype(F32))[0] * gain + bias).astype(BF16)
        normed[...] = low
        owner, rank = unit_ranks(owners)
        links.wait(*slots)
        for u in range(UNITS):
            own[u] = slot_buf[owner[u], rank[u]]
        for u in range(3):
            w_first[u, z, sx, y, c] = own[u]

        order = (1, 0, 2)

        def first(u, s):
            return ("first", u, s), lambda: spread(w_first, (u,), own.at[u], s, at)

        for u in order:
            links.start(*first(u, 0))
        rest_own.start()
        normed_t[:, 0:ROWS] = normed[...].astype(F32).T.astype(BF16)
        links.wait(*texts)
        live_text = lax.broadcasted_iota(jnp.int32, (TEXT, 1), 0) < LANG
        rows = text_buf[...].reshape(D, TEXT).astype(F32).T
        text_low = jnp.where(live_text, normalize(rows)[0] * gain + bias, 0.0)
        text_normed[...] = text_low.astype(BF16)
        normed_t[:, ROWS:KEYS] = text_low.T.astype(BF16)
        for p in range(4):
            for v, live in enumerate(live_column(counts, ROWS)):
                keyed[p, v * VIEW_ROWS : (v + 1) * VIEW_ROWS, 128:256] = jnp.broadcast_to(
                    jnp.where(live, 0.0, NEG), (VIEW_ROWS, 128)
                ).astype(BF16)
            keyed[p, ROWS:KEYS, 128:256] = jnp.broadcast_to(
                jnp.where(live_text, 0.0, NEG), (TEXT, 128)
            ).astype(BF16)

        def unit(u):
            return w_first[u].reshape(D, D)

        def project(u):
            if u == 1:
                k = dot(normed[...], unit(1)).astype(BF16)
                t = dot(text_normed[...], unit(1)).astype(BF16)
                for p in range(4):
                    pair = slice(p * 128, (p + 1) * 128)
                    keyed[p, 0:ROWS, 0:128] = k[:, pair]
                    keyed[p, ROWS:KEYS, 0:128] = t[:, pair]
            elif u == 0:
                q_t[...] = dot(unit(0), normed[...], 0, 1).astype(BF16) * BF16(0.125)
            else:
                v_t[:, 0:ROWS] = dot(unit(2), normed[...], 0, 1).astype(BF16)
                v_t[:, ROWS:KEYS] = dot(unit(2), text_normed[...], 0, 1).astype(BF16)

        for step in range(3 + 3):
            for s in (3, 2, 1, 0):
                g = step - s
                if not 0 <= g < 3:
                    continue
                u = order[g]
                links.wait(*first(u, s))
                if s < 3:
                    links.start(*first(u, s + 1))
                if (g, s) == (2, 0):
                    links.start(*rest(0, 0))
                if (g, s) == (2, 1):
                    links.start(*rest(1, 0))
                if (g, s) == (2, 2):
                    links.start(*rest(2, 0))
                if s == 3:
                    project(u)
        for copy in written:
            copy.start()

    plan = {
        0: ["local", (0, 0)], 1: [(1, 0)], 2: [(2, 0), (0, 1)], 3: [(1, 1)],
        4: [(2, 1), (0, 2)], 5: [(1, 2)], 6: [(2, 2), (0, 3)], 7: [(1, 3)],
    }

    def comm(t):
        for item in plan[t]:
            if item == "local":
                rest_own.wait()
                continue
            g, s = item
            links.wait(*rest(g, s))
            if s < 3:
                links.start(*rest(g, s + 1))

    row = lax.broadcasted_iota(jnp.int32, (128, ROWS), 0)
    one = jnp.where(row == 0, 1.0, 0.0).astype(BF16)
    for h in range(2):
        for k in range(4):
            pl.when(i == k)(functools.partial(comm, 2 * k + h))
        pair_q = q_t[pl.ds(pl.multiple_of(i * 128, 128), 128), :]
        mine = (row >= 64 * h) & (row < 64 * h + 64)
        q = jnp.where(mine, pair_q, jnp.zeros_like(pair_q))
        scores = dot(keyed[i], jnp.concatenate([q, one], axis=0))
        peak = jnp.max(scores, axis=0, keepdims=True)
        e = jnp.exp(scores - peak)
        total = jnp.sum(e, axis=0, keepdims=True)
        low = e.astype(BF16)
        probs[h] = low
        mixed = dot(v_t[pl.ds(pl.multiple_of(i * 128 + h * 64, 64), 64), :], low)
        inv = 1.0 / total
        att_t[h * 64 : (h + 1) * 64, :] = (mixed * inv).astype(BF16)
        inverse[0, h : h + 1, :] = inv

    @pl.when(i == 3)
    def _():
        links.wait(*rest(2, 3))
        for copy in written:
            copy.wait()


def front(owners, counts, masters, text, x, vec):
    hbm = pl.BlockSpec(memory_space=pl.ANY)
    copies = 3 + 7 + 3 * 8 + 3 * 8
    return pl.pallas_call(
        front_kernel,
        grid=(4,),
        in_specs=[smem(), smem(), vmem(), vmem(), vmem(), vmem()],
        out_specs=[
            pl.BlockSpec((128, ROWS), lambda i: (i, 0)),
            pl.BlockSpec((2, KEYS, ROWS), lambda i: (i, 0, 0)),
            pl.BlockSpec((1, 2, ROWS), lambda i: (i, 0, 0)),
        ]
        + [hbm] * 7,
        out_shape=[
            jax.ShapeDtypeStruct((D, ROWS), BF16),
            jax.ShapeDtypeStruct((HEADS, KEYS, ROWS), BF16),
            jax.ShapeDtypeStruct((4, 2, ROWS), F32),
            jax.ShapeDtypeStruct((D, ROWS), BF16),
            jax.ShapeDtypeStruct((4, KEYS, 128), BF16),
            jax.ShapeDtypeStruct((D, KEYS), BF16),
            jax.ShapeDtypeStruct((D, KEYS), BF16),
            jax.ShapeDtypeStruct((3, 4, 2, 2, 2, 16, D), BF16),
            jax.ShapeDtypeStruct((9, 4, 2, 2, 2, 16, D), BF16),
            jax.ShapeDtypeStruct((4, 2, 64, TEXT), BF16),
        ],
        scratch_shapes=[
            pltpu.VMEM((SLOTS, 4, 16, D), BF16),
            pltpu.VMEM((4, SLOTS, 16, D), BF16),
            pltpu.VMEM((UNITS, 16, D), BF16),
            pltpu.VMEM((3, 4, 2, 2, 2, 16, D), BF16),
            pltpu.VMEM((4, 2, 64, TEXT), BF16),
            pltpu.VMEM((D, ROWS), BF16),
            pltpu.VMEM((4, KEYS, 256), BF16),
            pltpu.VMEM((D, KEYS), BF16),
            pltpu.VMEM((ROWS, D), BF16),
            pltpu.VMEM((D, KEYS), BF16),
            pltpu.VMEM((TEXT, D), BF16),
            pltpu.SemaphoreType.DMA((copies,)),
            pltpu.SemaphoreType.DMA((copies,)),
            pltpu.SemaphoreType.DMA((7,)),
        ],
        compiler_params=pltpu.CompilerParams(
            collective_id=1, has_side_effects=True, vmem_limit_bytes=VMEM_LIMIT
        ),
    )(owners, counts, masters, text, x, vec)


def gather(owners, masters, text_t):
    packed = lax.all_gather(masters.astype(BF16), "wide", axis=2, tiled=True)
    packed = lax.all_gather(packed, "narrow", axis=0, tiled=True)
    same = owners[:, None] == owners[None, :]
    ids = jnp.arange(UNITS)
    rank = jnp.sum((same & (ids[None, :] < ids[:, None])).astype(jnp.int32), axis=1)
    units = jnp.take(packed.reshape(-1, D, D), owners * SLOTS + rank, axis=0)
    rows = lax.all_gather(text_t, "wide", axis=1, tiled=True)[0]
    return units, jnp.pad(rows, ((0, 0), (0, TEXT - LANG)))


def live_column(counts, rows):
    index = lax.broadcasted_iota(jnp.int32, (VIEW_ROWS, 1), 0)
    return [(index < counts[0, v]) for v in range(rows // VIEW_ROWS)]


def forward_kernel(
    counts, x, text_t, vec, w, att_t, probs, inverse, q_t, keyed, v_t, normed, text_normed
):
    i = pl.program_id(0)

    @pl.when(i == 0)
    def _():
        gain, bias = vec_row(vec, 0, D), vec_row(vec, D, D)
        normed[...] = (normalize(x[...].astype(F32))[0] * gain + bias).astype(BF16)
        rows = text_t[...].astype(F32).T
        live_text = lax.broadcasted_iota(jnp.int32, (TEXT, 1), 0) < LANG
        text_normed[...] = jnp.where(
            live_text, normalize(rows)[0] * gain + bias, 0.0
        ).astype(BF16)
        q_t[...] = dot(w[0], normed[...], 0, 1).astype(BF16) * BF16(0.125)
        v_t[:, 0:ROWS] = dot(w[2], normed[...], 0, 1).astype(BF16)
        v_t[:, ROWS:KEYS] = dot(w[2], text_normed[...], 0, 1).astype(BF16)
        for p in range(4):
            pair = slice(p * 128, (p + 1) * 128)
            keyed[p, 0:ROWS, 0:128] = dot(normed[...], w[1, :, pair]).astype(BF16)
            keyed[p, ROWS:KEYS, 0:128] = dot(text_normed[...], w[1, :, pair]).astype(BF16)
            for v, live in enumerate(live_column(counts, ROWS)):
                keyed[p, v * VIEW_ROWS : (v + 1) * VIEW_ROWS, 128:256] = jnp.broadcast_to(
                    jnp.where(live, 0.0, NEG), (VIEW_ROWS, 128)
                ).astype(BF16)
            keyed[p, ROWS:KEYS, 128:256] = jnp.broadcast_to(
                jnp.where(live_text, 0.0, NEG), (TEXT, 128)
            ).astype(BF16)

    row = lax.broadcasted_iota(jnp.int32, (128, ROWS), 0)
    one = jnp.where(row == 0, 1.0, 0.0).astype(BF16)
    pair_q = q_t[pl.ds(pl.multiple_of(i * 128, 128), 128), :]
    for h in range(2):
        mine = (row >= 64 * h) & (row < 64 * h + 64)
        q = jnp.where(mine, pair_q, jnp.zeros_like(pair_q))
        scores = dot(keyed[i], jnp.concatenate([q, one], axis=0))
        peak = jnp.max(scores, axis=0, keepdims=True)
        e = jnp.exp(scores - peak)
        total = jnp.sum(e, axis=0, keepdims=True)
        low = e.astype(BF16)
        probs[h] = low
        mixed = dot(v_t[pl.ds(pl.multiple_of(i * 128 + h * 64, 64), 64), :], low)
        inv = 1.0 / total
        att_t[h * 64 : (h + 1) * 64, :] = (mixed * inv).astype(BF16)
        inverse[0, h : h + 1, :] = inv


def attention_forward(counts, x, text_t, vec, units):
    return pl.pallas_call(
        forward_kernel,
        grid=(4,),
        in_specs=[smem(), vmem(), vmem(), vmem(), pl.BlockSpec((3, D, D), lambda i: (0, 0, 0))],
        out_specs=[
            pl.BlockSpec((128, ROWS), lambda i: (i, 0)),
            pl.BlockSpec((2, KEYS, ROWS), lambda i: (i, 0, 0)),
            pl.BlockSpec((1, 2, ROWS), lambda i: (i, 0, 0)),
            pl.BlockSpec((D, ROWS), lambda i: (0, 0)),
            pl.BlockSpec((4, KEYS, 256), lambda i: (0, 0, 0)),
            pl.BlockSpec((D, KEYS), lambda i: (0, 0)),
        ],
        out_shape=[
            jax.ShapeDtypeStruct((D, ROWS), BF16),
            jax.ShapeDtypeStruct((HEADS, KEYS, ROWS), BF16),
            jax.ShapeDtypeStruct((4, 2, ROWS), F32),
            jax.ShapeDtypeStruct((D, ROWS), BF16),
            jax.ShapeDtypeStruct((4, KEYS, 256), BF16),
            jax.ShapeDtypeStruct((D, KEYS), BF16),
        ],
        scratch_shapes=[pltpu.VMEM((ROWS, D), BF16), pltpu.VMEM((TEXT, D), BF16)],
        compiler_params=pltpu.CompilerParams(vmem_limit_bytes=VMEM_LIMIT),
    )(counts, x, text_t, vec, units)


def dense_kernel(
    counts, att_t, x, g, vec, w,
    layer_out, middle_back, back_t, grads, gain_grad, bias_grad, up_grad, down_grad,
    total, *, tile
):
    i = pl.program_id(0)
    steps = pl.num_programs(0)
    gain, bias = vec_row(vec, 2 * D, D), vec_row(vec, 3 * D, D)
    a = att_t[...]
    index = lax.broadcasted_iota(jnp.int32, (tile, 1), 0) + i * tile
    live = jnp.zeros((tile, 1), jnp.bool_)
    for v in range(VIEWS):
        live = live | ((index >= v * VIEW_ROWS) & (index < v * VIEW_ROWS + counts[0, v]))
    middle = x[...].astype(F32) + dot(a, w[0], 0, 0)
    normed, scale = normalize(middle)
    low = (normed * gain + bias).astype(BF16)
    out_back = jnp.where(live, g[...].astype(F32), 0.0)
    out_low = out_back.astype(BF16)

    @pl.when(i == 0)
    def _():
        total[...] = jnp.zeros_like(total)
        gain_grad[...] = jnp.zeros_like(gain_grad)
        bias_grad[...] = jnp.zeros_like(bias_grad)
        up_grad[...] = jnp.zeros_like(up_grad)
        down_grad[...] = jnp.zeros_like(down_grad)

    out = middle + vec_row(vec, 4 * D + FF, D)
    normed_back = jnp.zeros((tile, D), F32)
    for j in range(4):
        block = slice(j * D, (j + 1) * D)
        preact = dot(low, w[1 + j]) + vec_row(vec, 4 * D + j * D, D)
        phi = 0.5 + 0.5 * lax.erf(preact * 0.7071067811865476)
        active = (preact * phi).astype(BF16)
        slope = phi + preact * (jnp.exp(-0.5 * preact * preact) * 0.3989422804014327)
        out = out + dot(active, w[5 + j])
        preact_back = (dot(out_low, w[5 + j], 1, 1) * slope).astype(BF16)
        normed_back = normed_back + dot(preact_back, w[1 + j], 1, 1)
        total[1 + j] += dot(low, preact_back, 0, 0)
        total[5 + j] += dot(active, out_low, 0, 0)
        up_grad[:, block] += jnp.sum(preact_back.astype(F32), axis=0, keepdims=True)
    layer_out[...] = jnp.where(live, out, 0.0).astype(BF16)
    back = out_back + norm_back(normed_back, gain, normed, scale)
    middle_back[...] = back
    branch = back.astype(BF16)
    back_t[...] = dot(w[0], branch, 1, 1).astype(BF16)
    total[0] += dot(a, branch)
    gain_grad[...] += jnp.sum(normed_back * normed, axis=0, keepdims=True)
    bias_grad[...] += jnp.sum(normed_back, axis=0, keepdims=True)
    down_grad[...] += jnp.sum(out_back, axis=0, keepdims=True)

    @pl.when(i == steps - 1)
    def _():
        grads[...] = total[...].astype(BF16)


def dense(counts, att_t, x, g, vec, units, tile=640):
    rows = pl.BlockSpec((tile, D), lambda i: (i, 0))
    columns = pl.BlockSpec((D, tile), lambda i: (0, i))
    return pl.pallas_call(
        functools.partial(dense_kernel, tile=tile),
        grid=(ROWS // tile,),
        in_specs=[smem(), columns, rows, rows, vmem(), vmem()],
        out_specs=[
            rows,
            rows,
            columns,
            pl.BlockSpec((9, D, D), lambda i: (0, 0, 0)),
            pl.BlockSpec((1, D), lambda i: (0, 0)),
            pl.BlockSpec((1, D), lambda i: (0, 0)),
            pl.BlockSpec((1, FF), lambda i: (0, 0)),
            pl.BlockSpec((1, D), lambda i: (0, 0)),
        ],
        out_shape=[
            jax.ShapeDtypeStruct((ROWS, D), BF16),
            jax.ShapeDtypeStruct((ROWS, D), F32),
            jax.ShapeDtypeStruct((D, ROWS), BF16),
            jax.ShapeDtypeStruct((9, D, D), BF16),
            jax.ShapeDtypeStruct((1, D), F32),
            jax.ShapeDtypeStruct((1, D), F32),
            jax.ShapeDtypeStruct((1, FF), F32),
            jax.ShapeDtypeStruct((1, D), F32),
        ],
        scratch_shapes=[pltpu.VMEM((9, D, D), F32)],
        compiler_params=pltpu.CompilerParams(vmem_limit_bytes=VMEM_LIMIT),
    )(counts, att_t, x, g, vec, units)


def backward_kernel(probs, inverse, keyed, v_t, back_t, q_t, att_t, query_back, key_back, value_back):
    row = lax.broadcasted_iota(jnp.int32, (128, ROWS), 0)
    lane = lax.broadcasted_iota(jnp.int32, (KEYS, 128), 1)
    ones = jnp.where(lane < 2, 1.0, 0.0).astype(BF16)
    value = jnp.concatenate([v_t[...].astype(F32).T.astype(BF16), ones], axis=1)
    key_t = keyed[:, 0:128].astype(F32).T.astype(BF16)
    back = back_t[...].astype(F32)
    product = back * att_t[...].astype(F32)
    query = q_t[...].astype(F32)
    key_total = jnp.zeros((KEYS, 128), F32)
    value_total = jnp.zeros((KEYS, 128), F32)
    for h in range(2):
        half = slice(h * 64, (h + 1) * 64)
        inv = inverse[0, h : h + 1, :]
        delta = jnp.sum(product[half], axis=0, keepdims=True) * inv
        high = delta.astype(BF16).astype(F32)
        mine = (row >= 64 * h) & (row < 64 * h + 64)
        scaled = jnp.where(mine, back * inv, 0.0)
        tail = jnp.where(row == 0, -high, jnp.where(row == 1, high - delta, 0.0))
        right = jnp.concatenate([scaled.astype(BF16), tail.astype(BF16)], axis=0)
        low = probs[h]
        score_back = low * dot(value, right).astype(BF16)
        query_back[half, :] = (dot(key_t[half], score_back) * 0.125).astype(BF16)
        key_total += dot(score_back, jnp.where(mine, query, 0.0).T.astype(BF16))
        value_total += dot(low, scaled.T.astype(BF16))
    key_back[...] = key_total.astype(BF16)
    value_back[...] = value_total.astype(BF16)


def attention_backward(probs, inverse, keyed, v_t, back_t, q_t, att_t):
    return pl.pallas_call(
        backward_kernel,
        grid=(4,),
        in_specs=[
            pl.BlockSpec((2, KEYS, ROWS), lambda i: (i, 0, 0)),
            pl.BlockSpec((1, 2, ROWS), lambda i: (i, 0, 0)),
            pl.BlockSpec((None, KEYS, 256), lambda i: (i, 0, 0)),
            pl.BlockSpec((128, KEYS), lambda i: (i, 0)),
            pl.BlockSpec((128, ROWS), lambda i: (i, 0)),
            pl.BlockSpec((128, ROWS), lambda i: (i, 0)),
            pl.BlockSpec((128, ROWS), lambda i: (i, 0)),
        ],
        out_specs=[
            pl.BlockSpec((128, ROWS), lambda i: (i, 0)),
            pl.BlockSpec((KEYS, 128), lambda i: (0, i)),
            pl.BlockSpec((KEYS, 128), lambda i: (0, i)),
        ],
        out_shape=[
            jax.ShapeDtypeStruct((D, ROWS), BF16),
            jax.ShapeDtypeStruct((KEYS, D), BF16),
            jax.ShapeDtypeStruct((KEYS, D), BF16),
        ],
        compiler_params=pltpu.CompilerParams(vmem_limit_bytes=VMEM_LIMIT),
    )(probs, inverse, keyed, v_t, back_t, q_t, att_t)


def project_kernel(
    x, text_t, vec, w, middle_back, query_back, key_back, value_back, text_key, text_value,
    patch_grad, grads, gain_grad, bias_grad, text_grad_t, total
):
    i = pl.program_id(0)
    steps = pl.num_programs(0)
    gain, bias = vec_row(vec, 0, D), vec_row(vec, D, D)

    @pl.when(i == 0)
    def _():
        live = lax.broadcasted_iota(jnp.int32, (TEXT, 1), 0) < LANG
        normed, scale = normalize(text_t[...].astype(F32).T)
        low_t = jnp.where(live, normed * gain + bias, 0.0).T.astype(BF16)
        k, v = text_key[...], text_value[...]
        back = dot(k, w[1], 1, 1) + dot(v, w[2], 1, 1)
        text_grad_t[...] = norm_back(back, gain, normed, scale).T.astype(BF16)
        gain_grad[...] = jnp.sum(back * normed, axis=0, keepdims=True)
        bias_grad[...] = jnp.sum(back, axis=0, keepdims=True)
        total[0] = jnp.zeros((D, D), F32)
        total[1] = dot(low_t, k)
        total[2] = dot(low_t, v)

    normed, scale = normalize(x[...].astype(F32))
    low_t = (normed * gain + bias).T.astype(BF16)
    q, k, v = query_back[...], key_back[...], value_back[...]
    back = dot(q, w[0], 0, 1) + dot(k, w[1], 1, 1) + dot(v, w[2], 1, 1)
    patch_grad[...] = middle_back[...] + norm_back(back, gain, normed, scale)
    total[0] += dot(low_t, q, 1, 1)
    total[1] += dot(low_t, k)
    total[2] += dot(low_t, v)
    gain_grad[...] += jnp.sum(back * normed, axis=0, keepdims=True)
    bias_grad[...] += jnp.sum(back, axis=0, keepdims=True)

    @pl.when(i == steps - 1)
    def _():
        grads[...] = total[...].astype(BF16)


def project_back(x, text_t, vec, units, middle_back, query_back, key_back, value_back, tile=640):
    rows = pl.BlockSpec((tile, D), lambda i: (i, 0))
    text_rows = pl.BlockSpec((TEXT, D), lambda i: (ROWS // TEXT, 0))
    return pl.pallas_call(
        project_kernel,
        grid=(ROWS // tile,),
        in_specs=[
            rows,
            vmem(),
            vmem(),
            pl.BlockSpec((3, D, D), lambda i: (0, 0, 0)),
            rows,
            pl.BlockSpec((D, tile), lambda i: (0, i)),
            rows,
            rows,
            text_rows,
            text_rows,
        ],
        out_specs=[
            rows,
            pl.BlockSpec((3, D, D), lambda i: (0, 0, 0)),
            pl.BlockSpec((1, D), lambda i: (0, 0)),
            pl.BlockSpec((1, D), lambda i: (0, 0)),
            pl.BlockSpec((D, TEXT), lambda i: (0, 0)),
        ],
        out_shape=[
            jax.ShapeDtypeStruct((ROWS, D), F32),
            jax.ShapeDtypeStruct((3, D, D), BF16),
            jax.ShapeDtypeStruct((1, D), F32),
            jax.ShapeDtypeStruct((1, D), F32),
            jax.ShapeDtypeStruct((D, TEXT), BF16),
        ],
        scratch_shapes=[pltpu.VMEM((3, D, D), F32)],
        compiler_params=pltpu.CompilerParams(vmem_limit_bytes=VMEM_LIMIT),
    )(
        x, text_t, vec, units, middle_back, query_back, key_back, value_back, key_back, value_back
    )


def add(a, b):
    return (a.astype(F32) + b.astype(F32)).astype(BF16)


class Reducer:
    def __init__(self, name, links, at, source, kept, bufs):
        self.name, self.links, self.at = name, links, at
        self.source, self.kept = source, kept
        (self.c_buf, self.ya_buf, self.xb_buf, self.xa_buf, self.yb_buf, self.z_sum,
         self.z_buf) = bufs

    def start(self, stage, head):
        self.links.start(*self.copies(stage, head))

    def copies(self, stage, head):
        return (self.name, str(head), stage), lambda: self.parts(stage, head)

    def parts(self, stage, head):
        w, n, z, x, y, c = self.at
        to_z, to_x, to_y, to_c = partners(*self.at)
        whole = slice(None)
        if stage == 0:
            return [(self.source.at[(*head, whole, whole, whole, 1 - c)], self.c_buf.at[head], to_c)]
        elif stage == 1:
            return [
                (self.kept.at[(*head, pl.ds(0, 2), whole, 1 - y)], self.ya_buf.at[head], to_y),
                (self.kept.at[(*head, pl.ds(2, 2), 1 - x)], self.xb_buf.at[head], to_x),
            ]
        elif stage == 2:
            return [
                (self.kept.at[(*head, pl.ds(0, 2), 1 - x, y)], self.xa_buf.at[head], to_x),
                (self.kept.at[(*head, pl.ds(2, 2), x, 1 - y)], self.yb_buf.at[head], to_y),
            ]
        else:
            return [
                (self.z_sum.at[(*head, lax.rem(z + k, 4))], self.z_buf.at[(k - 1, *head)],
                 to_z[k - 1])
                for k in range(1, 4)
            ]
    def finish(self, stage, head):
        w, n, z, x, y, c = self.at
        self.links.wait(*self.copies(stage, head))
        kept = self.kept
        low, high = pl.ds(0, 2), pl.ds(2, 2)
        whole = slice(None)
        if stage == 0:
            kept[head] = add(kept[head], self.c_buf[head])
        elif stage == 1:
            a = (*head, low, whole, y)
            b = (*head, high, x)
            kept[a] = add(kept[a], self.ya_buf[head])
            kept[b] = add(kept[b], self.xb_buf[head])
        elif stage == 2:
            self.z_sum[(*head, low)] = add(kept[(*head, low, x, y)], self.xa_buf[head])
            self.z_sum[(*head, high)] = add(kept[(*head, high, x, y)], self.yb_buf[head])
        else:
            total = self.z_sum[(*head, z)].astype(F32)
            for k in range(3):
                total = total + self.z_buf[(k, *head)].astype(F32)
            return total.astype(BF16)


def reducer_scratch(lead, columns):
    shapes = [(4, 2, 2), (2, 2), (2, 2), (2,), (2,), (4,)]
    bufs = [pltpu.VMEM((*lead, *shape, 16, columns), BF16) for shape in shapes]
    return bufs + [pltpu.VMEM((3, *lead, 16, columns), BF16)]


def back_kernel(
    owners, probs, inverse, keyed, v_t, back_t, q_t, att_t, normed_t, rest, w_first, text_t, x,
    middle_back, vec, gain_two, bias_two, up, down,
    patch_grad, slot_grad, text_out, vec_out,
    rest_kept, *scratch
):
    rest_bufs, scratch = scratch[:7], scratch[7:]
    first_bufs, scratch = scratch[:7], scratch[7:]
    (first_all, first_kept, red, s_buf, r_buf, text_part, text_buf, v_own, vw_buf, v_sum, vn_buf,
     query_back, key_back, value_back, x_buf, middle_buf, patch_buf, send, recv, local) = scratch
    i = pl.program_id(0)
    at = place()
    w, n, z, sx, y, c = at
    links = Links(send, recv)
    whole = slice(None)
    rest_red = Reducer("rest", links, at, rest, rest_kept, rest_bufs)
    first_red = Reducer("first", links, at, first_all, first_kept, first_bufs)
    groups = [(pl.ds(3 * g, 3),) for g in range(3)]
    chunks = [(p, whole) for p in range(4)]
    read = [
        pltpu.make_async_copy(
            rest.at[:, :, :, :, c], rest_kept, local.at[0]
        ),
        pltpu.make_async_copy(x, x_buf, local.at[1]),
        pltpu.make_async_copy(middle_back, middle_buf, local.at[2]),
    ]
    write = pltpu.make_async_copy(patch_buf, patch_grad, local.at[3])

    def step_first(p, stage):
        total = first_red.finish(stage, chunks[p])
        if stage < 3:
            first_red.start(stage + 1, chunks[p])
        else:
            red[0:3, :, p * 128 : (p + 1) * 128] = total

    def step_rest(g, stage):
        total = rest_red.finish(stage, groups[g])
        if stage < 3:
            rest_red.start(stage + 1, groups[g])
        else:
            red[3 + 3 * g : 6 + 3 * g] = total

    plan = {
        0: [], 1: [(0, 0)], 2: [(1, 0)], 3: [(2, 0), (0, 1)], 4: [(1, 1)], 5: [(2, 1), (0, 2)],
        6: [(1, 2)], 7: [(2, 2), (0, 3)],
    }
    first_plan = {3: [(0, 0)], 4: [(0, 1)], 5: [(1, 0), (0, 2)], 6: [(1, 1), (0, 3)],
                  7: [(2, 0), (1, 2)]}

    def comm(t):
        if t == 0:
            for copy in read:
                copy.start()
            peers = narrow_peers(w, n) + wide_peers(w, n)
            greet(peers)
            offset = 4 * 2
            for piece in (gain_two, bias_two, up, down):
                for r in range(piece.shape[1] // 128):
                    v_own[offset : offset + 1, :] = piece[:, r * 128 : (r + 1) * 128]
                    offset += 1
            greeted(peers)
            for g in range(3):
                rest_red.start(0, groups[g])
            read[0].wait()
        for g, s in plan[t]:
            step_rest(g, s)
        for p, s in first_plan.get(t, []):
            step_first(p, s)

    row = lax.broadcasted_iota(jnp.int32, (128, ROWS), 0)
    lane = lax.broadcasted_iota(jnp.int32, (KEYS, 128), 1)
    ones = jnp.where(lane < 2, 1.0, 0.0).astype(BF16)
    value = jnp.concatenate([v_t[...].astype(F32).T.astype(BF16), ones], axis=1)
    key_t = keyed[...].astype(F32).T.astype(BF16)
    back = back_t[...].astype(F32)
    product = back * att_t[...].astype(F32)
    query = q_t[...].astype(F32)
    key_total = jnp.zeros((KEYS, 128), F32)
    value_total = jnp.zeros((KEYS, 128), F32)
    query_parts = []
    for h in range(2):
        for k in range(4):
            pl.when(i == k)(functools.partial(comm, 2 * k + h))
        half = slice(h * 64, (h + 1) * 64)
        inv = inverse[0, h : h + 1, :]
        delta = jnp.sum(product[half], axis=0, keepdims=True) * inv
        high = delta.astype(BF16).astype(F32)
        mine = (row >= 64 * h) & (row < 64 * h + 64)
        scaled = jnp.where(mine, back * inv, 0.0)
        tail = jnp.where(row == 0, -high, jnp.where(row == 1, high - delta, 0.0))
        right = jnp.concatenate([scaled.astype(BF16), tail.astype(BF16)], axis=0)
        low = probs[h]
        score_back = low * dot(value, right).astype(BF16)
        query_parts.append((dot(key_t[half], score_back) * 0.125).astype(BF16))
        key_total += dot(score_back, jnp.where(mine, query, 0.0).T.astype(BF16))
        value_total += dot(low, scaled.T.astype(BF16))
    q_low = jnp.concatenate(query_parts, axis=0)
    k_low = key_total.astype(BF16)
    v_low = value_total.astype(BF16)
    query_back[pl.ds(pl.multiple_of(i * 128, 128), 128), :] = q_low
    pair = pl.ds(pl.multiple_of(i * 128, 128), 128)
    key_back[:, pair] = k_low
    value_back[:, pair] = v_low
    pieces = (4, 2, 2, 2, 16, 128)
    parts = (
        dot(normed_t[:, 0:ROWS], q_low, 1, 1),
        dot(normed_t[...], k_low),
        dot(normed_t[...], v_low),
    )
    for u, part in enumerate(parts):
        first_all[i, u] = part.astype(BF16).reshape(pieces)
        first_kept[i, u] = first_all[i, u, :, :, :, c]
    for k in range(4):
        pl.when(i == k)(lambda p=k: first_red.start(0, chunks[p]))

    @pl.when(i == 3)
    def _():
        gain, bias = vec_row(vec, 0, D), vec_row(vec, D, D)
        w_q, w_k, w_v = [w_first[u].reshape(D, D) for u in range(3)]
        normed, scale = normalize(text_t[...].astype(F32).T)
        text_back = dot(key_back[ROWS:KEYS], w_k, 1, 1) + dot(value_back[ROWS:KEYS], w_v, 1, 1)
        text_part[...] = (
            norm_back(text_back, gain, normed, scale).T.astype(BF16).reshape(8, 64, TEXT)
        )
        text_buf[w] = text_part[w]
        texts = "text", lambda: [
            (text_part.at[peer[0]], text_buf.at[w], peer) for peer in wide_peers(w, n)
        ]
        links.start(*texts)
        gain_grad = jnp.sum(text_back * normed, axis=0, keepdims=True)
        bias_grad = jnp.sum(text_back, axis=0, keepdims=True)

        step_rest(1, 3)
        step_first(2, 1)
        step_first(1, 3)
        step_first(3, 0)
        read[1].wait()
        read[2].wait()
        tile = ROWS // 2
        for t in range(2):
            rows = slice(t * tile, (t + 1) * tile)
            normed, scale = normalize(x_buf[rows].astype(F32))
            projected = (
                dot(query_back[:, rows], w_q, 0, 1)
                + dot(key_back[rows], w_k, 1, 1)
                + dot(value_back[rows], w_v, 1, 1)
            )
            patch_buf[rows] = middle_buf[rows] + norm_back(projected, gain, normed, scale)
            gain_grad = gain_grad + jnp.sum(projected * normed, axis=0, keepdims=True)
            bias_grad = bias_grad + jnp.sum(projected, axis=0, keepdims=True)
            if t == 0:
                step_first(2, 2)
                step_first(3, 1)
        write.start()
        for offset, piece in ((0, gain_grad), (4, bias_grad)):
            for r in range(4):
                v_own[offset + r : offset + r + 1, :] = piece[:, r * 128 : (r + 1) * 128]
        vw_buf[w] = v_own[...]
        wides = "wide", lambda: [(v_own, vw_buf.at[w], peer) for peer in wide_peers(w, n)]
        links.start(*wides)
        step_first(3, 2)
        step_rest(2, 3)
        step_first(2, 3)
        links.wait(*texts)
        total = text_buf[0].astype(F32)
        for k in range(1, 8):
            total = total + text_buf[k].astype(F32)
        text_out[...] = total
        links.wait(*wides)
        total = vw_buf[0]
        for k in range(1, 8):
            total = total + vw_buf[k]
        v_sum[...] = total
        vn_buf[n] = total
        narrows = "narrow", lambda: [(v_sum, vn_buf.at[n], peer) for peer in narrow_peers(w, n)]
        links.start(*narrows)
        owner, rank = unit_ranks(owners)
        step_first(3, 3)
        for q in range(4):
            for s in range(SLOTS):
                unit = jnp.int32(0)
                for u in range(UNITS):
                    unit = unit + jnp.where((owner[u] == q) & (rank[u] == s), u, 0)
                s_buf[q, s] = red[jnp.minimum(unit, UNITS - 1)]
        slots = "slots", lambda: [
            (s_buf.at[peer[1]], r_buf.at[n], peer) for peer in narrow_peers(w, n)
        ]
        links.start(*slots)
        r_buf[n] = s_buf[n]
        links.wait(*narrows)
        vec_out[...] = (vn_buf[0] + vn_buf[1]) + (vn_buf[2] + vn_buf[3])
        links.wait(*slots)
        for q in range(4):
            slot_grad[:, q * 16 : (q + 1) * 16, :] = r_buf[q].astype(F32)
        write.wait()


def back(
    owners, probs, inverse, keyed, v_t, back_t, q_t, att_t, normed_t, rest, w_first, text_t, x,
    middle_back, vec, vecs
):
    hbm = pl.BlockSpec(memory_space=pl.ANY)
    copies = 3 * 8 + 4 * 8 + 7 + 7 + 3 + 3
    bf = lambda *s: pltpu.VMEM(s, BF16)
    return pl.pallas_call(
        back_kernel,
        grid=(4,),
        in_specs=[
            smem(),
            pl.BlockSpec((2, KEYS, ROWS), lambda i: (i, 0, 0)),
            pl.BlockSpec((1, 2, ROWS), lambda i: (i, 0, 0)),
            pl.BlockSpec((None, KEYS, 128), lambda i: (i, 0, 0)),
            pl.BlockSpec((128, KEYS), lambda i: (i, 0)),
            pl.BlockSpec((128, ROWS), lambda i: (i, 0)),
            pl.BlockSpec((128, ROWS), lambda i: (i, 0)),
            pl.BlockSpec((128, ROWS), lambda i: (i, 0)),
            vmem(),
            hbm,
            vmem(),
            vmem(),
            hbm,
            hbm,
            vmem(),
        ]
        + [vmem()] * 4,
        out_specs=[hbm, vmem(), vmem(), vmem()],
        out_shape=[
            jax.ShapeDtypeStruct((ROWS, D), F32),
            jax.ShapeDtypeStruct((SLOTS, 64, D), F32),
            jax.ShapeDtypeStruct((64, TEXT), F32),
            jax.ShapeDtypeStruct((VEC // 128, 128), F32),
        ],
        scratch_shapes=[bf(9, 4, 2, 2, 16, D)]
        + reducer_scratch((9,), D)
        + reducer_scratch((4, 3), 128)
        + [
            bf(4, 3, 4, 2, 2, 2, 16, 128),
            bf(4, 3, 4, 2, 2, 16, 128),
            bf(UNITS, 16, D),
            bf(4, SLOTS, 16, D),
            bf(4, SLOTS, 16, D),
            bf(8, 64, TEXT),
            bf(8, 64, TEXT),
            pltpu.VMEM((VEC // 128, 128), F32),
            pltpu.VMEM((8, VEC // 128, 128), F32),
            pltpu.VMEM((VEC // 128, 128), F32),
            pltpu.VMEM((4, VEC // 128, 128), F32),
            bf(D, ROWS),
            bf(KEYS, D),
            bf(KEYS, D),
            bf(ROWS, D),
            pltpu.VMEM((ROWS, D), F32),
            pltpu.VMEM((ROWS, D), F32),
            pltpu.SemaphoreType.DMA((copies,)),
            pltpu.SemaphoreType.DMA((copies,)),
            pltpu.SemaphoreType.DMA((4,)),
        ],
        compiler_params=pltpu.CompilerParams(
            collective_id=2, has_side_effects=True, vmem_limit_bytes=63 * 2**20
        ),
    )(
        owners, probs, inverse, keyed, v_t, back_t, q_t, att_t, normed_t,
        rest.reshape(9, 4, 2, 2, 2, 16, D), w_first, text_t, x, middle_back, vec, *vecs,
    )


def reduce_all(owners, rest, first, text, vecs):
    vec = lax.psum(jnp.concatenate(vecs, axis=1), ("wide", "narrow"))
    text_sum = lax.psum_scatter(text.astype(F32), "wide", scatter_dimension=0, tiled=True)
    all_units = jnp.concatenate([first, rest], axis=0).astype(F32)
    rows = lax.psum_scatter(all_units, "wide", scatter_dimension=1, tiled=True)
    same = owners[:, None] == owners[None, :]
    ids = jnp.arange(UNITS)
    rank = jnp.sum((same & (ids[None, :] < ids[:, None])).astype(jnp.int32), axis=1)
    pick = (owners[None, None, :] == jnp.arange(lax.axis_size("narrow"))[:, None, None]) & (
        rank[None, None, :] == jnp.arange(SLOTS)[None, :, None]
    )
    terms = jnp.einsum("nsu,urc->nsrc", pick.astype(F32), rows, precision=lax.Precision.HIGHEST)
    slots = lax.psum_scatter(terms, "narrow", scatter_dimension=0, tiled=True)
    return slots[0], text_sum, vec.reshape(VEC // 128, 128)


def adam(master, moment_one, moment_two, averaged, gradient, rate):
    moment_one = beta_one * moment_one + (1.0 - beta_one) * gradient
    moment_two = beta_two * moment_two + (1.0 - beta_two) * gradient * gradient
    mean_hat = moment_one / (1.0 - beta_one**STEP)
    second_hat = moment_two / (1.0 - beta_two**STEP)
    master = master - rate * (
        mean_hat / (jnp.sqrt(second_hat) + adam_eps) + weight_decay * master
    )
    averaged = average_keep * averaged + (1.0 - average_keep) * master
    return master, moment_one, moment_two, averaged


def unit_rates():
    blocks = FF // D
    fans = [2 * D // 3, 2 * D // 3, D, D // 64] + [D] * blocks + [FF] * blocks
    return [float(fan) ** -0.5 for fan in fans]


def update_kernel(
    owners, grad, masters, first, second, average, text_t, vec_grad, vec, vec_first, vec_second,
    vec_average,
    new_masters, new_first, new_second, new_average, new_copies, text_grad,
    vec_new_value, vec_new_first, vec_new_second, vec_new_average,
):
    s = pl.program_id(0)
    n = lax.axis_index("narrow")
    owner, rank = unit_ranks(owners)
    rate, filled = jnp.float32(0.0), jnp.int32(0)
    for u, value in enumerate(unit_rates()):
        match = (owner[u] == n) & (rank[u] == s)
        rate = rate + jnp.where(match, jnp.float32(value), jnp.float32(0.0))
        filled = filled + match.astype(jnp.int32)
    state = adam(masters[0, 0], first[0, 0], second[0, 0], average[0, 0], grad[0], rate)
    keep = jnp.broadcast_to(filled, state[0].shape) > 0
    state = [jnp.where(keep, part, 0.0) for part in state]
    for ref, part in zip((new_masters, new_first, new_second, new_average), state):
        ref[0, 0] = part
    new_copies[0, 0] = state[0].astype(BF16)

    @pl.when(s == 0)
    def _():
        text_grad[0] = text_t[:, 0:LANG]
        state = adam(
            vec[...], vec_first[...], vec_second[...], vec_average[...], vec_grad[...], vector_rate
        )
        for ref, part in zip(
            (vec_new_value, vec_new_first, vec_new_second, vec_new_average), state
        ):
            ref[...] = part


def update(owners, grad, masters, first, second, average, text_t, vec_grad, vec, v1, v2, va):
    rows = masters.shape[2]
    state = jax.ShapeDtypeStruct(masters.shape, F32)
    vector = jax.ShapeDtypeStruct(vec.shape, F32)
    slot = pl.BlockSpec((1, 1, rows, D), lambda s: (0, s, 0, 0))
    vec_spec = pl.BlockSpec(vec.shape, lambda s: (0, 0))
    return pl.pallas_call(
        update_kernel,
        grid=(SLOTS,),
        out_shape=[state] * 4
        + [
            jax.ShapeDtypeStruct(masters.shape, BF16),
            jax.ShapeDtypeStruct((1, text_t.shape[0], LANG), F32),
        ]
        + [vector] * 4,
        in_specs=[smem(), pl.BlockSpec((1, rows, D), lambda s: (s, 0, 0))]
        + [slot] * 4
        + [pl.BlockSpec(text_t.shape, lambda s: (0, 0))]
        + [vec_spec] * 5,
        out_specs=[slot] * 5
        + [pl.BlockSpec((1, text_t.shape[0], LANG), lambda s: (0, 0, 0))]
        + [vec_spec] * 4,
        compiler_params=pltpu.CompilerParams(vmem_limit_bytes=VMEM_LIMIT),
    )(owners, grad, masters, first, second, average, text_t, vec_grad, vec, v1, v2, va)


def local(
    patches, text_tokens, view_counts, out_grad, owners, masters, first_moment, second_moment,
    average, vec_value, vec_first, vec_second, vec_average,
):
    vec, v1, v2, va = [
        part.reshape(VEC // 128, 128) for part in (vec_value, vec_first, vec_second, vec_average)
    ]
    text_in = jnp.swapaxes(text_tokens, 1, 2)
    if lax.axis_size("wide") == 8 and lax.axis_size("narrow") == 4:
        (att_t, probs, inverse, q_t, keyed, v_t, normed_t, w_first, w_rest, text_t) = front(
            owners, view_counts, masters, text_in, patches, vec
        )
        layer_out, middle_back, back_t, rest, *vecs = dense(
            view_counts, att_t, patches, out_grad, vec, w_rest.reshape(9, D, D)
        )
        patch_grad, slot_grad, text_sum, vec_grad = back(
            owners, probs, inverse, keyed, v_t, back_t, q_t, att_t, normed_t, rest, w_first,
            text_t.reshape(D, TEXT), patches, middle_back, vec, vecs,
        )
    else:
        units, text_t = gather(owners, masters, text_in)
        att_t, probs, inverse, q_t, keyed, v_t = attention_forward(
            view_counts, patches, text_t, vec, units
        )
        layer_out, middle_back, back_t, rest, *vecs = dense(
            view_counts, att_t, patches, out_grad, vec, units[3:]
        )
        query_back, key_back, value_back = attention_backward(
            probs, inverse, keyed, v_t, back_t, q_t, att_t
        )
        patch_grad, first, gain_one, bias_one, text_part = project_back(
            patches, text_t, vec, units, middle_back, query_back, key_back, value_back
        )
        slot_grad, text_sum, vec_grad = reduce_all(
            owners, rest, first, text_part, (gain_one, bias_one, *vecs)
        )
    outs = update(
        owners, slot_grad, masters, first_moment, second_moment, average, text_sum, vec_grad, vec,
        v1, v2, va,
    )
    new_masters, new_first, new_second, new_average, new_copies, text_grad = outs[:6]
    vectors = [part.reshape(VEC) for part in outs[6:]]
    return (
        layer_out, patch_grad, jnp.swapaxes(text_grad, 1, 2), new_masters, new_first, new_second,
        new_average, new_copies, *vectors,
    )


def solution(mesh):
    rows = P(("wide", "narrow"), None)
    state = P("narrow", None, "wide", None)
    text = P("narrow", None, "wide")
    in_specs = (rows, text, rows, rows, P(), state, state, state, state, P(), P(), P(), P())
    out_specs = (rows, rows, text, state, state, state, state, state, P(), P(), P(), P())
    return jax.shard_map(local, mesh=mesh, in_specs=in_specs, out_specs=out_specs, check_vma=False)
```

```python
import functools

import jax
import jax.numpy as jnp
from jax import lax
from jax.experimental import pallas as pl
from jax.experimental.pallas import tpu as pltpu
from jax.sharding import PartitionSpec as P

D = 512
HEADS = 8
FF = 2048
VIEWS = 5
VIEW_ROWS = 256
ROWS = VIEWS * VIEW_ROWS
LANG = 77
TEXT = 128
KEYS = ROWS + TEXT
STEP = 5
UNITS = 12
SLOTS = 4
VEC = 5 * D + FF
F32 = jnp.float32
BF16 = jnp.bfloat16
MESH = pl.DeviceIdType.MESH
NEG = -1e30

norm_eps = 1e-05
beta_one = 0.5
beta_two = 0.5
adam_eps = 1e-08
weight_decay = 0.1
average_keep = 0.75
vector_rate = 0.25
VMEM_LIMIT = 60 * 2**20


def dot(left, right, left_dim=1, right_dim=0):
    return lax.dot_general(
        left, right, (((left_dim,), (right_dim,)), ((), ())), preferred_element_type=F32
    )


def vmem():
    return pl.BlockSpec(memory_space=pltpu.VMEM)


def smem():
    return pl.BlockSpec(memory_space=pltpu.SMEM)


def vec_row(vec, start, size):
    first = start // 128
    return jnp.concatenate([vec[first + r : first + r + 1, :] for r in range(size // 128)], axis=1)


def unit_ranks(owners_ref):
    owner = [owners_ref[u] for u in range(UNITS)]
    rank = []
    for u in range(UNITS):
        total = jnp.int32(0)
        for v in range(u):
            total = total + (owner[v] == owner[u]).astype(jnp.int32)
        rank.append(jnp.minimum(total, SLOTS - 1))
    return owner, rank


def normalize(values):
    center = values - jnp.mean(values, axis=-1, keepdims=True)
    spread = jnp.mean(center * center, axis=-1, keepdims=True)
    scale = lax.rsqrt(spread + norm_eps)
    return center * scale, scale


def norm_back(grads, gain, normed, scale):
    e = grads * gain
    return scale * (
        e
        - jnp.mean(e, axis=-1, keepdims=True)
        - normed * jnp.mean(e * normed, axis=-1, keepdims=True)
    )


def place():
    w = lax.axis_index("wide")
    n = lax.axis_index("narrow")
    return w, n, w // 2, w % 2, n // 2, n % 2


def narrow_peers(at):
    w, n = at[:2]
    return [(w, lax.rem(n + k, 4)) for k in range(1, 4)]


def wide_peers(at):
    w, n = at[:2]
    return [(lax.rem(w + k, 8), n) for k in range(1, 8)]


def chip_peers(at):
    w, n, z, x, y, c = at
    peers = []
    for k in range(1, 16):
        chip = lax.rem(z * 4 + x * 2 + y + k, 16)
        cz, cx, cy = chip // 4, (chip // 2) % 2, chip % 2
        peers.append((cz, cx, cy, (cz * 2 + cx, cy * 2 + c)))
    return peers


def all_peers(at):
    w, n, z, x, y, c = at
    return narrow_peers(at) + wide_peers(at) + [
        (lax.rem(w + k, 8), (1 - y) * 2 + c) for k in range(1, 8)
    ]


def greet(peers):
    barrier = pltpu.get_barrier_semaphore()
    for peer in peers:
        pl.semaphore_signal(barrier, inc=1, device_id=peer, device_id_type=MESH)


def greeted(peers):
    pl.semaphore_wait(pltpu.get_barrier_semaphore(), len(peers))


class Links:
    def __init__(self, send, recv):
        self.send, self.recv, self.slots = send, recv, {}

    def copies(self, key, parts):
        made = []
        for k, (src, dst, device) in enumerate(parts()):
            slot = self.slots.setdefault((key, k), len(self.slots))
            made.append(
                pltpu.make_async_remote_copy(
                    src_ref=src,
                    dst_ref=dst,
                    send_sem=self.send.at[slot],
                    recv_sem=self.recv.at[slot],
                    device_id=device,
                    device_id_type=MESH,
                )
            )
        return made

    def start(self, key, parts):
        for copy in self.copies(key, parts):
            copy.start()

    def wait(self, key, parts):
        for copy in self.copies(key, parts):
            copy.wait()


def partners(w, n, z, x, y, c):
    to_z = [(lax.rem(z + k, 4) * 2 + x, n) for k in range(1, 4)]
    return to_z, (z * 2 + 1 - x, n), (w, (1 - y) * 2 + c), (w, y * 2 + 1 - c)


def spread(ref, head, stage, at):
    w, n, z, x, y, c = at
    to_z, to_x, to_y, to_c = partners(*at)
    whole = slice(None)
    if stage == 0:
        parts = [((z, x, y, c), peer) for peer in to_z]
    elif stage == 1:
        parts = [((pl.ds(0, 2), x, y, c), to_x), ((pl.ds(2, 2), x, y, c), to_y)]
    elif stage == 2:
        parts = [((pl.ds(0, 2), whole, y, c), to_y), ((pl.ds(2, 2), x, whole, c), to_x)]
    else:
        parts = [((whole, whole, whole, c), to_c)]
    return [(ref.at[(*head, *part)], ref.at[(*head, *part)], peer) for part, peer in parts]


def add(a, b):
    return (a.astype(F32) + b.astype(F32)).astype(BF16)


class Reducer:
    def __init__(self, links, at, source, bufs):
        self.links, self.at, self.source = links, at, source
        (self.c_buf, self.ya_buf, self.xb_buf, self.xa_buf, self.yb_buf, self.z_sum,
         self.z_buf) = bufs

    def start(self, stage, head):
        self.links.start(*self.copies(stage, head))

    def copies(self, stage, head):
        return ("reduce", str(head), stage), lambda: self.parts(stage, head)

    def parts(self, stage, head):
        w, n, z, x, y, c = self.at
        to_z, to_x, to_y, to_c = partners(*self.at)
        whole, low, high = slice(None), pl.ds(0, 2), pl.ds(2, 2)
        source = self.source
        if stage == 0:
            return [(source.at[(*head, whole, whole, whole, 1 - c)], self.c_buf.at[head], to_c)]
        if stage == 1:
            return [
                (source.at[(*head, low, whole, 1 - y, c)], self.ya_buf.at[head], to_y),
                (source.at[(*head, high, 1 - x, whole, c)], self.xb_buf.at[head], to_x),
            ]
        if stage == 2:
            return [
                (source.at[(*head, low, 1 - x, y, c)], self.xa_buf.at[head], to_x),
                (source.at[(*head, high, x, 1 - y, c)], self.yb_buf.at[head], to_y),
            ]
        return [
            (self.z_sum.at[(*head, lax.rem(z + k, 4))], self.z_buf.at[(k - 1, *head)], to_z[k - 1])
            for k in range(1, 4)
        ]

    def finish(self, stage, head):
        w, n, z, x, y, c = self.at
        self.links.wait(*self.copies(stage, head))
        whole, low, high = slice(None), pl.ds(0, 2), pl.ds(2, 2)
        source = self.source
        if stage == 0:
            own = (*head, whole, whole, whole, c)
            source[own] = add(source[own], self.c_buf[head])
        elif stage == 1:
            a = (*head, low, whole, y, c)
            b = (*head, high, x, whole, c)
            source[a] = add(source[a], self.ya_buf[head])
            source[b] = add(source[b], self.xb_buf[head])
        elif stage == 2:
            self.z_sum[(*head, low)] = add(source[(*head, low, x, y, c)], self.xa_buf[head])
            self.z_sum[(*head, high)] = add(source[(*head, high, x, y, c)], self.yb_buf[head])
        else:
            total = self.z_sum[(*head, z)].astype(F32)
            for k in range(3):
                total = total + self.z_buf[(k, *head)].astype(F32)
            return total.astype(BF16)


PIECES = (4, 2, 2, 2, 16)
KEY_CHUNK = 352
DENSE_PLACE = (8, 0, 2, 4, 6, 1, 3, 5, 7)


def block_kernel(
    owners, counts, masters, text, x, vec, g,
    patch_out, layer_out, probs, slot_grad, text_out, vec_out,
    send_buf, slot_buf, w_first, w_rest, text_buf, q_t, keyed, key_bias, v_t, normed_t,
    text_normed, att_t, inverse, delta, p_buf, g_buf, middle_buf,
    rest_all, c_buf, ya_buf, xb_buf, xa_buf, yb_buf, z_sum, z_buf,
    first_all, first_c, first_d, red, s_buf, r_buf, text_part, text_sum,
    v_own, vw_buf, v_sum, vn_buf, l_own, lw_buf, l_sum, ln_buf,
    query_back, key_back, value_back, value_pair, key_pair_t, send, recv, local
):
    at = place()
    w, n, z, sx, y, c = at
    links = Links(send, recv)
    whole = slice(None)
    peers = all_peers(at)
    gain_one, bias_one = vec_row(vec, 0, D), vec_row(vec, D, D)
    live_text = lax.broadcasted_iota(jnp.int32, (TEXT, 1), 0) < LANG
    read_g = pltpu.make_async_copy(g, g_buf, local.at[2])
    write_layer = pltpu.make_async_copy(g_buf, layer_out, local.at[3])
    write_patch = pltpu.make_async_copy(middle_buf, patch_out, local.at[4])

    greet(peers)
    send_buf[...] = masters[0].reshape(SLOTS, 4, 16, D).astype(BF16)
    text_buf[z, sx] = jnp.zeros((64, TEXT), BF16)
    text_buf[z, sx, :, 0:LANG] = text[0]
    low = (normalize(x[...].astype(F32))[0] * gain_one + bias_one).astype(BF16)
    normed = g_buf
    normed[...] = low
    greeted(peers)
    slots = "slots", lambda: [
        (send_buf.at[:, peer[1]], slot_buf.at[n], peer) for peer in narrow_peers(at)
    ]
    links.start(*slots)
    texts = "text", lambda: [
        (text_buf.at[z, sx], text_buf.at[z, sx], peer) for peer in wide_peers(at)
    ]
    links.start(*texts)
    slot_buf[n] = send_buf[:, n]
    normed_t[:, 0:ROWS] = low.astype(F32).T.astype(BF16)
    owner, rank = unit_ranks(owners)
    links.wait(*slots)
    for u in range(3):
        w_first[u, z, sx, y, c] = slot_buf[owner[u], rank[u]]

    def first(u, s):
        return ("first", u, s), lambda: spread(w_first, (u,), s, at)

    def rest(group, s):
        return ("rest", group, s), lambda: spread(w_rest, (pl.ds(3 * group, 3),), s, at)

    order = (1, 0, 2)
    for u in order:
        links.start(*first(u, 0))
    for k, position in enumerate(DENSE_PLACE):
        w_rest[position, z, sx, y, c] = slot_buf[owner[3 + k], rank[3 + k]]
    for v, live in enumerate(live_column(counts, ROWS)):
        key_bias[v * VIEW_ROWS : (v + 1) * VIEW_ROWS, :] = jnp.broadcast_to(
            jnp.where(live, 0.0, NEG), (VIEW_ROWS, 128)
        ).astype(BF16)
    key_bias[ROWS:KEYS, :] = jnp.broadcast_to(
        jnp.where(live_text, 0.0, NEG), (TEXT, 128)
    ).astype(BF16)
    links.wait(*texts)
    rows = text_buf[...].reshape(D, TEXT).astype(F32).T
    text_low = jnp.where(live_text, normalize(rows)[0] * gain_one + bias_one, 0.0)
    text_normed[...] = text_low.astype(BF16)
    normed_t[:, ROWS:KEYS] = text_low.T.astype(BF16)

    def unit(u):
        return w_first[u].reshape(D, D)

    def project(u):
        if u == 1:
            k = dot(normed[...], unit(1)).astype(BF16)
            t = dot(text_normed[...], unit(1)).astype(BF16)
            for p in range(4):
                pair = slice(p * 128, (p + 1) * 128)
                keyed[p, 0:ROWS] = k[:, pair]
                keyed[p, ROWS:KEYS] = t[:, pair]
        elif u == 0:
            q_t[...] = dot(unit(0), normed[...], 0, 1).astype(BF16) * BF16(0.125)
        else:
            v_t[:, 0:ROWS] = dot(unit(2), normed[...], 0, 1).astype(BF16)
            v_t[:, ROWS:KEYS] = dot(unit(2), text_normed[...], 0, 1).astype(BF16)

    for step in range(3 + 3):
        for s in (3, 2, 1, 0):
            k = step - s
            if not 0 <= k < 3:
                continue
            u = order[k]
            links.wait(*first(u, s))
            if s < 3:
                links.start(*first(u, s + 1))
            if k == 2 and s < 3:
                links.start(*rest((2, 0, 1)[s], 0))
            if s == 3:
                project(u)

    read_g.start()

    gather_plan = {
        0: [(2, 0)], 1: [(0, 0)], 2: [(1, 0), (2, 1)], 3: [(0, 1)], 4: [(1, 1), (2, 2)],
        5: [(0, 2)], 6: [(1, 2), (2, 3)], 7: [(0, 3)],
    }

    def gather_point(t):
        for group, s in gather_plan[t]:
            links.wait(*rest(group, s))
            if s < 3:
                links.start(*rest(group, s + 1))

    row = lax.broadcasted_iota(jnp.int32, (128, ROWS), 0)
    one = jnp.where(row == 0, 1.0, 0.0).astype(BF16)

    def saved(t):
        return pltpu.make_async_copy(p_buf.at[t % 2], probs.at[t], local.at[t % 2])

    @pl.loop(0, HEADS)
    def _(t):
        for k in range(HEADS):
            pl.when(t == k)(functools.partial(gather_point, k))
        pl.when(t > 1)(lambda: saved(t - 2).wait())
        i, h = t // 2, t % 2
        pair_q = q_t[pl.ds(pl.multiple_of(i * 128, 128), 128), :]
        mine = (row >= 64 * h) & (row < 64 * h + 64)
        q = jnp.where(mine, pair_q, jnp.zeros_like(pair_q))
        keys = jnp.concatenate([keyed[i], key_bias[...]], axis=1)
        scores = dot(keys, jnp.concatenate([q, one], axis=0))
        peak = jnp.max(scores, axis=0, keepdims=True)
        total = jnp.zeros((1, ROWS), F32)
        for k in range(0, KEYS, KEY_CHUNK):
            e = jnp.exp(scores[k : k + KEY_CHUNK] - peak)
            total = total + jnp.sum(e, axis=0, keepdims=True)
            p_buf[h, k : k + KEY_CHUNK] = e.astype(BF16)
        head = pl.ds(pl.multiple_of(t * 64, 64), 64)
        mixed = dot(v_t[head, :], p_buf[h])
        inv = 1.0 / total
        att_t[head, :] = (mixed * inv).astype(BF16)
        inverse[t] = inv
        pl.when(t < HEADS - 2)(lambda: saved(t).start())

    links.wait(*rest(1, 3))
    read_g.wait()

    reducer = Reducer(links, at, rest_all, (c_buf, ya_buf, xb_buf, xa_buf, yb_buf, z_sum, z_buf))
    groups = [(pl.ds(2 * j, 2),) for j in range(4)] + [(pl.ds(8, 1),)]

    def step_rest(group, stage):
        total = reducer.finish(stage, groups[group])
        if stage < 3:
            reducer.start(stage + 1, groups[group])
        else:
            red[groups[group]] = total

    def dense_unit(position):
        return w_rest[position].reshape(D, D)

    @pl.when(w >= 0)
    def _():
        gain, bias = vec_row(vec, 2 * D, D), vec_row(vec, 3 * D, D)
        halves = [slice(k * ROWS // 2, (k + 1) * ROWS // 2) for k in range(2)]
        lows, outs = key_back, value_back
        normals, scales, backs, lives = [], [], [], []
        for k, rows in enumerate(halves):
            index = lax.broadcasted_iota(jnp.int32, (ROWS // 2, 1), 0) + k * (ROWS // 2)
            live = jnp.zeros((ROWS // 2, 1), jnp.bool_)
            for v in range(VIEWS):
                live = live | ((index >= v * VIEW_ROWS) & (index < v * VIEW_ROWS + counts[0, v]))
            middle = x[rows].astype(F32) + dot(att_t[:, rows], dense_unit(8), 0, 0)
            normal, scale = normalize(middle)
            middle_buf[rows] = middle + vec_row(vec, 4 * D + FF, D)
            normals.append(normal)
            scales.append(scale)
            lows[rows] = (normal * gain + bias).astype(BF16)
            backs.append(jnp.zeros((ROWS // 2, D), F32))
            lives.append(live)
            outs[rows] = jnp.where(live, g_buf[rows].astype(F32), 0.0).astype(BF16)
        for j in range(4):
            w_up, w_down = dense_unit(2 * j), dense_unit(2 * j + 1)
            up_total, down_total, up_grad = 0.0, 0.0, 0.0
            for k, rows in enumerate(halves):
                preact = dot(lows[rows], w_up) + vec_row(vec, 4 * D + j * D, D)
                phi = 0.5 + 0.5 * lax.erf(preact * 0.7071067811865476)
                active = (preact * phi).astype(BF16)
                slope = phi + preact * (jnp.exp(-0.5 * preact * preact) * 0.3989422804014327)
                middle_buf[rows] += dot(active, w_down)
                preact_back = (dot(outs[rows], w_down, 1, 1) * slope).astype(BF16)
                backs[k] = backs[k] + dot(preact_back, w_up, 1, 1)
                up_total = up_total + dot(lows[rows], preact_back, 0, 0)
                down_total = down_total + dot(active, outs[rows], 0, 0)
                up_grad = up_grad + jnp.sum(preact_back.astype(F32), axis=0, keepdims=True)
            rest_all[2 * j] = up_total.astype(BF16).reshape(*PIECES, D)
            rest_all[2 * j + 1] = down_total.astype(BF16).reshape(*PIECES, D)
            for r in range(4):
                v_own[16 + 4 * j + r : 17 + 4 * j + r, :] = up_grad[:, r * 128 : (r + 1) * 128]
            reducer.start(0, groups[j])
            for s in range(min(j, 3)):
                step_rest(j - 1 - s, s)
        for k, rows in enumerate(halves):
            g_buf[rows] = jnp.where(lives[k], middle_buf[rows], 0.0).astype(BF16)
        write_layer.start()
        out_total, gain_grad, bias_grad, down_grad = 0.0, 0.0, 0.0, 0.0
        for k, rows in enumerate(halves):
            out_back = outs[rows].astype(F32)
            back = out_back + norm_back(backs[k], gain, normals[k], scales[k])
            middle_buf[rows] = back
            branch = back.astype(BF16)
            out_total = out_total + dot(att_t[:, rows], branch)
            back_rows = dot(dense_unit(8), branch, 1, 1).astype(BF16)
            product = back_rows.astype(F32) * att_t[:, rows].astype(F32)
            for h in range(HEADS):
                part = jnp.sum(product[h * 64 : (h + 1) * 64], axis=0, keepdims=True)
                delta[h, :, rows] = part * inverse[h, :, rows]
            att_t[:, rows] = back_rows
            gain_grad = gain_grad + jnp.sum(backs[k] * normals[k], axis=0, keepdims=True)
            bias_grad = bias_grad + jnp.sum(backs[k], axis=0, keepdims=True)
            down_grad = down_grad + jnp.sum(out_back, axis=0, keepdims=True)
        rest_all[8] = out_total.astype(BF16).reshape(*PIECES, D)
        for offset, piece in ((8, gain_grad), (12, bias_grad), (32, down_grad)):
            for r in range(4):
                v_own[offset + r : offset + r + 1, :] = piece[:, r * 128 : (r + 1) * 128]
        v_own[0:8, :] = jnp.zeros((8, 128), F32)

    back_t = att_t

    def chunk_core(p):
        return ("chunk", p, 0), lambda: [
            (first_all.at[p, :, :, :, :, 1 - c], first_c.at[p], (w, y * 2 + 1 - c))
        ]

    chip = z * 4 + sx * 2 + y

    def chunk_chips(p):
        return ("chunk", p, 1), lambda: [
            (first_all.at[p, :, cz, cx, cy, c], first_d.at[p, chip], peer)
            for cz, cx, cy, peer in chip_peers(at)
        ]

    def chunk_middle(p):
        links.wait(*chunk_core(p))
        own = (p, whole, whole, whole, whole, c)
        first_all[own] = add(first_all[own], first_c[p])
        links.start(*chunk_chips(p))
        first_d[p, chip] = first_all[p, :, z, sx, y, c]

    def chunk_end(p):
        links.wait(*chunk_chips(p))
        total = jnp.sum(first_d[p].astype(F32), axis=0).astype(BF16)
        red[9:12, :, p * 128 : (p + 1) * 128] = total

    wides = "wide", lambda: [(v_own, vw_buf.at[w], peer) for peer in wide_peers(at)]
    narrows = "narrow", lambda: [(v_sum, vn_buf.at[n], peer) for peer in narrow_peers(at)]

    def vector_start():
        vw_buf[w] = v_own[...]
        links.start(*wides)

    def vector_middle():
        links.wait(*wides)
        total = vw_buf[0]
        for k in range(1, 8):
            total = total + vw_buf[k]
        v_sum[...] = total
        vn_buf[n] = total
        links.start(*narrows)

    def reduce_point(t):
        for group, s in {
            0: [(1, 2), (2, 1), (3, 0)], 1: [(4, 0)], 2: [(0, 3), (1, 3), (2, 2), (3, 1)],
            3: [(4, 1)], 4: [(2, 3), (3, 2)], 5: [(4, 2)], 6: [(3, 3)], 7: [(4, 3)],
        }[t]:
            step_rest(group, s)
        if t == 0:
            reducer.start(0, groups[4])
            vector_start()
        if t == 3:
            vector_middle()
        if t in (3, 5, 7):
            chunk_middle(3 - (t - 3) // 2)
        if t in (5, 7):
            chunk_end(3 - (t - 5) // 2)

    lane = lax.broadcasted_iota(jnp.int32, (KEYS, 128), 1)
    ones = jnp.where(lane < 2, 1.0, 0.0).astype(BF16)

    def fetched(t):
        return pltpu.make_async_copy(probs.at[t], p_buf.at[t % 2], local.at[t % 2])

    @pl.loop(0, HEADS)
    def _(step):
        for k in range(HEADS):
            pl.when(step == k)(functools.partial(reduce_point, k))
        i, h = 3 - step // 2, step % 2
        t = 2 * i + h
        pl.when(step > 1)(lambda: fetched(t).wait())
        pair = pl.ds(pl.multiple_of(i * 128, 128), 128)
        head = pl.ds(pl.multiple_of(t * 64, 64), 64)

        @pl.when(h == 0)
        def _():
            value_pair[...] = v_t[pair, :].astype(F32).T.astype(BF16)
            key_pair_t[...] = keyed[i].astype(F32).T.astype(BF16)

        back = back_t[pair, :].astype(F32)
        query = q_t[pair, :].astype(F32)
        inv = inverse[t]
        shift = delta[t]
        high = shift.astype(BF16).astype(F32)
        mine = (row >= 64 * h) & (row < 64 * h + 64)
        scaled = jnp.where(mine, back * inv, 0.0)
        tail = jnp.where(row == 0, -high, jnp.where(row == 1, high - shift, 0.0))
        right = jnp.concatenate([scaled.astype(BF16), tail.astype(BF16)], axis=0)
        value_half = dot(p_buf[h], scaled.T.astype(BF16)).astype(BF16)
        value = jnp.concatenate([value_pair[...], ones], axis=1)
        for k in range(0, KEYS, KEY_CHUNK):
            part = dot(value[k : k + KEY_CHUNK], right).astype(BF16)
            p_buf[h, k : k + KEY_CHUNK] = p_buf[h, k : k + KEY_CHUNK] * part
        key_head = key_pair_t[pl.ds(pl.multiple_of(h * 64, 64), 64), :]
        query_back[head, :] = (dot(key_head, p_buf[h]) * 0.125).astype(BF16)
        key_half = dot(p_buf[h], jnp.where(mine, query, 0.0).T.astype(BF16)).astype(BF16)
        pl.when(step < HEADS - 2)(lambda: fetched(t - 2).start())

        @pl.when(h == 0)
        def _():
            key_back[:, pair] = key_half
            value_back[:, pair] = value_half

        @pl.when(h == 1)
        def _():
            key_back[:, pair] += key_half
            value_back[:, pair] += value_half
            part = dot(normed_t[:, 0:ROWS], query_back[pair, :], 1, 1).astype(BF16)
            first_all[i, 0] = part.reshape(*PIECES, 128)
            both = jnp.concatenate([key_back[:, pair], value_back[:, pair]], axis=1)
            part = dot(normed_t[...], both).astype(BF16)
            for u in range(2):
                first_all[i, 1 + u] = part[:, u * 128 : (u + 1) * 128].reshape(*PIECES, 128)

        for k in range(4):
            pl.when(step == 2 * k + 1)(lambda p=3 - k: links.start(*chunk_core(p)))

    @pl.when(w >= 0)
    def _():
        w_q, w_k, w_v = unit(0), unit(1), unit(2)
        normal, scale = normalize(text_buf[...].reshape(D, TEXT).astype(F32).T)
        text_back = dot(key_back[ROWS:KEYS], w_k, 1, 1) + dot(value_back[ROWS:KEYS], w_v, 1, 1)
        text_part[...] = (
            norm_back(text_back, gain_one, normal, scale).T.astype(BF16).reshape(8, 64, TEXT)
        )
        gain_grad = jnp.sum(text_back * normal, axis=0, keepdims=True)
        bias_grad = jnp.sum(text_back, axis=0, keepdims=True)
        text_sum[w] = text_part[w]
        text_parts = "parts", lambda: [
            (text_part.at[peer[0]], text_sum.at[w], peer) for peer in wide_peers(at)
        ]
        chunk_middle(0)
        links.start(*text_parts)
        tile = ROWS // 2
        for t in range(2):
            rows = slice(t * tile, (t + 1) * tile)
            normal, scale = normalize(x[rows].astype(F32))
            projected = (
                dot(query_back[:, rows], w_q, 0, 1)
                + dot(key_back[rows], w_k, 1, 1)
                + dot(value_back[rows], w_v, 1, 1)
            )
            middle_buf[rows] += norm_back(projected, gain_one, normal, scale)
            gain_grad = gain_grad + jnp.sum(projected * normal, axis=0, keepdims=True)
            bias_grad = bias_grad + jnp.sum(projected, axis=0, keepdims=True)
        write_patch.start()
        for r in range(4):
            l_own[r : r + 1, :] = gain_grad[:, r * 128 : (r + 1) * 128]
            l_own[4 + r : 5 + r, :] = bias_grad[:, r * 128 : (r + 1) * 128]
        late_wides = "late wide", lambda: [(l_own, lw_buf.at[w], peer) for peer in wide_peers(at)]
        late_narrows = "late narrow", lambda: [
            (l_sum, ln_buf.at[n], peer) for peer in narrow_peers(at)
        ]
        lw_buf[w] = l_own[...]
        links.start(*late_wides)
        links.wait(*narrows)
        vec_out[...] = (vn_buf[0] + vn_buf[1]) + (vn_buf[2] + vn_buf[3])
        chunk_end(1)
        links.wait(*text_parts)
        text_out[...] = jnp.sum(text_sum[...].astype(F32), axis=0)
        chunk_end(0)
        owner, rank = unit_ranks(owners)
        for q in range(4):
            for s in range(SLOTS):
                spot = jnp.int32(0)
                for u in range(UNITS):
                    position = 9 + u if u < 3 else DENSE_PLACE[u - 3]
                    spot = spot + jnp.where((owner[u] == q) & (rank[u] == s), position, 0)
                s_buf[q, s] = red[jnp.minimum(spot, UNITS - 1)]
        grads = "grads", lambda: [
            (s_buf.at[peer[1]], r_buf.at[n], peer) for peer in narrow_peers(at)
        ]
        links.start(*grads)
        r_buf[n] = s_buf[n]
        links.wait(*late_wides)
        total = lw_buf[0]
        for k in range(1, 8):
            total = total + lw_buf[k]
        l_sum[...] = total
        ln_buf[n] = total
        links.start(*late_narrows)
        links.wait(*grads)
        for q in range(4):
            slot_grad[:, q * 16 : (q + 1) * 16, :] = r_buf[q].astype(F32)
        write_layer.wait()
        write_patch.wait()
        links.wait(*late_narrows)
        vec_out[0:8, :] = (ln_buf[0] + ln_buf[1]) + (ln_buf[2] + ln_buf[3])


def block(owners, counts, masters, text, x, vec, g):
    hbm = pl.BlockSpec(memory_space=pl.ANY)
    copies = 3 + 7 + 24 + 24 + 5 * 8 + 4 * 16 + 7 + 3 + 7 + 7 + 3 + 3
    bf = lambda *s: pltpu.VMEM(s, BF16)
    f32 = lambda *s: pltpu.VMEM(s, F32)
    rows = VEC // 128
    return pl.pallas_call(
        block_kernel,
        in_specs=[smem(), smem(), vmem(), vmem(), vmem(), vmem(), hbm],
        out_specs=[hbm, hbm, hbm, vmem(), vmem(), vmem()],
        out_shape=[
            jax.ShapeDtypeStruct((ROWS, D), F32),
            jax.ShapeDtypeStruct((ROWS, D), BF16),
            jax.ShapeDtypeStruct((6, KEYS, ROWS), BF16),
            jax.ShapeDtypeStruct((SLOTS, 64, D), F32),
            jax.ShapeDtypeStruct((64, TEXT), F32),
            jax.ShapeDtypeStruct((rows, 128), F32),
        ],
        scratch_shapes=[
            bf(SLOTS, 4, 16, D),
            bf(4, SLOTS, 16, D),
            bf(3, *PIECES, D),
            bf(9, *PIECES, D),
            bf(4, 2, 64, TEXT),
            bf(D, ROWS),
            bf(4, KEYS, 128),
            bf(KEYS, 128),
            bf(D, KEYS),
            bf(D, KEYS),
            bf(TEXT, D),
            bf(D, ROWS),
            f32(HEADS, 1, ROWS),
            f32(HEADS, 1, ROWS),
            bf(2, KEYS, ROWS),
            bf(ROWS, D),
            f32(ROWS, D),
            bf(9, *PIECES, D),
            bf(9, 4, 2, 2, 16, D),
            bf(9, 2, 2, 16, D),
            bf(9, 2, 2, 16, D),
            bf(9, 2, 16, D),
            bf(9, 2, 16, D),
            bf(9, 4, 16, D),
            bf(3, 9, 16, D),
            bf(4, 3, *PIECES, 128),
            bf(4, 3, 4, 2, 2, 16, 128),
            bf(4, 16, 3, 16, 128),
            bf(UNITS, 16, D),
            bf(4, SLOTS, 16, D),
            bf(4, SLOTS, 16, D),
            bf(8, 64, TEXT),
            bf(8, 64, TEXT),
            f32(rows, 128),
            f32(8, rows, 128),
            f32(rows, 128),
            f32(4, rows, 128),
            f32(8, 128),
            f32(8, 8, 128),
            f32(8, 128),
            f32(4, 8, 128),
            bf(D, ROWS),
            bf(KEYS, D),
            bf(KEYS, D),
            bf(KEYS, 128),
            bf(128, KEYS),
            pltpu.SemaphoreType.DMA((copies,)),
            pltpu.SemaphoreType.DMA((copies,)),
            pltpu.SemaphoreType.DMA((5,)),
        ],
        compiler_params=pltpu.CompilerParams(
            collective_id=1, has_side_effects=True, vmem_limit_bytes=63 * 2**20
        ),
    )(owners, counts, masters, text, x, vec, g)


def gather(owners, masters, text_t):
    packed = lax.all_gather(masters.astype(BF16), "wide", axis=2, tiled=True)
    packed = lax.all_gather(packed, "narrow", axis=0, tiled=True)
    same = owners[:, None] == owners[None, :]
    ids = jnp.arange(UNITS)
    rank = jnp.sum((same & (ids[None, :] < ids[:, None])).astype(jnp.int32), axis=1)
    units = jnp.take(packed.reshape(-1, D, D), owners * SLOTS + rank, axis=0)
    rows = lax.all_gather(text_t, "wide", axis=1, tiled=True)[0]
    return units, jnp.pad(rows, ((0, 0), (0, TEXT - LANG)))


def live_column(counts, rows):
    index = lax.broadcasted_iota(jnp.int32, (VIEW_ROWS, 1), 0)
    return [(index < counts[0, v]) for v in range(rows // VIEW_ROWS)]


def forward_kernel(
    counts, x, text_t, vec, w, att_t, probs, inverse, q_t, keyed, v_t, normed, text_normed
):
    i = pl.program_id(0)

    @pl.when(i == 0)
    def _():
        gain, bias = vec_row(vec, 0, D), vec_row(vec, D, D)
        normed[...] = (normalize(x[...].astype(F32))[0] * gain + bias).astype(BF16)
        rows = text_t[...].astype(F32).T
        live_text = lax.broadcasted_iota(jnp.int32, (TEXT, 1), 0) < LANG
        text_normed[...] = jnp.where(
            live_text, normalize(rows)[0] * gain + bias, 0.0
        ).astype(BF16)
        q_t[...] = dot(w[0], normed[...], 0, 1).astype(BF16) * BF16(0.125)
        v_t[:, 0:ROWS] = dot(w[2], normed[...], 0, 1).astype(BF16)
        v_t[:, ROWS:KEYS] = dot(w[2], text_normed[...], 0, 1).astype(BF16)
        for p in range(4):
            pair = slice(p * 128, (p + 1) * 128)
            keyed[p, 0:ROWS, 0:128] = dot(normed[...], w[1, :, pair]).astype(BF16)
            keyed[p, ROWS:KEYS, 0:128] = dot(text_normed[...], w[1, :, pair]).astype(BF16)
            for v, live in enumerate(live_column(counts, ROWS)):
                keyed[p, v * VIEW_ROWS : (v + 1) * VIEW_ROWS, 128:256] = jnp.broadcast_to(
                    jnp.where(live, 0.0, NEG), (VIEW_ROWS, 128)
                ).astype(BF16)
            keyed[p, ROWS:KEYS, 128:256] = jnp.broadcast_to(
                jnp.where(live_text, 0.0, NEG), (TEXT, 128)
            ).astype(BF16)

    row = lax.broadcasted_iota(jnp.int32, (128, ROWS), 0)
    one = jnp.where(row == 0, 1.0, 0.0).astype(BF16)
    pair_q = q_t[pl.ds(pl.multiple_of(i * 128, 128), 128), :]
    for h in range(2):
        mine = (row >= 64 * h) & (row < 64 * h + 64)
        q = jnp.where(mine, pair_q, jnp.zeros_like(pair_q))
        scores = dot(keyed[i], jnp.concatenate([q, one], axis=0))
        peak = jnp.max(scores, axis=0, keepdims=True)
        e = jnp.exp(scores - peak)
        total = jnp.sum(e, axis=0, keepdims=True)
        low = e.astype(BF16)
        probs[h] = low
        mixed = dot(v_t[pl.ds(pl.multiple_of(i * 128 + h * 64, 64), 64), :], low)
        inv = 1.0 / total
        att_t[h * 64 : (h + 1) * 64, :] = (mixed * inv).astype(BF16)
        inverse[0, h : h + 1, :] = inv


def attention_forward(counts, x, text_t, vec, units):
    return pl.pallas_call(
        forward_kernel,
        grid=(4,),
        in_specs=[smem(), vmem(), vmem(), vmem(), pl.BlockSpec((3, D, D), lambda i: (0, 0, 0))],
        out_specs=[
            pl.BlockSpec((128, ROWS), lambda i: (i, 0)),
            pl.BlockSpec((2, KEYS, ROWS), lambda i: (i, 0, 0)),
            pl.BlockSpec((1, 2, ROWS), lambda i: (i, 0, 0)),
            pl.BlockSpec((D, ROWS), lambda i: (0, 0)),
            pl.BlockSpec((4, KEYS, 256), lambda i: (0, 0, 0)),
            pl.BlockSpec((D, KEYS), lambda i: (0, 0)),
        ],
        out_shape=[
            jax.ShapeDtypeStruct((D, ROWS), BF16),
            jax.ShapeDtypeStruct((HEADS, KEYS, ROWS), BF16),
            jax.ShapeDtypeStruct((4, 2, ROWS), F32),
            jax.ShapeDtypeStruct((D, ROWS), BF16),
            jax.ShapeDtypeStruct((4, KEYS, 256), BF16),
            jax.ShapeDtypeStruct((D, KEYS), BF16),
        ],
        scratch_shapes=[pltpu.VMEM((ROWS, D), BF16), pltpu.VMEM((TEXT, D), BF16)],
        compiler_params=pltpu.CompilerParams(vmem_limit_bytes=VMEM_LIMIT),
    )(counts, x, text_t, vec, units)


def dense_kernel(
    counts, att_t, x, g, vec, w,
    layer_out, middle_back, back_t, grads, gain_grad, bias_grad, up_grad, down_grad,
    total, *, tile
):
    i = pl.program_id(0)
    steps = pl.num_programs(0)
    gain, bias = vec_row(vec, 2 * D, D), vec_row(vec, 3 * D, D)
    a = att_t[...]
    index = lax.broadcasted_iota(jnp.int32, (tile, 1), 0) + i * tile
    live = jnp.zeros((tile, 1), jnp.bool_)
    for v in range(VIEWS):
        live = live | ((index >= v * VIEW_ROWS) & (index < v * VIEW_ROWS + counts[0, v]))
    middle = x[...].astype(F32) + dot(a, w[0], 0, 0)
    normed, scale = normalize(middle)
    low = (normed * gain + bias).astype(BF16)
    out_back = jnp.where(live, g[...].astype(F32), 0.0)
    out_low = out_back.astype(BF16)

    @pl.when(i == 0)
    def _():
        total[...] = jnp.zeros_like(total)
        gain_grad[...] = jnp.zeros_like(gain_grad)
        bias_grad[...] = jnp.zeros_like(bias_grad)
        up_grad[...] = jnp.zeros_like(up_grad)
        down_grad[...] = jnp.zeros_like(down_grad)

    out = middle + vec_row(vec, 4 * D + FF, D)
    normed_back = jnp.zeros((tile, D), F32)
    for j in range(4):
        block = slice(j * D, (j + 1) * D)
        preact = dot(low, w[1 + j]) + vec_row(vec, 4 * D + j * D, D)
        phi = 0.5 + 0.5 * lax.erf(preact * 0.7071067811865476)
        active = (preact * phi).astype(BF16)
        slope = phi + preact * (jnp.exp(-0.5 * preact * preact) * 0.3989422804014327)
        out = out + dot(active, w[5 + j])
        preact_back = (dot(out_low, w[5 + j], 1, 1) * slope).astype(BF16)
        normed_back = normed_back + dot(preact_back, w[1 + j], 1, 1)
        total[1 + j] += dot(low, preact_back, 0, 0)
        total[5 + j] += dot(active, out_low, 0, 0)
        up_grad[:, block] += jnp.sum(preact_back.astype(F32), axis=0, keepdims=True)
    layer_out[...] = jnp.where(live, out, 0.0).astype(BF16)
    back = out_back + norm_back(normed_back, gain, normed, scale)
    middle_back[...] = back
    branch = back.astype(BF16)
    back_t[...] = dot(w[0], branch, 1, 1).astype(BF16)
    total[0] += dot(a, branch)
    gain_grad[...] += jnp.sum(normed_back * normed, axis=0, keepdims=True)
    bias_grad[...] += jnp.sum(normed_back, axis=0, keepdims=True)
    down_grad[...] += jnp.sum(out_back, axis=0, keepdims=True)

    @pl.when(i == steps - 1)
    def _():
        grads[...] = total[...].astype(BF16)


def dense(counts, att_t, x, g, vec, units, tile=640):
    rows = pl.BlockSpec((tile, D), lambda i: (i, 0))
    columns = pl.BlockSpec((D, tile), lambda i: (0, i))
    return pl.pallas_call(
        functools.partial(dense_kernel, tile=tile),
        grid=(ROWS // tile,),
        in_specs=[smem(), columns, rows, rows, vmem(), vmem()],
        out_specs=[
            rows,
            rows,
            columns,
            pl.BlockSpec((9, D, D), lambda i: (0, 0, 0)),
            pl.BlockSpec((1, D), lambda i: (0, 0)),
            pl.BlockSpec((1, D), lambda i: (0, 0)),
            pl.BlockSpec((1, FF), lambda i: (0, 0)),
            pl.BlockSpec((1, D), lambda i: (0, 0)),
        ],
        out_shape=[
            jax.ShapeDtypeStruct((ROWS, D), BF16),
            jax.ShapeDtypeStruct((ROWS, D), F32),
            jax.ShapeDtypeStruct((D, ROWS), BF16),
            jax.ShapeDtypeStruct((9, D, D), BF16),
            jax.ShapeDtypeStruct((1, D), F32),
            jax.ShapeDtypeStruct((1, D), F32),
            jax.ShapeDtypeStruct((1, FF), F32),
            jax.ShapeDtypeStruct((1, D), F32),
        ],
        scratch_shapes=[pltpu.VMEM((9, D, D), F32)],
        compiler_params=pltpu.CompilerParams(vmem_limit_bytes=VMEM_LIMIT),
    )(counts, att_t, x, g, vec, units)


def backward_kernel(probs, inverse, keyed, v_t, back_t, q_t, att_t, query_back, key_back, value_back):
    row = lax.broadcasted_iota(jnp.int32, (128, ROWS), 0)
    lane = lax.broadcasted_iota(jnp.int32, (KEYS, 128), 1)
    ones = jnp.where(lane < 2, 1.0, 0.0).astype(BF16)
    value = jnp.concatenate([v_t[...].astype(F32).T.astype(BF16), ones], axis=1)
    key_t = keyed[:, 0:128].astype(F32).T.astype(BF16)
    back = back_t[...].astype(F32)
    product = back * att_t[...].astype(F32)
    query = q_t[...].astype(F32)
    key_total = jnp.zeros((KEYS, 128), F32)
    value_total = jnp.zeros((KEYS, 128), F32)
    for h in range(2):
        half = slice(h * 64, (h + 1) * 64)
        inv = inverse[0, h : h + 1, :]
        delta = jnp.sum(product[half], axis=0, keepdims=True) * inv
        high = delta.astype(BF16).astype(F32)
        mine = (row >= 64 * h) & (row < 64 * h + 64)
        scaled = jnp.where(mine, back * inv, 0.0)
        tail = jnp.where(row == 0, -high, jnp.where(row == 1, high - delta, 0.0))
        right = jnp.concatenate([scaled.astype(BF16), tail.astype(BF16)], axis=0)
        low = probs[h]
        score_back = low * dot(value, right).astype(BF16)
        query_back[half, :] = (dot(key_t[half], score_back) * 0.125).astype(BF16)
        key_total += dot(score_back, jnp.where(mine, query, 0.0).T.astype(BF16))
        value_total += dot(low, scaled.T.astype(BF16))
    key_back[...] = key_total.astype(BF16)
    value_back[...] = value_total.astype(BF16)


def attention_backward(probs, inverse, keyed, v_t, back_t, q_t, att_t):
    return pl.pallas_call(
        backward_kernel,
        grid=(4,),
        in_specs=[
            pl.BlockSpec((2, KEYS, ROWS), lambda i: (i, 0, 0)),
            pl.BlockSpec((1, 2, ROWS), lambda i: (i, 0, 0)),
            pl.BlockSpec((None, KEYS, 256), lambda i: (i, 0, 0)),
            pl.BlockSpec((128, KEYS), lambda i: (i, 0)),
            pl.BlockSpec((128, ROWS), lambda i: (i, 0)),
            pl.BlockSpec((128, ROWS), lambda i: (i, 0)),
            pl.BlockSpec((128, ROWS), lambda i: (i, 0)),
        ],
        out_specs=[
            pl.BlockSpec((128, ROWS), lambda i: (i, 0)),
            pl.BlockSpec((KEYS, 128), lambda i: (0, i)),
            pl.BlockSpec((KEYS, 128), lambda i: (0, i)),
        ],
        out_shape=[
            jax.ShapeDtypeStruct((D, ROWS), BF16),
            jax.ShapeDtypeStruct((KEYS, D), BF16),
            jax.ShapeDtypeStruct((KEYS, D), BF16),
        ],
        compiler_params=pltpu.CompilerParams(vmem_limit_bytes=VMEM_LIMIT),
    )(probs, inverse, keyed, v_t, back_t, q_t, att_t)


def project_kernel(
    x, text_t, vec, w, middle_back, query_back, key_back, value_back, text_key, text_value,
    patch_grad, grads, gain_grad, bias_grad, text_grad_t, total
):
    i = pl.program_id(0)
    steps = pl.num_programs(0)
    gain, bias = vec_row(vec, 0, D), vec_row(vec, D, D)

    @pl.when(i == 0)
    def _():
        live = lax.broadcasted_iota(jnp.int32, (TEXT, 1), 0) < LANG
        normed, scale = normalize(text_t[...].astype(F32).T)
        low_t = jnp.where(live, normed * gain + bias, 0.0).T.astype(BF16)
        k, v = text_key[...], text_value[...]
        back = dot(k, w[1], 1, 1) + dot(v, w[2], 1, 1)
        text_grad_t[...] = norm_back(back, gain, normed, scale).T.astype(BF16)
        gain_grad[...] = jnp.sum(back * normed, axis=0, keepdims=True)
        bias_grad[...] = jnp.sum(back, axis=0, keepdims=True)
        total[0] = jnp.zeros((D, D), F32)
        total[1] = dot(low_t, k)
        total[2] = dot(low_t, v)

    normed, scale = normalize(x[...].astype(F32))
    low_t = (normed * gain + bias).T.astype(BF16)
    q, k, v = query_back[...], key_back[...], value_back[...]
    back = dot(q, w[0], 0, 1) + dot(k, w[1], 1, 1) + dot(v, w[2], 1, 1)
    patch_grad[...] = middle_back[...] + norm_back(back, gain, normed, scale)
    total[0] += dot(low_t, q, 1, 1)
    total[1] += dot(low_t, k)
    total[2] += dot(low_t, v)
    gain_grad[...] += jnp.sum(back * normed, axis=0, keepdims=True)
    bias_grad[...] += jnp.sum(back, axis=0, keepdims=True)

    @pl.when(i == steps - 1)
    def _():
        grads[...] = total[...].astype(BF16)


def project_back(x, text_t, vec, units, middle_back, query_back, key_back, value_back, tile=640):
    rows = pl.BlockSpec((tile, D), lambda i: (i, 0))
    text_rows = pl.BlockSpec((TEXT, D), lambda i: (ROWS // TEXT, 0))
    return pl.pallas_call(
        project_kernel,
        grid=(ROWS // tile,),
        in_specs=[
            rows,
            vmem(),
            vmem(),
            pl.BlockSpec((3, D, D), lambda i: (0, 0, 0)),
            rows,
            pl.BlockSpec((D, tile), lambda i: (0, i)),
            rows,
            rows,
            text_rows,
            text_rows,
        ],
        out_specs=[
            rows,
            pl.BlockSpec((3, D, D), lambda i: (0, 0, 0)),
            pl.BlockSpec((1, D), lambda i: (0, 0)),
            pl.BlockSpec((1, D), lambda i: (0, 0)),
            pl.BlockSpec((D, TEXT), lambda i: (0, 0)),
        ],
        out_shape=[
            jax.ShapeDtypeStruct((ROWS, D), F32),
            jax.ShapeDtypeStruct((3, D, D), BF16),
            jax.ShapeDtypeStruct((1, D), F32),
            jax.ShapeDtypeStruct((1, D), F32),
            jax.ShapeDtypeStruct((D, TEXT), BF16),
        ],
        scratch_shapes=[pltpu.VMEM((3, D, D), F32)],
        compiler_params=pltpu.CompilerParams(vmem_limit_bytes=VMEM_LIMIT),
    )(
        x, text_t, vec, units, middle_back, query_back, key_back, value_back, key_back, value_back
    )


def reduce_all(owners, rest, first, text, vecs):
    vec = lax.psum(jnp.concatenate(vecs, axis=1), ("wide", "narrow"))
    text_sum = lax.psum_scatter(text.astype(F32), "wide", scatter_dimension=0, tiled=True)
    all_units = jnp.concatenate([first, rest], axis=0).astype(F32)
    rows = lax.psum_scatter(all_units, "wide", scatter_dimension=1, tiled=True)
    same = owners[:, None] == owners[None, :]
    ids = jnp.arange(UNITS)
    rank = jnp.sum((same & (ids[None, :] < ids[:, None])).astype(jnp.int32), axis=1)
    pick = (owners[None, None, :] == jnp.arange(lax.axis_size("narrow"))[:, None, None]) & (
        rank[None, None, :] == jnp.arange(SLOTS)[None, :, None]
    )
    terms = jnp.einsum("nsu,urc->nsrc", pick.astype(F32), rows, precision=lax.Precision.HIGHEST)
    slots = lax.psum_scatter(terms, "narrow", scatter_dimension=0, tiled=True)
    return slots[0], text_sum, vec.reshape(VEC // 128, 128)


def adam(master, moment_one, moment_two, averaged, gradient, rate):
    moment_one = beta_one * moment_one + (1.0 - beta_one) * gradient
    moment_two = beta_two * moment_two + (1.0 - beta_two) * gradient * gradient
    mean_hat = moment_one / (1.0 - beta_one**STEP)
    second_hat = moment_two / (1.0 - beta_two**STEP)
    master = master - rate * (
        mean_hat / (jnp.sqrt(second_hat) + adam_eps) + weight_decay * master
    )
    averaged = average_keep * averaged + (1.0 - average_keep) * master
    return master, moment_one, moment_two, averaged


def unit_rates():
    blocks = FF // D
    fans = [2 * D // 3, 2 * D // 3, D, D // 64] + [D] * blocks + [FF] * blocks
    return [float(fan) ** -0.5 for fan in fans]


def update_kernel(
    owners, grad, masters, first, second, average, text_t, vec_grad, vec, vec_first, vec_second,
    vec_average, patch_in, layer_in,
    new_masters, new_first, new_second, new_average, new_copies, text_grad,
    vec_new_value, vec_new_first, vec_new_second, vec_new_average, patch_out, layer_out, local
):
    s = pl.program_id(0)
    handed = [
        pltpu.make_async_copy(patch_in, patch_out, local.at[0]),
        pltpu.make_async_copy(layer_in, layer_out, local.at[1]),
    ]

    @pl.when(s == 0)
    def _():
        for copy in handed:
            copy.start()

    n = lax.axis_index("narrow")
    owner, rank = unit_ranks(owners)
    rate, filled = jnp.float32(0.0), jnp.int32(0)
    for u, value in enumerate(unit_rates()):
        match = (owner[u] == n) & (rank[u] == s)
        rate = rate + jnp.where(match, jnp.float32(value), jnp.float32(0.0))
        filled = filled + match.astype(jnp.int32)
    state = adam(masters[0, 0], first[0, 0], second[0, 0], average[0, 0], grad[0], rate)
    keep = jnp.broadcast_to(filled, state[0].shape) > 0
    state = [jnp.where(keep, part, 0.0) for part in state]
    for ref, part in zip((new_masters, new_first, new_second, new_average), state):
        ref[0, 0] = part
    new_copies[0, 0] = state[0].astype(BF16)

    @pl.when(s == 0)
    def _():
        text_grad[0] = text_t[:, 0:LANG]
        state = adam(
            vec[...], vec_first[...], vec_second[...], vec_average[...], vec_grad[...], vector_rate
        )
        for ref, part in zip(
            (vec_new_value, vec_new_first, vec_new_second, vec_new_average), state
        ):
            ref[...] = part

    @pl.when(s == SLOTS - 1)
    def _():
        for copy in handed:
            copy.wait()


def update(
    owners, grad, masters, first, second, average, text_t, vec_grad, vec, v1, v2, va, patch, layer
):
    rows = masters.shape[2]
    state = jax.ShapeDtypeStruct(masters.shape, F32)
    vector = jax.ShapeDtypeStruct(vec.shape, F32)
    slot = pl.BlockSpec((1, 1, rows, D), lambda s: (0, s, 0, 0))
    vec_spec = pl.BlockSpec(vec.shape, lambda s: (0, 0))
    return pl.pallas_call(
        update_kernel,
        grid=(SLOTS,),
        out_shape=[state] * 4
        + [
            jax.ShapeDtypeStruct(masters.shape, BF16),
            jax.ShapeDtypeStruct((1, text_t.shape[0], LANG), F32),
        ]
        + [vector] * 4
        + [jax.ShapeDtypeStruct(patch.shape, F32), jax.ShapeDtypeStruct(layer.shape, BF16)],
        in_specs=[smem(), pl.BlockSpec((1, rows, D), lambda s: (s, 0, 0))]
        + [slot] * 4
        + [pl.BlockSpec(text_t.shape, lambda s: (0, 0))]
        + [vec_spec] * 5
        + [pl.BlockSpec(memory_space=pl.ANY)] * 2,
        out_specs=[slot] * 5
        + [pl.BlockSpec((1, text_t.shape[0], LANG), lambda s: (0, 0, 0))]
        + [vec_spec] * 4
        + [pl.BlockSpec(memory_space=pl.ANY)] * 2,
        scratch_shapes=[pltpu.SemaphoreType.DMA((2,))],
        compiler_params=pltpu.CompilerParams(vmem_limit_bytes=VMEM_LIMIT),
    )(
        owners, grad, masters, first, second, average, text_t, vec_grad, vec, v1, v2, va, patch, layer
    )


def local(
    patches, text_tokens, view_counts, out_grad, owners, masters, first_moment, second_moment,
    average, vec_value, vec_first, vec_second, vec_average,
):
    vec, v1, v2, va = [
        part.reshape(VEC // 128, 128) for part in (vec_value, vec_first, vec_second, vec_average)
    ]
    text_in = jnp.swapaxes(text_tokens, 1, 2)
    if lax.axis_size("wide") == 8 and lax.axis_size("narrow") == 4:
        patch_grad, layer_out, _, slot_grad, text_sum, vec_grad = block(
            owners, view_counts, masters, text_in, patches, vec, out_grad
        )
    else:
        units, text_t = gather(owners, masters, text_in)
        att_t, probs, inverse, q_t, keyed, v_t = attention_forward(
            view_counts, patches, text_t, vec, units
        )
        layer_out, middle_back, back_t, rest, *vecs = dense(
            view_counts, att_t, patches, out_grad, vec, units[3:]
        )
        query_back, key_back, value_back = attention_backward(
            probs, inverse, keyed, v_t, back_t, q_t, att_t
        )
        patch_grad, first, gain_one, bias_one, text_part = project_back(
            patches, text_t, vec, units, middle_back, query_back, key_back, value_back
        )
        slot_grad, text_sum, vec_grad = reduce_all(
            owners, rest, first, text_part, (gain_one, bias_one, *vecs)
        )
    outs = update(
        owners, slot_grad, masters, first_moment, second_moment, average, text_sum, vec_grad, vec,
        v1, v2, va, patch_grad, layer_out,
    )
    new_masters, new_first, new_second, new_average, new_copies, text_grad = outs[:6]
    vectors = [part.reshape(VEC) for part in outs[6:10]]
    patch_grad, layer_out = outs[10:]
    return (
        layer_out, patch_grad, jnp.swapaxes(text_grad, 1, 2), new_masters, new_first, new_second,
        new_average, new_copies, *vectors,
    )


def solution(mesh):
    rows = P(("wide", "narrow"), None)
    state = P("narrow", None, "wide", None)
    text = P("narrow", None, "wide")
    in_specs = (rows, text, rows, rows, P(), state, state, state, state, P(), P(), P(), P())
    out_specs = (rows, rows, text, state, state, state, state, state, P(), P(), P(), P())
    return jax.shard_map(local, mesh=mesh, in_specs=in_specs, out_specs=out_specs, check_vma=False)
```

```python
import functools

import jax
import jax.numpy as jnp
from jax import lax
from jax.experimental import pallas as pl
from jax.experimental.pallas import tpu as pltpu
from jax.sharding import PartitionSpec as P

D = 512
HEADS = 8
FF = 2048
VIEWS = 5
VIEW_ROWS = 256
ROWS = VIEWS * VIEW_ROWS
LANG = 77
TEXT = 128
KEYS = ROWS + TEXT
STEP = 5
UNITS = 12
SLOTS = 4
VEC = 5 * D + FF
F32 = jnp.float32
BF16 = jnp.bfloat16
MESH = pl.DeviceIdType.MESH
NEG = -1e30

norm_eps = 1e-05
beta_one = 0.5
beta_two = 0.5
adam_eps = 1e-08
weight_decay = 0.1
average_keep = 0.75
vector_rate = 0.25
VMEM_LIMIT = 60 * 2**20


def dot(left, right, left_dim=1, right_dim=0):
    return lax.dot_general(
        left, right, (((left_dim,), (right_dim,)), ((), ())), preferred_element_type=F32
    )


def vmem():
    return pl.BlockSpec(memory_space=pltpu.VMEM)


def smem():
    return pl.BlockSpec(memory_space=pltpu.SMEM)


def vec_row(vec, start, size):
    first = start // 128
    return jnp.concatenate([vec[first + r : first + r + 1, :] for r in range(size // 128)], axis=1)


def unit_ranks(owners_ref):
    owner = [owners_ref[u] for u in range(UNITS)]
    rank = []
    for u in range(UNITS):
        total = jnp.int32(0)
        for v in range(u):
            total = total + (owner[v] == owner[u]).astype(jnp.int32)
        rank.append(jnp.minimum(total, SLOTS - 1))
    return owner, rank


def normalize(values):
    center = values - jnp.mean(values, axis=-1, keepdims=True)
    spread = jnp.mean(center * center, axis=-1, keepdims=True)
    scale = lax.rsqrt(spread + norm_eps)
    return center * scale, scale


def norm_back(grads, gain, normed, scale):
    e = grads * gain
    return scale * (
        e
        - jnp.mean(e, axis=-1, keepdims=True)
        - normed * jnp.mean(e * normed, axis=-1, keepdims=True)
    )


def place():
    w = lax.axis_index("wide")
    n = lax.axis_index("narrow")
    return w, n, w // 2, w % 2, n // 2, n % 2


def narrow_peers(at):
    w, n = at[:2]
    return [(w, lax.rem(n + k, 4)) for k in range(1, 4)]


def wide_peers(at):
    w, n = at[:2]
    return [(lax.rem(w + k, 8), n) for k in range(1, 8)]


def chip_peers(at):
    w, n, z, x, y, c = at
    peers = []
    for k in range(1, 16):
        chip = lax.rem(z * 4 + x * 2 + y + k, 16)
        cz, cx, cy = chip // 4, (chip // 2) % 2, chip % 2
        peers.append((cz, cx, cy, (cz * 2 + cx, cy * 2 + c)))
    return peers


def all_peers(at):
    w, n, z, x, y, c = at
    return narrow_peers(at) + wide_peers(at) + [
        (lax.rem(w + k, 8), (1 - y) * 2 + c) for k in range(1, 8)
    ]


def greet(peers):
    barrier = pltpu.get_barrier_semaphore()
    for peer in peers:
        pl.semaphore_signal(barrier, inc=1, device_id=peer, device_id_type=MESH)


def greeted(peers):
    pl.semaphore_wait(pltpu.get_barrier_semaphore(), len(peers))


class Links:
    def __init__(self, send, recv):
        self.send, self.recv, self.slots = send, recv, {}

    def copies(self, key, parts):
        made = []
        for k, (src, dst, device) in enumerate(parts()):
            slot = self.slots.setdefault((key, k), len(self.slots))
            made.append(
                pltpu.make_async_remote_copy(
                    src_ref=src,
                    dst_ref=dst,
                    send_sem=self.send.at[slot],
                    recv_sem=self.recv.at[slot],
                    device_id=device,
                    device_id_type=MESH,
                )
            )
        return made

    def start(self, key, parts):
        for copy in self.copies(key, parts):
            copy.start()

    def wait(self, key, parts):
        for copy in self.copies(key, parts):
            copy.wait()


def partners(w, n, z, x, y, c):
    to_z = [(lax.rem(z + k, 4) * 2 + x, n) for k in range(1, 4)]
    return to_z, (z * 2 + 1 - x, n), (w, (1 - y) * 2 + c), (w, y * 2 + 1 - c)


def spread(ref, head, stage, at):
    w, n, z, x, y, c = at
    to_z, to_x, to_y, to_c = partners(*at)
    whole = slice(None)
    if stage == 0:
        parts = [((z, x, y, c), peer) for peer in to_z]
    elif stage == 1:
        parts = [((pl.ds(0, 2), x, y, c), to_x), ((pl.ds(2, 2), x, y, c), to_y)]
    elif stage == 2:
        parts = [((pl.ds(0, 2), whole, y, c), to_y), ((pl.ds(2, 2), x, whole, c), to_x)]
    else:
        parts = [((whole, whole, whole, c), to_c)]
    return [(ref.at[(*head, *part)], ref.at[(*head, *part)], peer) for part, peer in parts]


def add(a, b):
    return (a.astype(F32) + b.astype(F32)).astype(BF16)


class Reducer:
    def __init__(self, links, at, source, bufs):
        self.links, self.at, self.source = links, at, source
        (self.c_buf, self.ya_buf, self.xb_buf, self.xa_buf, self.yb_buf, self.z_sum,
         self.z_buf) = bufs

    def start(self, stage, head):
        self.links.start(*self.copies(stage, head))

    def copies(self, stage, head):
        return ("reduce", str(head), stage), lambda: self.parts(stage, head)

    def parts(self, stage, head):
        w, n, z, x, y, c = self.at
        to_z, to_x, to_y, to_c = partners(*self.at)
        whole, low, high = slice(None), pl.ds(0, 2), pl.ds(2, 2)
        source = self.source
        if stage == 0:
            return [(source.at[(*head, whole, whole, whole, 1 - c)], self.c_buf.at[head], to_c)]
        if stage == 1:
            return [
                (source.at[(*head, low, whole, 1 - y, c)], self.ya_buf.at[head], to_y),
                (source.at[(*head, high, 1 - x, whole, c)], self.xb_buf.at[head], to_x),
            ]
        if stage == 2:
            return [
                (source.at[(*head, low, 1 - x, y, c)], self.xa_buf.at[head], to_x),
                (source.at[(*head, high, x, 1 - y, c)], self.yb_buf.at[head], to_y),
            ]
        return [
            (self.z_sum.at[(*head, lax.rem(z + k, 4))], self.z_buf.at[(k - 1, *head)], to_z[k - 1])
            for k in range(1, 4)
        ]

    def finish(self, stage, head):
        w, n, z, x, y, c = self.at
        self.links.wait(*self.copies(stage, head))
        whole, low, high = slice(None), pl.ds(0, 2), pl.ds(2, 2)
        source = self.source
        if stage == 0:
            own = (*head, whole, whole, whole, c)
            source[own] = add(source[own], self.c_buf[head])
        elif stage == 1:
            a = (*head, low, whole, y, c)
            b = (*head, high, x, whole, c)
            source[a] = add(source[a], self.ya_buf[head])
            source[b] = add(source[b], self.xb_buf[head])
        elif stage == 2:
            self.z_sum[(*head, low)] = add(source[(*head, low, x, y, c)], self.xa_buf[head])
            self.z_sum[(*head, high)] = add(source[(*head, high, x, y, c)], self.yb_buf[head])
        else:
            total = self.z_sum[(*head, z)].astype(F32)
            for k in range(3):
                total = total + self.z_buf[(k, *head)].astype(F32)
            return total.astype(BF16)


PIECES = (4, 2, 2, 2, 16)
KEY_PARTS = ((0, 512), (512, 1024), (1024, 1408))
DENSE_PLACE = (8, 0, 2, 4, 6, 1, 3, 5, 7)


def block_kernel(
    owners, counts, masters, text, x, vec, g,
    patch_out, layer_out, probs, slot_grad, text_out, vec_out,
    send_buf, slot_buf, w_first, w_rest, text_buf, q_t, keyed, key_bias, v_t, normed_t,
    text_normed, att_t, inverse, delta, p_buf, g_buf, middle_buf,
    rest_all, c_buf, ya_buf, xb_buf, xa_buf, yb_buf, z_sum, z_buf,
    first_all, first_c, first_d, red, s_buf, r_buf, text_part, text_sum,
    v_own, vw_buf, v_sum, vn_buf, l_own, lw_buf, l_sum, ln_buf,
    query_back, key_back, value_back, value_pair, key_pair_t, send, recv, local
):
    at = place()
    w, n, z, sx, y, c = at
    links = Links(send, recv)
    whole = slice(None)
    peers = all_peers(at)
    gain_one, bias_one = vec_row(vec, 0, D), vec_row(vec, D, D)
    live_text = lax.broadcasted_iota(jnp.int32, (TEXT, 1), 0) < LANG
    read_g = pltpu.make_async_copy(g, g_buf, local.at[2])
    write_layer = pltpu.make_async_copy(g_buf, layer_out, local.at[3])
    write_patch = pltpu.make_async_copy(middle_buf, patch_out, local.at[4])

    greet(peers)
    send_buf[...] = masters[0].reshape(SLOTS, 4, 16, D).astype(BF16)
    text_buf[z, sx] = jnp.zeros((64, TEXT), BF16)
    text_buf[z, sx, :, 0:LANG] = text[0]
    low = (normalize(x[...].astype(F32))[0] * gain_one + bias_one).astype(BF16)
    normed = g_buf
    normed[...] = low
    greeted(peers)
    slots = "slots", lambda: [
        (send_buf.at[:, peer[1]], slot_buf.at[n], peer) for peer in narrow_peers(at)
    ]
    links.start(*slots)
    texts = "text", lambda: [
        (text_buf.at[z, sx], text_buf.at[z, sx], peer) for peer in wide_peers(at)
    ]
    links.start(*texts)
    slot_buf[n] = send_buf[:, n]
    normed_t[:, 0:ROWS] = low.astype(F32).T.astype(BF16)
    owner, rank = unit_ranks(owners)
    links.wait(*slots)
    for u in range(3):
        w_first[u, z, sx, y, c] = slot_buf[owner[u], rank[u]]

    def first(u, s):
        return ("first", u, s), lambda: spread(w_first, (u,), s, at)

    def rest(group, s):
        return ("rest", group, s), lambda: spread(w_rest, (pl.ds(3 * group, 3),), s, at)

    order = (1, 0, 2)
    for u in order:
        links.start(*first(u, 0))
    for k, position in enumerate(DENSE_PLACE):
        w_rest[position, z, sx, y, c] = slot_buf[owner[3 + k], rank[3 + k]]
    for v, live in enumerate(live_column(counts, ROWS)):
        key_bias[v * VIEW_ROWS : (v + 1) * VIEW_ROWS, :] = jnp.broadcast_to(
            jnp.where(live, 0.0, NEG), (VIEW_ROWS, 128)
        ).astype(BF16)
    key_bias[ROWS:KEYS, :] = jnp.broadcast_to(
        jnp.where(live_text, 0.0, NEG), (TEXT, 128)
    ).astype(BF16)
    links.wait(*texts)
    rows = text_buf[...].reshape(D, TEXT).astype(F32).T
    text_low = jnp.where(live_text, normalize(rows)[0] * gain_one + bias_one, 0.0)
    text_normed[...] = text_low.astype(BF16)
    normed_t[:, ROWS:KEYS] = text_low.T.astype(BF16)

    def unit(u):
        return w_first[u].reshape(D, D)

    def project(u):
        if u == 1:
            k = dot(normed[...], unit(1)).astype(BF16)
            t = dot(text_normed[...], unit(1)).astype(BF16)
            for p in range(4):
                pair = slice(p * 128, (p + 1) * 128)
                keyed[p, 0:ROWS] = k[:, pair]
                keyed[p, ROWS:KEYS] = t[:, pair]
        elif u == 0:
            q_t[...] = dot(unit(0), normed[...], 0, 1).astype(BF16) * BF16(0.125)
        else:
            v_t[:, 0:ROWS] = dot(unit(2), normed[...], 0, 1).astype(BF16)
            v_t[:, ROWS:KEYS] = dot(unit(2), text_normed[...], 0, 1).astype(BF16)

    for step in range(3 + 3):
        for s in (3, 2, 1, 0):
            k = step - s
            if not 0 <= k < 3:
                continue
            u = order[k]
            links.wait(*first(u, s))
            if s < 3:
                links.start(*first(u, s + 1))
            if k == 2 and s < 3:
                links.start(*rest((2, 0, 1)[s], 0))
            if s == 3:
                project(u)

    read_g.start()

    gather_plan = {
        0: [(2, 0)], 1: [(0, 0)], 2: [(1, 0), (2, 1)], 3: [(0, 1)], 4: [(1, 1), (2, 2)],
        5: [(0, 2)], 6: [(1, 2), (2, 3)], 7: [(0, 3)],
    }

    def gather_point(t):
        for group, s in gather_plan[t]:
            links.wait(*rest(group, s))
            if s < 3:
                links.start(*rest(group, s + 1))

    row = lax.broadcasted_iota(jnp.int32, (128, ROWS), 0)
    one = jnp.where(row == 0, 1.0, 0.0).astype(BF16)

    def saved(t):
        return pltpu.make_async_copy(p_buf.at[t % 2], probs.at[t], local.at[t % 2])

    @pl.loop(0, HEADS)
    def _(t):
        for k in range(HEADS):
            pl.when(t == k)(functools.partial(gather_point, k))
        pl.when(t > 1)(lambda: saved(t - 2).wait())
        i, h = t // 2, t % 2
        pair_q = q_t[pl.ds(pl.multiple_of(i * 128, 128), 128), :]
        mine = (row >= 64 * h) & (row < 64 * h + 64)
        q = jnp.where(mine, pair_q, jnp.zeros_like(pair_q))
        keys = jnp.concatenate([keyed[i], key_bias[...]], axis=1)
        scores = dot(keys, jnp.concatenate([q, one], axis=0))
        peak = jnp.max(scores, axis=0, keepdims=True)
        total = jnp.zeros((1, ROWS), F32)
        for first_key, end_key in KEY_PARTS:
            e = jnp.exp(scores[first_key:end_key] - peak)
            total = total + jnp.sum(e, axis=0, keepdims=True)
            p_buf[h, first_key:end_key] = e.astype(BF16)
        head = pl.ds(pl.multiple_of(t * 64, 64), 64)
        mixed = dot(v_t[head, :], p_buf[h])
        inv = 1.0 / total
        att_t[head, :] = (mixed * inv).astype(BF16)
        inverse[t] = inv
        pl.when(t < HEADS - 1)(lambda: saved(t).start())

    links.wait(*rest(1, 3))
    read_g.wait()
    saved(HEADS - 2).wait()

    def fetched(t):
        return pltpu.make_async_copy(probs.at[t], p_buf.at[t % 2], local.at[t % 2])

    reducer = Reducer(links, at, rest_all, (c_buf, ya_buf, xb_buf, xa_buf, yb_buf, z_sum, z_buf))
    groups = [(pl.ds(2 * j, 2),) for j in range(4)] + [(pl.ds(8, 1),)]

    def step_rest(group, stage):
        total = reducer.finish(stage, groups[group])
        if stage < 3:
            reducer.start(stage + 1, groups[group])
        else:
            red[groups[group]] = total

    def dense_unit(position):
        return w_rest[position].reshape(D, D)

    @pl.when(w >= 0)
    def _():
        gain, bias = vec_row(vec, 2 * D, D), vec_row(vec, 3 * D, D)
        halves = [slice(k * ROWS // 2, (k + 1) * ROWS // 2) for k in range(2)]
        lows, outs = p_buf.at[0, :, 0:D], p_buf.at[0, :, D : 2 * D]
        normals, scales, backs, lives = [], [], [], []
        for k, rows in enumerate(halves):
            index = lax.broadcasted_iota(jnp.int32, (ROWS // 2, 1), 0) + k * (ROWS // 2)
            live = jnp.zeros((ROWS // 2, 1), jnp.bool_)
            for v in range(VIEWS):
                live = live | ((index >= v * VIEW_ROWS) & (index < v * VIEW_ROWS + counts[0, v]))
            middle = x[rows].astype(F32) + dot(att_t[:, rows], dense_unit(8), 0, 0)
            normal, scale = normalize(middle)
            middle_buf[rows] = middle + vec_row(vec, 4 * D + FF, D)
            normals.append(normal)
            scales.append(scale)
            lows[rows] = (normal * gain + bias).astype(BF16)
            backs.append(jnp.zeros((ROWS // 2, D), F32))
            lives.append(live)
            outs[rows] = jnp.where(live, g_buf[rows].astype(F32), 0.0).astype(BF16)
        for j in range(4):
            w_up, w_down = dense_unit(2 * j), dense_unit(2 * j + 1)
            up_total, down_total, up_grad = 0.0, 0.0, 0.0
            for k, rows in enumerate(halves):
                preact = dot(lows[rows], w_up) + vec_row(vec, 4 * D + j * D, D)
                phi = 0.5 + 0.5 * lax.erf(preact * 0.7071067811865476)
                active = (preact * phi).astype(BF16)
                slope = phi + preact * (jnp.exp(-0.5 * preact * preact) * 0.3989422804014327)
                middle_buf[rows] += dot(active, w_down)
                preact_back = (dot(outs[rows], w_down, 1, 1) * slope).astype(BF16)
                backs[k] = backs[k] + dot(preact_back, w_up, 1, 1)
                up_total = up_total + dot(lows[rows], preact_back, 0, 0)
                down_total = down_total + dot(active, outs[rows], 0, 0)
                up_grad = up_grad + jnp.sum(preact_back.astype(F32), axis=0, keepdims=True)
            rest_all[2 * j] = up_total.astype(BF16).reshape(*PIECES, D)
            rest_all[2 * j + 1] = down_total.astype(BF16).reshape(*PIECES, D)
            for r in range(4):
                v_own[16 + 4 * j + r : 17 + 4 * j + r, :] = up_grad[:, r * 128 : (r + 1) * 128]
            reducer.start(0, groups[j])
            for s in range(min(j, 3)):
                step_rest(j - 1 - s, s)
        for k, rows in enumerate(halves):
            g_buf[rows] = jnp.where(lives[k], middle_buf[rows], 0.0).astype(BF16)
        write_layer.start()
        out_total, gain_grad, bias_grad, down_grad = 0.0, 0.0, 0.0, 0.0
        for k, rows in enumerate(halves):
            out_back = outs[rows].astype(F32)
            back = out_back + norm_back(backs[k], gain, normals[k], scales[k])
            middle_buf[rows] = back
            branch = back.astype(BF16)
            out_total = out_total + dot(att_t[:, rows], branch)
            back_rows = dot(dense_unit(8), branch, 1, 1).astype(BF16)
            product = back_rows.astype(F32) * att_t[:, rows].astype(F32)
            for h in range(HEADS):
                part = jnp.sum(product[h * 64 : (h + 1) * 64], axis=0, keepdims=True)
                delta[h, :, rows] = part * inverse[h, :, rows]
            att_t[:, rows] = back_rows
            gain_grad = gain_grad + jnp.sum(backs[k] * normals[k], axis=0, keepdims=True)
            bias_grad = bias_grad + jnp.sum(backs[k], axis=0, keepdims=True)
            down_grad = down_grad + jnp.sum(out_back, axis=0, keepdims=True)
        rest_all[8] = out_total.astype(BF16).reshape(*PIECES, D)
        for offset, piece in ((8, gain_grad), (12, bias_grad), (32, down_grad)):
            for r in range(4):
                v_own[offset + r : offset + r + 1, :] = piece[:, r * 128 : (r + 1) * 128]
        v_own[0:8, :] = jnp.zeros((8, 128), F32)

    fetched(HEADS - 2).start()
    back_t = att_t

    def chunk_core(p):
        return ("chunk", p, 0), lambda: [
            (first_all.at[p, :, :, :, :, 1 - c], first_c.at[p], (w, y * 2 + 1 - c))
        ]

    chip = z * 4 + sx * 2 + y

    def chunk_chips(p):
        return ("chunk", p, 1), lambda: [
            (first_all.at[p, :, cz, cx, cy, c], first_d.at[p, chip], peer)
            for cz, cx, cy, peer in chip_peers(at)
        ]

    def chunk_middle(p):
        links.wait(*chunk_core(p))
        own = (p, whole, whole, whole, whole, c)
        first_all[own] = add(first_all[own], first_c[p])
        links.start(*chunk_chips(p))
        first_d[p, chip] = first_all[p, :, z, sx, y, c]

    def chunk_end(p):
        links.wait(*chunk_chips(p))
        total = jnp.sum(first_d[p].astype(F32), axis=0).astype(BF16)
        red[9:12, :, p * 128 : (p + 1) * 128] = total

    wides = "wide", lambda: [(v_own, vw_buf.at[w], peer) for peer in wide_peers(at)]
    narrows = "narrow", lambda: [(v_sum, vn_buf.at[n], peer) for peer in narrow_peers(at)]

    def vector_start():
        vw_buf[w] = v_own[...]
        links.start(*wides)

    def vector_middle():
        links.wait(*wides)
        total = vw_buf[0]
        for k in range(1, 8):
            total = total + vw_buf[k]
        v_sum[...] = total
        vn_buf[n] = total
        links.start(*narrows)

    def reduce_point(t):
        for group, s in {
            0: [(1, 2), (2, 1), (3, 0)], 1: [(4, 0)], 2: [(0, 3), (1, 3), (2, 2), (3, 1)],
            3: [(4, 1)], 4: [(2, 3), (3, 2)], 5: [(4, 2)], 6: [(3, 3)], 7: [(4, 3)],
        }[t]:
            step_rest(group, s)
        if t == 0:
            reducer.start(0, groups[4])
            vector_start()
        if t == 3:
            vector_middle()
        if t in (3, 5, 7):
            chunk_middle(3 - (t - 3) // 2)
        if t in (5, 7):
            chunk_end(3 - (t - 5) // 2)

    lane = lax.broadcasted_iota(jnp.int32, (KEYS, 128), 1)
    ones = jnp.where(lane < 2, 1.0, 0.0).astype(BF16)

    @pl.loop(0, HEADS)
    def _(step):
        for k in range(HEADS):
            pl.when(step == k)(functools.partial(reduce_point, k))
        t = HEADS - 1 - step
        i, h = t // 2, t % 2
        pl.when(step > 0)(lambda: fetched(t).wait())
        pair = pl.ds(pl.multiple_of(i * 128, 128), 128)
        head = pl.ds(pl.multiple_of(t * 64, 64), 64)

        @pl.when(h == 1)
        def _():
            value_pair[...] = v_t[pair, :].astype(F32).T.astype(BF16)
            key_pair_t[...] = keyed[i].astype(F32).T.astype(BF16)

        inv = inverse[t]
        shift = delta[t]
        high = shift.astype(BF16).astype(F32)
        mine = (row >= 64 * h) & (row < 64 * h + 64)
        scaled = jnp.where(mine, back_t[pair, :].astype(F32) * inv, 0.0).astype(BF16)
        tail = jnp.where(row == 0, -high, jnp.where(row == 1, high - shift, 0.0)).astype(BF16)
        right = jnp.concatenate([scaled, tail], axis=0)
        value = jnp.concatenate([value_pair[...], ones], axis=1)
        key_head = key_pair_t[pl.ds(pl.multiple_of(h * 64, 64), 64), :]
        query_head = q_t[head, :]
        back_head = (back_t[head, :].astype(F32) * inv).astype(BF16)
        query_total = jnp.zeros((64, ROWS), F32)
        for first_key, end_key in KEY_PARTS:
            part = slice(first_key, end_key)
            low = p_buf[h, part]
            score_back = low * dot(value[part], right).astype(BF16)
            query_total = query_total + dot(key_head[:, part], score_back)
            key_back[head, part] = dot(query_head, score_back, 1, 1).astype(BF16)
            value_back[head, part] = dot(back_head, low, 1, 1).astype(BF16)
        query_back[head, :] = (query_total * 0.125).astype(BF16)
        pl.when(t > 1)(lambda: fetched(t - 2).start())

        @pl.when(h == 0)
        def _():
            part = dot(normed_t[:, 0:ROWS], query_back[pair, :], 1, 1).astype(BF16)
            first_all[i, 0] = part.reshape(*PIECES, 128)
            both = jnp.concatenate([key_back[pair, :], value_back[pair, :]], axis=0)
            part = dot(normed_t[...], both, 1, 1).astype(BF16)
            for u in range(2):
                first_all[i, 1 + u] = part[:, u * 128 : (u + 1) * 128].reshape(*PIECES, 128)

        for k in range(4):
            pl.when(step == 2 * k + 1)(lambda p=3 - k: links.start(*chunk_core(p)))

    @pl.when(w >= 0)
    def _():
        w_q, w_k, w_v = unit(0), unit(1), unit(2)
        normal, scale = normalize(text_buf[...].reshape(D, TEXT).astype(F32).T)
        text_back = dot(key_back[:, ROWS:KEYS], w_k, 0, 1) + dot(
            value_back[:, ROWS:KEYS], w_v, 0, 1
        )
        text_part[...] = (
            norm_back(text_back, gain_one, normal, scale).T.astype(BF16).reshape(8, 64, TEXT)
        )
        gain_grad = jnp.sum(text_back * normal, axis=0, keepdims=True)
        bias_grad = jnp.sum(text_back, axis=0, keepdims=True)
        text_sum[w] = text_part[w]
        text_parts = "parts", lambda: [
            (text_part.at[peer[0]], text_sum.at[w], peer) for peer in wide_peers(at)
        ]
        chunk_middle(0)
        links.start(*text_parts)
        tile = ROWS // 2
        for t in range(2):
            rows = slice(t * tile, (t + 1) * tile)
            normal, scale = normalize(x[rows].astype(F32))
            projected = (
                dot(query_back[:, rows], w_q, 0, 1)
                + dot(key_back[:, rows], w_k, 0, 1)
                + dot(value_back[:, rows], w_v, 0, 1)
            )
            middle_buf[rows] += norm_back(projected, gain_one, normal, scale)
            gain_grad = gain_grad + jnp.sum(projected * normal, axis=0, keepdims=True)
            bias_grad = bias_grad + jnp.sum(projected, axis=0, keepdims=True)
        write_patch.start()
        for r in range(4):
            l_own[r : r + 1, :] = gain_grad[:, r * 128 : (r + 1) * 128]
            l_own[4 + r : 5 + r, :] = bias_grad[:, r * 128 : (r + 1) * 128]
        late_wides = "late wide", lambda: [(l_own, lw_buf.at[w], peer) for peer in wide_peers(at)]
        late_narrows = "late narrow", lambda: [
            (l_sum, ln_buf.at[n], peer) for peer in narrow_peers(at)
        ]
        lw_buf[w] = l_own[...]
        links.start(*late_wides)
        links.wait(*narrows)
        vec_out[...] = (vn_buf[0] + vn_buf[1]) + (vn_buf[2] + vn_buf[3])
        chunk_end(1)
        links.wait(*text_parts)
        text_out[...] = jnp.sum(text_sum[...].astype(F32), axis=0)
        chunk_end(0)
        owner, rank = unit_ranks(owners)
        for q in range(4):
            for s in range(SLOTS):
                spot = jnp.int32(0)
                for u in range(UNITS):
                    position = 9 + u if u < 3 else DENSE_PLACE[u - 3]
                    spot = spot + jnp.where((owner[u] == q) & (rank[u] == s), position, 0)
                s_buf[q, s] = red[jnp.minimum(spot, UNITS - 1)]
        grads = "grads", lambda: [
            (s_buf.at[peer[1]], r_buf.at[n], peer) for peer in narrow_peers(at)
        ]
        links.start(*grads)
        r_buf[n] = s_buf[n]
        links.wait(*late_wides)
        total = lw_buf[0]
        for k in range(1, 8):
            total = total + lw_buf[k]
        l_sum[...] = total
        ln_buf[n] = total
        links.start(*late_narrows)
        links.wait(*grads)
        for q in range(4):
            slot_grad[:, q * 16 : (q + 1) * 16, :] = r_buf[q].astype(F32)
        write_layer.wait()
        write_patch.wait()
        links.wait(*late_narrows)
        vec_out[0:8, :] = (ln_buf[0] + ln_buf[1]) + (ln_buf[2] + ln_buf[3])


def block(owners, counts, masters, text, x, vec, g):
    hbm = pl.BlockSpec(memory_space=pl.ANY)
    copies = 3 + 7 + 24 + 24 + 5 * 8 + 4 * 16 + 7 + 3 + 7 + 7 + 3 + 3
    bf = lambda *s: pltpu.VMEM(s, BF16)
    f32 = lambda *s: pltpu.VMEM(s, F32)
    rows = VEC // 128
    return pl.pallas_call(
        block_kernel,
        in_specs=[smem(), smem(), vmem(), vmem(), vmem(), vmem(), hbm],
        out_specs=[hbm, hbm, hbm, vmem(), vmem(), vmem()],
        out_shape=[
            jax.ShapeDtypeStruct((ROWS, D), F32),
            jax.ShapeDtypeStruct((ROWS, D), BF16),
            jax.ShapeDtypeStruct((HEADS - 1, KEYS, ROWS), BF16),
            jax.ShapeDtypeStruct((SLOTS, 64, D), F32),
            jax.ShapeDtypeStruct((64, TEXT), F32),
            jax.ShapeDtypeStruct((rows, 128), F32),
        ],
        scratch_shapes=[
            bf(SLOTS, 4, 16, D),
            bf(4, SLOTS, 16, D),
            bf(3, *PIECES, D),
            bf(9, *PIECES, D),
            bf(4, 2, 64, TEXT),
            bf(D, ROWS),
            bf(4, KEYS, 128),
            bf(KEYS, 128),
            bf(D, KEYS),
            bf(D, KEYS),
            bf(TEXT, D),
            bf(D, ROWS),
            f32(HEADS, 1, ROWS),
            f32(HEADS, 1, ROWS),
            bf(2, KEYS, ROWS),
            bf(ROWS, D),
            f32(ROWS, D),
            bf(9, *PIECES, D),
            bf(9, 4, 2, 2, 16, D),
            bf(9, 2, 2, 16, D),
            bf(9, 2, 2, 16, D),
            bf(9, 2, 16, D),
            bf(9, 2, 16, D),
            bf(9, 4, 16, D),
            bf(3, 9, 16, D),
            bf(4, 3, *PIECES, 128),
            bf(4, 3, 4, 2, 2, 16, 128),
            bf(4, 16, 3, 16, 128),
            bf(UNITS, 16, D),
            bf(4, SLOTS, 16, D),
            bf(4, SLOTS, 16, D),
            bf(8, 64, TEXT),
            bf(8, 64, TEXT),
            f32(rows, 128),
            f32(8, rows, 128),
            f32(rows, 128),
            f32(4, rows, 128),
            f32(8, 128),
            f32(8, 8, 128),
            f32(8, 128),
            f32(4, 8, 128),
            bf(D, ROWS),
            bf(D, KEYS),
            bf(D, KEYS),
            bf(KEYS, 128),
            bf(128, KEYS),
            pltpu.SemaphoreType.DMA((copies,)),
            pltpu.SemaphoreType.DMA((copies,)),
            pltpu.SemaphoreType.DMA((5,)),
        ],
        compiler_params=pltpu.CompilerParams(
            collective_id=1, has_side_effects=True, vmem_limit_bytes=63 * 2**20
        ),
    )(owners, counts, masters, text, x, vec, g)


def gather(owners, masters, text_t):
    packed = lax.all_gather(masters.astype(BF16), "wide", axis=2, tiled=True)
    packed = lax.all_gather(packed, "narrow", axis=0, tiled=True)
    same = owners[:, None] == owners[None, :]
    ids = jnp.arange(UNITS)
    rank = jnp.sum((same & (ids[None, :] < ids[:, None])).astype(jnp.int32), axis=1)
    units = jnp.take(packed.reshape(-1, D, D), owners * SLOTS + rank, axis=0)
    rows = lax.all_gather(text_t, "wide", axis=1, tiled=True)[0]
    return units, jnp.pad(rows, ((0, 0), (0, TEXT - LANG)))


def live_column(counts, rows):
    index = lax.broadcasted_iota(jnp.int32, (VIEW_ROWS, 1), 0)
    return [(index < counts[0, v]) for v in range(rows // VIEW_ROWS)]


def forward_kernel(
    counts, x, text_t, vec, w, att_t, probs, inverse, q_t, keyed, v_t, normed, text_normed
):
    i = pl.program_id(0)

    @pl.when(i == 0)
    def _():
        gain, bias = vec_row(vec, 0, D), vec_row(vec, D, D)
        normed[...] = (normalize(x[...].astype(F32))[0] * gain + bias).astype(BF16)
        rows = text_t[...].astype(F32).T
        live_text = lax.broadcasted_iota(jnp.int32, (TEXT, 1), 0) < LANG
        text_normed[...] = jnp.where(
            live_text, normalize(rows)[0] * gain + bias, 0.0
        ).astype(BF16)
        q_t[...] = dot(w[0], normed[...], 0, 1).astype(BF16) * BF16(0.125)
        v_t[:, 0:ROWS] = dot(w[2], normed[...], 0, 1).astype(BF16)
        v_t[:, ROWS:KEYS] = dot(w[2], text_normed[...], 0, 1).astype(BF16)
        for p in range(4):
            pair = slice(p * 128, (p + 1) * 128)
            keyed[p, 0:ROWS, 0:128] = dot(normed[...], w[1, :, pair]).astype(BF16)
            keyed[p, ROWS:KEYS, 0:128] = dot(text_normed[...], w[1, :, pair]).astype(BF16)
            for v, live in enumerate(live_column(counts, ROWS)):
                keyed[p, v * VIEW_ROWS : (v + 1) * VIEW_ROWS, 128:256] = jnp.broadcast_to(
                    jnp.where(live, 0.0, NEG), (VIEW_ROWS, 128)
                ).astype(BF16)
            keyed[p, ROWS:KEYS, 128:256] = jnp.broadcast_to(
                jnp.where(live_text, 0.0, NEG), (TEXT, 128)
            ).astype(BF16)

    row = lax.broadcasted_iota(jnp.int32, (128, ROWS), 0)
    one = jnp.where(row == 0, 1.0, 0.0).astype(BF16)
    pair_q = q_t[pl.ds(pl.multiple_of(i * 128, 128), 128), :]
    for h in range(2):
        mine = (row >= 64 * h) & (row < 64 * h + 64)
        q = jnp.where(mine, pair_q, jnp.zeros_like(pair_q))
        scores = dot(keyed[i], jnp.concatenate([q, one], axis=0))
        peak = jnp.max(scores, axis=0, keepdims=True)
        e = jnp.exp(scores - peak)
        total = jnp.sum(e, axis=0, keepdims=True)
        low = e.astype(BF16)
        probs[h] = low
        mixed = dot(v_t[pl.ds(pl.multiple_of(i * 128 + h * 64, 64), 64), :], low)
        inv = 1.0 / total
        att_t[h * 64 : (h + 1) * 64, :] = (mixed * inv).astype(BF16)
        inverse[0, h : h + 1, :] = inv


def attention_forward(counts, x, text_t, vec, units):
    return pl.pallas_call(
        forward_kernel,
        grid=(4,),
        in_specs=[smem(), vmem(), vmem(), vmem(), pl.BlockSpec((3, D, D), lambda i: (0, 0, 0))],
        out_specs=[
            pl.BlockSpec((128, ROWS), lambda i: (i, 0)),
            pl.BlockSpec((2, KEYS, ROWS), lambda i: (i, 0, 0)),
            pl.BlockSpec((1, 2, ROWS), lambda i: (i, 0, 0)),
            pl.BlockSpec((D, ROWS), lambda i: (0, 0)),
            pl.BlockSpec((4, KEYS, 256), lambda i: (0, 0, 0)),
            pl.BlockSpec((D, KEYS), lambda i: (0, 0)),
        ],
        out_shape=[
            jax.ShapeDtypeStruct((D, ROWS), BF16),
            jax.ShapeDtypeStruct((HEADS, KEYS, ROWS), BF16),
            jax.ShapeDtypeStruct((4, 2, ROWS), F32),
            jax.ShapeDtypeStruct((D, ROWS), BF16),
            jax.ShapeDtypeStruct((4, KEYS, 256), BF16),
            jax.ShapeDtypeStruct((D, KEYS), BF16),
        ],
        scratch_shapes=[pltpu.VMEM((ROWS, D), BF16), pltpu.VMEM((TEXT, D), BF16)],
        compiler_params=pltpu.CompilerParams(vmem_limit_bytes=VMEM_LIMIT),
    )(counts, x, text_t, vec, units)


def dense_kernel(
    counts, att_t, x, g, vec, w,
    layer_out, middle_back, back_t, grads, gain_grad, bias_grad, up_grad, down_grad,
    total, *, tile
):
    i = pl.program_id(0)
    steps = pl.num_programs(0)
    gain, bias = vec_row(vec, 2 * D, D), vec_row(vec, 3 * D, D)
    a = att_t[...]
    index = lax.broadcasted_iota(jnp.int32, (tile, 1), 0) + i * tile
    live = jnp.zeros((tile, 1), jnp.bool_)
    for v in range(VIEWS):
        live = live | ((index >= v * VIEW_ROWS) & (index < v * VIEW_ROWS + counts[0, v]))
    middle = x[...].astype(F32) + dot(a, w[0], 0, 0)
    normed, scale = normalize(middle)
    low = (normed * gain + bias).astype(BF16)
    out_back = jnp.where(live, g[...].astype(F32), 0.0)
    out_low = out_back.astype(BF16)

    @pl.when(i == 0)
    def _():
        total[...] = jnp.zeros_like(total)
        gain_grad[...] = jnp.zeros_like(gain_grad)
        bias_grad[...] = jnp.zeros_like(bias_grad)
        up_grad[...] = jnp.zeros_like(up_grad)
        down_grad[...] = jnp.zeros_like(down_grad)

    out = middle + vec_row(vec, 4 * D + FF, D)
    normed_back = jnp.zeros((tile, D), F32)
    for j in range(4):
        block = slice(j * D, (j + 1) * D)
        preact = dot(low, w[1 + j]) + vec_row(vec, 4 * D + j * D, D)
        phi = 0.5 + 0.5 * lax.erf(preact * 0.7071067811865476)
        active = (preact * phi).astype(BF16)
        slope = phi + preact * (jnp.exp(-0.5 * preact * preact) * 0.3989422804014327)
        out = out + dot(active, w[5 + j])
        preact_back = (dot(out_low, w[5 + j], 1, 1) * slope).astype(BF16)
        normed_back = normed_back + dot(preact_back, w[1 + j], 1, 1)
        total[1 + j] += dot(low, preact_back, 0, 0)
        total[5 + j] += dot(active, out_low, 0, 0)
        up_grad[:, block] += jnp.sum(preact_back.astype(F32), axis=0, keepdims=True)
    layer_out[...] = jnp.where(live, out, 0.0).astype(BF16)
    back = out_back + norm_back(normed_back, gain, normed, scale)
    middle_back[...] = back
    branch = back.astype(BF16)
    back_t[...] = dot(w[0], branch, 1, 1).astype(BF16)
    total[0] += dot(a, branch)
    gain_grad[...] += jnp.sum(normed_back * normed, axis=0, keepdims=True)
    bias_grad[...] += jnp.sum(normed_back, axis=0, keepdims=True)
    down_grad[...] += jnp.sum(out_back, axis=0, keepdims=True)

    @pl.when(i == steps - 1)
    def _():
        grads[...] = total[...].astype(BF16)


def dense(counts, att_t, x, g, vec, units, tile=640):
    rows = pl.BlockSpec((tile, D), lambda i: (i, 0))
    columns = pl.BlockSpec((D, tile), lambda i: (0, i))
    return pl.pallas_call(
        functools.partial(dense_kernel, tile=tile),
        grid=(ROWS // tile,),
        in_specs=[smem(), columns, rows, rows, vmem(), vmem()],
        out_specs=[
            rows,
            rows,
            columns,
            pl.BlockSpec((9, D, D), lambda i: (0, 0, 0)),
            pl.BlockSpec((1, D), lambda i: (0, 0)),
            pl.BlockSpec((1, D), lambda i: (0, 0)),
            pl.BlockSpec((1, FF), lambda i: (0, 0)),
            pl.BlockSpec((1, D), lambda i: (0, 0)),
        ],
        out_shape=[
            jax.ShapeDtypeStruct((ROWS, D), BF16),
            jax.ShapeDtypeStruct((ROWS, D), F32),
            jax.ShapeDtypeStruct((D, ROWS), BF16),
            jax.ShapeDtypeStruct((9, D, D), BF16),
            jax.ShapeDtypeStruct((1, D), F32),
            jax.ShapeDtypeStruct((1, D), F32),
            jax.ShapeDtypeStruct((1, FF), F32),
            jax.ShapeDtypeStruct((1, D), F32),
        ],
        scratch_shapes=[pltpu.VMEM((9, D, D), F32)],
        compiler_params=pltpu.CompilerParams(vmem_limit_bytes=VMEM_LIMIT),
    )(counts, att_t, x, g, vec, units)


def backward_kernel(probs, inverse, keyed, v_t, back_t, q_t, att_t, query_back, key_back, value_back):
    row = lax.broadcasted_iota(jnp.int32, (128, ROWS), 0)
    lane = lax.broadcasted_iota(jnp.int32, (KEYS, 128), 1)
    ones = jnp.where(lane < 2, 1.0, 0.0).astype(BF16)
    value = jnp.concatenate([v_t[...].astype(F32).T.astype(BF16), ones], axis=1)
    key_t = keyed[:, 0:128].astype(F32).T.astype(BF16)
    back = back_t[...].astype(F32)
    product = back * att_t[...].astype(F32)
    query = q_t[...].astype(F32)
    key_total = jnp.zeros((KEYS, 128), F32)
    value_total = jnp.zeros((KEYS, 128), F32)
    for h in range(2):
        half = slice(h * 64, (h + 1) * 64)
        inv = inverse[0, h : h + 1, :]
        delta = jnp.sum(product[half], axis=0, keepdims=True) * inv
        high = delta.astype(BF16).astype(F32)
        mine = (row >= 64 * h) & (row < 64 * h + 64)
        scaled = jnp.where(mine, back * inv, 0.0)
        tail = jnp.where(row == 0, -high, jnp.where(row == 1, high - delta, 0.0))
        right = jnp.concatenate([scaled.astype(BF16), tail.astype(BF16)], axis=0)
        low = probs[h]
        score_back = low * dot(value, right).astype(BF16)
        query_back[half, :] = (dot(key_t[half], score_back) * 0.125).astype(BF16)
        key_total += dot(score_back, jnp.where(mine, query, 0.0).T.astype(BF16))
        value_total += dot(low, scaled.T.astype(BF16))
    key_back[...] = key_total.astype(BF16)
    value_back[...] = value_total.astype(BF16)


def attention_backward(probs, inverse, keyed, v_t, back_t, q_t, att_t):
    return pl.pallas_call(
        backward_kernel,
        grid=(4,),
        in_specs=[
            pl.BlockSpec((2, KEYS, ROWS), lambda i: (i, 0, 0)),
            pl.BlockSpec((1, 2, ROWS), lambda i: (i, 0, 0)),
            pl.BlockSpec((None, KEYS, 256), lambda i: (i, 0, 0)),
            pl.BlockSpec((128, KEYS), lambda i: (i, 0)),
            pl.BlockSpec((128, ROWS), lambda i: (i, 0)),
            pl.BlockSpec((128, ROWS), lambda i: (i, 0)),
            pl.BlockSpec((128, ROWS), lambda i: (i, 0)),
        ],
        out_specs=[
            pl.BlockSpec((128, ROWS), lambda i: (i, 0)),
            pl.BlockSpec((KEYS, 128), lambda i: (0, i)),
            pl.BlockSpec((KEYS, 128), lambda i: (0, i)),
        ],
        out_shape=[
            jax.ShapeDtypeStruct((D, ROWS), BF16),
            jax.ShapeDtypeStruct((KEYS, D), BF16),
            jax.ShapeDtypeStruct((KEYS, D), BF16),
        ],
        compiler_params=pltpu.CompilerParams(vmem_limit_bytes=VMEM_LIMIT),
    )(probs, inverse, keyed, v_t, back_t, q_t, att_t)


def project_kernel(
    x, text_t, vec, w, middle_back, query_back, key_back, value_back, text_key, text_value,
    patch_grad, grads, gain_grad, bias_grad, text_grad_t, total
):
    i = pl.program_id(0)
    steps = pl.num_programs(0)
    gain, bias = vec_row(vec, 0, D), vec_row(vec, D, D)

    @pl.when(i == 0)
    def _():
        live = lax.broadcasted_iota(jnp.int32, (TEXT, 1), 0) < LANG
        normed, scale = normalize(text_t[...].astype(F32).T)
        low_t = jnp.where(live, normed * gain + bias, 0.0).T.astype(BF16)
        k, v = text_key[...], text_value[...]
        back = dot(k, w[1], 1, 1) + dot(v, w[2], 1, 1)
        text_grad_t[...] = norm_back(back, gain, normed, scale).T.astype(BF16)
        gain_grad[...] = jnp.sum(back * normed, axis=0, keepdims=True)
        bias_grad[...] = jnp.sum(back, axis=0, keepdims=True)
        total[0] = jnp.zeros((D, D), F32)
        total[1] = dot(low_t, k)
        total[2] = dot(low_t, v)

    normed, scale = normalize(x[...].astype(F32))
    low_t = (normed * gain + bias).T.astype(BF16)
    q, k, v = query_back[...], key_back[...], value_back[...]
    back = dot(q, w[0], 0, 1) + dot(k, w[1], 1, 1) + dot(v, w[2], 1, 1)
    patch_grad[...] = middle_back[...] + norm_back(back, gain, normed, scale)
    total[0] += dot(low_t, q, 1, 1)
    total[1] += dot(low_t, k)
    total[2] += dot(low_t, v)
    gain_grad[...] += jnp.sum(back * normed, axis=0, keepdims=True)
    bias_grad[...] += jnp.sum(back, axis=0, keepdims=True)

    @pl.when(i == steps - 1)
    def _():
        grads[...] = total[...].astype(BF16)


def project_back(x, text_t, vec, units, middle_back, query_back, key_back, value_back, tile=640):
    rows = pl.BlockSpec((tile, D), lambda i: (i, 0))
    text_rows = pl.BlockSpec((TEXT, D), lambda i: (ROWS // TEXT, 0))
    return pl.pallas_call(
        project_kernel,
        grid=(ROWS // tile,),
        in_specs=[
            rows,
            vmem(),
            vmem(),
            pl.BlockSpec((3, D, D), lambda i: (0, 0, 0)),
            rows,
            pl.BlockSpec((D, tile), lambda i: (0, i)),
            rows,
            rows,
            text_rows,
            text_rows,
        ],
        out_specs=[
            rows,
            pl.BlockSpec((3, D, D), lambda i: (0, 0, 0)),
            pl.BlockSpec((1, D), lambda i: (0, 0)),
            pl.BlockSpec((1, D), lambda i: (0, 0)),
            pl.BlockSpec((D, TEXT), lambda i: (0, 0)),
        ],
        out_shape=[
            jax.ShapeDtypeStruct((ROWS, D), F32),
            jax.ShapeDtypeStruct((3, D, D), BF16),
            jax.ShapeDtypeStruct((1, D), F32),
            jax.ShapeDtypeStruct((1, D), F32),
            jax.ShapeDtypeStruct((D, TEXT), BF16),
        ],
        scratch_shapes=[pltpu.VMEM((3, D, D), F32)],
        compiler_params=pltpu.CompilerParams(vmem_limit_bytes=VMEM_LIMIT),
    )(
        x, text_t, vec, units, middle_back, query_back, key_back, value_back, key_back, value_back
    )


def reduce_all(owners, rest, first, text, vecs):
    vec = lax.psum(jnp.concatenate(vecs, axis=1), ("wide", "narrow"))
    text_sum = lax.psum_scatter(text.astype(F32), "wide", scatter_dimension=0, tiled=True)
    all_units = jnp.concatenate([first, rest], axis=0).astype(F32)
    rows = lax.psum_scatter(all_units, "wide", scatter_dimension=1, tiled=True)
    same = owners[:, None] == owners[None, :]
    ids = jnp.arange(UNITS)
    rank = jnp.sum((same & (ids[None, :] < ids[:, None])).astype(jnp.int32), axis=1)
    pick = (owners[None, None, :] == jnp.arange(lax.axis_size("narrow"))[:, None, None]) & (
        rank[None, None, :] == jnp.arange(SLOTS)[None, :, None]
    )
    terms = jnp.einsum("nsu,urc->nsrc", pick.astype(F32), rows, precision=lax.Precision.HIGHEST)
    slots = lax.psum_scatter(terms, "narrow", scatter_dimension=0, tiled=True)
    return slots[0], text_sum, vec.reshape(VEC // 128, 128)


def adam(master, moment_one, moment_two, averaged, gradient, rate):
    moment_one = beta_one * moment_one + (1.0 - beta_one) * gradient
    moment_two = beta_two * moment_two + (1.0 - beta_two) * gradient * gradient
    mean_hat = moment_one / (1.0 - beta_one**STEP)
    second_hat = moment_two / (1.0 - beta_two**STEP)
    master = master - rate * (
        mean_hat / (jnp.sqrt(second_hat) + adam_eps) + weight_decay * master
    )
    averaged = average_keep * averaged + (1.0 - average_keep) * master
    return master, moment_one, moment_two, averaged


def unit_rates():
    blocks = FF // D
    fans = [2 * D // 3, 2 * D // 3, D, D // 64] + [D] * blocks + [FF] * blocks
    return [float(fan) ** -0.5 for fan in fans]


def update_kernel(
    owners, grad, masters, first, second, average, text_t, vec_grad, vec, vec_first, vec_second,
    vec_average, patch_in, layer_in,
    new_masters, new_first, new_second, new_average, new_copies, text_grad,
    vec_new_value, vec_new_first, vec_new_second, vec_new_average, patch_out, layer_out,
):
    s = pl.program_id(0)
    patch_out[...] = patch_in[...]
    layer_out[...] = layer_in[...]
    n = lax.axis_index("narrow")
    owner, rank = unit_ranks(owners)
    rate, filled = jnp.float32(0.0), jnp.int32(0)
    for u, value in enumerate(unit_rates()):
        match = (owner[u] == n) & (rank[u] == s)
        rate = rate + jnp.where(match, jnp.float32(value), jnp.float32(0.0))
        filled = filled + match.astype(jnp.int32)
    state = adam(masters[0, 0], first[0, 0], second[0, 0], average[0, 0], grad[0], rate)
    keep = jnp.broadcast_to(filled, state[0].shape) > 0
    state = [jnp.where(keep, part, 0.0) for part in state]
    for ref, part in zip((new_masters, new_first, new_second, new_average), state):
        ref[0, 0] = part
    new_copies[0, 0] = state[0].astype(BF16)

    @pl.when(s == 0)
    def _():
        text_grad[0] = text_t[:, 0:LANG]
        state = adam(
            vec[...], vec_first[...], vec_second[...], vec_average[...], vec_grad[...], vector_rate
        )
        for ref, part in zip(
            (vec_new_value, vec_new_first, vec_new_second, vec_new_average), state
        ):
            ref[...] = part


def update(
    owners, grad, masters, first, second, average, text_t, vec_grad, vec, v1, v2, va, patch, layer
):
    rows = masters.shape[2]
    state = jax.ShapeDtypeStruct(masters.shape, F32)
    vector = jax.ShapeDtypeStruct(vec.shape, F32)
    slot = pl.BlockSpec((1, 1, rows, D), lambda s: (0, s, 0, 0))
    vec_spec = pl.BlockSpec(vec.shape, lambda s: (0, 0))
    handed = pl.BlockSpec((ROWS // SLOTS, D), lambda s: (s, 0))
    return pl.pallas_call(
        update_kernel,
        grid=(SLOTS,),
        out_shape=[state] * 4
        + [
            jax.ShapeDtypeStruct(masters.shape, BF16),
            jax.ShapeDtypeStruct((1, text_t.shape[0], LANG), F32),
        ]
        + [vector] * 4
        + [jax.ShapeDtypeStruct(patch.shape, F32), jax.ShapeDtypeStruct(layer.shape, BF16)],
        in_specs=[smem(), pl.BlockSpec((1, rows, D), lambda s: (s, 0, 0))]
        + [slot] * 4
        + [pl.BlockSpec(text_t.shape, lambda s: (0, 0))]
        + [vec_spec] * 5
        + [handed] * 2,
        out_specs=[slot] * 5
        + [pl.BlockSpec((1, text_t.shape[0], LANG), lambda s: (0, 0, 0))]
        + [vec_spec] * 4
        + [handed] * 2,
        compiler_params=pltpu.CompilerParams(vmem_limit_bytes=VMEM_LIMIT),
    )(
        owners, grad, masters, first, second, average, text_t, vec_grad, vec, v1, v2, va, patch, layer
    )


def local(
    patches, text_tokens, view_counts, out_grad, owners, masters, first_moment, second_moment,
    average, vec_value, vec_first, vec_second, vec_average,
):
    vec, v1, v2, va = [
        part.reshape(VEC // 128, 128) for part in (vec_value, vec_first, vec_second, vec_average)
    ]
    text_in = jnp.swapaxes(text_tokens, 1, 2)
    if lax.axis_size("wide") == 8 and lax.axis_size("narrow") == 4:
        patch_grad, layer_out, _, slot_grad, text_sum, vec_grad = block(
            owners, view_counts, masters, text_in, patches, vec, out_grad
        )
    else:
        units, text_t = gather(owners, masters, text_in)
        att_t, probs, inverse, q_t, keyed, v_t = attention_forward(
            view_counts, patches, text_t, vec, units
        )
        layer_out, middle_back, back_t, rest, *vecs = dense(
            view_counts, att_t, patches, out_grad, vec, units[3:]
        )
        query_back, key_back, value_back = attention_backward(
            probs, inverse, keyed, v_t, back_t, q_t, att_t
        )
        patch_grad, first, gain_one, bias_one, text_part = project_back(
            patches, text_t, vec, units, middle_back, query_back, key_back, value_back
        )
        slot_grad, text_sum, vec_grad = reduce_all(
            owners, rest, first, text_part, (gain_one, bias_one, *vecs)
        )
    outs = update(
        owners, slot_grad, masters, first_moment, second_moment, average, text_sum, vec_grad, vec,
        v1, v2, va, patch_grad, layer_out,
    )
    new_masters, new_first, new_second, new_average, new_copies, text_grad = outs[:6]
    vectors = [part.reshape(VEC) for part in outs[6:10]]
    patch_grad, layer_out = outs[10:]
    return (
        layer_out, patch_grad, jnp.swapaxes(text_grad, 1, 2), new_masters, new_first, new_second,
        new_average, new_copies, *vectors,
    )


def solution(mesh):
    rows = P(("wide", "narrow"), None)
    state = P("narrow", None, "wide", None)
    text = P("narrow", None, "wide")
    in_specs = (rows, text, rows, rows, P(), state, state, state, state, P(), P(), P(), P())
    out_specs = (rows, rows, text, state, state, state, state, state, P(), P(), P(), P())
    return jax.shard_map(local, mesh=mesh, in_specs=in_specs, out_specs=out_specs, check_vma=False)
```

```python
import functools

import jax
import jax.numpy as jnp
from jax import lax
from jax.experimental import pallas as pl
from jax.experimental.pallas import tpu as pltpu
from jax.sharding import PartitionSpec as P

D = 512
HEADS = 8
FF = 2048
VIEWS = 5
VIEW_ROWS = 256
ROWS = VIEWS * VIEW_ROWS
LANG = 77
TEXT = 128
KEYS = ROWS + TEXT
STEP = 5
UNITS = 12
SLOTS = 4
VEC = 5 * D + FF
F32 = jnp.float32
BF16 = jnp.bfloat16
MESH = pl.DeviceIdType.MESH
NEG = -1e30

norm_eps = 1e-05
beta_one = 0.5
beta_two = 0.5
adam_eps = 1e-08
weight_decay = 0.1
average_keep = 0.75
vector_rate = 0.25
VMEM_LIMIT = 60 * 2**20


def dot(left, right, left_dim=1, right_dim=0):
    return lax.dot_general(
        left, right, (((left_dim,), (right_dim,)), ((), ())), preferred_element_type=F32
    )


def vmem():
    return pl.BlockSpec(memory_space=pltpu.VMEM)


def smem():
    return pl.BlockSpec(memory_space=pltpu.SMEM)


def vec_row(vec, start, size):
    first = start // 128
    return jnp.concatenate([vec[first + r : first + r + 1, :] for r in range(size // 128)], axis=1)


def unit_ranks(owners_ref):
    owner = [owners_ref[u] for u in range(UNITS)]
    rank = []
    for u in range(UNITS):
        total = jnp.int32(0)
        for v in range(u):
            total = total + (owner[v] == owner[u]).astype(jnp.int32)
        rank.append(jnp.minimum(total, SLOTS - 1))
    return owner, rank


def normalize(values):
    center = values - jnp.mean(values, axis=-1, keepdims=True)
    spread = jnp.mean(center * center, axis=-1, keepdims=True)
    scale = lax.rsqrt(spread + norm_eps)
    return center * scale, scale


def norm_back(grads, gain, normed, scale):
    e = grads * gain
    return scale * (
        e
        - jnp.mean(e, axis=-1, keepdims=True)
        - normed * jnp.mean(e * normed, axis=-1, keepdims=True)
    )


def place():
    w = lax.axis_index("wide")
    n = lax.axis_index("narrow")
    return w, n, w // 2, w % 2, n // 2, n % 2


def narrow_peers(at):
    w, n = at[:2]
    return [(w, lax.rem(n + k, 4)) for k in range(1, 4)]


def wide_peers(at):
    w, n = at[:2]
    return [(lax.rem(w + k, 8), n) for k in range(1, 8)]


def chip_peers(at):
    w, n, z, x, y, c = at
    peers = []
    for k in range(1, 16):
        chip = lax.rem(z * 4 + x * 2 + y + k, 16)
        cz, cx, cy = chip // 4, (chip // 2) % 2, chip % 2
        peers.append((cz, cx, cy, (cz * 2 + cx, cy * 2 + c)))
    return peers


def all_peers(at):
    w, n, z, x, y, c = at
    return narrow_peers(at) + wide_peers(at) + [
        (lax.rem(w + k, 8), (1 - y) * 2 + c) for k in range(1, 8)
    ]


def greet(peers):
    barrier = pltpu.get_barrier_semaphore()
    for peer in peers:
        pl.semaphore_signal(barrier, inc=1, device_id=peer, device_id_type=MESH)


def greeted(peers):
    pl.semaphore_wait(pltpu.get_barrier_semaphore(), len(peers))


class Links:
    def __init__(self, send, recv):
        self.send, self.recv, self.slots = send, recv, {}

    def copies(self, key, parts):
        made = []
        for k, (src, dst, device) in enumerate(parts()):
            slot = self.slots.setdefault((key, k), len(self.slots))
            made.append(
                pltpu.make_async_remote_copy(
                    src_ref=src,
                    dst_ref=dst,
                    send_sem=self.send.at[slot],
                    recv_sem=self.recv.at[slot],
                    device_id=device,
                    device_id_type=MESH,
                )
            )
        return made

    def start(self, key, parts):
        for copy in self.copies(key, parts):
            copy.start()

    def wait(self, key, parts):
        for copy in self.copies(key, parts):
            copy.wait()


def partners(w, n, z, x, y, c):
    to_z = [(lax.rem(z + k, 4) * 2 + x, n) for k in range(1, 4)]
    return to_z, (z * 2 + 1 - x, n), (w, (1 - y) * 2 + c), (w, y * 2 + 1 - c)


def spread(ref, head, stage, at):
    w, n, z, x, y, c = at
    to_z, to_x, to_y, to_c = partners(*at)
    whole = slice(None)
    if stage == 0:
        parts = [((z, x, y, c), peer) for peer in to_z]
    elif stage == 1:
        parts = [((pl.ds(0, 2), x, y, c), to_x), ((pl.ds(2, 2), x, y, c), to_y)]
    elif stage == 2:
        parts = [((pl.ds(0, 2), whole, y, c), to_y), ((pl.ds(2, 2), x, whole, c), to_x)]
    else:
        parts = [((whole, whole, whole, c), to_c)]
    return [(ref.at[(*head, *part)], ref.at[(*head, *part)], peer) for part, peer in parts]


def add(a, b):
    return (a.astype(F32) + b.astype(F32)).astype(BF16)


class Reducer:
    def __init__(self, links, at, source, bufs):
        self.links, self.at, self.source = links, at, source
        (self.c_buf, self.ya_buf, self.xb_buf, self.xa_buf, self.yb_buf, self.z_sum,
         self.z_buf) = bufs

    def start(self, stage, head):
        self.links.start(*self.copies(stage, head))

    def copies(self, stage, head):
        return ("reduce", str(head), stage), lambda: self.parts(stage, head)

    def parts(self, stage, head):
        w, n, z, x, y, c = self.at
        to_z, to_x, to_y, to_c = partners(*self.at)
        whole, low, high = slice(None), pl.ds(0, 2), pl.ds(2, 2)
        source = self.source
        if stage == 0:
            return [(source.at[(*head, whole, whole, whole, 1 - c)], self.c_buf.at[head], to_c)]
        if stage == 1:
            return [
                (source.at[(*head, low, whole, 1 - y, c)], self.ya_buf.at[head], to_y),
                (source.at[(*head, high, 1 - x, whole, c)], self.xb_buf.at[head], to_x),
            ]
        if stage == 2:
            return [
                (source.at[(*head, low, 1 - x, y, c)], self.xa_buf.at[head], to_x),
                (source.at[(*head, high, x, 1 - y, c)], self.yb_buf.at[head], to_y),
            ]
        return [
            (self.z_sum.at[(*head, lax.rem(z + k, 4))], self.z_buf.at[(k - 1, *head)], to_z[k - 1])
            for k in range(1, 4)
        ]

    def finish(self, stage, head):
        w, n, z, x, y, c = self.at
        self.links.wait(*self.copies(stage, head))
        whole, low, high = slice(None), pl.ds(0, 2), pl.ds(2, 2)
        source = self.source
        if stage == 0:
            own = (*head, whole, whole, whole, c)
            source[own] = add(source[own], self.c_buf[head])
        elif stage == 1:
            a = (*head, low, whole, y, c)
            b = (*head, high, x, whole, c)
            source[a] = add(source[a], self.ya_buf[head])
            source[b] = add(source[b], self.xb_buf[head])
        elif stage == 2:
            self.z_sum[(*head, low)] = add(source[(*head, low, x, y, c)], self.xa_buf[head])
            self.z_sum[(*head, high)] = add(source[(*head, high, x, y, c)], self.yb_buf[head])
        else:
            total = self.z_sum[(*head, z)].astype(F32)
            for k in range(3):
                total = total + self.z_buf[(k, *head)].astype(F32)
            return total.astype(BF16)


PIECES = (4, 2, 2, 2, 16)
KEY_PARTS = ((0, 512), (512, 1024), (1024, 1408))
DENSE_PLACE = (8, 0, 2, 4, 6, 1, 3, 5, 7)


def block_kernel(
    owners, counts, masters, text, x, vec, g,
    patch_out, layer_out, probs, slot_grad, text_out, vec_out,
    send_buf, slot_buf, w_first, w_rest, text_buf, q_t, keyed, key_bias, v_t, normed_t,
    text_normed, att_t, inverse, delta, p_buf, g_buf, middle_buf,
    rest_all, c_buf, ya_buf, xb_buf, xa_buf, yb_buf, z_sum, z_buf,
    first_all, first_c, first_d, red, s_buf, r_buf, text_part, text_sum,
    v_own, vw_buf, v_sum, vn_buf, l_own, lw_buf, l_sum, ln_buf,
    query_back, key_back, value_back, value_pair, key_pair_t, send, recv, local
):
    at = place()
    w, n, z, sx, y, c = at
    links = Links(send, recv)
    whole = slice(None)
    peers = all_peers(at)
    gain_one, bias_one = vec_row(vec, 0, D), vec_row(vec, D, D)
    live_text = lax.broadcasted_iota(jnp.int32, (TEXT, 1), 0) < LANG
    read_g = pltpu.make_async_copy(g, g_buf, local.at[2])
    write_layer = pltpu.make_async_copy(g_buf, layer_out, local.at[3])
    write_patch = pltpu.make_async_copy(middle_buf, patch_out, local.at[4])

    greet(peers)
    send_buf[...] = masters[0].reshape(SLOTS, 4, 16, D).astype(BF16)
    text_buf[z, sx] = jnp.zeros((64, TEXT), BF16)
    text_buf[z, sx, :, 0:LANG] = text[0]
    low = (normalize(x[...].astype(F32))[0] * gain_one + bias_one).astype(BF16)
    normed = g_buf
    normed[...] = low
    greeted(peers)
    slots = "slots", lambda: [
        (send_buf.at[:, peer[1]], slot_buf.at[n], peer) for peer in narrow_peers(at)
    ]
    links.start(*slots)
    texts = "text", lambda: [
        (text_buf.at[z, sx], text_buf.at[z, sx], peer) for peer in wide_peers(at)
    ]
    links.start(*texts)
    slot_buf[n] = send_buf[:, n]
    normed_t[:, 0:ROWS] = low.astype(F32).T.astype(BF16)
    owner, rank = unit_ranks(owners)
    links.wait(*slots)
    for u in range(3):
        w_first[u, z, sx, y, c] = slot_buf[owner[u], rank[u]]

    def first(u, s):
        return ("first", u, s), lambda: spread(w_first, (u,), s, at)

    def rest(group, s):
        return ("rest", group, s), lambda: spread(w_rest, (pl.ds(3 * group, 3),), s, at)

    order = (1, 0, 2)
    for u in order:
        links.start(*first(u, 0))
    for k, position in enumerate(DENSE_PLACE):
        w_rest[position, z, sx, y, c] = slot_buf[owner[3 + k], rank[3 + k]]
    for v, live in enumerate(live_column(counts, ROWS)):
        key_bias[v * VIEW_ROWS : (v + 1) * VIEW_ROWS, :] = jnp.broadcast_to(
            jnp.where(live, 0.0, NEG), (VIEW_ROWS, 128)
        ).astype(BF16)
    key_bias[ROWS:KEYS, :] = jnp.broadcast_to(
        jnp.where(live_text, 0.0, NEG), (TEXT, 128)
    ).astype(BF16)
    links.wait(*texts)
    rows = text_buf[...].reshape(D, TEXT).astype(F32).T
    text_low = jnp.where(live_text, normalize(rows)[0] * gain_one + bias_one, 0.0)
    text_normed[...] = text_low.astype(BF16)
    normed_t[:, ROWS:KEYS] = text_low.T.astype(BF16)

    def unit(u):
        return w_first[u].reshape(D, D)

    def project(u):
        if u == 1:
            k = dot(normed[...], unit(1)).astype(BF16)
            t = dot(text_normed[...], unit(1)).astype(BF16)
            for p in range(4):
                pair = slice(p * 128, (p + 1) * 128)
                keyed[p, 0:ROWS] = k[:, pair]
                keyed[p, ROWS:KEYS] = t[:, pair]
        elif u == 0:
            q_t[...] = dot(unit(0), normed[...], 0, 1).astype(BF16) * BF16(0.125)
        else:
            v_t[:, 0:ROWS] = dot(unit(2), normed[...], 0, 1).astype(BF16)
            v_t[:, ROWS:KEYS] = dot(unit(2), text_normed[...], 0, 1).astype(BF16)

    for step in range(3 + 3):
        for s in (3, 2, 1, 0):
            k = step - s
            if not 0 <= k < 3:
                continue
            u = order[k]
            links.wait(*first(u, s))
            if s < 3:
                links.start(*first(u, s + 1))
            if k == 2 and s < 3:
                links.start(*rest((2, 0, 1)[s], 0))
            if s == 3:
                project(u)

    read_g.start()

    gather_plan = {
        0: [(2, 0)], 1: [(0, 0)], 2: [(2, 1)], 3: [(1, 0)], 4: [(2, 2), (0, 1)], 5: [],
        6: [(1, 1), (0, 2)], 7: [(2, 3)],
    }

    def gather_point(t):
        for group, s in gather_plan[t]:
            links.wait(*rest(group, s))
            if s < 3:
                links.start(*rest(group, s + 1))

    row = lax.broadcasted_iota(jnp.int32, (128, ROWS), 0)
    one = jnp.where(row == 0, 1.0, 0.0).astype(BF16)

    def saved(t):
        return pltpu.make_async_copy(p_buf.at[t % 2], probs.at[t], local.at[t % 2])

    @pl.loop(0, HEADS)
    def _(t):
        for k in range(HEADS):
            pl.when(t == k)(functools.partial(gather_point, k))
        pl.when(t > 1)(lambda: saved(t - 2).wait())
        i, h = t // 2, t % 2
        pair_q = q_t[pl.ds(pl.multiple_of(i * 128, 128), 128), :]
        mine = (row >= 64 * h) & (row < 64 * h + 64)
        q = jnp.where(mine, pair_q, jnp.zeros_like(pair_q))
        keys = jnp.concatenate([keyed[i], key_bias[...]], axis=1)
        scores = dot(keys, jnp.concatenate([q, one], axis=0))
        peak = jnp.max(scores, axis=0, keepdims=True)
        for first_key, end_key in KEY_PARTS:
            p_buf[h, first_key:end_key] = jnp.exp(scores[first_key:end_key] - peak).astype(BF16)
        head = pl.ds(pl.multiple_of(t * 64, 64), 64)
        summed = jnp.concatenate([v_t[head, :], jnp.ones((16, KEYS), BF16)], axis=0)
        mixed = dot(summed, p_buf[h])
        inv = 1.0 / mixed[64:65]
        att_t[head, :] = (mixed[0:64] * inv).astype(BF16)
        inverse[t] = inv
        pl.when(t < HEADS - 1)(lambda: saved(t).start())

    read_g.wait()
    saved(HEADS - 2).wait()

    def fetched(t):
        return pltpu.make_async_copy(probs.at[t], p_buf.at[t % 2], local.at[t % 2])

    reducer = Reducer(links, at, rest_all, (c_buf, ya_buf, xb_buf, xa_buf, yb_buf, z_sum, z_buf))
    dense_order = (3, 0, 1, 2)
    groups = [(pl.ds(2 * j, 2),) for j in dense_order] + [(pl.ds(8, 1),)]

    def step_rest(group, stage):
        total = reducer.finish(stage, groups[group])
        if stage < 3:
            reducer.start(stage + 1, groups[group])
        else:
            red[groups[group]] = total

    def dense_unit(position):
        return w_rest[position].reshape(D, D)

    @pl.when(w >= 0)
    def _():
        gain, bias = vec_row(vec, 2 * D, D), vec_row(vec, 3 * D, D)
        halves = [slice(k * ROWS // 2, (k + 1) * ROWS // 2) for k in range(2)]
        lows, outs = p_buf.at[0, :, 0:D], p_buf.at[0, :, D : 2 * D]
        normals, scales, backs, lives = [], [], [], []
        for k, rows in enumerate(halves):
            index = lax.broadcasted_iota(jnp.int32, (ROWS // 2, 1), 0) + k * (ROWS // 2)
            live = jnp.zeros((ROWS // 2, 1), jnp.bool_)
            for v in range(VIEWS):
                live = live | ((index >= v * VIEW_ROWS) & (index < v * VIEW_ROWS + counts[0, v]))
            middle = x[rows].astype(F32) + dot(att_t[:, rows], dense_unit(8), 0, 0)
            normal, scale = normalize(middle)
            middle_buf[rows] = middle + vec_row(vec, 4 * D + FF, D)
            normals.append(normal)
            scales.append(scale)
            lows[rows] = (normal * gain + bias).astype(BF16)
            backs.append(jnp.zeros((ROWS // 2, D), F32))
            lives.append(live)
            outs[rows] = jnp.where(live, g_buf[rows].astype(F32), 0.0).astype(BF16)
        for turn, j in enumerate(dense_order):
            if turn == 1:
                links.wait(*rest(1, 2))
                links.start(*rest(1, 3))
                links.wait(*rest(0, 3))
            if turn == 2:
                links.wait(*rest(1, 3))
            w_up, w_down = dense_unit(2 * j), dense_unit(2 * j + 1)
            up_total, down_total, up_grad = 0.0, 0.0, 0.0
            for k, rows in enumerate(halves):
                preact = dot(lows[rows], w_up) + vec_row(vec, 4 * D + j * D, D)
                phi = 0.5 + 0.5 * lax.erf(preact * 0.7071067811865476)
                active = (preact * phi).astype(BF16)
                slope = phi + preact * (jnp.exp(-0.5 * preact * preact) * 0.3989422804014327)
                middle_buf[rows] += dot(active, w_down)
                preact_back = (dot(outs[rows], w_down, 1, 1) * slope).astype(BF16)
                backs[k] = backs[k] + dot(preact_back, w_up, 1, 1)
                up_total = up_total + dot(lows[rows], preact_back, 0, 0)
                down_total = down_total + dot(active, outs[rows], 0, 0)
                up_grad = up_grad + jnp.sum(preact_back.astype(F32), axis=0, keepdims=True)
            rest_all[2 * j] = up_total.astype(BF16).reshape(*PIECES, D)
            rest_all[2 * j + 1] = down_total.astype(BF16).reshape(*PIECES, D)
            for r in range(4):
                v_own[16 + 4 * j + r : 17 + 4 * j + r, :] = up_grad[:, r * 128 : (r + 1) * 128]
            reducer.start(0, groups[turn])
            for s in range(min(turn, 3)):
                step_rest(turn - 1 - s, s)
        for k, rows in enumerate(halves):
            g_buf[rows] = jnp.where(lives[k], middle_buf[rows], 0.0).astype(BF16)
        write_layer.start()
        out_total, gain_grad, bias_grad, down_grad = 0.0, 0.0, 0.0, 0.0
        for k, rows in enumerate(halves):
            out_back = outs[rows].astype(F32)
            back = out_back + norm_back(backs[k], gain, normals[k], scales[k])
            middle_buf[rows] = back
            branch = back.astype(BF16)
            out_total = out_total + dot(att_t[:, rows], branch)
            back_rows = dot(dense_unit(8), branch, 1, 1).astype(BF16)
            product = back_rows.astype(F32) * att_t[:, rows].astype(F32)
            for h in range(HEADS):
                part = jnp.sum(product[h * 64 : (h + 1) * 64], axis=0, keepdims=True)
                delta[h, :, rows] = part * inverse[h, :, rows]
            att_t[:, rows] = back_rows
            gain_grad = gain_grad + jnp.sum(backs[k] * normals[k], axis=0, keepdims=True)
            bias_grad = bias_grad + jnp.sum(backs[k], axis=0, keepdims=True)
            down_grad = down_grad + jnp.sum(out_back, axis=0, keepdims=True)
        rest_all[8] = out_total.astype(BF16).reshape(*PIECES, D)
        for offset, piece in ((8, gain_grad), (12, bias_grad), (32, down_grad)):
            for r in range(4):
                v_own[offset + r : offset + r + 1, :] = piece[:, r * 128 : (r + 1) * 128]
        v_own[0:8, :] = jnp.zeros((8, 128), F32)

    fetched(HEADS - 2).start()
    back_t = att_t

    def chunk_core(p):
        return ("chunk", p, 0), lambda: [
            (first_all.at[p, :, :, :, :, 1 - c], first_c.at[p], (w, y * 2 + 1 - c))
        ]

    chip = z * 4 + sx * 2 + y

    def chunk_chips(p):
        return ("chunk", p, 1), lambda: [
            (first_all.at[p, :, cz, cx, cy, c], first_d.at[p, chip], peer)
            for cz, cx, cy, peer in chip_peers(at)
        ]

    def chunk_middle(p):
        links.wait(*chunk_core(p))
        own = (p, whole, whole, whole, whole, c)
        first_all[own] = add(first_all[own], first_c[p])
        links.start(*chunk_chips(p))
        first_d[p, chip] = first_all[p, :, z, sx, y, c]

    def chunk_end(p):
        links.wait(*chunk_chips(p))
        total = jnp.sum(first_d[p].astype(F32), axis=0).astype(BF16)
        red[9:12, :, p * 128 : (p + 1) * 128] = total

    wides = "wide", lambda: [(v_own, vw_buf.at[w], peer) for peer in wide_peers(at)]
    narrows = "narrow", lambda: [(v_sum, vn_buf.at[n], peer) for peer in narrow_peers(at)]

    def vector_start():
        vw_buf[w] = v_own[...]
        links.start(*wides)

    def vector_middle():
        links.wait(*wides)
        total = vw_buf[0]
        for k in range(1, 8):
            total = total + vw_buf[k]
        v_sum[...] = total
        vn_buf[n] = total
        links.start(*narrows)

    def reduce_point(t):
        for group, s in {
            0: [(1, 2), (2, 1), (3, 0)], 1: [(4, 0)], 2: [(0, 3), (1, 3), (2, 2), (3, 1)],
            3: [(4, 1)], 4: [(2, 3), (3, 2)], 5: [(4, 2)], 6: [(3, 3)], 7: [(4, 3)],
        }[t]:
            step_rest(group, s)
        if t == 0:
            reducer.start(0, groups[4])
            vector_start()
        if t == 3:
            vector_middle()
        if t in (3, 5, 7):
            chunk_middle(3 - (t - 3) // 2)
        if t in (5, 7):
            chunk_end(3 - (t - 5) // 2)

    lane = lax.broadcasted_iota(jnp.int32, (KEYS, 128), 1)
    ones = jnp.where(lane < 2, 1.0, 0.0).astype(BF16)

    @pl.loop(0, HEADS)
    def _(step):
        for k in range(HEADS):
            pl.when(step == k)(functools.partial(reduce_point, k))
        t = HEADS - 1 - step
        i, h = t // 2, t % 2
        pl.when(step > 0)(lambda: fetched(t).wait())
        pair = pl.ds(pl.multiple_of(i * 128, 128), 128)
        head = pl.ds(pl.multiple_of(t * 64, 64), 64)

        @pl.when(h == 1)
        def _():
            value_pair[...] = v_t[pair, :].astype(F32).T.astype(BF16)
            key_pair_t[...] = keyed[i].astype(F32).T.astype(BF16)

        inv = inverse[t]
        shift = delta[t]
        high = shift.astype(BF16).astype(F32)
        mine = (row >= 64 * h) & (row < 64 * h + 64)
        scaled = jnp.where(mine, back_t[pair, :].astype(F32) * inv, 0.0).astype(BF16)
        tail = jnp.where(row == 0, -high, jnp.where(row == 1, high - shift, 0.0)).astype(BF16)
        right = jnp.concatenate([scaled, tail], axis=0)
        value = jnp.concatenate([value_pair[...], ones], axis=1)
        key_head = key_pair_t[pl.ds(pl.multiple_of(h * 64, 64), 64), :]
        query_head = q_t[head, :]
        back_head = (back_t[head, :].astype(F32) * inv).astype(BF16)
        query_total = jnp.zeros((64, ROWS), F32)
        for first_key, end_key in KEY_PARTS:
            part = slice(first_key, end_key)
            low = p_buf[h, part]
            score_back = low * dot(value[part], right).astype(BF16)
            query_total = query_total + dot(key_head[:, part], score_back)
            key_back[head, part] = dot(query_head, score_back, 1, 1).astype(BF16)
            value_back[head, part] = dot(back_head, low, 1, 1).astype(BF16)
        query_back[head, :] = (query_total * 0.125).astype(BF16)
        pl.when(t > 1)(lambda: fetched(t - 2).start())

        @pl.when(h == 0)
        def _():
            part = dot(normed_t[:, 0:ROWS], query_back[pair, :], 1, 1).astype(BF16)
            first_all[i, 0] = part.reshape(*PIECES, 128)
            both = jnp.concatenate([key_back[pair, :], value_back[pair, :]], axis=0)
            part = dot(normed_t[...], both, 1, 1).astype(BF16)
            for u in range(2):
                first_all[i, 1 + u] = part[:, u * 128 : (u + 1) * 128].reshape(*PIECES, 128)

        for k in range(4):
            pl.when(step == 2 * k + 1)(lambda p=3 - k: links.start(*chunk_core(p)))

    @pl.when(w >= 0)
    def _():
        w_q, w_k, w_v = unit(0), unit(1), unit(2)
        normal, scale = normalize(text_buf[...].reshape(D, TEXT).astype(F32).T)
        text_back = dot(key_back[:, ROWS:KEYS], w_k, 0, 1) + dot(
            value_back[:, ROWS:KEYS], w_v, 0, 1
        )
        text_part[...] = (
            norm_back(text_back, gain_one, normal, scale).T.astype(BF16).reshape(8, 64, TEXT)
        )
        gain_grad = jnp.sum(text_back * normal, axis=0, keepdims=True)
        bias_grad = jnp.sum(text_back, axis=0, keepdims=True)
        text_sum[w] = text_part[w]
        text_parts = "parts", lambda: [
            (text_part.at[peer[0]], text_sum.at[w], peer) for peer in wide_peers(at)
        ]
        chunk_middle(0)
        links.start(*text_parts)
        tile = ROWS // 2
        for t in range(2):
            rows = slice(t * tile, (t + 1) * tile)
            normal, scale = normalize(x[rows].astype(F32))
            projected = (
                dot(query_back[:, rows], w_q, 0, 1)
                + dot(key_back[:, rows], w_k, 0, 1)
                + dot(value_back[:, rows], w_v, 0, 1)
            )
            middle_buf[rows] += norm_back(projected, gain_one, normal, scale)
            gain_grad = gain_grad + jnp.sum(projected * normal, axis=0, keepdims=True)
            bias_grad = bias_grad + jnp.sum(projected, axis=0, keepdims=True)
        write_patch.start()
        for r in range(4):
            l_own[r : r + 1, :] = gain_grad[:, r * 128 : (r + 1) * 128]
            l_own[4 + r : 5 + r, :] = bias_grad[:, r * 128 : (r + 1) * 128]
        late_wides = "late wide", lambda: [(l_own, lw_buf.at[w], peer) for peer in wide_peers(at)]
        late_narrows = "late narrow", lambda: [
            (l_sum, ln_buf.at[n], peer) for peer in narrow_peers(at)
        ]
        lw_buf[w] = l_own[...]
        links.start(*late_wides)
        links.wait(*narrows)
        vec_out[...] = (vn_buf[0] + vn_buf[1]) + (vn_buf[2] + vn_buf[3])
        chunk_end(1)
        links.wait(*text_parts)
        text_out[...] = jnp.sum(text_sum[...].astype(F32), axis=0)
        chunk_end(0)
        owner, rank = unit_ranks(owners)
        for q in range(4):
            for s in range(SLOTS):
                spot = jnp.int32(0)
                for u in range(UNITS):
                    position = 9 + u if u < 3 else DENSE_PLACE[u - 3]
                    spot = spot + jnp.where((owner[u] == q) & (rank[u] == s), position, 0)
                s_buf[q, s] = red[jnp.minimum(spot, UNITS - 1)]
        grads = "grads", lambda: [
            (s_buf.at[peer[1]], r_buf.at[n], peer) for peer in narrow_peers(at)
        ]
        links.start(*grads)
        r_buf[n] = s_buf[n]
        links.wait(*late_wides)
        total = lw_buf[0]
        for k in range(1, 8):
            total = total + lw_buf[k]
        l_sum[...] = total
        ln_buf[n] = total
        links.start(*late_narrows)
        links.wait(*grads)
        for q in range(4):
            slot_grad[:, q * 16 : (q + 1) * 16, :] = r_buf[q].astype(F32)
        write_layer.wait()
        write_patch.wait()
        links.wait(*late_narrows)
        vec_out[0:8, :] = (ln_buf[0] + ln_buf[1]) + (ln_buf[2] + ln_buf[3])


def block(owners, counts, masters, text, x, vec, g):
    hbm = pl.BlockSpec(memory_space=pl.ANY)
    copies = 3 + 7 + 24 + 24 + 5 * 8 + 4 * 16 + 7 + 3 + 7 + 7 + 3 + 3
    bf = lambda *s: pltpu.VMEM(s, BF16)
    f32 = lambda *s: pltpu.VMEM(s, F32)
    rows = VEC // 128
    return pl.pallas_call(
        block_kernel,
        in_specs=[smem(), smem(), vmem(), vmem(), vmem(), vmem(), hbm],
        out_specs=[hbm, hbm, hbm, vmem(), vmem(), vmem()],
        out_shape=[
            jax.ShapeDtypeStruct((ROWS, D), F32),
            jax.ShapeDtypeStruct((ROWS, D), BF16),
            jax.ShapeDtypeStruct((HEADS - 1, KEYS, ROWS), BF16),
            jax.ShapeDtypeStruct((SLOTS, 64, D), F32),
            jax.ShapeDtypeStruct((64, TEXT), F32),
            jax.ShapeDtypeStruct((rows, 128), F32),
        ],
        scratch_shapes=[
            bf(SLOTS, 4, 16, D),
            bf(4, SLOTS, 16, D),
            bf(3, *PIECES, D),
            bf(9, *PIECES, D),
            bf(4, 2, 64, TEXT),
            bf(D, ROWS),
            bf(4, KEYS, 128),
            bf(KEYS, 128),
            bf(D, KEYS),
            bf(D, KEYS),
            bf(TEXT, D),
            bf(D, ROWS),
            f32(HEADS, 1, ROWS),
            f32(HEADS, 1, ROWS),
            bf(2, KEYS, ROWS),
            bf(ROWS, D),
            f32(ROWS, D),
            bf(9, *PIECES, D),
            bf(9, 4, 2, 2, 16, D),
            bf(9, 2, 2, 16, D),
            bf(9, 2, 2, 16, D),
            bf(9, 2, 16, D),
            bf(9, 2, 16, D),
            bf(9, 4, 16, D),
            bf(3, 9, 16, D),
            bf(4, 3, *PIECES, 128),
            bf(4, 3, 4, 2, 2, 16, 128),
            bf(4, 16, 3, 16, 128),
            bf(UNITS, 16, D),
            bf(4, SLOTS, 16, D),
            bf(4, SLOTS, 16, D),
            bf(8, 64, TEXT),
            bf(8, 64, TEXT),
            f32(rows, 128),
            f32(8, rows, 128),
            f32(rows, 128),
            f32(4, rows, 128),
            f32(8, 128),
            f32(8, 8, 128),
            f32(8, 128),
            f32(4, 8, 128),
            bf(D, ROWS),
            bf(D, KEYS),
            bf(D, KEYS),
            bf(KEYS, 128),
            bf(128, KEYS),
            pltpu.SemaphoreType.DMA((copies,)),
            pltpu.SemaphoreType.DMA((copies,)),
            pltpu.SemaphoreType.DMA((5,)),
        ],
        compiler_params=pltpu.CompilerParams(
            collective_id=1, has_side_effects=True, vmem_limit_bytes=63 * 2**20
        ),
    )(owners, counts, masters, text, x, vec, g)


def gather(owners, masters, text_t):
    packed = lax.all_gather(masters.astype(BF16), "wide", axis=2, tiled=True)
    packed = lax.all_gather(packed, "narrow", axis=0, tiled=True)
    same = owners[:, None] == owners[None, :]
    ids = jnp.arange(UNITS)
    rank = jnp.sum((same & (ids[None, :] < ids[:, None])).astype(jnp.int32), axis=1)
    units = jnp.take(packed.reshape(-1, D, D), owners * SLOTS + rank, axis=0)
    rows = lax.all_gather(text_t, "wide", axis=1, tiled=True)[0]
    return units, jnp.pad(rows, ((0, 0), (0, TEXT - LANG)))


def live_column(counts, rows):
    index = lax.broadcasted_iota(jnp.int32, (VIEW_ROWS, 1), 0)
    return [(index < counts[0, v]) for v in range(rows // VIEW_ROWS)]


def forward_kernel(
    counts, x, text_t, vec, w, att_t, probs, inverse, q_t, keyed, v_t, normed, text_normed
):
    i = pl.program_id(0)

    @pl.when(i == 0)
    def _():
        gain, bias = vec_row(vec, 0, D), vec_row(vec, D, D)
        normed[...] = (normalize(x[...].astype(F32))[0] * gain + bias).astype(BF16)
        rows = text_t[...].astype(F32).T
        live_text = lax.broadcasted_iota(jnp.int32, (TEXT, 1), 0) < LANG
        text_normed[...] = jnp.where(
            live_text, normalize(rows)[0] * gain + bias, 0.0
        ).astype(BF16)
        q_t[...] = dot(w[0], normed[...], 0, 1).astype(BF16) * BF16(0.125)
        v_t[:, 0:ROWS] = dot(w[2], normed[...], 0, 1).astype(BF16)
        v_t[:, ROWS:KEYS] = dot(w[2], text_normed[...], 0, 1).astype(BF16)
        for p in range(4):
            pair = slice(p * 128, (p + 1) * 128)
            keyed[p, 0:ROWS, 0:128] = dot(normed[...], w[1, :, pair]).astype(BF16)
            keyed[p, ROWS:KEYS, 0:128] = dot(text_normed[...], w[1, :, pair]).astype(BF16)
            for v, live in enumerate(live_column(counts, ROWS)):
                keyed[p, v * VIEW_ROWS : (v + 1) * VIEW_ROWS, 128:256] = jnp.broadcast_to(
                    jnp.where(live, 0.0, NEG), (VIEW_ROWS, 128)
                ).astype(BF16)
            keyed[p, ROWS:KEYS, 128:256] = jnp.broadcast_to(
                jnp.where(live_text, 0.0, NEG), (TEXT, 128)
            ).astype(BF16)

    row = lax.broadcasted_iota(jnp.int32, (128, ROWS), 0)
    one = jnp.where(row == 0, 1.0, 0.0).astype(BF16)
    pair_q = q_t[pl.ds(pl.multiple_of(i * 128, 128), 128), :]
    for h in range(2):
        mine = (row >= 64 * h) & (row < 64 * h + 64)
        q = jnp.where(mine, pair_q, jnp.zeros_like(pair_q))
        scores = dot(keyed[i], jnp.concatenate([q, one], axis=0))
        peak = jnp.max(scores, axis=0, keepdims=True)
        e = jnp.exp(scores - peak)
        total = jnp.sum(e, axis=0, keepdims=True)
        low = e.astype(BF16)
        probs[h] = low
        mixed = dot(v_t[pl.ds(pl.multiple_of(i * 128 + h * 64, 64), 64), :], low)
        inv = 1.0 / total
        att_t[h * 64 : (h + 1) * 64, :] = (mixed * inv).astype(BF16)
        inverse[0, h : h + 1, :] = inv


def attention_forward(counts, x, text_t, vec, units):
    return pl.pallas_call(
        forward_kernel,
        grid=(4,),
        in_specs=[smem(), vmem(), vmem(), vmem(), pl.BlockSpec((3, D, D), lambda i: (0, 0, 0))],
        out_specs=[
            pl.BlockSpec((128, ROWS), lambda i: (i, 0)),
            pl.BlockSpec((2, KEYS, ROWS), lambda i: (i, 0, 0)),
            pl.BlockSpec((1, 2, ROWS), lambda i: (i, 0, 0)),
            pl.BlockSpec((D, ROWS), lambda i: (0, 0)),
            pl.BlockSpec((4, KEYS, 256), lambda i: (0, 0, 0)),
            pl.BlockSpec((D, KEYS), lambda i: (0, 0)),
        ],
        out_shape=[
            jax.ShapeDtypeStruct((D, ROWS), BF16),
            jax.ShapeDtypeStruct((HEADS, KEYS, ROWS), BF16),
            jax.ShapeDtypeStruct((4, 2, ROWS), F32),
            jax.ShapeDtypeStruct((D, ROWS), BF16),
            jax.ShapeDtypeStruct((4, KEYS, 256), BF16),
            jax.ShapeDtypeStruct((D, KEYS), BF16),
        ],
        scratch_shapes=[pltpu.VMEM((ROWS, D), BF16), pltpu.VMEM((TEXT, D), BF16)],
        compiler_params=pltpu.CompilerParams(vmem_limit_bytes=VMEM_LIMIT),
    )(counts, x, text_t, vec, units)


def dense_kernel(
    counts, att_t, x, g, vec, w,
    layer_out, middle_back, back_t, grads, gain_grad, bias_grad, up_grad, down_grad,
    total, *, tile
):
    i = pl.program_id(0)
    steps = pl.num_programs(0)
    gain, bias = vec_row(vec, 2 * D, D), vec_row(vec, 3 * D, D)
    a = att_t[...]
    index = lax.broadcasted_iota(jnp.int32, (tile, 1), 0) + i * tile
    live = jnp.zeros((tile, 1), jnp.bool_)
    for v in range(VIEWS):
        live = live | ((index >= v * VIEW_ROWS) & (index < v * VIEW_ROWS + counts[0, v]))
    middle = x[...].astype(F32) + dot(a, w[0], 0, 0)
    normed, scale = normalize(middle)
    low = (normed * gain + bias).astype(BF16)
    out_back = jnp.where(live, g[...].astype(F32), 0.0)
    out_low = out_back.astype(BF16)

    @pl.when(i == 0)
    def _():
        total[...] = jnp.zeros_like(total)
        gain_grad[...] = jnp.zeros_like(gain_grad)
        bias_grad[...] = jnp.zeros_like(bias_grad)
        up_grad[...] = jnp.zeros_like(up_grad)
        down_grad[...] = jnp.zeros_like(down_grad)

    out = middle + vec_row(vec, 4 * D + FF, D)
    normed_back = jnp.zeros((tile, D), F32)
    for j in range(4):
        block = slice(j * D, (j + 1) * D)
        preact = dot(low, w[1 + j]) + vec_row(vec, 4 * D + j * D, D)
        phi = 0.5 + 0.5 * lax.erf(preact * 0.7071067811865476)
        active = (preact * phi).astype(BF16)
        slope = phi + preact * (jnp.exp(-0.5 * preact * preact) * 0.3989422804014327)
        out = out + dot(active, w[5 + j])
        preact_back = (dot(out_low, w[5 + j], 1, 1) * slope).astype(BF16)
        normed_back = normed_back + dot(preact_back, w[1 + j], 1, 1)
        total[1 + j] += dot(low, preact_back, 0, 0)
        total[5 + j] += dot(active, out_low, 0, 0)
        up_grad[:, block] += jnp.sum(preact_back.astype(F32), axis=0, keepdims=True)
    layer_out[...] = jnp.where(live, out, 0.0).astype(BF16)
    back = out_back + norm_back(normed_back, gain, normed, scale)
    middle_back[...] = back
    branch = back.astype(BF16)
    back_t[...] = dot(w[0], branch, 1, 1).astype(BF16)
    total[0] += dot(a, branch)
    gain_grad[...] += jnp.sum(normed_back * normed, axis=0, keepdims=True)
    bias_grad[...] += jnp.sum(normed_back, axis=0, keepdims=True)
    down_grad[...] += jnp.sum(out_back, axis=0, keepdims=True)

    @pl.when(i == steps - 1)
    def _():
        grads[...] = total[...].astype(BF16)


def dense(counts, att_t, x, g, vec, units, tile=640):
    rows = pl.BlockSpec((tile, D), lambda i: (i, 0))
    columns = pl.BlockSpec((D, tile), lambda i: (0, i))
    return pl.pallas_call(
        functools.partial(dense_kernel, tile=tile),
        grid=(ROWS // tile,),
        in_specs=[smem(), columns, rows, rows, vmem(), vmem()],
        out_specs=[
            rows,
            rows,
            columns,
            pl.BlockSpec((9, D, D), lambda i: (0, 0, 0)),
            pl.BlockSpec((1, D), lambda i: (0, 0)),
            pl.BlockSpec((1, D), lambda i: (0, 0)),
            pl.BlockSpec((1, FF), lambda i: (0, 0)),
            pl.BlockSpec((1, D), lambda i: (0, 0)),
        ],
        out_shape=[
            jax.ShapeDtypeStruct((ROWS, D), BF16),
            jax.ShapeDtypeStruct((ROWS, D), F32),
            jax.ShapeDtypeStruct((D, ROWS), BF16),
            jax.ShapeDtypeStruct((9, D, D), BF16),
            jax.ShapeDtypeStruct((1, D), F32),
            jax.ShapeDtypeStruct((1, D), F32),
            jax.ShapeDtypeStruct((1, FF), F32),
            jax.ShapeDtypeStruct((1, D), F32),
        ],
        scratch_shapes=[pltpu.VMEM((9, D, D), F32)],
        compiler_params=pltpu.CompilerParams(vmem_limit_bytes=VMEM_LIMIT),
    )(counts, att_t, x, g, vec, units)


def backward_kernel(probs, inverse, keyed, v_t, back_t, q_t, att_t, query_back, key_back, value_back):
    row = lax.broadcasted_iota(jnp.int32, (128, ROWS), 0)
    lane = lax.broadcasted_iota(jnp.int32, (KEYS, 128), 1)
    ones = jnp.where(lane < 2, 1.0, 0.0).astype(BF16)
    value = jnp.concatenate([v_t[...].astype(F32).T.astype(BF16), ones], axis=1)
    key_t = keyed[:, 0:128].astype(F32).T.astype(BF16)
    back = back_t[...].astype(F32)
    product = back * att_t[...].astype(F32)
    query = q_t[...].astype(F32)
    key_total = jnp.zeros((KEYS, 128), F32)
    value_total = jnp.zeros((KEYS, 128), F32)
    for h in range(2):
        half = slice(h * 64, (h + 1) * 64)
        inv = inverse[0, h : h + 1, :]
        delta = jnp.sum(product[half], axis=0, keepdims=True) * inv
        high = delta.astype(BF16).astype(F32)
        mine = (row >= 64 * h) & (row < 64 * h + 64)
        scaled = jnp.where(mine, back * inv, 0.0)
        tail = jnp.where(row == 0, -high, jnp.where(row == 1, high - delta, 0.0))
        right = jnp.concatenate([scaled.astype(BF16), tail.astype(BF16)], axis=0)
        low = probs[h]
        score_back = low * dot(value, right).astype(BF16)
        query_back[half, :] = (dot(key_t[half], score_back) * 0.125).astype(BF16)
        key_total += dot(score_back, jnp.where(mine, query, 0.0).T.astype(BF16))
        value_total += dot(low, scaled.T.astype(BF16))
    key_back[...] = key_total.astype(BF16)
    value_back[...] = value_total.astype(BF16)


def attention_backward(probs, inverse, keyed, v_t, back_t, q_t, att_t):
    return pl.pallas_call(
        backward_kernel,
        grid=(4,),
        in_specs=[
            pl.BlockSpec((2, KEYS, ROWS), lambda i: (i, 0, 0)),
            pl.BlockSpec((1, 2, ROWS), lambda i: (i, 0, 0)),
            pl.BlockSpec((None, KEYS, 256), lambda i: (i, 0, 0)),
            pl.BlockSpec((128, KEYS), lambda i: (i, 0)),
            pl.BlockSpec((128, ROWS), lambda i: (i, 0)),
            pl.BlockSpec((128, ROWS), lambda i: (i, 0)),
            pl.BlockSpec((128, ROWS), lambda i: (i, 0)),
        ],
        out_specs=[
            pl.BlockSpec((128, ROWS), lambda i: (i, 0)),
            pl.BlockSpec((KEYS, 128), lambda i: (0, i)),
            pl.BlockSpec((KEYS, 128), lambda i: (0, i)),
        ],
        out_shape=[
            jax.ShapeDtypeStruct((D, ROWS), BF16),
            jax.ShapeDtypeStruct((KEYS, D), BF16),
            jax.ShapeDtypeStruct((KEYS, D), BF16),
        ],
        compiler_params=pltpu.CompilerParams(vmem_limit_bytes=VMEM_LIMIT),
    )(probs, inverse, keyed, v_t, back_t, q_t, att_t)


def project_kernel(
    x, text_t, vec, w, middle_back, query_back, key_back, value_back, text_key, text_value,
    patch_grad, grads, gain_grad, bias_grad, text_grad_t, total
):
    i = pl.program_id(0)
    steps = pl.num_programs(0)
    gain, bias = vec_row(vec, 0, D), vec_row(vec, D, D)

    @pl.when(i == 0)
    def _():
        live = lax.broadcasted_iota(jnp.int32, (TEXT, 1), 0) < LANG
        normed, scale = normalize(text_t[...].astype(F32).T)
        low_t = jnp.where(live, normed * gain + bias, 0.0).T.astype(BF16)
        k, v = text_key[...], text_value[...]
        back = dot(k, w[1], 1, 1) + dot(v, w[2], 1, 1)
        text_grad_t[...] = norm_back(back, gain, normed, scale).T.astype(BF16)
        gain_grad[...] = jnp.sum(back * normed, axis=0, keepdims=True)
        bias_grad[...] = jnp.sum(back, axis=0, keepdims=True)
        total[0] = jnp.zeros((D, D), F32)
        total[1] = dot(low_t, k)
        total[2] = dot(low_t, v)

    normed, scale = normalize(x[...].astype(F32))
    low_t = (normed * gain + bias).T.astype(BF16)
    q, k, v = query_back[...], key_back[...], value_back[...]
    back = dot(q, w[0], 0, 1) + dot(k, w[1], 1, 1) + dot(v, w[2], 1, 1)
    patch_grad[...] = middle_back[...] + norm_back(back, gain, normed, scale)
    total[0] += dot(low_t, q, 1, 1)
    total[1] += dot(low_t, k)
    total[2] += dot(low_t, v)
    gain_grad[...] += jnp.sum(back * normed, axis=0, keepdims=True)
    bias_grad[...] += jnp.sum(back, axis=0, keepdims=True)

    @pl.when(i == steps - 1)
    def _():
        grads[...] = total[...].astype(BF16)


def project_back(x, text_t, vec, units, middle_back, query_back, key_back, value_back, tile=640):
    rows = pl.BlockSpec((tile, D), lambda i: (i, 0))
    text_rows = pl.BlockSpec((TEXT, D), lambda i: (ROWS // TEXT, 0))
    return pl.pallas_call(
        project_kernel,
        grid=(ROWS // tile,),
        in_specs=[
            rows,
            vmem(),
            vmem(),
            pl.BlockSpec((3, D, D), lambda i: (0, 0, 0)),
            rows,
            pl.BlockSpec((D, tile), lambda i: (0, i)),
            rows,
            rows,
            text_rows,
            text_rows,
        ],
        out_specs=[
            rows,
            pl.BlockSpec((3, D, D), lambda i: (0, 0, 0)),
            pl.BlockSpec((1, D), lambda i: (0, 0)),
            pl.BlockSpec((1, D), lambda i: (0, 0)),
            pl.BlockSpec((D, TEXT), lambda i: (0, 0)),
        ],
        out_shape=[
            jax.ShapeDtypeStruct((ROWS, D), F32),
            jax.ShapeDtypeStruct((3, D, D), BF16),
            jax.ShapeDtypeStruct((1, D), F32),
            jax.ShapeDtypeStruct((1, D), F32),
            jax.ShapeDtypeStruct((D, TEXT), BF16),
        ],
        scratch_shapes=[pltpu.VMEM((3, D, D), F32)],
        compiler_params=pltpu.CompilerParams(vmem_limit_bytes=VMEM_LIMIT),
    )(
        x, text_t, vec, units, middle_back, query_back, key_back, value_back, key_back, value_back
    )


def reduce_all(owners, rest, first, text, vecs):
    vec = lax.psum(jnp.concatenate(vecs, axis=1), ("wide", "narrow"))
    text_sum = lax.psum_scatter(text.astype(F32), "wide", scatter_dimension=0, tiled=True)
    all_units = jnp.concatenate([first, rest], axis=0).astype(F32)
    rows = lax.psum_scatter(all_units, "wide", scatter_dimension=1, tiled=True)
    same = owners[:, None] == owners[None, :]
    ids = jnp.arange(UNITS)
    rank = jnp.sum((same & (ids[None, :] < ids[:, None])).astype(jnp.int32), axis=1)
    pick = (owners[None, None, :] == jnp.arange(lax.axis_size("narrow"))[:, None, None]) & (
        rank[None, None, :] == jnp.arange(SLOTS)[None, :, None]
    )
    terms = jnp.einsum("nsu,urc->nsrc", pick.astype(F32), rows, precision=lax.Precision.HIGHEST)
    slots = lax.psum_scatter(terms, "narrow", scatter_dimension=0, tiled=True)
    return slots[0], text_sum, vec.reshape(VEC // 128, 128)


def adam(master, moment_one, moment_two, averaged, gradient, rate):
    moment_one = beta_one * moment_one + (1.0 - beta_one) * gradient
    moment_two = beta_two * moment_two + (1.0 - beta_two) * gradient * gradient
    mean_hat = moment_one / (1.0 - beta_one**STEP)
    second_hat = moment_two / (1.0 - beta_two**STEP)
    master = master - rate * (
        mean_hat / (jnp.sqrt(second_hat) + adam_eps) + weight_decay * master
    )
    averaged = average_keep * averaged + (1.0 - average_keep) * master
    return master, moment_one, moment_two, averaged


def unit_rates():
    blocks = FF // D
    fans = [2 * D // 3, 2 * D // 3, D, D // 64] + [D] * blocks + [FF] * blocks
    return [float(fan) ** -0.5 for fan in fans]


def update_kernel(
    owners, grad, masters, first, second, average, text_t, vec_grad, vec, vec_first, vec_second,
    vec_average, patch_in, layer_in,
    new_masters, new_first, new_second, new_average, new_copies, text_grad,
    vec_new_value, vec_new_first, vec_new_second, vec_new_average, patch_out, layer_out,
):
    s = pl.program_id(0)
    patch_out[...] = patch_in[...]
    layer_out[...] = layer_in[...]
    n = lax.axis_index("narrow")
    owner, rank = unit_ranks(owners)
    rate, filled = jnp.float32(0.0), jnp.int32(0)
    for u, value in enumerate(unit_rates()):
        match = (owner[u] == n) & (rank[u] == s)
        rate = rate + jnp.where(match, jnp.float32(value), jnp.float32(0.0))
        filled = filled + match.astype(jnp.int32)
    state = adam(masters[0, 0], first[0, 0], second[0, 0], average[0, 0], grad[0], rate)
    keep = jnp.broadcast_to(filled, state[0].shape) > 0
    state = [jnp.where(keep, part, 0.0) for part in state]
    for ref, part in zip((new_masters, new_first, new_second, new_average), state):
        ref[0, 0] = part
    new_copies[0, 0] = state[0].astype(BF16)

    @pl.when(s == 0)
    def _():
        text_grad[0] = text_t[:, 0:LANG]
        state = adam(
            vec[...], vec_first[...], vec_second[...], vec_average[...], vec_grad[...], vector_rate
        )
        for ref, part in zip(
            (vec_new_value, vec_new_first, vec_new_second, vec_new_average), state
        ):
            ref[...] = part


def update(
    owners, grad, masters, first, second, average, text_t, vec_grad, vec, v1, v2, va, patch, layer
):
    rows = masters.shape[2]
    state = jax.ShapeDtypeStruct(masters.shape, F32)
    vector = jax.ShapeDtypeStruct(vec.shape, F32)
    slot = pl.BlockSpec((1, 1, rows, D), lambda s: (0, s, 0, 0))
    vec_spec = pl.BlockSpec(vec.shape, lambda s: (0, 0))
    handed = pl.BlockSpec((ROWS // SLOTS, D), lambda s: (s, 0))
    return pl.pallas_call(
        update_kernel,
        grid=(SLOTS,),
        out_shape=[state] * 4
        + [
            jax.ShapeDtypeStruct(masters.shape, BF16),
            jax.ShapeDtypeStruct((1, text_t.shape[0], LANG), F32),
        ]
        + [vector] * 4
        + [jax.ShapeDtypeStruct(patch.shape, F32), jax.ShapeDtypeStruct(layer.shape, BF16)],
        in_specs=[smem(), pl.BlockSpec((1, rows, D), lambda s: (s, 0, 0))]
        + [slot] * 4
        + [pl.BlockSpec(text_t.shape, lambda s: (0, 0))]
        + [vec_spec] * 5
        + [handed] * 2,
        out_specs=[slot] * 5
        + [pl.BlockSpec((1, text_t.shape[0], LANG), lambda s: (0, 0, 0))]
        + [vec_spec] * 4
        + [handed] * 2,
        compiler_params=pltpu.CompilerParams(vmem_limit_bytes=VMEM_LIMIT),
    )(
        owners, grad, masters, first, second, average, text_t, vec_grad, vec, v1, v2, va, patch, layer
    )


def local(
    patches, text_tokens, view_counts, out_grad, owners, masters, first_moment, second_moment,
    average, vec_value, vec_first, vec_second, vec_average,
):
    vec, v1, v2, va = [
        part.reshape(VEC // 128, 128) for part in (vec_value, vec_first, vec_second, vec_average)
    ]
    text_in = jnp.swapaxes(text_tokens, 1, 2)
    if lax.axis_size("wide") == 8 and lax.axis_size("narrow") == 4:
        patch_grad, layer_out, _, slot_grad, text_sum, vec_grad = block(
            owners, view_counts, masters, text_in, patches, vec, out_grad
        )
    else:
        units, text_t = gather(owners, masters, text_in)
        att_t, probs, inverse, q_t, keyed, v_t = attention_forward(
            view_counts, patches, text_t, vec, units
        )
        layer_out, middle_back, back_t, rest, *vecs = dense(
            view_counts, att_t, patches, out_grad, vec, units[3:]
        )
        query_back, key_back, value_back = attention_backward(
            probs, inverse, keyed, v_t, back_t, q_t, att_t
        )
        patch_grad, first, gain_one, bias_one, text_part = project_back(
            patches, text_t, vec, units, middle_back, query_back, key_back, value_back
        )
        slot_grad, text_sum, vec_grad = reduce_all(
            owners, rest, first, text_part, (gain_one, bias_one, *vecs)
        )
    outs = update(
        owners, slot_grad, masters, first_moment, second_moment, average, text_sum, vec_grad, vec,
        v1, v2, va, patch_grad, layer_out,
    )
    new_masters, new_first, new_second, new_average, new_copies, text_grad = outs[:6]
    vectors = [part.reshape(VEC) for part in outs[6:10]]
    patch_grad, layer_out = outs[10:]
    return (
        layer_out, patch_grad, jnp.swapaxes(text_grad, 1, 2), new_masters, new_first, new_second,
        new_average, new_copies, *vectors,
    )


def solution(mesh):
    rows = P(("wide", "narrow"), None)
    state = P("narrow", None, "wide", None)
    text = P("narrow", None, "wide")
    in_specs = (rows, text, rows, rows, P(), state, state, state, state, P(), P(), P(), P())
    out_specs = (rows, rows, text, state, state, state, state, state, P(), P(), P(), P())
    return jax.shard_map(local, mesh=mesh, in_specs=in_specs, out_specs=out_specs, check_vma=False)
```

```python
import functools

import jax
import jax.numpy as jnp
from jax import lax
from jax.experimental import pallas as pl
from jax.experimental.pallas import tpu as pltpu
from jax.sharding import PartitionSpec as P

D = 512
HEADS = 8
FF = 2048
VIEWS = 5
VIEW_ROWS = 256
ROWS = VIEWS * VIEW_ROWS
LANG = 77
TEXT = 128
KEYS = ROWS + TEXT
STEP = 5
UNITS = 12
SLOTS = 4
VEC = 5 * D + FF
F32 = jnp.float32
BF16 = jnp.bfloat16
MESH = pl.DeviceIdType.MESH
NEG = -1e30

norm_eps = 1e-05
beta_one = 0.5
beta_two = 0.5
adam_eps = 1e-08
weight_decay = 0.1
average_keep = 0.75
vector_rate = 0.25
VMEM_LIMIT = 60 * 2**20


def dot(left, right, left_dim=1, right_dim=0):
    return lax.dot_general(
        left, right, (((left_dim,), (right_dim,)), ((), ())), preferred_element_type=F32
    )


def vmem():
    return pl.BlockSpec(memory_space=pltpu.VMEM)


def smem():
    return pl.BlockSpec(memory_space=pltpu.SMEM)


def vec_row(vec, start, size):
    first = start // 128
    return jnp.concatenate([vec[first + r : first + r + 1, :] for r in range(size // 128)], axis=1)


def unit_ranks(owners_ref):
    owner = [owners_ref[u] for u in range(UNITS)]
    rank = []
    for u in range(UNITS):
        total = jnp.int32(0)
        for v in range(u):
            total = total + (owner[v] == owner[u]).astype(jnp.int32)
        rank.append(jnp.minimum(total, SLOTS - 1))
    return owner, rank


def normalize(values):
    center = values - jnp.mean(values, axis=-1, keepdims=True)
    spread = jnp.mean(center * center, axis=-1, keepdims=True)
    scale = lax.rsqrt(spread + norm_eps)
    return center * scale, scale


def norm_back(grads, gain, normed, scale):
    e = grads * gain
    return scale * (
        e
        - jnp.mean(e, axis=-1, keepdims=True)
        - normed * jnp.mean(e * normed, axis=-1, keepdims=True)
    )


def place():
    w = lax.axis_index("wide")
    n = lax.axis_index("narrow")
    return w, n, w // 2, w % 2, n // 2, n % 2


def narrow_peers(at):
    w, n = at[:2]
    return [(w, lax.rem(n + k, 4)) for k in range(1, 4)]


def wide_peers(at):
    w, n = at[:2]
    return [(lax.rem(w + k, 8), n) for k in range(1, 8)]


def chip_peers(at):
    w, n, z, x, y, c = at
    peers = []
    for k in range(1, 16):
        chip = lax.rem(z * 4 + x * 2 + y + k, 16)
        cz, cx, cy = chip // 4, (chip // 2) % 2, chip % 2
        peers.append((cz, cx, cy, (cz * 2 + cx, cy * 2 + c)))
    return peers


def all_peers(at):
    w, n, z, x, y, c = at
    return narrow_peers(at) + wide_peers(at) + [
        (lax.rem(w + k, 8), (1 - y) * 2 + c) for k in range(1, 8)
    ]


def greet(peers):
    barrier = pltpu.get_barrier_semaphore()
    for peer in peers:
        pl.semaphore_signal(barrier, inc=1, device_id=peer, device_id_type=MESH)


def greeted(peers):
    pl.semaphore_wait(pltpu.get_barrier_semaphore(), len(peers))


class Links:
    def __init__(self, send, recv):
        self.send, self.recv, self.slots = send, recv, {}

    def copies(self, key, parts):
        made = []
        for k, (src, dst, device) in enumerate(parts()):
            slot = self.slots.setdefault((key, k), len(self.slots))
            made.append(
                pltpu.make_async_remote_copy(
                    src_ref=src,
                    dst_ref=dst,
                    send_sem=self.send.at[slot],
                    recv_sem=self.recv.at[slot],
                    device_id=device,
                    device_id_type=MESH,
                )
            )
        return made

    def start(self, key, parts):
        for copy in self.copies(key, parts):
            copy.start()

    def wait(self, key, parts):
        for copy in self.copies(key, parts):
            copy.wait()


def partners(w, n, z, x, y, c):
    to_z = [(lax.rem(z + k, 4) * 2 + x, n) for k in range(1, 4)]
    return to_z, (z * 2 + 1 - x, n), (w, (1 - y) * 2 + c), (w, y * 2 + 1 - c)


def spread(ref, head, stage, at):
    w, n, z, x, y, c = at
    to_z, to_x, to_y, to_c = partners(*at)
    whole = slice(None)
    if stage == 0:
        parts = [((z, x, y, c), peer) for peer in to_z]
    elif stage == 1:
        parts = [((pl.ds(0, 2), x, y, c), to_x), ((pl.ds(2, 2), x, y, c), to_y)]
    elif stage == 2:
        parts = [((pl.ds(0, 2), whole, y, c), to_y), ((pl.ds(2, 2), x, whole, c), to_x)]
    else:
        parts = [((whole, whole, whole, c), to_c)]
    return [(ref.at[(*head, *part)], ref.at[(*head, *part)], peer) for part, peer in parts]


def add(a, b):
    return a + b


class Reducer:
    def __init__(self, links, at, source, bufs):
        self.links, self.at, self.source = links, at, source
        (self.c_buf, self.ya_buf, self.xb_buf, self.xa_buf, self.yb_buf, self.z_sum,
         self.z_buf) = bufs

    def start(self, stage, head):
        self.links.start(*self.copies(stage, head))

    def copies(self, stage, head):
        return ("reduce", str(head), stage), lambda: self.parts(stage, head)

    def parts(self, stage, head):
        w, n, z, x, y, c = self.at
        to_z, to_x, to_y, to_c = partners(*self.at)
        whole, low, high = slice(None), pl.ds(0, 2), pl.ds(2, 2)
        source = self.source
        if stage == 0:
            return [(source.at[(*head, whole, whole, whole, 1 - c)], self.c_buf.at[head], to_c)]
        if stage == 1:
            return [
                (source.at[(*head, low, whole, 1 - y, c)], self.ya_buf.at[head], to_y),
                (source.at[(*head, high, 1 - x, whole, c)], self.xb_buf.at[head], to_x),
            ]
        if stage == 2:
            return [
                (source.at[(*head, low, 1 - x, y, c)], self.xa_buf.at[head], to_x),
                (source.at[(*head, high, x, 1 - y, c)], self.yb_buf.at[head], to_y),
            ]
        return [
            (self.z_sum.at[(*head, lax.rem(z + k, 4))], self.z_buf.at[(k - 1, *head)], to_z[k - 1])
            for k in range(1, 4)
        ]

    def finish(self, stage, head):
        w, n, z, x, y, c = self.at
        self.links.wait(*self.copies(stage, head))
        whole, low, high = slice(None), pl.ds(0, 2), pl.ds(2, 2)
        source = self.source
        if stage == 0:
            own = (*head, whole, whole, whole, c)
            source[own] = add(source[own], self.c_buf[head])
        elif stage == 1:
            a = (*head, low, whole, y, c)
            b = (*head, high, x, whole, c)
            source[a] = add(source[a], self.ya_buf[head])
            source[b] = add(source[b], self.xb_buf[head])
        elif stage == 2:
            self.z_sum[(*head, low)] = add(source[(*head, low, x, y, c)], self.xa_buf[head])
            self.z_sum[(*head, high)] = add(source[(*head, high, x, y, c)], self.yb_buf[head])
        else:
            total = self.z_sum[(*head, z)].astype(F32)
            for k in range(3):
                total = total + self.z_buf[(k, *head)].astype(F32)
            return total.astype(BF16)


PIECES = (4, 2, 2, 2, 16)
KEY_PARTS = ((0, 512), (512, 1024), (1024, 1408))
DENSE_PLACE = (8, 0, 2, 4, 6, 1, 3, 5, 7)


def block_kernel(
    owners, counts, masters, text, x, vec, g,
    patch_out, layer_out, probs, slot_grad, text_out, vec_out,
    send_buf, slot_buf, w_first, w_rest, text_buf, q_t, keyed, key_bias, v_t, normed_t,
    text_normed, att_t, inverse, delta, p_buf, g_buf, middle_buf,
    rest_all, c_buf, ya_buf, xb_buf, xa_buf, yb_buf, z_sum, z_buf,
    first_all, first_c, first_d, red, s_buf, r_buf, text_part, text_sum,
    v_own, vw_buf, v_sum, vn_buf, l_own, lw_buf, l_sum, ln_buf,
    query_back, key_back, value_back, value_pair, key_pair_t, send, recv, local
):
    at = place()
    w, n, z, sx, y, c = at
    links = Links(send, recv)
    whole = slice(None)
    peers = all_peers(at)
    gain_one, bias_one = vec_row(vec, 0, D), vec_row(vec, D, D)
    live_text = lax.broadcasted_iota(jnp.int32, (TEXT, 1), 0) < LANG
    read_g = pltpu.make_async_copy(g, g_buf, local.at[2])
    write_layer = pltpu.make_async_copy(g_buf, layer_out, local.at[3])
    write_patch = pltpu.make_async_copy(middle_buf, patch_out, local.at[4])

    greet(peers)
    send_buf[...] = masters[0].reshape(SLOTS, 4, 16, D).astype(BF16)
    text_buf[z, sx] = jnp.zeros((64, TEXT), BF16)
    text_buf[z, sx, :, 0:LANG] = text[0]
    low = (normalize(x[...].astype(F32))[0] * gain_one + bias_one).astype(BF16)
    normed = g_buf
    normed[...] = low
    greeted(peers)
    slots = "slots", lambda: [
        (send_buf.at[:, peer[1]], slot_buf.at[n], peer) for peer in narrow_peers(at)
    ]
    links.start(*slots)
    texts = "text", lambda: [
        (text_buf.at[z, sx], text_buf.at[z, sx], peer) for peer in wide_peers(at)
    ]
    links.start(*texts)
    slot_buf[n] = send_buf[:, n]
    normed_t[:, 0:ROWS] = low.astype(F32).T.astype(BF16)
    owner, rank = unit_ranks(owners)
    links.wait(*slots)
    for u in range(3):
        w_first[u, z, sx, y, c] = slot_buf[owner[u], rank[u]]

    def first(u, s):
        return ("first", u, s), lambda: spread(w_first, (u,), s, at)

    def rest(group, s):
        return ("rest", group, s), lambda: spread(w_rest, (pl.ds(3 * group, 3),), s, at)

    order = (1, 0, 2)
    for u in order:
        links.start(*first(u, 0))
    for k, position in enumerate(DENSE_PLACE):
        w_rest[position, z, sx, y, c] = slot_buf[owner[3 + k], rank[3 + k]]
    for v, live in enumerate(live_column(counts, ROWS)):
        key_bias[v * VIEW_ROWS : (v + 1) * VIEW_ROWS, :] = jnp.broadcast_to(
            jnp.where(live, 0.0, NEG), (VIEW_ROWS, 128)
        ).astype(BF16)
    key_bias[ROWS:KEYS, :] = jnp.broadcast_to(
        jnp.where(live_text, 0.0, NEG), (TEXT, 128)
    ).astype(BF16)
    links.wait(*texts)
    rows = text_buf[...].reshape(D, TEXT).astype(F32).T
    text_low = jnp.where(live_text, normalize(rows)[0] * gain_one + bias_one, 0.0)
    text_normed[...] = text_low.astype(BF16)
    normed_t[:, ROWS:KEYS] = text_low.T.astype(BF16)

    def unit(u):
        return w_first[u].reshape(D, D)

    def project(u):
        if u == 1:
            k = dot(normed[...], unit(1)).astype(BF16)
            t = dot(text_normed[...], unit(1)).astype(BF16)
            for p in range(4):
                pair = slice(p * 128, (p + 1) * 128)
                keyed[p, 0:ROWS] = k[:, pair]
                keyed[p, ROWS:KEYS] = t[:, pair]
        elif u == 0:
            q_t[...] = dot(unit(0), normed[...], 0, 1).astype(BF16) * BF16(0.125)
        else:
            v_t[:, 0:ROWS] = dot(unit(2), normed[...], 0, 1).astype(BF16)
            v_t[:, ROWS:KEYS] = dot(unit(2), text_normed[...], 0, 1).astype(BF16)

    for step in range(3 + 3):
        for s in (3, 2, 1, 0):
            k = step - s
            if not 0 <= k < 3:
                continue
            u = order[k]
            if (k, s) == (2, 3):
                continue
            links.wait(*first(u, s))
            if s < 3:
                links.start(*first(u, s + 1))
            if k == 2 and s < 3:
                links.start(*rest((2, 0, 1)[s], 0))
            if s == 3:
                project(u)

    gather_plan = {
        0: [(2, 0)], 1: [(0, 0)], 2: [(2, 1)], 3: [(1, 0)], 4: [(2, 2), (0, 1)], 5: [],
        6: [(1, 1), (0, 2)], 7: [(2, 3)],
    }

    def gather_point(t):
        for group, s in gather_plan[t]:
            links.wait(*rest(group, s))
            if s < 3:
                links.start(*rest(group, s + 1))

    row = lax.broadcasted_iota(jnp.int32, (128, ROWS), 0)
    one = jnp.where(row == 0, 1.0, 0.0).astype(BF16)

    def saved(t):
        return pltpu.make_async_copy(p_buf.at[t % 2], probs.at[t], local.at[t % 2])

    def values():
        links.wait(*first(2, 3))
        project(2)
        read_g.start()

    def mix(t):
        head = pl.ds(pl.multiple_of(t * 64, 64), 64)
        summed = jnp.concatenate([v_t[head, :], jnp.ones((16, KEYS), BF16)], axis=0)
        mixed = dot(summed, p_buf[t % 2])
        inv = 1.0 / mixed[64:65]
        att_t[head, :] = (mixed[0:64] * inv).astype(BF16)
        inverse[t] = inv

    @pl.loop(0, HEADS)
    def _(t):
        for k in range(HEADS):
            pl.when(t == k)(functools.partial(gather_point, k))
        pl.when(t == 1)(values)
        pl.when(t > 1)(lambda: saved(t - 2).wait())
        pl.when(t > 0)(lambda: mix(t - 1))
        i, h = t // 2, t % 2
        pair_q = q_t[pl.ds(pl.multiple_of(i * 128, 128), 128), :]
        mine = (row >= 64 * h) & (row < 64 * h + 64)
        q = jnp.where(mine, pair_q, jnp.zeros_like(pair_q))
        keys = jnp.concatenate([keyed[i], key_bias[...]], axis=1)
        scores = dot(keys, jnp.concatenate([q, one], axis=0))
        peak = jnp.max(scores, axis=0, keepdims=True)
        for first_key, end_key in KEY_PARTS:
            p_buf[h, first_key:end_key] = jnp.exp(scores[first_key:end_key] - peak).astype(BF16)
        pl.when(t < HEADS - 1)(lambda: saved(t).start())

    mix(HEADS - 1)
    read_g.wait()
    saved(HEADS - 2).wait()

    def fetched(t):
        return pltpu.make_async_copy(probs.at[t], p_buf.at[t % 2], local.at[t % 2])

    reducer = Reducer(links, at, rest_all, (c_buf, ya_buf, xb_buf, xa_buf, yb_buf, z_sum, z_buf))
    dense_order = (3, 0, 1, 2)
    groups = [(pl.ds(2 * j, 2),) for j in dense_order] + [(pl.ds(8, 1),)]

    def step_rest(group, stage):
        total = reducer.finish(stage, groups[group])
        if stage < 3:
            reducer.start(stage + 1, groups[group])
        else:
            red[groups[group]] = total

    def dense_unit(position):
        return w_rest[position].reshape(D, D)

    @pl.when(w >= 0)
    def _():
        gain, bias = vec_row(vec, 2 * D, D), vec_row(vec, 3 * D, D)
        halves = [slice(k * ROWS // 2, (k + 1) * ROWS // 2) for k in range(2)]
        lows, outs = p_buf.at[0, :, 0:D], p_buf.at[0, :, D : 2 * D]
        normals, scales, backs, lives = [], [], [], []
        for k, rows in enumerate(halves):
            index = lax.broadcasted_iota(jnp.int32, (ROWS // 2, 1), 0) + k * (ROWS // 2)
            live = jnp.zeros((ROWS // 2, 1), jnp.bool_)
            for v in range(VIEWS):
                live = live | ((index >= v * VIEW_ROWS) & (index < v * VIEW_ROWS + counts[0, v]))
            middle = x[rows].astype(F32) + dot(att_t[:, rows], dense_unit(8), 0, 0)
            normal, scale = normalize(middle)
            middle_buf[rows] = middle + vec_row(vec, 4 * D + FF, D)
            normals.append(normal)
            scales.append(scale)
            lows[rows] = (normal * gain + bias).astype(BF16)
            backs.append(jnp.zeros((ROWS // 2, D), F32))
            lives.append(live)
            outs[rows] = jnp.where(live, g_buf[rows].astype(F32), 0.0).astype(BF16)
        for turn, j in enumerate(dense_order):
            if turn == 1:
                links.wait(*rest(1, 2))
                links.start(*rest(1, 3))
                links.wait(*rest(0, 3))
            if turn == 2:
                links.wait(*rest(1, 3))
            w_up, w_down = dense_unit(2 * j), dense_unit(2 * j + 1)
            up_total, down_total, up_grad = 0.0, 0.0, 0.0
            for k, rows in enumerate(halves):
                preact = dot(lows[rows], w_up) + vec_row(vec, 4 * D + j * D, D)
                phi = 0.5 + 0.5 * lax.erf(preact * 0.7071067811865476)
                active = (preact * phi).astype(BF16)
                slope = phi + preact * (jnp.exp(-0.5 * preact * preact) * 0.3989422804014327)
                middle_buf[rows] += dot(active, w_down)
                preact_back = (dot(outs[rows], w_down, 1, 1) * slope).astype(BF16)
                backs[k] = backs[k] + dot(preact_back, w_up, 1, 1)
                up_total = up_total + dot(lows[rows], preact_back, 0, 0)
                down_total = down_total + dot(active, outs[rows], 0, 0)
                up_grad = up_grad + jnp.sum(preact_back.astype(F32), axis=0, keepdims=True)
            rest_all[2 * j] = up_total.astype(BF16).reshape(*PIECES, D)
            rest_all[2 * j + 1] = down_total.astype(BF16).reshape(*PIECES, D)
            for r in range(4):
                v_own[16 + 4 * j + r : 17 + 4 * j + r, :] = up_grad[:, r * 128 : (r + 1) * 128]
            reducer.start(0, groups[turn])
            for s in range(min(turn, 3)):
                step_rest(turn - 1 - s, s)
        for k, rows in enumerate(halves):
            g_buf[rows] = jnp.where(lives[k], middle_buf[rows], 0.0).astype(BF16)
        write_layer.start()
        out_total, gain_grad, bias_grad, down_grad = 0.0, 0.0, 0.0, 0.0
        for k, rows in enumerate(halves):
            out_back = outs[rows].astype(F32)
            back = out_back + norm_back(backs[k], gain, normals[k], scales[k])
            middle_buf[rows] = back
            branch = back.astype(BF16)
            out_total = out_total + dot(att_t[:, rows], branch)
            back_rows = dot(dense_unit(8), branch, 1, 1).astype(BF16)
            product = back_rows.astype(F32) * att_t[:, rows].astype(F32)
            for h in range(HEADS):
                part = jnp.sum(product[h * 64 : (h + 1) * 64], axis=0, keepdims=True)
                delta[h, :, rows] = part * inverse[h, :, rows]
            att_t[:, rows] = back_rows
            gain_grad = gain_grad + jnp.sum(backs[k] * normals[k], axis=0, keepdims=True)
            bias_grad = bias_grad + jnp.sum(backs[k], axis=0, keepdims=True)
            down_grad = down_grad + jnp.sum(out_back, axis=0, keepdims=True)
        rest_all[8] = out_total.astype(BF16).reshape(*PIECES, D)
        for offset, piece in ((8, gain_grad), (12, bias_grad), (32, down_grad)):
            for r in range(4):
                v_own[offset + r : offset + r + 1, :] = piece[:, r * 128 : (r + 1) * 128]
        v_own[0:8, :] = jnp.zeros((8, 128), F32)

    fetched(HEADS - 2).start()
    back_t = att_t

    def chunk_core(p):
        return ("chunk", p, 0), lambda: [
            (first_all.at[p, :, :, :, :, 1 - c], first_c.at[p], (w, y * 2 + 1 - c))
        ]

    chip = z * 4 + sx * 2 + y

    def chunk_chips(p):
        return ("chunk", p, 1), lambda: [
            (first_all.at[p, :, cz, cx, cy, c], first_d.at[p, chip], peer)
            for cz, cx, cy, peer in chip_peers(at)
        ]

    def chunk_middle(p):
        links.wait(*chunk_core(p))
        own = (p, whole, whole, whole, whole, c)
        first_all[own] = add(first_all[own], first_c[p])
        links.start(*chunk_chips(p))
        first_d[p, chip] = first_all[p, :, z, sx, y, c]

    def chunk_end(p):
        links.wait(*chunk_chips(p))
        total = jnp.sum(first_d[p].astype(F32), axis=0).astype(BF16)
        red[9:12, :, p * 128 : (p + 1) * 128] = total

    wides = "wide", lambda: [(v_own, vw_buf.at[w], peer) for peer in wide_peers(at)]
    narrows = "narrow", lambda: [(v_sum, vn_buf.at[n], peer) for peer in narrow_peers(at)]

    def vector_start():
        vw_buf[w] = v_own[...]
        links.start(*wides)

    def vector_middle():
        links.wait(*wides)
        total = vw_buf[0]
        for k in range(1, 8):
            total = total + vw_buf[k]
        v_sum[...] = total
        vn_buf[n] = total
        links.start(*narrows)

    def reduce_point(t):
        for group, s in {
            0: [(1, 2), (2, 1), (3, 0)], 1: [(4, 0)], 2: [(0, 3), (1, 3), (2, 2), (3, 1)],
            3: [(4, 1)], 4: [(2, 3), (3, 2)], 5: [(4, 2)], 6: [(3, 3)], 7: [(4, 3)],
        }[t]:
            step_rest(group, s)
        if t == 0:
            reducer.start(0, groups[4])
            vector_start()
        if t == 3:
            vector_middle()
        if t in (3, 5, 7):
            chunk_middle(3 - (t - 3) // 2)
        if t == 6:
            chunk_end(3)

    lane = lax.broadcasted_iota(jnp.int32, (KEYS, 128), 1)
    ones = jnp.where(lane < 2, 1.0, 0.0).astype(BF16)

    @pl.loop(0, HEADS)
    def _(step):
        for k in range(HEADS):
            pl.when(step == k)(functools.partial(reduce_point, k))
        t = HEADS - 1 - step
        i, h = t // 2, t % 2
        pl.when(step > 0)(lambda: fetched(t).wait())
        pair = pl.ds(pl.multiple_of(i * 128, 128), 128)
        head = pl.ds(pl.multiple_of(t * 64, 64), 64)

        @pl.when(h == 1)
        def _():
            value_pair[...] = v_t[pair, :].astype(F32).T.astype(BF16)
            key_pair_t[...] = keyed[i].astype(F32).T.astype(BF16)

        inv = inverse[t]
        shift = delta[t]
        high = shift.astype(BF16).astype(F32)
        mine = (row >= 64 * h) & (row < 64 * h + 64)
        scaled = jnp.where(mine, back_t[pair, :].astype(F32) * inv, 0.0).astype(BF16)
        tail = jnp.where(row == 0, -high, jnp.where(row == 1, high - shift, 0.0)).astype(BF16)
        right = jnp.concatenate([scaled, tail], axis=0)
        value = jnp.concatenate([value_pair[...], ones], axis=1)
        key_head = key_pair_t[pl.ds(pl.multiple_of(h * 64, 64), 64), :]
        query_head = q_t[head, :]
        back_head = (back_t[head, :].astype(F32) * inv).astype(BF16)
        query_total = jnp.zeros((64, ROWS), F32)
        for first_key, end_key in KEY_PARTS:
            part = slice(first_key, end_key)
            low = p_buf[h, part]
            score_back = low * dot(value[part], right).astype(BF16)
            query_total = query_total + dot(key_head[:, part], score_back)
            key_back[head, part] = dot(query_head, score_back, 1, 1).astype(BF16)
            value_back[head, part] = dot(back_head, low, 1, 1).astype(BF16)
        query_back[head, :] = (query_total * 0.125).astype(BF16)
        pl.when(t > 1)(lambda: fetched(t - 2).start())

        @pl.when(h == 0)
        def _():
            part = dot(normed_t[:, 0:ROWS], query_back[pair, :], 1, 1).astype(BF16)
            first_all[i, 0] = part.reshape(*PIECES, 128)
            both = jnp.concatenate([key_back[pair, :], value_back[pair, :]], axis=0)
            part = dot(normed_t[...], both, 1, 1).astype(BF16)
            for u in range(2):
                first_all[i, 1 + u] = part[:, u * 128 : (u + 1) * 128].reshape(*PIECES, 128)

        for k in range(4):
            pl.when(step == 2 * k + 1)(lambda p=3 - k: links.start(*chunk_core(p)))

    @pl.when(w >= 0)
    def _():
        w_q, w_k, w_v = unit(0), unit(1), unit(2)
        normal, scale = normalize(text_buf[...].reshape(D, TEXT).astype(F32).T)
        text_back = dot(key_back[:, ROWS:KEYS], w_k, 0, 1) + dot(
            value_back[:, ROWS:KEYS], w_v, 0, 1
        )
        text_part[...] = (
            norm_back(text_back, gain_one, normal, scale).T.astype(BF16).reshape(8, 64, TEXT)
        )
        gain_grad = jnp.sum(text_back * normal, axis=0, keepdims=True)
        bias_grad = jnp.sum(text_back, axis=0, keepdims=True)
        text_sum[w] = text_part[w]
        text_parts = "parts", lambda: [
            (text_part.at[peer[0]], text_sum.at[w], peer) for peer in wide_peers(at)
        ]
        chunk_middle(0)
        links.start(*text_parts)
        chunk_end(2)
        tile = ROWS // 2
        kept = []
        for t in range(2):
            rows = slice(t * tile, (t + 1) * tile)
            normal, scale = normalize(x[rows].astype(F32))
            projected = (
                dot(query_back[:, rows], w_q, 0, 1)
                + dot(key_back[:, rows], w_k, 0, 1)
                + dot(value_back[:, rows], w_v, 0, 1)
            )
            kept.append((rows, projected, normal, scale))
            gain_grad = gain_grad + jnp.sum(projected * normal, axis=0, keepdims=True)
            bias_grad = bias_grad + jnp.sum(projected, axis=0, keepdims=True)
        for r in range(4):
            l_own[r : r + 1, :] = gain_grad[:, r * 128 : (r + 1) * 128]
            l_own[4 + r : 5 + r, :] = bias_grad[:, r * 128 : (r + 1) * 128]
        late_wides = "late wide", lambda: [(l_own, lw_buf.at[w], peer) for peer in wide_peers(at)]
        late_narrows = "late narrow", lambda: [
            (l_sum, ln_buf.at[n], peer) for peer in narrow_peers(at)
        ]
        lw_buf[w] = l_own[...]
        links.start(*late_wides)
        for rows, projected, normal, scale in kept:
            middle_buf[rows] += norm_back(projected, gain_one, normal, scale)
        write_patch.start()
        links.wait(*narrows)
        vec_out[...] = (vn_buf[0] + vn_buf[1]) + (vn_buf[2] + vn_buf[3])
        owner, rank = unit_ranks(owners)
        spots = []
        for q in range(4):
            for s in range(SLOTS):
                spot = jnp.int32(0)
                for u in range(UNITS):
                    position = 9 + u if u < 3 else DENSE_PLACE[u - 3]
                    spot = spot + jnp.where((owner[u] == q) & (rank[u] == s), position, 0)
                spots.append((q, s, jnp.minimum(spot, UNITS - 1)))

        def grads(part, columns):
            return ("grads", part), lambda: [
                (s_buf.at[peer[1], :, :, columns], r_buf.at[n, :, :, columns], peer)
                for peer in narrow_peers(at)
            ]

        def send_grads(part, columns):
            for q, s, spot in spots:
                s_buf[q, s, :, columns] = red[spot, :, columns]
            links.start(*grads(part, columns))
            r_buf[n, :, :, columns] = s_buf[n, :, :, columns]

        others, last = slice(128, 512), slice(0, 128)
        chunk_end(1)
        send_grads(0, others)
        links.wait(*text_parts)
        text_out[...] = jnp.sum(text_sum[...].astype(F32), axis=0)
        chunk_end(0)
        send_grads(1, last)
        links.wait(*late_wides)
        total = lw_buf[0]
        for k in range(1, 8):
            total = total + lw_buf[k]
        l_sum[...] = total
        ln_buf[n] = total
        links.start(*late_narrows)
        links.wait(*grads(0, others))
        links.wait(*grads(1, last))
        for q in range(4):
            slot_grad[:, q * 16 : (q + 1) * 16, :] = r_buf[q].astype(F32)
        write_layer.wait()
        write_patch.wait()
        links.wait(*late_narrows)
        vec_out[0:8, :] = (ln_buf[0] + ln_buf[1]) + (ln_buf[2] + ln_buf[3])


def block(owners, counts, masters, text, x, vec, g):
    hbm = pl.BlockSpec(memory_space=pl.ANY)
    copies = 3 + 7 + 24 + 24 + 5 * 8 + 4 * 16 + 7 + 3 + 7 + 7 + 3 + 6
    bf = lambda *s: pltpu.VMEM(s, BF16)
    f32 = lambda *s: pltpu.VMEM(s, F32)
    rows = VEC // 128
    return pl.pallas_call(
        block_kernel,
        in_specs=[smem(), smem(), vmem(), vmem(), vmem(), vmem(), hbm],
        out_specs=[hbm, hbm, hbm, vmem(), vmem(), vmem()],
        out_shape=[
            jax.ShapeDtypeStruct((ROWS, D), F32),
            jax.ShapeDtypeStruct((ROWS, D), BF16),
            jax.ShapeDtypeStruct((HEADS - 1, KEYS, ROWS), BF16),
            jax.ShapeDtypeStruct((SLOTS, 64, D), F32),
            jax.ShapeDtypeStruct((64, TEXT), F32),
            jax.ShapeDtypeStruct((rows, 128), F32),
        ],
        scratch_shapes=[
            bf(SLOTS, 4, 16, D),
            bf(4, SLOTS, 16, D),
            bf(3, *PIECES, D),
            bf(9, *PIECES, D),
            bf(4, 2, 64, TEXT),
            bf(D, ROWS),
            bf(4, KEYS, 128),
            bf(KEYS, 128),
            bf(D, KEYS),
            bf(D, KEYS),
            bf(TEXT, D),
            bf(D, ROWS),
            f32(HEADS, 1, ROWS),
            f32(HEADS, 1, ROWS),
            bf(2, KEYS, ROWS),
            bf(ROWS, D),
            f32(ROWS, D),
            bf(9, *PIECES, D),
            bf(9, 4, 2, 2, 16, D),
            bf(9, 2, 2, 16, D),
            bf(9, 2, 2, 16, D),
            bf(9, 2, 16, D),
            bf(9, 2, 16, D),
            bf(9, 4, 16, D),
            bf(3, 9, 16, D),
            bf(4, 3, *PIECES, 128),
            bf(4, 3, 4, 2, 2, 16, 128),
            bf(4, 16, 3, 16, 128),
            bf(UNITS, 16, D),
            bf(4, SLOTS, 16, D),
            bf(4, SLOTS, 16, D),
            bf(8, 64, TEXT),
            bf(8, 64, TEXT),
            f32(rows, 128),
            f32(8, rows, 128),
            f32(rows, 128),
            f32(4, rows, 128),
            f32(8, 128),
            f32(8, 8, 128),
            f32(8, 128),
            f32(4, 8, 128),
            bf(D, ROWS),
            bf(D, KEYS),
            bf(D, KEYS),
            bf(KEYS, 128),
            bf(128, KEYS),
            pltpu.SemaphoreType.DMA((copies,)),
            pltpu.SemaphoreType.DMA((copies,)),
            pltpu.SemaphoreType.DMA((5,)),
        ],
        compiler_params=pltpu.CompilerParams(
            collective_id=1, has_side_effects=True, vmem_limit_bytes=63 * 2**20
        ),
    )(owners, counts, masters, text, x, vec, g)


def gather(owners, masters, text_t):
    packed = lax.all_gather(masters.astype(BF16), "wide", axis=2, tiled=True)
    packed = lax.all_gather(packed, "narrow", axis=0, tiled=True)
    same = owners[:, None] == owners[None, :]
    ids = jnp.arange(UNITS)
    rank = jnp.sum((same & (ids[None, :] < ids[:, None])).astype(jnp.int32), axis=1)
    units = jnp.take(packed.reshape(-1, D, D), owners * SLOTS + rank, axis=0)
    rows = lax.all_gather(text_t, "wide", axis=1, tiled=True)[0]
    return units, jnp.pad(rows, ((0, 0), (0, TEXT - LANG)))


def live_column(counts, rows):
    index = lax.broadcasted_iota(jnp.int32, (VIEW_ROWS, 1), 0)
    return [(index < counts[0, v]) for v in range(rows // VIEW_ROWS)]


def forward_kernel(
    counts, x, text_t, vec, w, att_t, probs, inverse, q_t, keyed, v_t, normed, text_normed
):
    i = pl.program_id(0)

    @pl.when(i == 0)
    def _():
        gain, bias = vec_row(vec, 0, D), vec_row(vec, D, D)
        normed[...] = (normalize(x[...].astype(F32))[0] * gain + bias).astype(BF16)
        rows = text_t[...].astype(F32).T
        live_text = lax.broadcasted_iota(jnp.int32, (TEXT, 1), 0) < LANG
        text_normed[...] = jnp.where(
            live_text, normalize(rows)[0] * gain + bias, 0.0
        ).astype(BF16)
        q_t[...] = dot(w[0], normed[...], 0, 1).astype(BF16) * BF16(0.125)
        v_t[:, 0:ROWS] = dot(w[2], normed[...], 0, 1).astype(BF16)
        v_t[:, ROWS:KEYS] = dot(w[2], text_normed[...], 0, 1).astype(BF16)
        for p in range(4):
            pair = slice(p * 128, (p + 1) * 128)
            keyed[p, 0:ROWS, 0:128] = dot(normed[...], w[1, :, pair]).astype(BF16)
            keyed[p, ROWS:KEYS, 0:128] = dot(text_normed[...], w[1, :, pair]).astype(BF16)
            for v, live in enumerate(live_column(counts, ROWS)):
                keyed[p, v * VIEW_ROWS : (v + 1) * VIEW_ROWS, 128:256] = jnp.broadcast_to(
                    jnp.where(live, 0.0, NEG), (VIEW_ROWS, 128)
                ).astype(BF16)
            keyed[p, ROWS:KEYS, 128:256] = jnp.broadcast_to(
                jnp.where(live_text, 0.0, NEG), (TEXT, 128)
            ).astype(BF16)

    row = lax.broadcasted_iota(jnp.int32, (128, ROWS), 0)
    one = jnp.where(row == 0, 1.0, 0.0).astype(BF16)
    pair_q = q_t[pl.ds(pl.multiple_of(i * 128, 128), 128), :]
    for h in range(2):
        mine = (row >= 64 * h) & (row < 64 * h + 64)
        q = jnp.where(mine, pair_q, jnp.zeros_like(pair_q))
        scores = dot(keyed[i], jnp.concatenate([q, one], axis=0))
        peak = jnp.max(scores, axis=0, keepdims=True)
        e = jnp.exp(scores - peak)
        total = jnp.sum(e, axis=0, keepdims=True)
        low = e.astype(BF16)
        probs[h] = low
        mixed = dot(v_t[pl.ds(pl.multiple_of(i * 128 + h * 64, 64), 64), :], low)
        inv = 1.0 / total
        att_t[h * 64 : (h + 1) * 64, :] = (mixed * inv).astype(BF16)
        inverse[0, h : h + 1, :] = inv


def attention_forward(counts, x, text_t, vec, units):
    return pl.pallas_call(
        forward_kernel,
        grid=(4,),
        in_specs=[smem(), vmem(), vmem(), vmem(), pl.BlockSpec((3, D, D), lambda i: (0, 0, 0))],
        out_specs=[
            pl.BlockSpec((128, ROWS), lambda i: (i, 0)),
            pl.BlockSpec((2, KEYS, ROWS), lambda i: (i, 0, 0)),
            pl.BlockSpec((1, 2, ROWS), lambda i: (i, 0, 0)),
            pl.BlockSpec((D, ROWS), lambda i: (0, 0)),
            pl.BlockSpec((4, KEYS, 256), lambda i: (0, 0, 0)),
            pl.BlockSpec((D, KEYS), lambda i: (0, 0)),
        ],
        out_shape=[
            jax.ShapeDtypeStruct((D, ROWS), BF16),
            jax.ShapeDtypeStruct((HEADS, KEYS, ROWS), BF16),
            jax.ShapeDtypeStruct((4, 2, ROWS), F32),
            jax.ShapeDtypeStruct((D, ROWS), BF16),
            jax.ShapeDtypeStruct((4, KEYS, 256), BF16),
            jax.ShapeDtypeStruct((D, KEYS), BF16),
        ],
        scratch_shapes=[pltpu.VMEM((ROWS, D), BF16), pltpu.VMEM((TEXT, D), BF16)],
        compiler_params=pltpu.CompilerParams(vmem_limit_bytes=VMEM_LIMIT),
    )(counts, x, text_t, vec, units)


def dense_kernel(
    counts, att_t, x, g, vec, w,
    layer_out, middle_back, back_t, grads, gain_grad, bias_grad, up_grad, down_grad,
    total, *, tile
):
    i = pl.program_id(0)
    steps = pl.num_programs(0)
    gain, bias = vec_row(vec, 2 * D, D), vec_row(vec, 3 * D, D)
    a = att_t[...]
    index = lax.broadcasted_iota(jnp.int32, (tile, 1), 0) + i * tile
    live = jnp.zeros((tile, 1), jnp.bool_)
    for v in range(VIEWS):
        live = live | ((index >= v * VIEW_ROWS) & (index < v * VIEW_ROWS + counts[0, v]))
    middle = x[...].astype(F32) + dot(a, w[0], 0, 0)
    normed, scale = normalize(middle)
    low = (normed * gain + bias).astype(BF16)
    out_back = jnp.where(live, g[...].astype(F32), 0.0)
    out_low = out_back.astype(BF16)

    @pl.when(i == 0)
    def _():
        total[...] = jnp.zeros_like(total)
        gain_grad[...] = jnp.zeros_like(gain_grad)
        bias_grad[...] = jnp.zeros_like(bias_grad)
        up_grad[...] = jnp.zeros_like(up_grad)
        down_grad[...] = jnp.zeros_like(down_grad)

    out = middle + vec_row(vec, 4 * D + FF, D)
    normed_back = jnp.zeros((tile, D), F32)
    for j in range(4):
        block = slice(j * D, (j + 1) * D)
        preact = dot(low, w[1 + j]) + vec_row(vec, 4 * D + j * D, D)
        phi = 0.5 + 0.5 * lax.erf(preact * 0.7071067811865476)
        active = (preact * phi).astype(BF16)
        slope = phi + preact * (jnp.exp(-0.5 * preact * preact) * 0.3989422804014327)
        out = out + dot(active, w[5 + j])
        preact_back = (dot(out_low, w[5 + j], 1, 1) * slope).astype(BF16)
        normed_back = normed_back + dot(preact_back, w[1 + j], 1, 1)
        total[1 + j] += dot(low, preact_back, 0, 0)
        total[5 + j] += dot(active, out_low, 0, 0)
        up_grad[:, block] += jnp.sum(preact_back.astype(F32), axis=0, keepdims=True)
    layer_out[...] = jnp.where(live, out, 0.0).astype(BF16)
    back = out_back + norm_back(normed_back, gain, normed, scale)
    middle_back[...] = back
    branch = back.astype(BF16)
    back_t[...] = dot(w[0], branch, 1, 1).astype(BF16)
    total[0] += dot(a, branch)
    gain_grad[...] += jnp.sum(normed_back * normed, axis=0, keepdims=True)
    bias_grad[...] += jnp.sum(normed_back, axis=0, keepdims=True)
    down_grad[...] += jnp.sum(out_back, axis=0, keepdims=True)

    @pl.when(i == steps - 1)
    def _():
        grads[...] = total[...].astype(BF16)


def dense(counts, att_t, x, g, vec, units, tile=640):
    rows = pl.BlockSpec((tile, D), lambda i: (i, 0))
    columns = pl.BlockSpec((D, tile), lambda i: (0, i))
    return pl.pallas_call(
        functools.partial(dense_kernel, tile=tile),
        grid=(ROWS // tile,),
        in_specs=[smem(), columns, rows, rows, vmem(), vmem()],
        out_specs=[
            rows,
            rows,
            columns,
            pl.BlockSpec((9, D, D), lambda i: (0, 0, 0)),
            pl.BlockSpec((1, D), lambda i: (0, 0)),
            pl.BlockSpec((1, D), lambda i: (0, 0)),
            pl.BlockSpec((1, FF), lambda i: (0, 0)),
            pl.BlockSpec((1, D), lambda i: (0, 0)),
        ],
        out_shape=[
            jax.ShapeDtypeStruct((ROWS, D), BF16),
            jax.ShapeDtypeStruct((ROWS, D), F32),
            jax.ShapeDtypeStruct((D, ROWS), BF16),
            jax.ShapeDtypeStruct((9, D, D), BF16),
            jax.ShapeDtypeStruct((1, D), F32),
            jax.ShapeDtypeStruct((1, D), F32),
            jax.ShapeDtypeStruct((1, FF), F32),
            jax.ShapeDtypeStruct((1, D), F32),
        ],
        scratch_shapes=[pltpu.VMEM((9, D, D), F32)],
        compiler_params=pltpu.CompilerParams(vmem_limit_bytes=VMEM_LIMIT),
    )(counts, att_t, x, g, vec, units)


def backward_kernel(probs, inverse, keyed, v_t, back_t, q_t, att_t, query_back, key_back, value_back):
    row = lax.broadcasted_iota(jnp.int32, (128, ROWS), 0)
    lane = lax.broadcasted_iota(jnp.int32, (KEYS, 128), 1)
    ones = jnp.where(lane < 2, 1.0, 0.0).astype(BF16)
    value = jnp.concatenate([v_t[...].astype(F32).T.astype(BF16), ones], axis=1)
    key_t = keyed[:, 0:128].astype(F32).T.astype(BF16)
    back = back_t[...].astype(F32)
    product = back * att_t[...].astype(F32)
    query = q_t[...].astype(F32)
    key_total = jnp.zeros((KEYS, 128), F32)
    value_total = jnp.zeros((KEYS, 128), F32)
    for h in range(2):
        half = slice(h * 64, (h + 1) * 64)
        inv = inverse[0, h : h + 1, :]
        delta = jnp.sum(product[half], axis=0, keepdims=True) * inv
        high = delta.astype(BF16).astype(F32)
        mine = (row >= 64 * h) & (row < 64 * h + 64)
        scaled = jnp.where(mine, back * inv, 0.0)
        tail = jnp.where(row == 0, -high, jnp.where(row == 1, high - delta, 0.0))
        right = jnp.concatenate([scaled.astype(BF16), tail.astype(BF16)], axis=0)
        low = probs[h]
        score_back = low * dot(value, right).astype(BF16)
        query_back[half, :] = (dot(key_t[half], score_back) * 0.125).astype(BF16)
        key_total += dot(score_back, jnp.where(mine, query, 0.0).T.astype(BF16))
        value_total += dot(low, scaled.T.astype(BF16))
    key_back[...] = key_total.astype(BF16)
    value_back[...] = value_total.astype(BF16)


def attention_backward(probs, inverse, keyed, v_t, back_t, q_t, att_t):
    return pl.pallas_call(
        backward_kernel,
        grid=(4,),
        in_specs=[
            pl.BlockSpec((2, KEYS, ROWS), lambda i: (i, 0, 0)),
            pl.BlockSpec((1, 2, ROWS), lambda i: (i, 0, 0)),
            pl.BlockSpec((None, KEYS, 256), lambda i: (i, 0, 0)),
            pl.BlockSpec((128, KEYS), lambda i: (i, 0)),
            pl.BlockSpec((128, ROWS), lambda i: (i, 0)),
            pl.BlockSpec((128, ROWS), lambda i: (i, 0)),
            pl.BlockSpec((128, ROWS), lambda i: (i, 0)),
        ],
        out_specs=[
            pl.BlockSpec((128, ROWS), lambda i: (i, 0)),
            pl.BlockSpec((KEYS, 128), lambda i: (0, i)),
            pl.BlockSpec((KEYS, 128), lambda i: (0, i)),
        ],
        out_shape=[
            jax.ShapeDtypeStruct((D, ROWS), BF16),
            jax.ShapeDtypeStruct((KEYS, D), BF16),
            jax.ShapeDtypeStruct((KEYS, D), BF16),
        ],
        compiler_params=pltpu.CompilerParams(vmem_limit_bytes=VMEM_LIMIT),
    )(probs, inverse, keyed, v_t, back_t, q_t, att_t)


def project_kernel(
    x, text_t, vec, w, middle_back, query_back, key_back, value_back, text_key, text_value,
    patch_grad, grads, gain_grad, bias_grad, text_grad_t, total
):
    i = pl.program_id(0)
    steps = pl.num_programs(0)
    gain, bias = vec_row(vec, 0, D), vec_row(vec, D, D)

    @pl.when(i == 0)
    def _():
        live = lax.broadcasted_iota(jnp.int32, (TEXT, 1), 0) < LANG
        normed, scale = normalize(text_t[...].astype(F32).T)
        low_t = jnp.where(live, normed * gain + bias, 0.0).T.astype(BF16)
        k, v = text_key[...], text_value[...]
        back = dot(k, w[1], 1, 1) + dot(v, w[2], 1, 1)
        text_grad_t[...] = norm_back(back, gain, normed, scale).T.astype(BF16)
        gain_grad[...] = jnp.sum(back * normed, axis=0, keepdims=True)
        bias_grad[...] = jnp.sum(back, axis=0, keepdims=True)
        total[0] = jnp.zeros((D, D), F32)
        total[1] = dot(low_t, k)
        total[2] = dot(low_t, v)

    normed, scale = normalize(x[...].astype(F32))
    low_t = (normed * gain + bias).T.astype(BF16)
    q, k, v = query_back[...], key_back[...], value_back[...]
    back = dot(q, w[0], 0, 1) + dot(k, w[1], 1, 1) + dot(v, w[2], 1, 1)
    patch_grad[...] = middle_back[...] + norm_back(back, gain, normed, scale)
    total[0] += dot(low_t, q, 1, 1)
    total[1] += dot(low_t, k)
    total[2] += dot(low_t, v)
    gain_grad[...] += jnp.sum(back * normed, axis=0, keepdims=True)
    bias_grad[...] += jnp.sum(back, axis=0, keepdims=True)

    @pl.when(i == steps - 1)
    def _():
        grads[...] = total[...].astype(BF16)


def project_back(x, text_t, vec, units, middle_back, query_back, key_back, value_back, tile=640):
    rows = pl.BlockSpec((tile, D), lambda i: (i, 0))
    text_rows = pl.BlockSpec((TEXT, D), lambda i: (ROWS // TEXT, 0))
    return pl.pallas_call(
        project_kernel,
        grid=(ROWS // tile,),
        in_specs=[
            rows,
            vmem(),
            vmem(),
            pl.BlockSpec((3, D, D), lambda i: (0, 0, 0)),
            rows,
            pl.BlockSpec((D, tile), lambda i: (0, i)),
            rows,
            rows,
            text_rows,
            text_rows,
        ],
        out_specs=[
            rows,
            pl.BlockSpec((3, D, D), lambda i: (0, 0, 0)),
            pl.BlockSpec((1, D), lambda i: (0, 0)),
            pl.BlockSpec((1, D), lambda i: (0, 0)),
            pl.BlockSpec((D, TEXT), lambda i: (0, 0)),
        ],
        out_shape=[
            jax.ShapeDtypeStruct((ROWS, D), F32),
            jax.ShapeDtypeStruct((3, D, D), BF16),
            jax.ShapeDtypeStruct((1, D), F32),
            jax.ShapeDtypeStruct((1, D), F32),
            jax.ShapeDtypeStruct((D, TEXT), BF16),
        ],
        scratch_shapes=[pltpu.VMEM((3, D, D), F32)],
        compiler_params=pltpu.CompilerParams(vmem_limit_bytes=VMEM_LIMIT),
    )(
        x, text_t, vec, units, middle_back, query_back, key_back, value_back, key_back, value_back
    )


def reduce_all(owners, rest, first, text, vecs):
    vec = lax.psum(jnp.concatenate(vecs, axis=1), ("wide", "narrow"))
    text_sum = lax.psum_scatter(text.astype(F32), "wide", scatter_dimension=0, tiled=True)
    all_units = jnp.concatenate([first, rest], axis=0).astype(F32)
    rows = lax.psum_scatter(all_units, "wide", scatter_dimension=1, tiled=True)
    same = owners[:, None] == owners[None, :]
    ids = jnp.arange(UNITS)
    rank = jnp.sum((same & (ids[None, :] < ids[:, None])).astype(jnp.int32), axis=1)
    pick = (owners[None, None, :] == jnp.arange(lax.axis_size("narrow"))[:, None, None]) & (
        rank[None, None, :] == jnp.arange(SLOTS)[None, :, None]
    )
    terms = jnp.einsum("nsu,urc->nsrc", pick.astype(F32), rows, precision=lax.Precision.HIGHEST)
    slots = lax.psum_scatter(terms, "narrow", scatter_dimension=0, tiled=True)
    return slots[0], text_sum, vec.reshape(VEC // 128, 128)


def adam(master, moment_one, moment_two, averaged, gradient, rate):
    moment_one = beta_one * moment_one + (1.0 - beta_one) * gradient
    moment_two = beta_two * moment_two + (1.0 - beta_two) * gradient * gradient
    mean_hat = moment_one / (1.0 - beta_one**STEP)
    second_hat = moment_two / (1.0 - beta_two**STEP)
    master = master - rate * (
        mean_hat / (jnp.sqrt(second_hat) + adam_eps) + weight_decay * master
    )
    averaged = average_keep * averaged + (1.0 - average_keep) * master
    return master, moment_one, moment_two, averaged


def unit_rates():
    blocks = FF // D
    fans = [2 * D // 3, 2 * D // 3, D, D // 64] + [D] * blocks + [FF] * blocks
    return [float(fan) ** -0.5 for fan in fans]


def update_kernel(
    owners, grad, masters, first, second, average, text_t, vec_grad, vec, vec_first, vec_second,
    vec_average, patch_in, layer_in,
    new_masters, new_first, new_second, new_average, new_copies, text_grad,
    vec_new_value, vec_new_first, vec_new_second, vec_new_average, patch_out, layer_out,
):
    s = pl.program_id(0)
    patch_out[...] = patch_in[...]
    layer_out[...] = layer_in[...]
    n = lax.axis_index("narrow")
    owner, rank = unit_ranks(owners)
    rate, filled = jnp.float32(0.0), jnp.int32(0)
    for u, value in enumerate(unit_rates()):
        match = (owner[u] == n) & (rank[u] == s)
        rate = rate + jnp.where(match, jnp.float32(value), jnp.float32(0.0))
        filled = filled + match.astype(jnp.int32)
    state = adam(masters[0, 0], first[0, 0], second[0, 0], average[0, 0], grad[0], rate)
    keep = jnp.broadcast_to(filled, state[0].shape) > 0
    state = [jnp.where(keep, part, 0.0) for part in state]
    for ref, part in zip((new_masters, new_first, new_second, new_average), state):
        ref[0, 0] = part
    new_copies[0, 0] = state[0].astype(BF16)

    @pl.when(s == 0)
    def _():
        text_grad[0] = text_t[:, 0:LANG]
        state = adam(
            vec[...], vec_first[...], vec_second[...], vec_average[...], vec_grad[...], vector_rate
        )
        for ref, part in zip(
            (vec_new_value, vec_new_first, vec_new_second, vec_new_average), state
        ):
            ref[...] = part


def update(
    owners, grad, masters, first, second, average, text_t, vec_grad, vec, v1, v2, va, patch, layer
):
    rows = masters.shape[2]
    state = jax.ShapeDtypeStruct(masters.shape, F32)
    vector = jax.ShapeDtypeStruct(vec.shape, F32)
    slot = pl.BlockSpec((1, 1, rows, D), lambda s: (0, s, 0, 0))
    vec_spec = pl.BlockSpec(vec.shape, lambda s: (0, 0))
    handed = pl.BlockSpec((ROWS // SLOTS, D), lambda s: (s, 0))
    return pl.pallas_call(
        update_kernel,
        grid=(SLOTS,),
        out_shape=[state] * 4
        + [
            jax.ShapeDtypeStruct(masters.shape, BF16),
            jax.ShapeDtypeStruct((1, text_t.shape[0], LANG), F32),
        ]
        + [vector] * 4
        + [jax.ShapeDtypeStruct(patch.shape, F32), jax.ShapeDtypeStruct(layer.shape, BF16)],
        in_specs=[smem(), pl.BlockSpec((1, rows, D), lambda s: (s, 0, 0))]
        + [slot] * 4
        + [pl.BlockSpec(text_t.shape, lambda s: (0, 0))]
        + [vec_spec] * 5
        + [handed] * 2,
        out_specs=[slot] * 5
        + [pl.BlockSpec((1, text_t.shape[0], LANG), lambda s: (0, 0, 0))]
        + [vec_spec] * 4
        + [handed] * 2,
        compiler_params=pltpu.CompilerParams(vmem_limit_bytes=VMEM_LIMIT),
    )(
        owners, grad, masters, first, second, average, text_t, vec_grad, vec, v1, v2, va, patch, layer
    )


def local(
    patches, text_tokens, view_counts, out_grad, owners, masters, first_moment, second_moment,
    average, vec_value, vec_first, vec_second, vec_average,
):
    vec, v1, v2, va = [
        part.reshape(VEC // 128, 128) for part in (vec_value, vec_first, vec_second, vec_average)
    ]
    text_in = jnp.swapaxes(text_tokens, 1, 2)
    if lax.axis_size("wide") == 8 and lax.axis_size("narrow") == 4:
        patch_grad, layer_out, _, slot_grad, text_sum, vec_grad = block(
            owners, view_counts, masters, text_in, patches, vec, out_grad
        )
    else:
        units, text_t = gather(owners, masters, text_in)
        att_t, probs, inverse, q_t, keyed, v_t = attention_forward(
            view_counts, patches, text_t, vec, units
        )
        layer_out, middle_back, back_t, rest, *vecs = dense(
            view_counts, att_t, patches, out_grad, vec, units[3:]
        )
        query_back, key_back, value_back = attention_backward(
            probs, inverse, keyed, v_t, back_t, q_t, att_t
        )
        patch_grad, first, gain_one, bias_one, text_part = project_back(
            patches, text_t, vec, units, middle_back, query_back, key_back, value_back
        )
        slot_grad, text_sum, vec_grad = reduce_all(
            owners, rest, first, text_part, (gain_one, bias_one, *vecs)
        )
    outs = update(
        owners, slot_grad, masters, first_moment, second_moment, average, text_sum, vec_grad, vec,
        v1, v2, va, patch_grad, layer_out,
    )
    new_masters, new_first, new_second, new_average, new_copies, text_grad = outs[:6]
    vectors = [part.reshape(VEC) for part in outs[6:10]]
    patch_grad, layer_out = outs[10:]
    return (
        layer_out, patch_grad, jnp.swapaxes(text_grad, 1, 2), new_masters, new_first, new_second,
        new_average, new_copies, *vectors,
    )


def solution(mesh):
    rows = P(("wide", "narrow"), None)
    state = P("narrow", None, "wide", None)
    text = P("narrow", None, "wide")
    in_specs = (rows, text, rows, rows, P(), state, state, state, state, P(), P(), P(), P())
    out_specs = (rows, rows, text, state, state, state, state, state, P(), P(), P(), P())
    return jax.shard_map(local, mesh=mesh, in_specs=in_specs, out_specs=out_specs, check_vma=False)
```

```python
import functools

import jax
import jax.numpy as jnp
from jax import lax
from jax.experimental import pallas as pl
from jax.experimental.pallas import tpu as pltpu
from jax.sharding import PartitionSpec as P

D = 512
HEADS = 8
FF = 2048
VIEWS = 5
VIEW_ROWS = 256
ROWS = VIEWS * VIEW_ROWS
LANG = 77
TEXT = 128
KEYS = ROWS + TEXT
STEP = 5
UNITS = 12
SLOTS = 4
VEC = 5 * D + FF
F32 = jnp.float32
BF16 = jnp.bfloat16
MESH = pl.DeviceIdType.MESH
NEG = -1e30

norm_eps = 1e-05
beta_one = 0.5
beta_two = 0.5
adam_eps = 1e-08
weight_decay = 0.1
average_keep = 0.75
vector_rate = 0.25
VMEM_LIMIT = 60 * 2**20


def dot(left, right, left_dim=1, right_dim=0):
    return lax.dot_general(
        left, right, (((left_dim,), (right_dim,)), ((), ())), preferred_element_type=F32
    )


def vmem():
    return pl.BlockSpec(memory_space=pltpu.VMEM)


def smem():
    return pl.BlockSpec(memory_space=pltpu.SMEM)


def vec_row(vec, start, size):
    first = start // 128
    return jnp.concatenate([vec[first + r : first + r + 1, :] for r in range(size // 128)], axis=1)


def unit_ranks(owners_ref):
    owner = [owners_ref[u] for u in range(UNITS)]
    rank = []
    for u in range(UNITS):
        total = jnp.int32(0)
        for v in range(u):
            total = total + (owner[v] == owner[u]).astype(jnp.int32)
        rank.append(jnp.minimum(total, SLOTS - 1))
    return owner, rank


def normalize(values):
    center = values - jnp.mean(values, axis=-1, keepdims=True)
    spread = jnp.mean(center * center, axis=-1, keepdims=True)
    scale = lax.rsqrt(spread + norm_eps)
    return center * scale, scale


def norm_back(grads, gain, normed, scale):
    e = grads * gain
    return scale * (
        e
        - jnp.mean(e, axis=-1, keepdims=True)
        - normed * jnp.mean(e * normed, axis=-1, keepdims=True)
    )


def place():
    w = lax.axis_index("wide")
    n = lax.axis_index("narrow")
    return w, n, w // 2, w % 2, n // 2, n % 2


def narrow_peers(at):
    w, n = at[:2]
    return [(w, lax.rem(n + k, 4)) for k in range(1, 4)]


def wide_peers(at):
    w, n = at[:2]
    return [(lax.rem(w + k, 8), n) for k in range(1, 8)]


def chip_peers(at):
    w, n, z, x, y, c = at
    peers = []
    for k in range(1, 16):
        chip = lax.rem(z * 4 + x * 2 + y + k, 16)
        cz, cx, cy = chip // 4, (chip // 2) % 2, chip % 2
        peers.append((cz, cx, cy, (cz * 2 + cx, cy * 2 + c)))
    return peers


def all_peers(at):
    w, n, z, x, y, c = at
    return narrow_peers(at) + wide_peers(at) + [
        (lax.rem(w + k, 8), (1 - y) * 2 + c) for k in range(1, 8)
    ]


def greet(peers):
    barrier = pltpu.get_barrier_semaphore()
    for peer in peers:
        pl.semaphore_signal(barrier, inc=1, device_id=peer, device_id_type=MESH)


def greeted(peers):
    pl.semaphore_wait(pltpu.get_barrier_semaphore(), len(peers))


class Links:
    def __init__(self, send, recv):
        self.send, self.recv, self.slots = send, recv, {}

    def copies(self, key, parts):
        made = []
        for k, (src, dst, device) in enumerate(parts()):
            slot = self.slots.setdefault((key, k), len(self.slots))
            made.append(
                pltpu.make_async_remote_copy(
                    src_ref=src,
                    dst_ref=dst,
                    send_sem=self.send.at[slot],
                    recv_sem=self.recv.at[slot],
                    device_id=device,
                    device_id_type=MESH,
                )
            )
        return made

    def start(self, key, parts):
        for copy in self.copies(key, parts):
            copy.start()

    def wait(self, key, parts):
        for copy in self.copies(key, parts):
            copy.wait()


def partners(w, n, z, x, y, c):
    to_z = [(lax.rem(z + k, 4) * 2 + x, n) for k in range(1, 4)]
    return to_z, (z * 2 + 1 - x, n), (w, (1 - y) * 2 + c), (w, y * 2 + 1 - c)


def spread(ref, head, stage, at):
    w, n, z, x, y, c = at
    to_z, to_x, to_y, to_c = partners(*at)
    whole = slice(None)
    if stage == 0:
        parts = [((z, x, y, c), peer) for peer in to_z]
    elif stage == 1:
        parts = [((pl.ds(0, 2), x, y, c), to_x), ((pl.ds(2, 2), x, y, c), to_y)]
    elif stage == 2:
        parts = [((pl.ds(0, 2), whole, y, c), to_y), ((pl.ds(2, 2), x, whole, c), to_x)]
    else:
        parts = [((whole, whole, whole, c), to_c)]
    return [(ref.at[(*head, *part)], ref.at[(*head, *part)], peer) for part, peer in parts]


def add(a, b):
    return a + b


class Reducer:
    def __init__(self, name, links, at, source, bufs, shift=None):
        self.name, self.links, self.at, self.source = name, links, at, source
        self.shift = shift or (lambda head: head)
        (self.c_buf, self.ya_buf, self.xb_buf, self.xa_buf, self.yb_buf, self.z_sum,
         self.z_buf) = bufs

    def start(self, stage, head):
        self.links.start(*self.copies(stage, head))

    def copies(self, stage, head):
        return (self.name, str(head), stage), lambda: self.parts(stage, head)

    def parts(self, stage, head):
        w, n, z, x, y, c = self.at
        to_z, to_x, to_y, to_c = partners(*self.at)
        whole, low, high = slice(None), pl.ds(0, 2), pl.ds(2, 2)
        source, buf = self.source, self.shift(head)
        if stage == 0:
            return [(source.at[(*head, whole, whole, whole, 1 - c)], self.c_buf.at[buf], to_c)]
        if stage == 1:
            return [
                (source.at[(*head, low, whole, 1 - y, c)], self.ya_buf.at[buf], to_y),
                (source.at[(*head, high, 1 - x, whole, c)], self.xb_buf.at[buf], to_x),
            ]
        if stage == 2:
            return [
                (source.at[(*head, low, 1 - x, y, c)], self.xa_buf.at[buf], to_x),
                (source.at[(*head, high, x, 1 - y, c)], self.yb_buf.at[buf], to_y),
            ]
        return [
            (self.z_sum.at[(*buf, lax.rem(z + k, 4))], self.z_buf.at[(k - 1, *buf)], to_z[k - 1])
            for k in range(1, 4)
        ]

    def finish(self, stage, head):
        w, n, z, x, y, c = self.at
        self.links.wait(*self.copies(stage, head))
        whole, low, high = slice(None), pl.ds(0, 2), pl.ds(2, 2)
        source, buf = self.source, self.shift(head)
        if stage == 0:
            own = (*head, whole, whole, whole, c)
            source[own] = add(source[own], self.c_buf[buf])
        elif stage == 1:
            a = (*head, low, whole, y, c)
            b = (*head, high, x, whole, c)
            source[a] = add(source[a], self.ya_buf[buf])
            source[b] = add(source[b], self.xb_buf[buf])
        elif stage == 2:
            self.z_sum[(*buf, low)] = add(source[(*head, low, x, y, c)], self.xa_buf[buf])
            self.z_sum[(*buf, high)] = add(source[(*head, high, x, y, c)], self.yb_buf[buf])
        else:
            total = self.z_sum[(*buf, z)].astype(F32)
            for k in range(3):
                total = total + self.z_buf[(k, *buf)].astype(F32)
            return total.astype(BF16)


PIECES = (4, 2, 2, 2, 16)
KEY_PARTS = ((0, 512), (512, 1024), (1024, 1408))
DENSE_PLACE = (8, 0, 2, 4, 6, 1, 3, 5, 7)


def block_kernel(
    owners, counts, masters, text, x, vec, g,
    patch_out, layer_out, probs, slot_grad, text_out, vec_out,
    send_buf, slot_buf, w_first, w_rest, text_buf, q_t, keyed, key_bias, v_t, normed_t,
    text_normed, att_t, inverse, delta, p_buf, g_buf, middle_buf,
    rest_all, c_buf, ya_buf, xb_buf, xa_buf, yb_buf, z_sum, z_buf,
    first_all, first_c, first_d, fa_buf, fb_buf, fc_buf, fd_buf, fz_sum, fz_buf, red, s_buf, r_buf, text_part, text_sum,
    v_own, vw_buf, v_sum, vn_buf, l_own, lw_buf, l_sum, ln_buf,
    query_back, key_back, value_back, value_pair, key_pair_t, send, recv, local
):
    at = place()
    w, n, z, sx, y, c = at
    links = Links(send, recv)
    whole = slice(None)
    peers = all_peers(at)
    gain_one, bias_one = vec_row(vec, 0, D), vec_row(vec, D, D)
    live_text = lax.broadcasted_iota(jnp.int32, (TEXT, 1), 0) < LANG
    read_g = pltpu.make_async_copy(g, g_buf, local.at[2])
    write_layer = pltpu.make_async_copy(g_buf, layer_out, local.at[3])
    write_patch = pltpu.make_async_copy(middle_buf, patch_out, local.at[4])

    greet(peers)
    send_buf[...] = masters[0].reshape(SLOTS, 4, 16, D).astype(BF16)
    text_buf[z, sx] = jnp.zeros((64, TEXT), BF16)
    text_buf[z, sx, :, 0:LANG] = text[0]
    low = (normalize(x[...].astype(F32))[0] * gain_one + bias_one).astype(BF16)
    normed = g_buf
    normed[...] = low
    greeted(peers)
    slots = "slots", lambda: [
        (send_buf.at[:, peer[1]], slot_buf.at[n], peer) for peer in narrow_peers(at)
    ]
    links.start(*slots)
    texts = "text", lambda: [
        (text_buf.at[z, sx], text_buf.at[z, sx], peer) for peer in wide_peers(at)
    ]
    links.start(*texts)
    slot_buf[n] = send_buf[:, n]
    normed_t[:, 0:ROWS] = low.astype(F32).T.astype(BF16)
    owner, rank = unit_ranks(owners)
    links.wait(*slots)
    for u in range(3):
        w_first[u, z, sx, y, c] = slot_buf[owner[u], rank[u]]

    def first(u, s):
        return ("first", u, s), lambda: spread(w_first, (u,), s, at)

    def rest(group, s):
        return ("rest", group, s), lambda: spread(w_rest, (pl.ds(3 * group, 3),), s, at)

    order = (1, 0, 2)
    for u in order:
        links.start(*first(u, 0))
    for k, position in enumerate(DENSE_PLACE):
        w_rest[position, z, sx, y, c] = slot_buf[owner[3 + k], rank[3 + k]]
    for v, live in enumerate(live_column(counts, ROWS)):
        key_bias[v * VIEW_ROWS : (v + 1) * VIEW_ROWS, :] = jnp.broadcast_to(
            jnp.where(live, 0.0, NEG), (VIEW_ROWS, 128)
        ).astype(BF16)
    key_bias[ROWS:KEYS, :] = jnp.broadcast_to(
        jnp.where(live_text, 0.0, NEG), (TEXT, 128)
    ).astype(BF16)
    links.wait(*texts)
    rows = text_buf[...].reshape(D, TEXT).astype(F32).T
    text_low = jnp.where(live_text, normalize(rows)[0] * gain_one + bias_one, 0.0)
    text_normed[...] = text_low.astype(BF16)
    normed_t[:, ROWS:KEYS] = text_low.T.astype(BF16)

    def unit(u):
        return w_first[u].reshape(D, D)

    def project(u):
        if u == 1:
            k = dot(normed[...], unit(1)).astype(BF16)
            t = dot(text_normed[...], unit(1)).astype(BF16)
            for p in range(4):
                pair = slice(p * 128, (p + 1) * 128)
                keyed[p, 0:ROWS] = k[:, pair]
                keyed[p, ROWS:KEYS] = t[:, pair]
        elif u == 0:
            q_t[...] = dot(unit(0), normed[...], 0, 1).astype(BF16) * BF16(0.125)
        else:
            v_t[:, 0:ROWS] = dot(unit(2), normed[...], 0, 1).astype(BF16)
            v_t[:, ROWS:KEYS] = dot(unit(2), text_normed[...], 0, 1).astype(BF16)

    for step in range(3 + 3):
        for s in (3, 2, 1, 0):
            k = step - s
            if not 0 <= k < 3:
                continue
            u = order[k]
            if (k, s) == (2, 3):
                continue
            links.wait(*first(u, s))
            if s < 3:
                links.start(*first(u, s + 1))
            if k == 2 and s < 3:
                links.start(*rest((2, 1, 0)[s], 0))
            if s == 3:
                project(u)

    gather_plan = {
        0: [(2, 0)], 1: [(1, 0)], 2: [(2, 1)], 3: [(0, 0)], 4: [(2, 2), (1, 1)], 5: [],
        6: [(0, 1), (1, 2)], 7: [(2, 3)],
    }

    def gather_point(t):
        for group, s in gather_plan[t]:
            links.wait(*rest(group, s))
            if s < 3:
                links.start(*rest(group, s + 1))

    row = lax.broadcasted_iota(jnp.int32, (128, ROWS), 0)
    one = jnp.where(row == 0, 1.0, 0.0).astype(BF16)

    def saved(t):
        return pltpu.make_async_copy(p_buf.at[t % 2], probs.at[t], local.at[t % 2])

    def values():
        links.wait(*first(2, 3))
        project(2)
        read_g.start()

    def mix(t):
        head = pl.ds(pl.multiple_of(t * 64, 64), 64)
        summed = jnp.concatenate([v_t[head, :], jnp.ones((16, KEYS), BF16)], axis=0)
        mixed = dot(summed, p_buf[t % 2])
        inv = 1.0 / mixed[64:65]
        att_t[head, :] = (mixed[0:64] * inv).astype(BF16)
        inverse[t] = inv

    @pl.loop(0, HEADS)
    def _(t):
        for k in range(HEADS):
            pl.when(t == k)(functools.partial(gather_point, k))
        pl.when(t == 1)(values)
        pl.when(t > 1)(lambda: saved(t - 2).wait())
        pl.when(t > 0)(lambda: mix(t - 1))
        i, h = t // 2, t % 2
        pair_q = q_t[pl.ds(pl.multiple_of(i * 128, 128), 128), :]
        mine = (row >= 64 * h) & (row < 64 * h + 64)
        q = jnp.where(mine, pair_q, jnp.zeros_like(pair_q))
        keys = jnp.concatenate([keyed[i], key_bias[...]], axis=1)
        scores = dot(keys, jnp.concatenate([q, one], axis=0))
        peak = jnp.max(scores, axis=0, keepdims=True)
        for first_key, end_key in KEY_PARTS:
            p_buf[h, first_key:end_key] = jnp.exp(scores[first_key:end_key] - peak).astype(BF16)
        pl.when(t < HEADS - 1)(lambda: saved(t).start())

    mix(HEADS - 1)
    read_g.wait()
    saved(HEADS - 2).wait()

    def fetched(t):
        return pltpu.make_async_copy(probs.at[t], p_buf.at[t % 2], local.at[t % 2])

    reducer = Reducer(
        "reduce", links, at, rest_all, (c_buf, ya_buf, xb_buf, xa_buf, yb_buf, z_sum, z_buf)
    )
    dense_order = (3, 2, 1, 0)
    groups = [(pl.ds(4, 4),), (pl.ds(0, 4),), (pl.ds(8, 1),)]

    def step_rest(group, stage):
        total = reducer.finish(stage, groups[group])
        if stage < 3:
            reducer.start(stage + 1, groups[group])
        else:
            red[groups[group]] = total

    def dense_unit(position):
        return w_rest[position].reshape(D, D)

    @pl.when(w >= 0)
    def _():
        gain, bias = vec_row(vec, 2 * D, D), vec_row(vec, 3 * D, D)
        halves = [slice(k * ROWS // 2, (k + 1) * ROWS // 2) for k in range(2)]
        lows, outs = p_buf.at[0, :, 0:D], p_buf.at[0, :, D : 2 * D]
        normals, scales, backs, lives = [], [], [], []
        for k, rows in enumerate(halves):
            index = lax.broadcasted_iota(jnp.int32, (ROWS // 2, 1), 0) + k * (ROWS // 2)
            live = jnp.zeros((ROWS // 2, 1), jnp.bool_)
            for v in range(VIEWS):
                live = live | ((index >= v * VIEW_ROWS) & (index < v * VIEW_ROWS + counts[0, v]))
            middle = x[rows].astype(F32) + dot(att_t[:, rows], dense_unit(8), 0, 0)
            normal, scale = normalize(middle)
            middle_buf[rows] = middle + vec_row(vec, 4 * D + FF, D)
            normals.append(normal)
            scales.append(scale)
            lows[rows] = (normal * gain + bias).astype(BF16)
            backs.append(jnp.zeros((ROWS // 2, D), F32))
            lives.append(live)
            outs[rows] = jnp.where(live, g_buf[rows].astype(F32), 0.0).astype(BF16)
        for turn, j in enumerate(dense_order):
            if turn == 1:
                links.wait(*rest(0, 2))
                links.start(*rest(0, 3))
                links.wait(*rest(1, 3))
            if turn == 2:
                links.wait(*rest(0, 3))
            w_up, w_down = dense_unit(2 * j), dense_unit(2 * j + 1)
            up_total, down_total, up_grad = 0.0, 0.0, 0.0
            for k, rows in enumerate(halves):
                preact = dot(lows[rows], w_up) + vec_row(vec, 4 * D + j * D, D)
                phi = 0.5 + 0.5 * lax.erf(preact * 0.7071067811865476)
                active = (preact * phi).astype(BF16)
                slope = phi + preact * (jnp.exp(-0.5 * preact * preact) * 0.3989422804014327)
                middle_buf[rows] += dot(active, w_down)
                preact_back = (dot(outs[rows], w_down, 1, 1) * slope).astype(BF16)
                backs[k] = backs[k] + dot(preact_back, w_up, 1, 1)
                up_total = up_total + dot(lows[rows], preact_back, 0, 0)
                down_total = down_total + dot(active, outs[rows], 0, 0)
                up_grad = up_grad + jnp.sum(preact_back.astype(F32), axis=0, keepdims=True)
            rest_all[2 * j] = up_total.astype(BF16).reshape(*PIECES, D)
            rest_all[2 * j + 1] = down_total.astype(BF16).reshape(*PIECES, D)
            for r in range(4):
                v_own[16 + 4 * j + r : 17 + 4 * j + r, :] = up_grad[:, r * 128 : (r + 1) * 128]
            if turn == 1:
                reducer.start(0, groups[0])
            if turn > 1:
                step_rest(0, turn - 2)
            if turn == 3:
                reducer.start(0, groups[1])
        for k, rows in enumerate(halves):
            g_buf[rows] = jnp.where(lives[k], middle_buf[rows], 0.0).astype(BF16)
        write_layer.start()
        out_total, gain_grad, bias_grad, down_grad = 0.0, 0.0, 0.0, 0.0
        for k, rows in enumerate(halves):
            out_back = outs[rows].astype(F32)
            back = out_back + norm_back(backs[k], gain, normals[k], scales[k])
            middle_buf[rows] = back
            branch = back.astype(BF16)
            out_total = out_total + dot(att_t[:, rows], branch)
            back_rows = dot(dense_unit(8), branch, 1, 1).astype(BF16)
            product = back_rows.astype(F32) * att_t[:, rows].astype(F32)
            for h in range(HEADS):
                part = jnp.sum(product[h * 64 : (h + 1) * 64], axis=0, keepdims=True)
                delta[h, :, rows] = part * inverse[h, :, rows]
            att_t[:, rows] = back_rows
            gain_grad = gain_grad + jnp.sum(backs[k] * normals[k], axis=0, keepdims=True)
            bias_grad = bias_grad + jnp.sum(backs[k], axis=0, keepdims=True)
            down_grad = down_grad + jnp.sum(out_back, axis=0, keepdims=True)
        rest_all[8] = out_total.astype(BF16).reshape(*PIECES, D)
        for offset, piece in ((8, gain_grad), (12, bias_grad), (32, down_grad)):
            for r in range(4):
                v_own[offset + r : offset + r + 1, :] = piece[:, r * 128 : (r + 1) * 128]
        v_own[0:8, :] = jnp.zeros((8, 128), F32)

    fetched(HEADS - 2).start()
    back_t = att_t

    def chunk_core(p):
        return ("chunk", p, 0), lambda: [
            (first_all.at[p, :, :, :, :, 1 - c], first_c.at[p], (w, y * 2 + 1 - c))
        ]

    chip = z * 4 + sx * 2 + y

    def chunk_chips(p):
        return ("chunk", p, 1), lambda: [
            (first_all.at[p, :, cz, cx, cy, c], first_d.at[p, chip], peer)
            for cz, cx, cy, peer in chip_peers(at)
        ]

    def chunk_middle(p):
        links.wait(*chunk_core(p))
        own = (p, whole, whole, whole, whole, c)
        first_all[own] = add(first_all[own], first_c[p])
        links.start(*chunk_chips(p))
        first_d[p, chip] = first_all[p, :, z, sx, y, c]

    def chunk_end(p):
        links.wait(*chunk_chips(p))
        total = jnp.sum(first_d[p].astype(F32), axis=0).astype(BF16)
        red[9:12, :, p * 128 : (p + 1) * 128] = total

    staged = Reducer(
        "staged", links, at, first_all,
        (first_c.at[pl.ds(2, 2)], fa_buf, fb_buf, fc_buf, fd_buf, fz_sum, fz_buf),
        lambda head: (head[0] - 2, *head[1:]),
    )

    def step_chunk(p, stage):
        total = staged.finish(stage, (p, whole))
        if stage < 3:
            staged.start(stage + 1, (p, whole))
        else:
            red[9:12, :, p * 128 : (p + 1) * 128] = total

    wides = "wide", lambda: [(v_own, vw_buf.at[w], peer) for peer in wide_peers(at)]
    narrows = "narrow", lambda: [(v_sum, vn_buf.at[n], peer) for peer in narrow_peers(at)]

    def vector_start():
        vw_buf[w] = v_own[...]
        links.start(*wides)

    def vector_middle():
        links.wait(*wides)
        total = vw_buf[0]
        for k in range(1, 8):
            total = total + vw_buf[k]
        v_sum[...] = total
        vn_buf[n] = total
        links.start(*narrows)

    def reduce_point(t):
        for group, s in {
            0: [(0, 2), (1, 0)], 1: [(2, 0)], 2: [(1, 1)], 3: [(0, 3), (2, 1)], 4: [(1, 2)],
            5: [(2, 2)], 6: [], 7: [(1, 3), (2, 3)],
        }[t]:
            step_rest(group, s)
        if t == 0:
            reducer.start(0, groups[2])
            vector_start()
        if t == 3:
            vector_middle()
        for p, s in {
            3: [(3, 0)], 4: [(3, 1)], 5: [(3, 2), (2, 0)], 6: [(2, 1)], 7: [(3, 3), (2, 2)]
        }.get(t, []):
            step_chunk(p, s)
        if t == 7:
            chunk_middle(1)

    def start_chunk(p):
        if p > 1:
            staged.start(0, (p, whole))
        else:
            links.start(*chunk_core(p))

    lane = lax.broadcasted_iota(jnp.int32, (KEYS, 128), 1)
    ones = jnp.where(lane < 2, 1.0, 0.0).astype(BF16)

    @pl.loop(0, HEADS)
    def _(step):
        for k in range(HEADS):
            pl.when(step == k)(functools.partial(reduce_point, k))
        t = HEADS - 1 - step
        i, h = t // 2, t % 2
        pl.when(step > 0)(lambda: fetched(t).wait())
        pair = pl.ds(pl.multiple_of(i * 128, 128), 128)
        head = pl.ds(pl.multiple_of(t * 64, 64), 64)

        @pl.when(h == 1)
        def _():
            value_pair[...] = v_t[pair, :].astype(F32).T.astype(BF16)
            key_pair_t[...] = keyed[i].astype(F32).T.astype(BF16)

        inv = inverse[t]
        shift = delta[t]
        high = shift.astype(BF16).astype(F32)
        mine = (row >= 64 * h) & (row < 64 * h + 64)
        scaled = jnp.where(mine, back_t[pair, :].astype(F32) * inv, 0.0).astype(BF16)
        tail = jnp.where(row == 0, -high, jnp.where(row == 1, high - shift, 0.0)).astype(BF16)
        right = jnp.concatenate([scaled, tail], axis=0)
        value = jnp.concatenate([value_pair[...], ones], axis=1)
        key_head = key_pair_t[pl.ds(pl.multiple_of(h * 64, 64), 64), :]
        query_head = q_t[head, :]
        back_head = (back_t[head, :].astype(F32) * inv).astype(BF16)
        query_total = jnp.zeros((64, ROWS), F32)
        for first_key, end_key in KEY_PARTS:
            part = slice(first_key, end_key)
            low = p_buf[h, part]
            score_back = low * dot(value[part], right).astype(BF16)
            query_total = query_total + dot(key_head[:, part], score_back)
            key_back[head, part] = dot(query_head, score_back, 1, 1).astype(BF16)
            value_back[head, part] = dot(back_head, low, 1, 1).astype(BF16)
        query_back[head, :] = (query_total * 0.125).astype(BF16)
        pl.when(t > 1)(lambda: fetched(t - 2).start())

        @pl.when(h == 0)
        def _():
            part = dot(normed_t[:, 0:ROWS], query_back[pair, :], 1, 1).astype(BF16)
            first_all[i, 0] = part.reshape(*PIECES, 128)
            both = jnp.concatenate([key_back[pair, :], value_back[pair, :]], axis=0)
            part = dot(normed_t[...], both, 1, 1).astype(BF16)
            for u in range(2):
                first_all[i, 1 + u] = part[:, u * 128 : (u + 1) * 128].reshape(*PIECES, 128)

        for k in range(4):
            pl.when(step == 2 * k + 1)(functools.partial(start_chunk, 3 - k))

    @pl.when(w >= 0)
    def _():
        w_q, w_k, w_v = unit(0), unit(1), unit(2)
        normal, scale = normalize(text_buf[...].reshape(D, TEXT).astype(F32).T)
        text_back = dot(key_back[:, ROWS:KEYS], w_k, 0, 1) + dot(
            value_back[:, ROWS:KEYS], w_v, 0, 1
        )
        text_part[...] = (
            norm_back(text_back, gain_one, normal, scale).T.astype(BF16).reshape(8, 64, TEXT)
        )
        gain_grad = jnp.sum(text_back * normal, axis=0, keepdims=True)
        bias_grad = jnp.sum(text_back, axis=0, keepdims=True)
        text_sum[w] = text_part[w]
        text_parts = "parts", lambda: [
            (text_part.at[peer[0]], text_sum.at[w], peer) for peer in wide_peers(at)
        ]
        chunk_middle(0)
        links.start(*text_parts)
        step_chunk(2, 3)
        tile = ROWS // 2
        kept = []
        for t in range(2):
            rows = slice(t * tile, (t + 1) * tile)
            normal, scale = normalize(x[rows].astype(F32))
            projected = (
                dot(query_back[:, rows], w_q, 0, 1)
                + dot(key_back[:, rows], w_k, 0, 1)
                + dot(value_back[:, rows], w_v, 0, 1)
            )
            kept.append((rows, projected, normal, scale))
            gain_grad = gain_grad + jnp.sum(projected * normal, axis=0, keepdims=True)
            bias_grad = bias_grad + jnp.sum(projected, axis=0, keepdims=True)
        for r in range(4):
            l_own[r : r + 1, :] = gain_grad[:, r * 128 : (r + 1) * 128]
            l_own[4 + r : 5 + r, :] = bias_grad[:, r * 128 : (r + 1) * 128]
        late_wides = "late wide", lambda: [(l_own, lw_buf.at[w], peer) for peer in wide_peers(at)]
        late_narrows = "late narrow", lambda: [
            (l_sum, ln_buf.at[n], peer) for peer in narrow_peers(at)
        ]
        lw_buf[w] = l_own[...]
        links.start(*late_wides)
        for rows, projected, normal, scale in kept:
            middle_buf[rows] += norm_back(projected, gain_one, normal, scale)
        write_patch.start()
        links.wait(*narrows)
        vec_out[...] = (vn_buf[0] + vn_buf[1]) + (vn_buf[2] + vn_buf[3])
        owner, rank = unit_ranks(owners)
        spots = []
        for q in range(4):
            for s in range(SLOTS):
                spot = jnp.int32(0)
                for u in range(UNITS):
                    position = 9 + u if u < 3 else DENSE_PLACE[u - 3]
                    spot = spot + jnp.where((owner[u] == q) & (rank[u] == s), position, 0)
                spots.append((q, s, jnp.minimum(spot, UNITS - 1)))

        def grads(part, columns):
            return ("grads", part), lambda: [
                (s_buf.at[peer[1], :, :, columns], r_buf.at[n, :, :, columns], peer)
                for peer in narrow_peers(at)
            ]

        def send_grads(part, columns):
            for q, s, spot in spots:
                s_buf[q, s, :, columns] = red[spot, :, columns]
            links.start(*grads(part, columns))
            r_buf[n, :, :, columns] = s_buf[n, :, :, columns]

        others, last = slice(128, 512), slice(0, 128)
        chunk_end(1)
        send_grads(0, others)
        links.wait(*text_parts)
        text_out[...] = jnp.sum(text_sum[...].astype(F32), axis=0)
        chunk_end(0)
        send_grads(1, last)
        links.wait(*late_wides)
        total = lw_buf[0]
        for k in range(1, 8):
            total = total + lw_buf[k]
        l_sum[...] = total
        ln_buf[n] = total
        links.start(*late_narrows)
        links.wait(*grads(0, others))
        links.wait(*grads(1, last))
        for q in range(4):
            slot_grad[:, q * 16 : (q + 1) * 16, :] = r_buf[q].astype(F32)
        write_layer.wait()
        write_patch.wait()
        links.wait(*late_narrows)
        vec_out[0:8, :] = (ln_buf[0] + ln_buf[1]) + (ln_buf[2] + ln_buf[3])


def block(owners, counts, masters, text, x, vec, g):
    hbm = pl.BlockSpec(memory_space=pl.ANY)
    copies = 3 + 7 + 24 + 24 + 3 * 8 + 2 * 8 + 2 * 16 + 7 + 3 + 7 + 7 + 3 + 6
    bf = lambda *s: pltpu.VMEM(s, BF16)
    f32 = lambda *s: pltpu.VMEM(s, F32)
    rows = VEC // 128
    return pl.pallas_call(
        block_kernel,
        in_specs=[smem(), smem(), vmem(), vmem(), vmem(), vmem(), hbm],
        out_specs=[hbm, hbm, hbm, vmem(), vmem(), vmem()],
        out_shape=[
            jax.ShapeDtypeStruct((ROWS, D), F32),
            jax.ShapeDtypeStruct((ROWS, D), BF16),
            jax.ShapeDtypeStruct((HEADS - 1, KEYS, ROWS), BF16),
            jax.ShapeDtypeStruct((SLOTS, 64, D), F32),
            jax.ShapeDtypeStruct((64, TEXT), F32),
            jax.ShapeDtypeStruct((rows, 128), F32),
        ],
        scratch_shapes=[
            bf(SLOTS, 4, 16, D),
            bf(4, SLOTS, 16, D),
            bf(3, *PIECES, D),
            bf(9, *PIECES, D),
            bf(4, 2, 64, TEXT),
            bf(D, ROWS),
            bf(4, KEYS, 128),
            bf(KEYS, 128),
            bf(D, KEYS),
            bf(D, KEYS),
            bf(TEXT, D),
            bf(D, ROWS),
            f32(HEADS, 1, ROWS),
            f32(HEADS, 1, ROWS),
            bf(2, KEYS, ROWS),
            bf(ROWS, D),
            f32(ROWS, D),
            bf(9, *PIECES, D),
            bf(9, 4, 2, 2, 16, D),
            bf(9, 2, 2, 16, D),
            bf(9, 2, 2, 16, D),
            bf(9, 2, 16, D),
            bf(9, 2, 16, D),
            bf(9, 4, 16, D),
            bf(3, 9, 16, D),
            bf(4, 3, *PIECES, 128),
            bf(4, 3, 4, 2, 2, 16, 128),
            bf(2, 16, 3, 16, 128),
            bf(2, 3, 2, 2, 16, 128),
            bf(2, 3, 2, 2, 16, 128),
            bf(2, 3, 2, 16, 128),
            bf(2, 3, 2, 16, 128),
            bf(2, 3, 4, 16, 128),
            bf(3, 2, 3, 16, 128),
            bf(UNITS, 16, D),
            bf(4, SLOTS, 16, D),
            bf(4, SLOTS, 16, D),
            bf(8, 64, TEXT),
            bf(8, 64, TEXT),
            f32(rows, 128),
            f32(8, rows, 128),
            f32(rows, 128),
            f32(4, rows, 128),
            f32(8, 128),
            f32(8, 8, 128),
            f32(8, 128),
            f32(4, 8, 128),
            bf(D, ROWS),
            bf(D, KEYS),
            bf(D, KEYS),
            bf(KEYS, 128),
            bf(128, KEYS),
            pltpu.SemaphoreType.DMA((copies,)),
            pltpu.SemaphoreType.DMA((copies,)),
            pltpu.SemaphoreType.DMA((5,)),
        ],
        compiler_params=pltpu.CompilerParams(
            collective_id=1, has_side_effects=True, vmem_limit_bytes=63 * 2**20
        ),
    )(owners, counts, masters, text, x, vec, g)


def gather(owners, masters, text_t):
    packed = lax.all_gather(masters.astype(BF16), "wide", axis=2, tiled=True)
    packed = lax.all_gather(packed, "narrow", axis=0, tiled=True)
    same = owners[:, None] == owners[None, :]
    ids = jnp.arange(UNITS)
    rank = jnp.sum((same & (ids[None, :] < ids[:, None])).astype(jnp.int32), axis=1)
    units = jnp.take(packed.reshape(-1, D, D), owners * SLOTS + rank, axis=0)
    rows = lax.all_gather(text_t, "wide", axis=1, tiled=True)[0]
    return units, jnp.pad(rows, ((0, 0), (0, TEXT - LANG)))


def live_column(counts, rows):
    index = lax.broadcasted_iota(jnp.int32, (VIEW_ROWS, 1), 0)
    return [(index < counts[0, v]) for v in range(rows // VIEW_ROWS)]


def forward_kernel(
    counts, x, text_t, vec, w, att_t, probs, inverse, q_t, keyed, v_t, normed, text_normed
):
    i = pl.program_id(0)

    @pl.when(i == 0)
    def _():
        gain, bias = vec_row(vec, 0, D), vec_row(vec, D, D)
        normed[...] = (normalize(x[...].astype(F32))[0] * gain + bias).astype(BF16)
        rows = text_t[...].astype(F32).T
        live_text = lax.broadcasted_iota(jnp.int32, (TEXT, 1), 0) < LANG
        text_normed[...] = jnp.where(
            live_text, normalize(rows)[0] * gain + bias, 0.0
        ).astype(BF16)
        q_t[...] = dot(w[0], normed[...], 0, 1).astype(BF16) * BF16(0.125)
        v_t[:, 0:ROWS] = dot(w[2], normed[...], 0, 1).astype(BF16)
        v_t[:, ROWS:KEYS] = dot(w[2], text_normed[...], 0, 1).astype(BF16)
        for p in range(4):
            pair = slice(p * 128, (p + 1) * 128)
            keyed[p, 0:ROWS, 0:128] = dot(normed[...], w[1, :, pair]).astype(BF16)
            keyed[p, ROWS:KEYS, 0:128] = dot(text_normed[...], w[1, :, pair]).astype(BF16)
            for v, live in enumerate(live_column(counts, ROWS)):
                keyed[p, v * VIEW_ROWS : (v + 1) * VIEW_ROWS, 128:256] = jnp.broadcast_to(
                    jnp.where(live, 0.0, NEG), (VIEW_ROWS, 128)
                ).astype(BF16)
            keyed[p, ROWS:KEYS, 128:256] = jnp.broadcast_to(
                jnp.where(live_text, 0.0, NEG), (TEXT, 128)
            ).astype(BF16)

    row = lax.broadcasted_iota(jnp.int32, (128, ROWS), 0)
    one = jnp.where(row == 0, 1.0, 0.0).astype(BF16)
    pair_q = q_t[pl.ds(pl.multiple_of(i * 128, 128), 128), :]
    for h in range(2):
        mine = (row >= 64 * h) & (row < 64 * h + 64)
        q = jnp.where(mine, pair_q, jnp.zeros_like(pair_q))
        scores = dot(keyed[i], jnp.concatenate([q, one], axis=0))
        peak = jnp.max(scores, axis=0, keepdims=True)
        e = jnp.exp(scores - peak)
        total = jnp.sum(e, axis=0, keepdims=True)
        low = e.astype(BF16)
        probs[h] = low
        mixed = dot(v_t[pl.ds(pl.multiple_of(i * 128 + h * 64, 64), 64), :], low)
        inv = 1.0 / total
        att_t[h * 64 : (h + 1) * 64, :] = (mixed * inv).astype(BF16)
        inverse[0, h : h + 1, :] = inv


def attention_forward(counts, x, text_t, vec, units):
    return pl.pallas_call(
        forward_kernel,
        grid=(4,),
        in_specs=[smem(), vmem(), vmem(), vmem(), pl.BlockSpec((3, D, D), lambda i: (0, 0, 0))],
        out_specs=[
            pl.BlockSpec((128, ROWS), lambda i: (i, 0)),
            pl.BlockSpec((2, KEYS, ROWS), lambda i: (i, 0, 0)),
            pl.BlockSpec((1, 2, ROWS), lambda i: (i, 0, 0)),
            pl.BlockSpec((D, ROWS), lambda i: (0, 0)),
            pl.BlockSpec((4, KEYS, 256), lambda i: (0, 0, 0)),
            pl.BlockSpec((D, KEYS), lambda i: (0, 0)),
        ],
        out_shape=[
            jax.ShapeDtypeStruct((D, ROWS), BF16),
            jax.ShapeDtypeStruct((HEADS, KEYS, ROWS), BF16),
            jax.ShapeDtypeStruct((4, 2, ROWS), F32),
            jax.ShapeDtypeStruct((D, ROWS), BF16),
            jax.ShapeDtypeStruct((4, KEYS, 256), BF16),
            jax.ShapeDtypeStruct((D, KEYS), BF16),
        ],
        scratch_shapes=[pltpu.VMEM((ROWS, D), BF16), pltpu.VMEM((TEXT, D), BF16)],
        compiler_params=pltpu.CompilerParams(vmem_limit_bytes=VMEM_LIMIT),
    )(counts, x, text_t, vec, units)


def dense_kernel(
    counts, att_t, x, g, vec, w,
    layer_out, middle_back, back_t, grads, gain_grad, bias_grad, up_grad, down_grad,
    total, *, tile
):
    i = pl.program_id(0)
    steps = pl.num_programs(0)
    gain, bias = vec_row(vec, 2 * D, D), vec_row(vec, 3 * D, D)
    a = att_t[...]
    index = lax.broadcasted_iota(jnp.int32, (tile, 1), 0) + i * tile
    live = jnp.zeros((tile, 1), jnp.bool_)
    for v in range(VIEWS):
        live = live | ((index >= v * VIEW_ROWS) & (index < v * VIEW_ROWS + counts[0, v]))
    middle = x[...].astype(F32) + dot(a, w[0], 0, 0)
    normed, scale = normalize(middle)
    low = (normed * gain + bias).astype(BF16)
    out_back = jnp.where(live, g[...].astype(F32), 0.0)
    out_low = out_back.astype(BF16)

    @pl.when(i == 0)
    def _():
        total[...] = jnp.zeros_like(total)
        gain_grad[...] = jnp.zeros_like(gain_grad)
        bias_grad[...] = jnp.zeros_like(bias_grad)
        up_grad[...] = jnp.zeros_like(up_grad)
        down_grad[...] = jnp.zeros_like(down_grad)

    out = middle + vec_row(vec, 4 * D + FF, D)
    normed_back = jnp.zeros((tile, D), F32)
    for j in range(4):
        block = slice(j * D, (j + 1) * D)
        preact = dot(low, w[1 + j]) + vec_row(vec, 4 * D + j * D, D)
        phi = 0.5 + 0.5 * lax.erf(preact * 0.7071067811865476)
        active = (preact * phi).astype(BF16)
        slope = phi + preact * (jnp.exp(-0.5 * preact * preact) * 0.3989422804014327)
        out = out + dot(active, w[5 + j])
        preact_back = (dot(out_low, w[5 + j], 1, 1) * slope).astype(BF16)
        normed_back = normed_back + dot(preact_back, w[1 + j], 1, 1)
        total[1 + j] += dot(low, preact_back, 0, 0)
        total[5 + j] += dot(active, out_low, 0, 0)
        up_grad[:, block] += jnp.sum(preact_back.astype(F32), axis=0, keepdims=True)
    layer_out[...] = jnp.where(live, out, 0.0).astype(BF16)
    back = out_back + norm_back(normed_back, gain, normed, scale)
    middle_back[...] = back
    branch = back.astype(BF16)
    back_t[...] = dot(w[0], branch, 1, 1).astype(BF16)
    total[0] += dot(a, branch)
    gain_grad[...] += jnp.sum(normed_back * normed, axis=0, keepdims=True)
    bias_grad[...] += jnp.sum(normed_back, axis=0, keepdims=True)
    down_grad[...] += jnp.sum(out_back, axis=0, keepdims=True)

    @pl.when(i == steps - 1)
    def _():
        grads[...] = total[...].astype(BF16)


def dense(counts, att_t, x, g, vec, units, tile=640):
    rows = pl.BlockSpec((tile, D), lambda i: (i, 0))
    columns = pl.BlockSpec((D, tile), lambda i: (0, i))
    return pl.pallas_call(
        functools.partial(dense_kernel, tile=tile),
        grid=(ROWS // tile,),
        in_specs=[smem(), columns, rows, rows, vmem(), vmem()],
        out_specs=[
            rows,
            rows,
            columns,
            pl.BlockSpec((9, D, D), lambda i: (0, 0, 0)),
            pl.BlockSpec((1, D), lambda i: (0, 0)),
            pl.BlockSpec((1, D), lambda i: (0, 0)),
            pl.BlockSpec((1, FF), lambda i: (0, 0)),
            pl.BlockSpec((1, D), lambda i: (0, 0)),
        ],
        out_shape=[
            jax.ShapeDtypeStruct((ROWS, D), BF16),
            jax.ShapeDtypeStruct((ROWS, D), F32),
            jax.ShapeDtypeStruct((D, ROWS), BF16),
            jax.ShapeDtypeStruct((9, D, D), BF16),
            jax.ShapeDtypeStruct((1, D), F32),
            jax.ShapeDtypeStruct((1, D), F32),
            jax.ShapeDtypeStruct((1, FF), F32),
            jax.ShapeDtypeStruct((1, D), F32),
        ],
        scratch_shapes=[pltpu.VMEM((9, D, D), F32)],
        compiler_params=pltpu.CompilerParams(vmem_limit_bytes=VMEM_LIMIT),
    )(counts, att_t, x, g, vec, units)


def backward_kernel(probs, inverse, keyed, v_t, back_t, q_t, att_t, query_back, key_back, value_back):
    row = lax.broadcasted_iota(jnp.int32, (128, ROWS), 0)
    lane = lax.broadcasted_iota(jnp.int32, (KEYS, 128), 1)
    ones = jnp.where(lane < 2, 1.0, 0.0).astype(BF16)
    value = jnp.concatenate([v_t[...].astype(F32).T.astype(BF16), ones], axis=1)
    key_t = keyed[:, 0:128].astype(F32).T.astype(BF16)
    back = back_t[...].astype(F32)
    product = back * att_t[...].astype(F32)
    query = q_t[...].astype(F32)
    key_total = jnp.zeros((KEYS, 128), F32)
    value_total = jnp.zeros((KEYS, 128), F32)
    for h in range(2):
        half = slice(h * 64, (h + 1) * 64)
        inv = inverse[0, h : h + 1, :]
        delta = jnp.sum(product[half], axis=0, keepdims=True) * inv
        high = delta.astype(BF16).astype(F32)
        mine = (row >= 64 * h) & (row < 64 * h + 64)
        scaled = jnp.where(mine, back * inv, 0.0)
        tail = jnp.where(row == 0, -high, jnp.where(row == 1, high - delta, 0.0))
        right = jnp.concatenate([scaled.astype(BF16), tail.astype(BF16)], axis=0)
        low = probs[h]
        score_back = low * dot(value, right).astype(BF16)
        query_back[half, :] = (dot(key_t[half], score_back) * 0.125).astype(BF16)
        key_total += dot(score_back, jnp.where(mine, query, 0.0).T.astype(BF16))
        value_total += dot(low, scaled.T.astype(BF16))
    key_back[...] = key_total.astype(BF16)
    value_back[...] = value_total.astype(BF16)


def attention_backward(probs, inverse, keyed, v_t, back_t, q_t, att_t):
    return pl.pallas_call(
        backward_kernel,
        grid=(4,),
        in_specs=[
            pl.BlockSpec((2, KEYS, ROWS), lambda i: (i, 0, 0)),
            pl.BlockSpec((1, 2, ROWS), lambda i: (i, 0, 0)),
            pl.BlockSpec((None, KEYS, 256), lambda i: (i, 0, 0)),
            pl.BlockSpec((128, KEYS), lambda i: (i, 0)),
            pl.BlockSpec((128, ROWS), lambda i: (i, 0)),
            pl.BlockSpec((128, ROWS), lambda i: (i, 0)),
            pl.BlockSpec((128, ROWS), lambda i: (i, 0)),
        ],
        out_specs=[
            pl.BlockSpec((128, ROWS), lambda i: (i, 0)),
            pl.BlockSpec((KEYS, 128), lambda i: (0, i)),
            pl.BlockSpec((KEYS, 128), lambda i: (0, i)),
        ],
        out_shape=[
            jax.ShapeDtypeStruct((D, ROWS), BF16),
            jax.ShapeDtypeStruct((KEYS, D), BF16),
            jax.ShapeDtypeStruct((KEYS, D), BF16),
        ],
        compiler_params=pltpu.CompilerParams(vmem_limit_bytes=VMEM_LIMIT),
    )(probs, inverse, keyed, v_t, back_t, q_t, att_t)


def project_kernel(
    x, text_t, vec, w, middle_back, query_back, key_back, value_back, text_key, text_value,
    patch_grad, grads, gain_grad, bias_grad, text_grad_t, total
):
    i = pl.program_id(0)
    steps = pl.num_programs(0)
    gain, bias = vec_row(vec, 0, D), vec_row(vec, D, D)

    @pl.when(i == 0)
    def _():
        live = lax.broadcasted_iota(jnp.int32, (TEXT, 1), 0) < LANG
        normed, scale = normalize(text_t[...].astype(F32).T)
        low_t = jnp.where(live, normed * gain + bias, 0.0).T.astype(BF16)
        k, v = text_key[...], text_value[...]
        back = dot(k, w[1], 1, 1) + dot(v, w[2], 1, 1)
        text_grad_t[...] = norm_back(back, gain, normed, scale).T.astype(BF16)
        gain_grad[...] = jnp.sum(back * normed, axis=0, keepdims=True)
        bias_grad[...] = jnp.sum(back, axis=0, keepdims=True)
        total[0] = jnp.zeros((D, D), F32)
        total[1] = dot(low_t, k)
        total[2] = dot(low_t, v)

    normed, scale = normalize(x[...].astype(F32))
    low_t = (normed * gain + bias).T.astype(BF16)
    q, k, v = query_back[...], key_back[...], value_back[...]
    back = dot(q, w[0], 0, 1) + dot(k, w[1], 1, 1) + dot(v, w[2], 1, 1)
    patch_grad[...] = middle_back[...] + norm_back(back, gain, normed, scale)
    total[0] += dot(low_t, q, 1, 1)
    total[1] += dot(low_t, k)
    total[2] += dot(low_t, v)
    gain_grad[...] += jnp.sum(back * normed, axis=0, keepdims=True)
    bias_grad[...] += jnp.sum(back, axis=0, keepdims=True)

    @pl.when(i == steps - 1)
    def _():
        grads[...] = total[...].astype(BF16)


def project_back(x, text_t, vec, units, middle_back, query_back, key_back, value_back, tile=640):
    rows = pl.BlockSpec((tile, D), lambda i: (i, 0))
    text_rows = pl.BlockSpec((TEXT, D), lambda i: (ROWS // TEXT, 0))
    return pl.pallas_call(
        project_kernel,
        grid=(ROWS // tile,),
        in_specs=[
            rows,
            vmem(),
            vmem(),
            pl.BlockSpec((3, D, D), lambda i: (0, 0, 0)),
            rows,
            pl.BlockSpec((D, tile), lambda i: (0, i)),
            rows,
            rows,
            text_rows,
            text_rows,
        ],
        out_specs=[
            rows,
            pl.BlockSpec((3, D, D), lambda i: (0, 0, 0)),
            pl.BlockSpec((1, D), lambda i: (0, 0)),
            pl.BlockSpec((1, D), lambda i: (0, 0)),
            pl.BlockSpec((D, TEXT), lambda i: (0, 0)),
        ],
        out_shape=[
            jax.ShapeDtypeStruct((ROWS, D), F32),
            jax.ShapeDtypeStruct((3, D, D), BF16),
            jax.ShapeDtypeStruct((1, D), F32),
            jax.ShapeDtypeStruct((1, D), F32),
            jax.ShapeDtypeStruct((D, TEXT), BF16),
        ],
        scratch_shapes=[pltpu.VMEM((3, D, D), F32)],
        compiler_params=pltpu.CompilerParams(vmem_limit_bytes=VMEM_LIMIT),
    )(
        x, text_t, vec, units, middle_back, query_back, key_back, value_back, key_back, value_back
    )


def reduce_all(owners, rest, first, text, vecs):
    vec = lax.psum(jnp.concatenate(vecs, axis=1), ("wide", "narrow"))
    text_sum = lax.psum_scatter(text.astype(F32), "wide", scatter_dimension=0, tiled=True)
    all_units = jnp.concatenate([first, rest], axis=0).astype(F32)
    rows = lax.psum_scatter(all_units, "wide", scatter_dimension=1, tiled=True)
    same = owners[:, None] == owners[None, :]
    ids = jnp.arange(UNITS)
    rank = jnp.sum((same & (ids[None, :] < ids[:, None])).astype(jnp.int32), axis=1)
    pick = (owners[None, None, :] == jnp.arange(lax.axis_size("narrow"))[:, None, None]) & (
        rank[None, None, :] == jnp.arange(SLOTS)[None, :, None]
    )
    terms = jnp.einsum("nsu,urc->nsrc", pick.astype(F32), rows, precision=lax.Precision.HIGHEST)
    slots = lax.psum_scatter(terms, "narrow", scatter_dimension=0, tiled=True)
    return slots[0], text_sum, vec.reshape(VEC // 128, 128)


def adam(master, moment_one, moment_two, averaged, gradient, rate):
    moment_one = beta_one * moment_one + (1.0 - beta_one) * gradient
    moment_two = beta_two * moment_two + (1.0 - beta_two) * gradient * gradient
    mean_hat = moment_one / (1.0 - beta_one**STEP)
    second_hat = moment_two / (1.0 - beta_two**STEP)
    master = master - rate * (
        mean_hat / (jnp.sqrt(second_hat) + adam_eps) + weight_decay * master
    )
    averaged = average_keep * averaged + (1.0 - average_keep) * master
    return master, moment_one, moment_two, averaged


def unit_rates():
    blocks = FF // D
    fans = [2 * D // 3, 2 * D // 3, D, D // 64] + [D] * blocks + [FF] * blocks
    return [float(fan) ** -0.5 for fan in fans]


def update_kernel(
    owners, grad, masters, first, second, average, text_t, vec_grad, vec, vec_first, vec_second,
    vec_average, patch_in, layer_in,
    new_masters, new_first, new_second, new_average, new_copies, text_grad,
    vec_new_value, vec_new_first, vec_new_second, vec_new_average, patch_out, layer_out,
):
    s = pl.program_id(0)
    patch_out[...] = patch_in[...]
    layer_out[...] = layer_in[...]
    n = lax.axis_index("narrow")
    owner, rank = unit_ranks(owners)
    rate, filled = jnp.float32(0.0), jnp.int32(0)
    for u, value in enumerate(unit_rates()):
        match = (owner[u] == n) & (rank[u] == s)
        rate = rate + jnp.where(match, jnp.float32(value), jnp.float32(0.0))
        filled = filled + match.astype(jnp.int32)
    state = adam(masters[0, 0], first[0, 0], second[0, 0], average[0, 0], grad[0], rate)
    keep = jnp.broadcast_to(filled, state[0].shape) > 0
    state = [jnp.where(keep, part, 0.0) for part in state]
    for ref, part in zip((new_masters, new_first, new_second, new_average), state):
        ref[0, 0] = part
    new_copies[0, 0] = state[0].astype(BF16)

    @pl.when(s == 0)
    def _():
        text_grad[0] = text_t[:, 0:LANG]
        state = adam(
            vec[...], vec_first[...], vec_second[...], vec_average[...], vec_grad[...], vector_rate
        )
        for ref, part in zip(
            (vec_new_value, vec_new_first, vec_new_second, vec_new_average), state
        ):
            ref[...] = part


def update(
    owners, grad, masters, first, second, average, text_t, vec_grad, vec, v1, v2, va, patch, layer
):
    rows = masters.shape[2]
    state = jax.ShapeDtypeStruct(masters.shape, F32)
    vector = jax.ShapeDtypeStruct(vec.shape, F32)
    slot = pl.BlockSpec((1, 1, rows, D), lambda s: (0, s, 0, 0))
    vec_spec = pl.BlockSpec(vec.shape, lambda s: (0, 0))
    handed = pl.BlockSpec((ROWS // SLOTS, D), lambda s: (s, 0))
    return pl.pallas_call(
        update_kernel,
        grid=(SLOTS,),
        out_shape=[state] * 4
        + [
            jax.ShapeDtypeStruct(masters.shape, BF16),
            jax.ShapeDtypeStruct((1, text_t.shape[0], LANG), F32),
        ]
        + [vector] * 4
        + [jax.ShapeDtypeStruct(patch.shape, F32), jax.ShapeDtypeStruct(layer.shape, BF16)],
        in_specs=[smem(), pl.BlockSpec((1, rows, D), lambda s: (s, 0, 0))]
        + [slot] * 4
        + [pl.BlockSpec(text_t.shape, lambda s: (0, 0))]
        + [vec_spec] * 5
        + [handed] * 2,
        out_specs=[slot] * 5
        + [pl.BlockSpec((1, text_t.shape[0], LANG), lambda s: (0, 0, 0))]
        + [vec_spec] * 4
        + [handed] * 2,
        compiler_params=pltpu.CompilerParams(vmem_limit_bytes=VMEM_LIMIT),
    )(
        owners, grad, masters, first, second, average, text_t, vec_grad, vec, v1, v2, va, patch, layer
    )


def local(
    patches, text_tokens, view_counts, out_grad, owners, masters, first_moment, second_moment,
    average, vec_value, vec_first, vec_second, vec_average,
):
    vec, v1, v2, va = [
        part.reshape(VEC // 128, 128) for part in (vec_value, vec_first, vec_second, vec_average)
    ]
    text_in = jnp.swapaxes(text_tokens, 1, 2)
    if lax.axis_size("wide") == 8 and lax.axis_size("narrow") == 4:
        patch_grad, layer_out, _, slot_grad, text_sum, vec_grad = block(
            owners, view_counts, masters, text_in, patches, vec, out_grad
        )
    else:
        units, text_t = gather(owners, masters, text_in)
        att_t, probs, inverse, q_t, keyed, v_t = attention_forward(
            view_counts, patches, text_t, vec, units
        )
        layer_out, middle_back, back_t, rest, *vecs = dense(
            view_counts, att_t, patches, out_grad, vec, units[3:]
        )
        query_back, key_back, value_back = attention_backward(
            probs, inverse, keyed, v_t, back_t, q_t, att_t
        )
        patch_grad, first, gain_one, bias_one, text_part = project_back(
            patches, text_t, vec, units, middle_back, query_back, key_back, value_back
        )
        slot_grad, text_sum, vec_grad = reduce_all(
            owners, rest, first, text_part, (gain_one, bias_one, *vecs)
        )
    outs = update(
        owners, slot_grad, masters, first_moment, second_moment, average, text_sum, vec_grad, vec,
        v1, v2, va, patch_grad, layer_out,
    )
    new_masters, new_first, new_second, new_average, new_copies, text_grad = outs[:6]
    vectors = [part.reshape(VEC) for part in outs[6:10]]
    patch_grad, layer_out = outs[10:]
    return (
        layer_out, patch_grad, jnp.swapaxes(text_grad, 1, 2), new_masters, new_first, new_second,
        new_average, new_copies, *vectors,
    )


def solution(mesh):
    rows = P(("wide", "narrow"), None)
    state = P("narrow", None, "wide", None)
    text = P("narrow", None, "wide")
    in_specs = (rows, text, rows, rows, P(), state, state, state, state, P(), P(), P(), P())
    out_specs = (rows, rows, text, state, state, state, state, state, P(), P(), P(), P())
    return jax.shard_map(local, mesh=mesh, in_specs=in_specs, out_specs=out_specs, check_vma=False)
```

```python
import functools

import jax
import jax.numpy as jnp
from jax import lax
from jax.experimental import pallas as pl
from jax.experimental.pallas import tpu as pltpu
from jax.sharding import PartitionSpec as P

D = 512
HEADS = 8
FF = 2048
VIEWS = 5
VIEW_ROWS = 256
ROWS = VIEWS * VIEW_ROWS
LANG = 77
TEXT = 128
KEYS = ROWS + TEXT
STEP = 5
UNITS = 12
SLOTS = 4
VEC = 5 * D + FF
F32 = jnp.float32
BF16 = jnp.bfloat16
MESH = pl.DeviceIdType.MESH
NEG = -1e30

norm_eps = 1e-05
beta_one = 0.5
beta_two = 0.5
adam_eps = 1e-08
weight_decay = 0.1
average_keep = 0.75
vector_rate = 0.25
VMEM_LIMIT = 60 * 2**20


def dot(left, right, left_dim=1, right_dim=0):
    return lax.dot_general(
        left, right, (((left_dim,), (right_dim,)), ((), ())), preferred_element_type=F32
    )


def vmem():
    return pl.BlockSpec(memory_space=pltpu.VMEM)


def smem():
    return pl.BlockSpec(memory_space=pltpu.SMEM)


def vec_row(vec, start, size):
    first = start // 128
    return jnp.concatenate([vec[first + r : first + r + 1, :] for r in range(size // 128)], axis=1)


def unit_ranks(owners_ref):
    owner = [owners_ref[u] for u in range(UNITS)]
    rank = []
    for u in range(UNITS):
        total = jnp.int32(0)
        for v in range(u):
            total = total + (owner[v] == owner[u]).astype(jnp.int32)
        rank.append(jnp.minimum(total, SLOTS - 1))
    return owner, rank


def normalize(values):
    center = values - jnp.mean(values, axis=-1, keepdims=True)
    spread = jnp.mean(center * center, axis=-1, keepdims=True)
    scale = lax.rsqrt(spread + norm_eps)
    return center * scale, scale


def norm_back(grads, gain, normed, scale):
    e = grads * gain
    return scale * (
        e
        - jnp.mean(e, axis=-1, keepdims=True)
        - normed * jnp.mean(e * normed, axis=-1, keepdims=True)
    )


def place():
    w = lax.axis_index("wide")
    n = lax.axis_index("narrow")
    return w, n, w // 2, w % 2, n // 2, n % 2


def narrow_peers(at):
    w, n = at[:2]
    return [(w, lax.rem(n + k, 4)) for k in range(1, 4)]


def wide_peers(at):
    w, n = at[:2]
    return [(lax.rem(w + k, 8), n) for k in range(1, 8)]


def chip_peers(at):
    w, n, z, x, y, c = at
    peers = []
    for k in range(1, 16):
        chip = lax.rem(z * 4 + x * 2 + y + k, 16)
        cz, cx, cy = chip // 4, (chip // 2) % 2, chip % 2
        peers.append((cz, cx, cy, (cz * 2 + cx, cy * 2 + c)))
    return peers


def all_peers(at):
    w, n, z, x, y, c = at
    return narrow_peers(at) + wide_peers(at) + [
        (lax.rem(w + k, 8), (1 - y) * 2 + c) for k in range(1, 8)
    ]


def greet(peers):
    barrier = pltpu.get_barrier_semaphore()
    for peer in peers:
        pl.semaphore_signal(barrier, inc=1, device_id=peer, device_id_type=MESH)


def greeted(peers):
    pl.semaphore_wait(pltpu.get_barrier_semaphore(), len(peers))


class Links:
    def __init__(self, send, recv):
        self.send, self.recv, self.slots = send, recv, {}

    def copies(self, key, parts):
        made = []
        for k, (src, dst, device) in enumerate(parts()):
            slot = self.slots.setdefault((key, k), len(self.slots))
            made.append(
                pltpu.make_async_remote_copy(
                    src_ref=src,
                    dst_ref=dst,
                    send_sem=self.send.at[slot],
                    recv_sem=self.recv.at[slot],
                    device_id=device,
                    device_id_type=MESH,
                )
            )
        return made

    def start(self, key, parts):
        for copy in self.copies(key, parts):
            copy.start()

    def wait(self, key, parts):
        for copy in self.copies(key, parts):
            copy.wait()


def partners(w, n, z, x, y, c):
    to_z = [(lax.rem(z + k, 4) * 2 + x, n) for k in range(1, 4)]
    return to_z, (z * 2 + 1 - x, n), (w, (1 - y) * 2 + c), (w, y * 2 + 1 - c)


def spread(ref, head, stage, at):
    w, n, z, x, y, c = at
    to_z, to_x, to_y, to_c = partners(*at)
    whole = slice(None)
    if stage == 0:
        parts = [((z, x, y, c), peer) for peer in to_z]
    elif stage == 1:
        parts = [((pl.ds(0, 2), x, y, c), to_x), ((pl.ds(2, 2), x, y, c), to_y)]
    elif stage == 2:
        parts = [((pl.ds(0, 2), whole, y, c), to_y), ((pl.ds(2, 2), x, whole, c), to_x)]
    else:
        parts = [((whole, whole, whole, c), to_c)]
    return [(ref.at[(*head, *part)], ref.at[(*head, *part)], peer) for part, peer in parts]


def add(a, b):
    return a + b


class Reducer:
    def __init__(self, name, links, at, source, bufs, shift=None):
        self.name, self.links, self.at, self.source = name, links, at, source
        self.shift = shift or (lambda head: head)
        (self.c_buf, self.ya_buf, self.xb_buf, self.xa_buf, self.yb_buf, self.z_sum,
         self.z_buf) = bufs

    def start(self, stage, head):
        self.links.start(*self.copies(stage, head))

    def copies(self, stage, head):
        return (self.name, str(head), stage), lambda: self.parts(stage, head)

    def parts(self, stage, head):
        w, n, z, x, y, c = self.at
        to_z, to_x, to_y, to_c = partners(*self.at)
        whole, low, high = slice(None), pl.ds(0, 2), pl.ds(2, 2)
        source, buf = self.source, self.shift(head)
        if stage == 0:
            return [(source.at[(*head, whole, whole, whole, 1 - c)], self.c_buf.at[buf], to_c)]
        if stage == 1:
            return [
                (source.at[(*head, low, whole, 1 - y, c)], self.ya_buf.at[buf], to_y),
                (source.at[(*head, high, 1 - x, whole, c)], self.xb_buf.at[buf], to_x),
            ]
        if stage == 2:
            return [
                (source.at[(*head, low, 1 - x, y, c)], self.xa_buf.at[buf], to_x),
                (source.at[(*head, high, x, 1 - y, c)], self.yb_buf.at[buf], to_y),
            ]
        return [
            (self.z_sum.at[(*buf, lax.rem(z + k, 4))], self.z_buf.at[(k - 1, *buf)], to_z[k - 1])
            for k in range(1, 4)
        ]

    def finish(self, stage, head):
        w, n, z, x, y, c = self.at
        self.links.wait(*self.copies(stage, head))
        whole, low, high = slice(None), pl.ds(0, 2), pl.ds(2, 2)
        source, buf = self.source, self.shift(head)
        if stage == 0:
            own = (*head, whole, whole, whole, c)
            source[own] = add(source[own], self.c_buf[buf])
        elif stage == 1:
            a = (*head, low, whole, y, c)
            b = (*head, high, x, whole, c)
            source[a] = add(source[a], self.ya_buf[buf])
            source[b] = add(source[b], self.xb_buf[buf])
        elif stage == 2:
            self.z_sum[(*buf, low)] = add(source[(*head, low, x, y, c)], self.xa_buf[buf])
            self.z_sum[(*buf, high)] = add(source[(*head, high, x, y, c)], self.yb_buf[buf])
        else:
            total = self.z_sum[(*buf, z)].astype(F32)
            for k in range(3):
                total = total + self.z_buf[(k, *buf)].astype(F32)
            return total.astype(BF16)


PIECES = (4, 2, 2, 2, 16)
KEY_PARTS = ((0, 512), (512, 1024), (1024, 1408))
DENSE_PLACE = (8, 0, 2, 4, 6, 1, 3, 5, 7)


def block_kernel(
    owners, counts, masters, text, x, vec, g,
    patch_out, layer_out, probs, slot_grad, text_out, vec_out,
    send_buf, slot_buf, w_first, w_rest, text_buf, q_t, keyed, key_bias, v_t, normed_t,
    text_normed, att_t, inverse, delta, p_buf, g_buf, middle_buf,
    rest_all, c_buf, ya_buf, xb_buf, xa_buf, yb_buf, z_sum, z_buf,
    first_all, first_c, first_d, fa_buf, fb_buf, fc_buf, fd_buf, fz_sum, fz_buf, red, s_buf, r_buf, text_part, text_sum,
    v_own, vw_buf, v_sum, vn_buf, l_own, lw_buf, l_sum, ln_buf,
    query_back, key_back, value_back, value_pair, key_pair_t, send, recv, local
):
    at = place()
    w, n, z, sx, y, c = at
    links = Links(send, recv)
    whole = slice(None)
    peers = all_peers(at)
    gain_one, bias_one = vec_row(vec, 0, D), vec_row(vec, D, D)
    live_text = lax.broadcasted_iota(jnp.int32, (TEXT, 1), 0) < LANG
    read_g = pltpu.make_async_copy(g, g_buf, local.at[2])
    write_layer = pltpu.make_async_copy(g_buf, layer_out, local.at[3])
    write_patch = pltpu.make_async_copy(middle_buf, patch_out, local.at[4])

    greet(peers)
    send_buf[...] = masters[0].reshape(SLOTS, 4, 16, D).astype(BF16)
    text_buf[z, sx] = jnp.zeros((64, TEXT), BF16)
    text_buf[z, sx, :, 0:LANG] = text[0]
    greeted(peers)
    slots = "slots", lambda: [
        (send_buf.at[:, peer[1]], slot_buf.at[n], peer) for peer in narrow_peers(at)
    ]
    links.start(*slots)
    texts = "text", lambda: [
        (text_buf.at[z, sx], text_buf.at[z, sx], peer) for peer in wide_peers(at)
    ]
    links.start(*texts)
    slot_buf[n] = send_buf[:, n]
    low = (normalize(x[...].astype(F32))[0] * gain_one + bias_one).astype(BF16)
    normed = g_buf
    normed[...] = low
    normed_t[:, 0:ROWS] = low.astype(F32).T.astype(BF16)
    owner, rank = unit_ranks(owners)
    links.wait(*slots)
    for u in range(3):
        w_first[u, z, sx, y, c] = slot_buf[owner[u], rank[u]]

    def first(u, s):
        return ("first", u, s), lambda: spread(w_first, (u,), s, at)

    def rest(group, s):
        return ("rest", group, s), lambda: spread(w_rest, (pl.ds(3 * group, 3),), s, at)

    order = (1, 0, 2)
    for u in order:
        links.start(*first(u, 0))
    for k, position in enumerate(DENSE_PLACE):
        w_rest[position, z, sx, y, c] = slot_buf[owner[3 + k], rank[3 + k]]
    for v, live in enumerate(live_column(counts, ROWS)):
        key_bias[v * VIEW_ROWS : (v + 1) * VIEW_ROWS, :] = jnp.broadcast_to(
            jnp.where(live, 0.0, NEG), (VIEW_ROWS, 128)
        ).astype(BF16)
    key_bias[ROWS:KEYS, :] = jnp.broadcast_to(
        jnp.where(live_text, 0.0, NEG), (TEXT, 128)
    ).astype(BF16)
    def read_text():
        links.wait(*texts)
        rows = text_buf[...].reshape(D, TEXT).astype(F32).T
        text_low = jnp.where(live_text, normalize(rows)[0] * gain_one + bias_one, 0.0)
        text_normed[...] = text_low.astype(BF16)
        normed_t[:, ROWS:KEYS] = text_low.T.astype(BF16)

    def unit(u):
        return w_first[u].reshape(D, D)

    def project(u):
        if u == 1:
            k = dot(normed[...], unit(1)).astype(BF16)
            t = dot(text_normed[...], unit(1)).astype(BF16)
            for p in range(4):
                pair = slice(p * 128, (p + 1) * 128)
                keyed[p, 0:ROWS] = k[:, pair]
                keyed[p, ROWS:KEYS] = t[:, pair]
        elif u == 0:
            q_t[...] = dot(unit(0), normed[...], 0, 1).astype(BF16) * BF16(0.125)
        else:
            v_t[:, 0:ROWS] = dot(unit(2), normed[...], 0, 1).astype(BF16)
            v_t[:, ROWS:KEYS] = dot(unit(2), text_normed[...], 0, 1).astype(BF16)

    for step in range(3 + 3):
        for s in (3, 2, 1, 0):
            k = step - s
            if not 0 <= k < 3:
                continue
            u = order[k]
            if (k, s) == (2, 3):
                continue
            links.wait(*first(u, s))
            if s < 3:
                links.start(*first(u, s + 1))
            if k == 2 and s < 3:
                links.start(*rest((2, 1, 0)[s], 0))
            if (k, s) == (1, 1):
                read_text()
            if s == 3:
                project(u)

    gather_plan = {
        0: [(2, 0)], 1: [(1, 0)], 2: [(2, 1)], 3: [(0, 0)], 4: [(2, 2), (1, 1)], 5: [],
        6: [(0, 1), (1, 2)], 7: [(2, 3)],
    }

    def gather_point(t):
        for group, s in gather_plan[t]:
            links.wait(*rest(group, s))
            if s < 3:
                links.start(*rest(group, s + 1))

    row = lax.broadcasted_iota(jnp.int32, (128, ROWS), 0)
    one = jnp.where(row == 0, 1.0, 0.0).astype(BF16)

    def saved(t):
        return pltpu.make_async_copy(p_buf.at[t % 2], probs.at[t], local.at[t % 2])

    def values():
        links.wait(*first(2, 3))
        project(2)
        read_g.start()

    def mix(t):
        head = pl.ds(pl.multiple_of(t * 64, 64), 64)
        summed = jnp.concatenate([v_t[head, :], jnp.ones((16, KEYS), BF16)], axis=0)
        mixed = dot(summed, p_buf[t % 2])
        inv = 1.0 / mixed[64:65]
        att_t[head, :] = (mixed[0:64] * inv).astype(BF16)
        inverse[t] = inv

    @pl.loop(0, HEADS)
    def _(t):
        for k in range(HEADS):
            pl.when(t == k)(functools.partial(gather_point, k))
        pl.when(t == 1)(values)
        pl.when(t > 1)(lambda: saved(t - 2).wait())
        pl.when(t > 0)(lambda: mix(t - 1))
        i, h = t // 2, t % 2
        pair_q = q_t[pl.ds(pl.multiple_of(i * 128, 128), 128), :]
        mine = (row >= 64 * h) & (row < 64 * h + 64)
        q = jnp.where(mine, pair_q, jnp.zeros_like(pair_q))
        keys = jnp.concatenate([keyed[i], key_bias[...]], axis=1)
        scores = dot(keys, jnp.concatenate([q, one], axis=0))
        peak = jnp.max(scores, axis=0, keepdims=True)
        for first_key, end_key in KEY_PARTS:
            p_buf[h, first_key:end_key] = jnp.exp(scores[first_key:end_key] - peak).astype(BF16)
        pl.when(t < HEADS - 1)(lambda: saved(t).start())

    mix(HEADS - 1)
    read_g.wait()
    saved(HEADS - 2).wait()

    def fetched(t):
        return pltpu.make_async_copy(probs.at[t], p_buf.at[t % 2], local.at[t % 2])

    reducer = Reducer(
        "reduce", links, at, rest_all, (c_buf, ya_buf, xb_buf, xa_buf, yb_buf, z_sum, z_buf)
    )
    dense_order = (3, 2, 1, 0)
    groups = [(pl.ds(4, 4),), (pl.ds(0, 4),), (pl.ds(8, 1),)]

    def step_rest(group, stage):
        total = reducer.finish(stage, groups[group])
        if stage < 3:
            reducer.start(stage + 1, groups[group])
        else:
            red[groups[group]] = total

    def dense_unit(position):
        return w_rest[position].reshape(D, D)

    @pl.when(w >= 0)
    def _():
        gain, bias = vec_row(vec, 2 * D, D), vec_row(vec, 3 * D, D)
        halves = [slice(k * ROWS // 2, (k + 1) * ROWS // 2) for k in range(2)]
        lows, outs = p_buf.at[0, :, 0:D], p_buf.at[0, :, D : 2 * D]
        normals, scales, backs, lives = [], [], [], []
        for k, rows in enumerate(halves):
            index = lax.broadcasted_iota(jnp.int32, (ROWS // 2, 1), 0) + k * (ROWS // 2)
            live = jnp.zeros((ROWS // 2, 1), jnp.bool_)
            for v in range(VIEWS):
                live = live | ((index >= v * VIEW_ROWS) & (index < v * VIEW_ROWS + counts[0, v]))
            middle = x[rows].astype(F32) + dot(att_t[:, rows], dense_unit(8), 0, 0)
            normal, scale = normalize(middle)
            middle_buf[rows] = middle + vec_row(vec, 4 * D + FF, D)
            normals.append(normal)
            scales.append(scale)
            lows[rows] = (normal * gain + bias).astype(BF16)
            backs.append(jnp.zeros((ROWS // 2, D), F32))
            lives.append(live)
            outs[rows] = jnp.where(live, g_buf[rows].astype(F32), 0.0).astype(BF16)
        for turn, j in enumerate(dense_order):
            if turn == 1:
                links.wait(*rest(0, 2))
                links.start(*rest(0, 3))
                links.wait(*rest(1, 3))
            if turn == 2:
                links.wait(*rest(0, 3))
            w_up, w_down = dense_unit(2 * j), dense_unit(2 * j + 1)
            up_total, down_total, up_grad = 0.0, 0.0, 0.0
            for k, rows in enumerate(halves):
                preact = dot(lows[rows], w_up) + vec_row(vec, 4 * D + j * D, D)
                phi = 0.5 + 0.5 * lax.erf(preact * 0.7071067811865476)
                active = (preact * phi).astype(BF16)
                slope = phi + preact * (jnp.exp(-0.5 * preact * preact) * 0.3989422804014327)
                middle_buf[rows] += dot(active, w_down)
                preact_back = (dot(outs[rows], w_down, 1, 1) * slope).astype(BF16)
                backs[k] = backs[k] + dot(preact_back, w_up, 1, 1)
                up_total = up_total + dot(lows[rows], preact_back, 0, 0)
                down_total = down_total + dot(active, outs[rows], 0, 0)
                up_grad = up_grad + jnp.sum(preact_back.astype(F32), axis=0, keepdims=True)
            rest_all[2 * j] = up_total.astype(BF16).reshape(*PIECES, D)
            rest_all[2 * j + 1] = down_total.astype(BF16).reshape(*PIECES, D)
            for r in range(4):
                v_own[16 + 4 * j + r : 17 + 4 * j + r, :] = up_grad[:, r * 128 : (r + 1) * 128]
            if turn == 1:
                reducer.start(0, groups[0])
            if turn > 1:
                step_rest(0, turn - 2)
            if turn == 3:
                reducer.start(0, groups[1])
        for k, rows in enumerate(halves):
            g_buf[rows] = jnp.where(lives[k], middle_buf[rows], 0.0).astype(BF16)
        write_layer.start()
        out_total, gain_grad, bias_grad, down_grad = 0.0, 0.0, 0.0, 0.0
        for k, rows in enumerate(halves):
            out_back = outs[rows].astype(F32)
            back = out_back + norm_back(backs[k], gain, normals[k], scales[k])
            middle_buf[rows] = back
            branch = back.astype(BF16)
            out_total = out_total + dot(att_t[:, rows], branch)
            back_rows = dot(dense_unit(8), branch, 1, 1).astype(BF16)
            product = back_rows.astype(F32) * att_t[:, rows].astype(F32)
            for h in range(HEADS):
                part = jnp.sum(product[h * 64 : (h + 1) * 64], axis=0, keepdims=True)
                delta[h, :, rows] = part * inverse[h, :, rows]
            att_t[:, rows] = back_rows
            gain_grad = gain_grad + jnp.sum(backs[k] * normals[k], axis=0, keepdims=True)
            bias_grad = bias_grad + jnp.sum(backs[k], axis=0, keepdims=True)
            down_grad = down_grad + jnp.sum(out_back, axis=0, keepdims=True)
        rest_all[8] = out_total.astype(BF16).reshape(*PIECES, D)
        for offset, piece in ((8, gain_grad), (12, bias_grad), (32, down_grad)):
            for r in range(4):
                v_own[offset + r : offset + r + 1, :] = piece[:, r * 128 : (r + 1) * 128]
        v_own[0:8, :] = jnp.zeros((8, 128), F32)

    fetched(HEADS - 2).start()
    back_t = att_t

    def chunk_core(p):
        return ("chunk", p, 0), lambda: [
            (first_all.at[p, :, :, :, :, 1 - c], first_c.at[p], (w, y * 2 + 1 - c))
        ]

    chip = z * 4 + sx * 2 + y

    def chunk_chips(p):
        return ("chunk", p, 1), lambda: [
            (first_all.at[p, :, cz, cx, cy, c], first_d.at[p, chip], peer)
            for cz, cx, cy, peer in chip_peers(at)
        ]

    def chunk_middle(p):
        links.wait(*chunk_core(p))
        own = (p, whole, whole, whole, whole, c)
        first_all[own] = add(first_all[own], first_c[p])
        links.start(*chunk_chips(p))
        first_d[p, chip] = first_all[p, :, z, sx, y, c]

    def chunk_end(p):
        links.wait(*chunk_chips(p))
        total = jnp.sum(first_d[p].astype(F32), axis=0).astype(BF16)
        red[9:12, :, p * 128 : (p + 1) * 128] = total

    staged = Reducer(
        "staged", links, at, first_all,
        (first_c.at[pl.ds(2, 2)], fa_buf, fb_buf, fc_buf, fd_buf, fz_sum, fz_buf),
        lambda head: (head[0] - 2, *head[1:]),
    )

    def step_chunk(p, stage):
        total = staged.finish(stage, (p, whole))
        if stage < 3:
            staged.start(stage + 1, (p, whole))
        else:
            red[9:12, :, p * 128 : (p + 1) * 128] = total

    wides = "wide", lambda: [(v_own, vw_buf.at[w], peer) for peer in wide_peers(at)]
    narrows = "narrow", lambda: [(v_sum, vn_buf.at[n], peer) for peer in narrow_peers(at)]

    def vector_start():
        vw_buf[w] = v_own[...]
        links.start(*wides)

    def vector_middle():
        links.wait(*wides)
        total = vw_buf[0]
        for k in range(1, 8):
            total = total + vw_buf[k]
        v_sum[...] = total
        vn_buf[n] = total
        links.start(*narrows)

    def reduce_point(t):
        for group, s in {
            0: [(0, 2), (1, 0)], 1: [(2, 0)], 2: [(1, 1)], 3: [(0, 3), (2, 1)], 4: [(1, 2)],
            5: [(2, 2)], 6: [], 7: [(1, 3), (2, 3)],
        }[t]:
            step_rest(group, s)
        if t == 0:
            reducer.start(0, groups[2])
            vector_start()
        if t == 3:
            vector_middle()
        for p, s in {
            3: [(3, 0)], 4: [(3, 1)], 5: [(3, 2), (2, 0)], 6: [(2, 1)], 7: [(3, 3), (2, 2)]
        }.get(t, []):
            step_chunk(p, s)
        if t == 7:
            chunk_middle(1)

    def start_chunk(p):
        if p > 1:
            staged.start(0, (p, whole))
        else:
            links.start(*chunk_core(p))

    lane = lax.broadcasted_iota(jnp.int32, (KEYS, 128), 1)
    ones = jnp.where(lane < 2, 1.0, 0.0).astype(BF16)

    @pl.loop(0, HEADS)
    def _(step):
        for k in range(HEADS):
            pl.when(step == k)(functools.partial(reduce_point, k))
        t = HEADS - 1 - step
        i, h = t // 2, t % 2
        pl.when(step > 0)(lambda: fetched(t).wait())
        pair = pl.ds(pl.multiple_of(i * 128, 128), 128)
        head = pl.ds(pl.multiple_of(t * 64, 64), 64)

        @pl.when(h == 1)
        def _():
            value_pair[...] = v_t[pair, :].astype(F32).T.astype(BF16)
            key_pair_t[...] = keyed[i].astype(F32).T.astype(BF16)

        inv = inverse[t]
        shift = delta[t]
        high = shift.astype(BF16).astype(F32)
        mine = (row >= 64 * h) & (row < 64 * h + 64)
        scaled = jnp.where(mine, back_t[pair, :].astype(F32) * inv, 0.0).astype(BF16)
        tail = jnp.where(row == 0, -high, jnp.where(row == 1, high - shift, 0.0)).astype(BF16)
        right = jnp.concatenate([scaled, tail], axis=0)
        value = jnp.concatenate([value_pair[...], ones], axis=1)
        key_head = key_pair_t[pl.ds(pl.multiple_of(h * 64, 64), 64), :]
        query_head = q_t[head, :]
        back_head = (back_t[head, :].astype(F32) * inv).astype(BF16)
        query_total = jnp.zeros((64, ROWS), F32)
        for first_key, end_key in KEY_PARTS:
            part = slice(first_key, end_key)
            low = p_buf[h, part]
            score_back = low * dot(value[part], right).astype(BF16)
            query_total = query_total + dot(key_head[:, part], score_back)
            key_back[head, part] = dot(query_head, score_back, 1, 1).astype(BF16)
            value_back[head, part] = dot(back_head, low, 1, 1).astype(BF16)
        query_back[head, :] = (query_total * 0.125).astype(BF16)
        pl.when(t > 1)(lambda: fetched(t - 2).start())

        @pl.when(h == 0)
        def _():
            part = dot(normed_t[:, 0:ROWS], query_back[pair, :], 1, 1).astype(BF16)
            first_all[i, 0] = part.reshape(*PIECES, 128)
            both = jnp.concatenate([key_back[pair, :], value_back[pair, :]], axis=0)
            part = dot(normed_t[...], both, 1, 1).astype(BF16)
            for u in range(2):
                first_all[i, 1 + u] = part[:, u * 128 : (u + 1) * 128].reshape(*PIECES, 128)

        for k in range(4):
            pl.when(step == 2 * k + 1)(functools.partial(start_chunk, 3 - k))

    @pl.when(w >= 0)
    def _():
        w_q, w_k, w_v = unit(0), unit(1), unit(2)
        normal, scale = normalize(text_buf[...].reshape(D, TEXT).astype(F32).T)
        text_back = dot(key_back[:, ROWS:KEYS], w_k, 0, 1) + dot(
            value_back[:, ROWS:KEYS], w_v, 0, 1
        )
        text_part[...] = (
            norm_back(text_back, gain_one, normal, scale).T.astype(BF16).reshape(8, 64, TEXT)
        )
        gain_grad = jnp.sum(text_back * normal, axis=0, keepdims=True)
        bias_grad = jnp.sum(text_back, axis=0, keepdims=True)
        text_sum[w] = text_part[w]
        text_parts = "parts", lambda: [
            (text_part.at[peer[0]], text_sum.at[w], peer) for peer in wide_peers(at)
        ]
        chunk_middle(0)
        links.start(*text_parts)
        step_chunk(2, 3)
        tile = ROWS // 2
        kept = []
        for t in range(2):
            rows = slice(t * tile, (t + 1) * tile)
            normal, scale = normalize(x[rows].astype(F32))
            projected = (
                dot(query_back[:, rows], w_q, 0, 1)
                + dot(key_back[:, rows], w_k, 0, 1)
                + dot(value_back[:, rows], w_v, 0, 1)
            )
            kept.append((rows, projected, normal, scale))
            gain_grad = gain_grad + jnp.sum(projected * normal, axis=0, keepdims=True)
            bias_grad = bias_grad + jnp.sum(projected, axis=0, keepdims=True)
        for r in range(4):
            l_own[r : r + 1, :] = gain_grad[:, r * 128 : (r + 1) * 128]
            l_own[4 + r : 5 + r, :] = bias_grad[:, r * 128 : (r + 1) * 128]
        late_wides = "late wide", lambda: [(l_own, lw_buf.at[w], peer) for peer in wide_peers(at)]
        late_narrows = "late narrow", lambda: [
            (l_sum, ln_buf.at[n], peer) for peer in narrow_peers(at)
        ]
        lw_buf[w] = l_own[...]
        links.start(*late_wides)
        for rows, projected, normal, scale in kept:
            middle_buf[rows] += norm_back(projected, gain_one, normal, scale)
        write_patch.start()
        links.wait(*narrows)
        vec_out[...] = (vn_buf[0] + vn_buf[1]) + (vn_buf[2] + vn_buf[3])
        owner, rank = unit_ranks(owners)
        spots = []
        for q in range(4):
            for s in range(SLOTS):
                spot = jnp.int32(0)
                for u in range(UNITS):
                    position = 9 + u if u < 3 else DENSE_PLACE[u - 3]
                    spot = spot + jnp.where((owner[u] == q) & (rank[u] == s), position, 0)
                spots.append((q, s, jnp.minimum(spot, UNITS - 1)))

        def grads(part, columns):
            return ("grads", part), lambda: [
                (s_buf.at[peer[1], :, :, columns], r_buf.at[n, :, :, columns], peer)
                for peer in narrow_peers(at)
            ]

        def send_grads(part, columns):
            for q, s, spot in spots:
                s_buf[q, s, :, columns] = red[spot, :, columns]
            links.start(*grads(part, columns))
            r_buf[n, :, :, columns] = s_buf[n, :, :, columns]

        others, last = slice(128, 512), slice(0, 128)
        chunk_end(1)
        send_grads(0, others)
        links.wait(*text_parts)
        text_out[...] = jnp.sum(text_sum[...].astype(F32), axis=0)
        chunk_end(0)
        send_grads(1, last)
        links.wait(*late_wides)
        total = lw_buf[0]
        for k in range(1, 8):
            total = total + lw_buf[k]
        l_sum[...] = total
        ln_buf[n] = total
        links.start(*late_narrows)
        links.wait(*grads(0, others))
        links.wait(*grads(1, last))
        for q in range(4):
            slot_grad[:, q * 16 : (q + 1) * 16, :] = r_buf[q]
        write_layer.wait()
        write_patch.wait()
        links.wait(*late_narrows)
        vec_out[0:8, :] = (ln_buf[0] + ln_buf[1]) + (ln_buf[2] + ln_buf[3])


def block(owners, counts, masters, text, x, vec, g):
    hbm = pl.BlockSpec(memory_space=pl.ANY)
    copies = 3 + 7 + 24 + 24 + 3 * 8 + 2 * 8 + 2 * 16 + 7 + 3 + 7 + 7 + 3 + 6
    bf = lambda *s: pltpu.VMEM(s, BF16)
    f32 = lambda *s: pltpu.VMEM(s, F32)
    rows = VEC // 128
    return pl.pallas_call(
        block_kernel,
        in_specs=[smem(), smem(), vmem(), vmem(), vmem(), vmem(), hbm],
        out_specs=[hbm, hbm, hbm, vmem(), vmem(), vmem()],
        out_shape=[
            jax.ShapeDtypeStruct((ROWS, D), F32),
            jax.ShapeDtypeStruct((ROWS, D), BF16),
            jax.ShapeDtypeStruct((HEADS - 1, KEYS, ROWS), BF16),
            jax.ShapeDtypeStruct((SLOTS, 64, D), BF16),
            jax.ShapeDtypeStruct((64, TEXT), F32),
            jax.ShapeDtypeStruct((rows, 128), F32),
        ],
        scratch_shapes=[
            bf(SLOTS, 4, 16, D),
            bf(4, SLOTS, 16, D),
            bf(3, *PIECES, D),
            bf(9, *PIECES, D),
            bf(4, 2, 64, TEXT),
            bf(D, ROWS),
            bf(4, KEYS, 128),
            bf(KEYS, 128),
            bf(D, KEYS),
            bf(D, KEYS),
            bf(TEXT, D),
            bf(D, ROWS),
            f32(HEADS, 1, ROWS),
            f32(HEADS, 1, ROWS),
            bf(2, KEYS, ROWS),
            bf(ROWS, D),
            f32(ROWS, D),
            bf(9, *PIECES, D),
            bf(9, 4, 2, 2, 16, D),
            bf(9, 2, 2, 16, D),
            bf(9, 2, 2, 16, D),
            bf(9, 2, 16, D),
            bf(9, 2, 16, D),
            bf(9, 4, 16, D),
            bf(3, 9, 16, D),
            bf(4, 3, *PIECES, 128),
            bf(4, 3, 4, 2, 2, 16, 128),
            bf(2, 16, 3, 16, 128),
            bf(2, 3, 2, 2, 16, 128),
            bf(2, 3, 2, 2, 16, 128),
            bf(2, 3, 2, 16, 128),
            bf(2, 3, 2, 16, 128),
            bf(2, 3, 4, 16, 128),
            bf(3, 2, 3, 16, 128),
            bf(UNITS, 16, D),
            bf(4, SLOTS, 16, D),
            bf(4, SLOTS, 16, D),
            bf(8, 64, TEXT),
            bf(8, 64, TEXT),
            f32(rows, 128),
            f32(8, rows, 128),
            f32(rows, 128),
            f32(4, rows, 128),
            f32(8, 128),
            f32(8, 8, 128),
            f32(8, 128),
            f32(4, 8, 128),
            bf(D, ROWS),
            bf(D, KEYS),
            bf(D, KEYS),
            bf(KEYS, 128),
            bf(128, KEYS),
            pltpu.SemaphoreType.DMA((copies,)),
            pltpu.SemaphoreType.DMA((copies,)),
            pltpu.SemaphoreType.DMA((5,)),
        ],
        compiler_params=pltpu.CompilerParams(
            collective_id=1, has_side_effects=True, vmem_limit_bytes=63 * 2**20
        ),
    )(owners, counts, masters, text, x, vec, g)


def gather(owners, masters, text_t):
    packed = lax.all_gather(masters.astype(BF16), "wide", axis=2, tiled=True)
    packed = lax.all_gather(packed, "narrow", axis=0, tiled=True)
    same = owners[:, None] == owners[None, :]
    ids = jnp.arange(UNITS)
    rank = jnp.sum((same & (ids[None, :] < ids[:, None])).astype(jnp.int32), axis=1)
    units = jnp.take(packed.reshape(-1, D, D), owners * SLOTS + rank, axis=0)
    rows = lax.all_gather(text_t, "wide", axis=1, tiled=True)[0]
    return units, jnp.pad(rows, ((0, 0), (0, TEXT - LANG)))


def live_column(counts, rows):
    index = lax.broadcasted_iota(jnp.int32, (VIEW_ROWS, 1), 0)
    return [(index < counts[0, v]) for v in range(rows // VIEW_ROWS)]


def forward_kernel(
    counts, x, text_t, vec, w, att_t, probs, inverse, q_t, keyed, v_t, normed, text_normed
):
    i = pl.program_id(0)

    @pl.when(i == 0)
    def _():
        gain, bias = vec_row(vec, 0, D), vec_row(vec, D, D)
        normed[...] = (normalize(x[...].astype(F32))[0] * gain + bias).astype(BF16)
        rows = text_t[...].astype(F32).T
        live_text = lax.broadcasted_iota(jnp.int32, (TEXT, 1), 0) < LANG
        text_normed[...] = jnp.where(
            live_text, normalize(rows)[0] * gain + bias, 0.0
        ).astype(BF16)
        q_t[...] = dot(w[0], normed[...], 0, 1).astype(BF16) * BF16(0.125)
        v_t[:, 0:ROWS] = dot(w[2], normed[...], 0, 1).astype(BF16)
        v_t[:, ROWS:KEYS] = dot(w[2], text_normed[...], 0, 1).astype(BF16)
        for p in range(4):
            pair = slice(p * 128, (p + 1) * 128)
            keyed[p, 0:ROWS, 0:128] = dot(normed[...], w[1, :, pair]).astype(BF16)
            keyed[p, ROWS:KEYS, 0:128] = dot(text_normed[...], w[1, :, pair]).astype(BF16)
            for v, live in enumerate(live_column(counts, ROWS)):
                keyed[p, v * VIEW_ROWS : (v + 1) * VIEW_ROWS, 128:256] = jnp.broadcast_to(
                    jnp.where(live, 0.0, NEG), (VIEW_ROWS, 128)
                ).astype(BF16)
            keyed[p, ROWS:KEYS, 128:256] = jnp.broadcast_to(
                jnp.where(live_text, 0.0, NEG), (TEXT, 128)
            ).astype(BF16)

    row = lax.broadcasted_iota(jnp.int32, (128, ROWS), 0)
    one = jnp.where(row == 0, 1.0, 0.0).astype(BF16)
    pair_q = q_t[pl.ds(pl.multiple_of(i * 128, 128), 128), :]
    for h in range(2):
        mine = (row >= 64 * h) & (row < 64 * h + 64)
        q = jnp.where(mine, pair_q, jnp.zeros_like(pair_q))
        scores = dot(keyed[i], jnp.concatenate([q, one], axis=0))
        peak = jnp.max(scores, axis=0, keepdims=True)
        e = jnp.exp(scores - peak)
        total = jnp.sum(e, axis=0, keepdims=True)
        low = e.astype(BF16)
        probs[h] = low
        mixed = dot(v_t[pl.ds(pl.multiple_of(i * 128 + h * 64, 64), 64), :], low)
        inv = 1.0 / total
        att_t[h * 64 : (h + 1) * 64, :] = (mixed * inv).astype(BF16)
        inverse[0, h : h + 1, :] = inv


def attention_forward(counts, x, text_t, vec, units):
    return pl.pallas_call(
        forward_kernel,
        grid=(4,),
        in_specs=[smem(), vmem(), vmem(), vmem(), pl.BlockSpec((3, D, D), lambda i: (0, 0, 0))],
        out_specs=[
            pl.BlockSpec((128, ROWS), lambda i: (i, 0)),
            pl.BlockSpec((2, KEYS, ROWS), lambda i: (i, 0, 0)),
            pl.BlockSpec((1, 2, ROWS), lambda i: (i, 0, 0)),
            pl.BlockSpec((D, ROWS), lambda i: (0, 0)),
            pl.BlockSpec((4, KEYS, 256), lambda i: (0, 0, 0)),
            pl.BlockSpec((D, KEYS), lambda i: (0, 0)),
        ],
        out_shape=[
            jax.ShapeDtypeStruct((D, ROWS), BF16),
            jax.ShapeDtypeStruct((HEADS, KEYS, ROWS), BF16),
            jax.ShapeDtypeStruct((4, 2, ROWS), F32),
            jax.ShapeDtypeStruct((D, ROWS), BF16),
            jax.ShapeDtypeStruct((4, KEYS, 256), BF16),
            jax.ShapeDtypeStruct((D, KEYS), BF16),
        ],
        scratch_shapes=[pltpu.VMEM((ROWS, D), BF16), pltpu.VMEM((TEXT, D), BF16)],
        compiler_params=pltpu.CompilerParams(vmem_limit_bytes=VMEM_LIMIT),
    )(counts, x, text_t, vec, units)


def dense_kernel(
    counts, att_t, x, g, vec, w,
    layer_out, middle_back, back_t, grads, gain_grad, bias_grad, up_grad, down_grad,
    total, *, tile
):
    i = pl.program_id(0)
    steps = pl.num_programs(0)
    gain, bias = vec_row(vec, 2 * D, D), vec_row(vec, 3 * D, D)
    a = att_t[...]
    index = lax.broadcasted_iota(jnp.int32, (tile, 1), 0) + i * tile
    live = jnp.zeros((tile, 1), jnp.bool_)
    for v in range(VIEWS):
        live = live | ((index >= v * VIEW_ROWS) & (index < v * VIEW_ROWS + counts[0, v]))
    middle = x[...].astype(F32) + dot(a, w[0], 0, 0)
    normed, scale = normalize(middle)
    low = (normed * gain + bias).astype(BF16)
    out_back = jnp.where(live, g[...].astype(F32), 0.0)
    out_low = out_back.astype(BF16)

    @pl.when(i == 0)
    def _():
        total[...] = jnp.zeros_like(total)
        gain_grad[...] = jnp.zeros_like(gain_grad)
        bias_grad[...] = jnp.zeros_like(bias_grad)
        up_grad[...] = jnp.zeros_like(up_grad)
        down_grad[...] = jnp.zeros_like(down_grad)

    out = middle + vec_row(vec, 4 * D + FF, D)
    normed_back = jnp.zeros((tile, D), F32)
    for j in range(4):
        block = slice(j * D, (j + 1) * D)
        preact = dot(low, w[1 + j]) + vec_row(vec, 4 * D + j * D, D)
        phi = 0.5 + 0.5 * lax.erf(preact * 0.7071067811865476)
        active = (preact * phi).astype(BF16)
        slope = phi + preact * (jnp.exp(-0.5 * preact * preact) * 0.3989422804014327)
        out = out + dot(active, w[5 + j])
        preact_back = (dot(out_low, w[5 + j], 1, 1) * slope).astype(BF16)
        normed_back = normed_back + dot(preact_back, w[1 + j], 1, 1)
        total[1 + j] += dot(low, preact_back, 0, 0)
        total[5 + j] += dot(active, out_low, 0, 0)
        up_grad[:, block] += jnp.sum(preact_back.astype(F32), axis=0, keepdims=True)
    layer_out[...] = jnp.where(live, out, 0.0).astype(BF16)
    back = out_back + norm_back(normed_back, gain, normed, scale)
    middle_back[...] = back
    branch = back.astype(BF16)
    back_t[...] = dot(w[0], branch, 1, 1).astype(BF16)
    total[0] += dot(a, branch)
    gain_grad[...] += jnp.sum(normed_back * normed, axis=0, keepdims=True)
    bias_grad[...] += jnp.sum(normed_back, axis=0, keepdims=True)
    down_grad[...] += jnp.sum(out_back, axis=0, keepdims=True)

    @pl.when(i == steps - 1)
    def _():
        grads[...] = total[...].astype(BF16)


def dense(counts, att_t, x, g, vec, units, tile=640):
    rows = pl.BlockSpec((tile, D), lambda i: (i, 0))
    columns = pl.BlockSpec((D, tile), lambda i: (0, i))
    return pl.pallas_call(
        functools.partial(dense_kernel, tile=tile),
        grid=(ROWS // tile,),
        in_specs=[smem(), columns, rows, rows, vmem(), vmem()],
        out_specs=[
            rows,
            rows,
            columns,
            pl.BlockSpec((9, D, D), lambda i: (0, 0, 0)),
            pl.BlockSpec((1, D), lambda i: (0, 0)),
            pl.BlockSpec((1, D), lambda i: (0, 0)),
            pl.BlockSpec((1, FF), lambda i: (0, 0)),
            pl.BlockSpec((1, D), lambda i: (0, 0)),
        ],
        out_shape=[
            jax.ShapeDtypeStruct((ROWS, D), BF16),
            jax.ShapeDtypeStruct((ROWS, D), F32),
            jax.ShapeDtypeStruct((D, ROWS), BF16),
            jax.ShapeDtypeStruct((9, D, D), BF16),
            jax.ShapeDtypeStruct((1, D), F32),
            jax.ShapeDtypeStruct((1, D), F32),
            jax.ShapeDtypeStruct((1, FF), F32),
            jax.ShapeDtypeStruct((1, D), F32),
        ],
        scratch_shapes=[pltpu.VMEM((9, D, D), F32)],
        compiler_params=pltpu.CompilerParams(vmem_limit_bytes=VMEM_LIMIT),
    )(counts, att_t, x, g, vec, units)


def backward_kernel(probs, inverse, keyed, v_t, back_t, q_t, att_t, query_back, key_back, value_back):
    row = lax.broadcasted_iota(jnp.int32, (128, ROWS), 0)
    lane = lax.broadcasted_iota(jnp.int32, (KEYS, 128), 1)
    ones = jnp.where(lane < 2, 1.0, 0.0).astype(BF16)
    value = jnp.concatenate([v_t[...].astype(F32).T.astype(BF16), ones], axis=1)
    key_t = keyed[:, 0:128].astype(F32).T.astype(BF16)
    back = back_t[...].astype(F32)
    product = back * att_t[...].astype(F32)
    query = q_t[...].astype(F32)
    key_total = jnp.zeros((KEYS, 128), F32)
    value_total = jnp.zeros((KEYS, 128), F32)
    for h in range(2):
        half = slice(h * 64, (h + 1) * 64)
        inv = inverse[0, h : h + 1, :]
        delta = jnp.sum(product[half], axis=0, keepdims=True) * inv
        high = delta.astype(BF16).astype(F32)
        mine = (row >= 64 * h) & (row < 64 * h + 64)
        scaled = jnp.where(mine, back * inv, 0.0)
        tail = jnp.where(row == 0, -high, jnp.where(row == 1, high - delta, 0.0))
        right = jnp.concatenate([scaled.astype(BF16), tail.astype(BF16)], axis=0)
        low = probs[h]
        score_back = low * dot(value, right).astype(BF16)
        query_back[half, :] = (dot(key_t[half], score_back) * 0.125).astype(BF16)
        key_total += dot(score_back, jnp.where(mine, query, 0.0).T.astype(BF16))
        value_total += dot(low, scaled.T.astype(BF16))
    key_back[...] = key_total.astype(BF16)
    value_back[...] = value_total.astype(BF16)


def attention_backward(probs, inverse, keyed, v_t, back_t, q_t, att_t):
    return pl.pallas_call(
        backward_kernel,
        grid=(4,),
        in_specs=[
            pl.BlockSpec((2, KEYS, ROWS), lambda i: (i, 0, 0)),
            pl.BlockSpec((1, 2, ROWS), lambda i: (i, 0, 0)),
            pl.BlockSpec((None, KEYS, 256), lambda i: (i, 0, 0)),
            pl.BlockSpec((128, KEYS), lambda i: (i, 0)),
            pl.BlockSpec((128, ROWS), lambda i: (i, 0)),
            pl.BlockSpec((128, ROWS), lambda i: (i, 0)),
            pl.BlockSpec((128, ROWS), lambda i: (i, 0)),
        ],
        out_specs=[
            pl.BlockSpec((128, ROWS), lambda i: (i, 0)),
            pl.BlockSpec((KEYS, 128), lambda i: (0, i)),
            pl.BlockSpec((KEYS, 128), lambda i: (0, i)),
        ],
        out_shape=[
            jax.ShapeDtypeStruct((D, ROWS), BF16),
            jax.ShapeDtypeStruct((KEYS, D), BF16),
            jax.ShapeDtypeStruct((KEYS, D), BF16),
        ],
        compiler_params=pltpu.CompilerParams(vmem_limit_bytes=VMEM_LIMIT),
    )(probs, inverse, keyed, v_t, back_t, q_t, att_t)


def project_kernel(
    x, text_t, vec, w, middle_back, query_back, key_back, value_back, text_key, text_value,
    patch_grad, grads, gain_grad, bias_grad, text_grad_t, total
):
    i = pl.program_id(0)
    steps = pl.num_programs(0)
    gain, bias = vec_row(vec, 0, D), vec_row(vec, D, D)

    @pl.when(i == 0)
    def _():
        live = lax.broadcasted_iota(jnp.int32, (TEXT, 1), 0) < LANG
        normed, scale = normalize(text_t[...].astype(F32).T)
        low_t = jnp.where(live, normed * gain + bias, 0.0).T.astype(BF16)
        k, v = text_key[...], text_value[...]
        back = dot(k, w[1], 1, 1) + dot(v, w[2], 1, 1)
        text_grad_t[...] = norm_back(back, gain, normed, scale).T.astype(BF16)
        gain_grad[...] = jnp.sum(back * normed, axis=0, keepdims=True)
        bias_grad[...] = jnp.sum(back, axis=0, keepdims=True)
        total[0] = jnp.zeros((D, D), F32)
        total[1] = dot(low_t, k)
        total[2] = dot(low_t, v)

    normed, scale = normalize(x[...].astype(F32))
    low_t = (normed * gain + bias).T.astype(BF16)
    q, k, v = query_back[...], key_back[...], value_back[...]
    back = dot(q, w[0], 0, 1) + dot(k, w[1], 1, 1) + dot(v, w[2], 1, 1)
    patch_grad[...] = middle_back[...] + norm_back(back, gain, normed, scale)
    total[0] += dot(low_t, q, 1, 1)
    total[1] += dot(low_t, k)
    total[2] += dot(low_t, v)
    gain_grad[...] += jnp.sum(back * normed, axis=0, keepdims=True)
    bias_grad[...] += jnp.sum(back, axis=0, keepdims=True)

    @pl.when(i == steps - 1)
    def _():
        grads[...] = total[...].astype(BF16)


def project_back(x, text_t, vec, units, middle_back, query_back, key_back, value_back, tile=640):
    rows = pl.BlockSpec((tile, D), lambda i: (i, 0))
    text_rows = pl.BlockSpec((TEXT, D), lambda i: (ROWS // TEXT, 0))
    return pl.pallas_call(
        project_kernel,
        grid=(ROWS // tile,),
        in_specs=[
            rows,
            vmem(),
            vmem(),
            pl.BlockSpec((3, D, D), lambda i: (0, 0, 0)),
            rows,
            pl.BlockSpec((D, tile), lambda i: (0, i)),
            rows,
            rows,
            text_rows,
            text_rows,
        ],
        out_specs=[
            rows,
            pl.BlockSpec((3, D, D), lambda i: (0, 0, 0)),
            pl.BlockSpec((1, D), lambda i: (0, 0)),
            pl.BlockSpec((1, D), lambda i: (0, 0)),
            pl.BlockSpec((D, TEXT), lambda i: (0, 0)),
        ],
        out_shape=[
            jax.ShapeDtypeStruct((ROWS, D), F32),
            jax.ShapeDtypeStruct((3, D, D), BF16),
            jax.ShapeDtypeStruct((1, D), F32),
            jax.ShapeDtypeStruct((1, D), F32),
            jax.ShapeDtypeStruct((D, TEXT), BF16),
        ],
        scratch_shapes=[pltpu.VMEM((3, D, D), F32)],
        compiler_params=pltpu.CompilerParams(vmem_limit_bytes=VMEM_LIMIT),
    )(
        x, text_t, vec, units, middle_back, query_back, key_back, value_back, key_back, value_back
    )


def reduce_all(owners, rest, first, text, vecs):
    vec = lax.psum(jnp.concatenate(vecs, axis=1), ("wide", "narrow"))
    text_sum = lax.psum_scatter(text.astype(F32), "wide", scatter_dimension=0, tiled=True)
    all_units = jnp.concatenate([first, rest], axis=0).astype(F32)
    rows = lax.psum_scatter(all_units, "wide", scatter_dimension=1, tiled=True)
    same = owners[:, None] == owners[None, :]
    ids = jnp.arange(UNITS)
    rank = jnp.sum((same & (ids[None, :] < ids[:, None])).astype(jnp.int32), axis=1)
    pick = (owners[None, None, :] == jnp.arange(lax.axis_size("narrow"))[:, None, None]) & (
        rank[None, None, :] == jnp.arange(SLOTS)[None, :, None]
    )
    terms = jnp.einsum("nsu,urc->nsrc", pick.astype(F32), rows, precision=lax.Precision.HIGHEST)
    slots = lax.psum_scatter(terms, "narrow", scatter_dimension=0, tiled=True)
    return slots[0], text_sum, vec.reshape(VEC // 128, 128)


def adam(master, moment_one, moment_two, averaged, gradient, rate):
    moment_one = beta_one * moment_one + (1.0 - beta_one) * gradient
    moment_two = beta_two * moment_two + (1.0 - beta_two) * gradient * gradient
    mean_hat = moment_one / (1.0 - beta_one**STEP)
    second_hat = moment_two / (1.0 - beta_two**STEP)
    master = master - rate * (
        mean_hat / (jnp.sqrt(second_hat) + adam_eps) + weight_decay * master
    )
    averaged = average_keep * averaged + (1.0 - average_keep) * master
    return master, moment_one, moment_two, averaged


def unit_rates():
    blocks = FF // D
    fans = [2 * D // 3, 2 * D // 3, D, D // 64] + [D] * blocks + [FF] * blocks
    return [float(fan) ** -0.5 for fan in fans]


def update_kernel(
    owners, grad, masters, first, second, average, text_t, vec_grad, vec, vec_first, vec_second,
    vec_average, patch_in, layer_in,
    new_masters, new_first, new_second, new_average, new_copies, text_grad,
    vec_new_value, vec_new_first, vec_new_second, vec_new_average, patch_out, layer_out,
):
    s = pl.program_id(0)
    patch_out[...] = patch_in[...]
    layer_out[...] = layer_in[...]
    n = lax.axis_index("narrow")
    owner, rank = unit_ranks(owners)
    rate, filled = jnp.float32(0.0), jnp.int32(0)
    for u, value in enumerate(unit_rates()):
        match = (owner[u] == n) & (rank[u] == s)
        rate = rate + jnp.where(match, jnp.float32(value), jnp.float32(0.0))
        filled = filled + match.astype(jnp.int32)
    state = adam(masters[0, 0], first[0, 0], second[0, 0], average[0, 0], grad[0].astype(F32), rate)
    keep = jnp.broadcast_to(filled, state[0].shape) > 0
    state = [jnp.where(keep, part, 0.0) for part in state]
    for ref, part in zip((new_masters, new_first, new_second, new_average), state):
        ref[0, 0] = part
    new_copies[0, 0] = state[0].astype(BF16)

    @pl.when(s == 0)
    def _():
        text_grad[0] = text_t[:, 0:LANG]
        state = adam(
            vec[...], vec_first[...], vec_second[...], vec_average[...], vec_grad[...], vector_rate
        )
        for ref, part in zip(
            (vec_new_value, vec_new_first, vec_new_second, vec_new_average), state
        ):
            ref[...] = part


def update(
    owners, grad, masters, first, second, average, text_t, vec_grad, vec, v1, v2, va, patch, layer
):
    rows = masters.shape[2]
    state = jax.ShapeDtypeStruct(masters.shape, F32)
    vector = jax.ShapeDtypeStruct(vec.shape, F32)
    slot = pl.BlockSpec((1, 1, rows, D), lambda s: (0, s, 0, 0))
    vec_spec = pl.BlockSpec(vec.shape, lambda s: (0, 0))
    handed = pl.BlockSpec((ROWS // SLOTS, D), lambda s: (s, 0))
    return pl.pallas_call(
        update_kernel,
        grid=(SLOTS,),
        out_shape=[state] * 4
        + [
            jax.ShapeDtypeStruct(masters.shape, BF16),
            jax.ShapeDtypeStruct((1, text_t.shape[0], LANG), F32),
        ]
        + [vector] * 4
        + [jax.ShapeDtypeStruct(patch.shape, F32), jax.ShapeDtypeStruct(layer.shape, BF16)],
        in_specs=[smem(), pl.BlockSpec((1, rows, D), lambda s: (s, 0, 0))]
        + [slot] * 4
        + [pl.BlockSpec(text_t.shape, lambda s: (0, 0))]
        + [vec_spec] * 5
        + [handed] * 2,
        out_specs=[slot] * 5
        + [pl.BlockSpec((1, text_t.shape[0], LANG), lambda s: (0, 0, 0))]
        + [vec_spec] * 4
        + [handed] * 2,
        compiler_params=pltpu.CompilerParams(vmem_limit_bytes=VMEM_LIMIT),
    )(
        owners, grad, masters, first, second, average, text_t, vec_grad, vec, v1, v2, va, patch, layer
    )


def local(
    patches, text_tokens, view_counts, out_grad, owners, masters, first_moment, second_moment,
    average, vec_value, vec_first, vec_second, vec_average,
):
    vec, v1, v2, va = [
        part.reshape(VEC // 128, 128) for part in (vec_value, vec_first, vec_second, vec_average)
    ]
    text_in = jnp.swapaxes(text_tokens, 1, 2)
    if lax.axis_size("wide") == 8 and lax.axis_size("narrow") == 4:
        patch_grad, layer_out, _, slot_grad, text_sum, vec_grad = block(
            owners, view_counts, masters, text_in, patches, vec, out_grad
        )
    else:
        units, text_t = gather(owners, masters, text_in)
        att_t, probs, inverse, q_t, keyed, v_t = attention_forward(
            view_counts, patches, text_t, vec, units
        )
        layer_out, middle_back, back_t, rest, *vecs = dense(
            view_counts, att_t, patches, out_grad, vec, units[3:]
        )
        query_back, key_back, value_back = attention_backward(
            probs, inverse, keyed, v_t, back_t, q_t, att_t
        )
        patch_grad, first, gain_one, bias_one, text_part = project_back(
            patches, text_t, vec, units, middle_back, query_back, key_back, value_back
        )
        slot_grad, text_sum, vec_grad = reduce_all(
            owners, rest, first, text_part, (gain_one, bias_one, *vecs)
        )
    outs = update(
        owners, slot_grad, masters, first_moment, second_moment, average, text_sum, vec_grad, vec,
        v1, v2, va, patch_grad, layer_out,
    )
    new_masters, new_first, new_second, new_average, new_copies, text_grad = outs[:6]
    vectors = [part.reshape(VEC) for part in outs[6:10]]
    patch_grad, layer_out = outs[10:]
    return (
        layer_out, patch_grad, jnp.swapaxes(text_grad, 1, 2), new_masters, new_first, new_second,
        new_average, new_copies, *vectors,
    )


def solution(mesh):
    rows = P(("wide", "narrow"), None)
    state = P("narrow", None, "wide", None)
    text = P("narrow", None, "wide")
    in_specs = (rows, text, rows, rows, P(), state, state, state, state, P(), P(), P(), P())
    out_specs = (rows, rows, text, state, state, state, state, state, P(), P(), P(), P())
    return jax.shard_map(local, mesh=mesh, in_specs=in_specs, out_specs=out_specs, check_vma=False)
```

```python
import functools

import jax
import jax.numpy as jnp
from jax import lax
from jax.experimental import pallas as pl
from jax.experimental.pallas import tpu as pltpu
from jax.sharding import PartitionSpec as P

D = 512
HEADS = 8
FF = 2048
VIEWS = 5
VIEW_ROWS = 256
ROWS = VIEWS * VIEW_ROWS
LANG = 77
TEXT = 128
KEYS = ROWS + TEXT
STEP = 5
UNITS = 12
SLOTS = 4
VEC = 5 * D + FF
F32 = jnp.float32
BF16 = jnp.bfloat16
MESH = pl.DeviceIdType.MESH
NEG = -1e30

norm_eps = 1e-05
beta_one = 0.5
beta_two = 0.5
adam_eps = 1e-08
weight_decay = 0.1
average_keep = 0.75
vector_rate = 0.25
VMEM_LIMIT = 60 * 2**20


def dot(left, right, left_dim=1, right_dim=0):
    return lax.dot_general(
        left, right, (((left_dim,), (right_dim,)), ((), ())), preferred_element_type=F32
    )


def vmem():
    return pl.BlockSpec(memory_space=pltpu.VMEM)


def smem():
    return pl.BlockSpec(memory_space=pltpu.SMEM)


def vec_row(vec, start, size):
    first = start // 128
    return jnp.concatenate([vec[first + r : first + r + 1, :] for r in range(size // 128)], axis=1)


def unit_ranks(owners_ref):
    owner = [owners_ref[u] for u in range(UNITS)]
    rank = []
    for u in range(UNITS):
        total = jnp.int32(0)
        for v in range(u):
            total = total + (owner[v] == owner[u]).astype(jnp.int32)
        rank.append(jnp.minimum(total, SLOTS - 1))
    return owner, rank


def normalize(values):
    center = values - jnp.mean(values, axis=-1, keepdims=True)
    spread = jnp.mean(center * center, axis=-1, keepdims=True)
    scale = lax.rsqrt(spread + norm_eps)
    return center * scale, scale


def norm_back(grads, gain, normed, scale):
    e = grads * gain
    return scale * (
        e
        - jnp.mean(e, axis=-1, keepdims=True)
        - normed * jnp.mean(e * normed, axis=-1, keepdims=True)
    )


def place():
    w = lax.axis_index("wide")
    n = lax.axis_index("narrow")
    return w, n, w // 2, w % 2, n // 2, n % 2


def narrow_peers(at):
    w, n = at[:2]
    return [(w, lax.rem(n + k, 4)) for k in range(1, 4)]


def wide_peers(at):
    w, n = at[:2]
    return [(lax.rem(w + k, 8), n) for k in range(1, 8)]


def chip_peers(at):
    w, n, z, x, y, c = at
    peers = []
    for k in range(1, 16):
        chip = lax.rem(z * 4 + x * 2 + y + k, 16)
        cz, cx, cy = chip // 4, (chip // 2) % 2, chip % 2
        peers.append((cz, cx, cy, (cz * 2 + cx, cy * 2 + c)))
    return peers


def all_peers(at):
    w, n, z, x, y, c = at
    return narrow_peers(at) + wide_peers(at) + [
        (lax.rem(w + k, 8), (1 - y) * 2 + c) for k in range(1, 8)
    ]


def greet(peers):
    barrier = pltpu.get_barrier_semaphore()
    for peer in peers:
        pl.semaphore_signal(barrier, inc=1, device_id=peer, device_id_type=MESH)


def greeted(peers):
    pl.semaphore_wait(pltpu.get_barrier_semaphore(), len(peers))


class Links:
    def __init__(self, send, recv):
        self.send, self.recv, self.slots = send, recv, {}

    def copies(self, key, parts):
        made = []
        for k, (src, dst, device) in enumerate(parts()):
            slot = self.slots.setdefault((key, k), len(self.slots))
            made.append(
                pltpu.make_async_remote_copy(
                    src_ref=src,
                    dst_ref=dst,
                    send_sem=self.send.at[slot],
                    recv_sem=self.recv.at[slot],
                    device_id=device,
                    device_id_type=MESH,
                )
            )
        return made

    def start(self, key, parts):
        for copy in self.copies(key, parts):
            copy.start()

    def wait(self, key, parts):
        for copy in self.copies(key, parts):
            copy.wait()


def partners(w, n, z, x, y, c):
    to_z = [(lax.rem(z + k, 4) * 2 + x, n) for k in range(1, 4)]
    return to_z, (z * 2 + 1 - x, n), (w, (1 - y) * 2 + c), (w, y * 2 + 1 - c)


def spread(ref, head, stage, at, tail=()):
    w, n, z, x, y, c = at
    to_z, to_x, to_y, to_c = partners(*at)
    whole = slice(None)
    if stage == 0:
        parts = [((z, x, y, c), peer) for peer in to_z]
    elif stage == 1:
        parts = [((pl.ds(0, 2), x, y, c), to_x), ((pl.ds(2, 2), x, y, c), to_y)]
    elif stage == 2:
        parts = [((pl.ds(0, 2), whole, y, c), to_y), ((pl.ds(2, 2), x, whole, c), to_x)]
    else:
        parts = [((whole, whole, whole, c), to_c)]
    pieces = [(ref.at[(*head, *part, *tail)], peer) for part, peer in parts]
    return [(piece, piece, peer) for piece, peer in pieces]


def add(a, b):
    return a + b


class Reducer:
    def __init__(self, name, links, at, source, bufs, shift=None):
        self.name, self.links, self.at, self.source = name, links, at, source
        self.shift = shift or (lambda head: head)
        (self.c_buf, self.ya_buf, self.xb_buf, self.xa_buf, self.yb_buf, self.z_sum,
         self.z_buf) = bufs

    def start(self, stage, head):
        self.links.start(*self.copies(stage, head))

    def copies(self, stage, head):
        return (self.name, str(head), stage), lambda: self.parts(stage, head)

    def parts(self, stage, head):
        w, n, z, x, y, c = self.at
        to_z, to_x, to_y, to_c = partners(*self.at)
        whole, low, high = slice(None), pl.ds(0, 2), pl.ds(2, 2)
        source, buf = self.source, self.shift(head)
        if stage == 0:
            return [(source.at[(*head, whole, whole, whole, 1 - c)], self.c_buf.at[buf], to_c)]
        if stage == 1:
            return [
                (source.at[(*head, low, whole, 1 - y, c)], self.ya_buf.at[buf], to_y),
                (source.at[(*head, high, 1 - x, whole, c)], self.xb_buf.at[buf], to_x),
            ]
        if stage == 2:
            return [
                (source.at[(*head, low, 1 - x, y, c)], self.xa_buf.at[buf], to_x),
                (source.at[(*head, high, x, 1 - y, c)], self.yb_buf.at[buf], to_y),
            ]
        return [
            (self.z_sum.at[(*buf, lax.rem(z + k, 4))], self.z_buf.at[(k - 1, *buf)], to_z[k - 1])
            for k in range(1, 4)
        ]

    def finish(self, stage, head):
        w, n, z, x, y, c = self.at
        self.links.wait(*self.copies(stage, head))
        whole, low, high = slice(None), pl.ds(0, 2), pl.ds(2, 2)
        source, buf = self.source, self.shift(head)
        if stage == 0:
            own = (*head, whole, whole, whole, c)
            source[own] = add(source[own], self.c_buf[buf])
        elif stage == 1:
            a = (*head, low, whole, y, c)
            b = (*head, high, x, whole, c)
            source[a] = add(source[a], self.ya_buf[buf])
            source[b] = add(source[b], self.xb_buf[buf])
        elif stage == 2:
            self.z_sum[(*buf, low)] = add(source[(*head, low, x, y, c)], self.xa_buf[buf])
            self.z_sum[(*buf, high)] = add(source[(*head, high, x, y, c)], self.yb_buf[buf])
        else:
            total = self.z_sum[(*buf, z)].astype(F32)
            for k in range(3):
                total = total + self.z_buf[(k, *buf)].astype(F32)
            return total.astype(BF16)


PIECES = (4, 2, 2, 2, 16)
KEY_PARTS = ((0, 512), (512, 1024), (1024, 1408))
DENSE_PLACE = (8, 0, 2, 4, 6, 1, 3, 5, 7)


def block_kernel(
    owners, counts, masters, text, x, vec, g,
    patch_out, layer_out, probs, slot_grad, text_out, vec_out,
    send_buf, slot_first, slot_second, w_first, w_rest, text_buf, q_t, keyed, key_bias, v_t, normed_t,
    text_normed, att_t, inverse, delta, p_buf, g_buf, middle_buf,
    rest_all, c_buf, ya_buf, xb_buf, xa_buf, yb_buf, z_sum, z_buf,
    first_all, first_c, first_d, fa_buf, fb_buf, fc_buf, fd_buf, fz_sum, fz_buf, red, s_buf, r_buf, text_part, text_sum,
    v_own, vw_buf, v_sum, vn_buf, l_own, lw_buf, l_sum, ln_buf,
    query_back, key_back, value_back, value_pair, key_pair_t, send, recv, local
):
    at = place()
    w, n, z, sx, y, c = at
    links = Links(send, recv)
    whole = slice(None)
    peers = all_peers(at)
    gain_one, bias_one = vec_row(vec, 0, D), vec_row(vec, D, D)
    live_text = lax.broadcasted_iota(jnp.int32, (TEXT, 1), 0) < LANG
    read_g = pltpu.make_async_copy(g, g_buf, local.at[2])
    write_layer = pltpu.make_async_copy(g_buf, layer_out, local.at[3])
    write_patch = pltpu.make_async_copy(middle_buf, patch_out, local.at[4])

    greet(peers)
    send_buf[...] = masters[0].reshape(SLOTS, 4, 16, D).astype(BF16)
    text_buf[z, sx] = jnp.zeros((64, TEXT), BF16)
    text_buf[z, sx, :, 0:LANG] = text[0]
    greeted(peers)
    halves = [slice(0, D // 2), slice(D // 2, D)]
    slot_bufs = (slot_first, slot_second)

    def slots(half):
        return ("slots", half), lambda: [
            (send_buf.at[:, peer[1], :, halves[half]], slot_bufs[half].at[n], peer)
            for peer in narrow_peers(at)
        ]

    links.start(*slots(0))
    links.start(*slots(1))
    texts = "text", lambda: [
        (text_buf.at[z, sx], text_buf.at[z, sx], peer) for peer in wide_peers(at)
    ]
    links.start(*texts)
    for half in range(2):
        slot_bufs[half][n] = send_buf[:, n, :, halves[half]]
    low = (normalize(x[...].astype(F32))[0] * gain_one + bias_one).astype(BF16)
    normed = g_buf
    normed[...] = low
    normed_t[:, 0:ROWS] = low.astype(F32).T.astype(BF16)
    owner, rank = unit_ranks(owners)
    def first(half, s):
        tail = (slice(None), halves[half])
        return ("first", half, s), lambda: spread(w_first, (slice(None),), s, at, tail)

    for half in range(2):
        links.wait(*slots(half))
        for u in range(3):
            w_first[u, z, sx, y, c, :, halves[half]] = slot_bufs[half][owner[u], rank[u]]
        links.start(*first(half, 0))

    def rest(group, s):
        return ("rest", group, s), lambda: spread(w_rest, (pl.ds(3 * group, 3),), s, at)

    for k, position in enumerate(DENSE_PLACE):
        for half in range(2):
            w_rest[position, z, sx, y, c, :, halves[half]] = slot_bufs[half][
                owner[3 + k], rank[3 + k]
            ]
    for v, live in enumerate(live_column(counts, ROWS)):
        key_bias[v * VIEW_ROWS : (v + 1) * VIEW_ROWS, :] = jnp.broadcast_to(
            jnp.where(live, 0.0, NEG), (VIEW_ROWS, 128)
        ).astype(BF16)
    key_bias[ROWS:KEYS, :] = jnp.broadcast_to(
        jnp.where(live_text, 0.0, NEG), (TEXT, 128)
    ).astype(BF16)
    def read_text():
        links.wait(*texts)
        rows = text_buf[...].reshape(D, TEXT).astype(F32).T
        text_low = jnp.where(live_text, normalize(rows)[0] * gain_one + bias_one, 0.0)
        text_normed[...] = text_low.astype(BF16)
        normed_t[:, ROWS:KEYS] = text_low.T.astype(BF16)

    def unit(u):
        return w_first[u].reshape(D, D)

    def project(half):
        w_q, w_k, w_v = [w_first[u, :, :, :, :, :, halves[half]].reshape(D, D // 2) for u in range(3)]
        k = dot(normed[...], w_k).astype(BF16)
        t = dot(text_normed[...], w_k).astype(BF16)
        for p in range(2):
            pair = slice(p * 128, (p + 1) * 128)
            keyed[2 * half + p, 0:ROWS] = k[:, pair]
            keyed[2 * half + p, ROWS:KEYS] = t[:, pair]
        q_t[halves[half], :] = dot(w_q, normed[...], 0, 1).astype(BF16) * BF16(0.125)
        v_t[halves[half], 0:ROWS] = dot(w_v, normed[...], 0, 1).astype(BF16)
        v_t[halves[half], ROWS:KEYS] = dot(w_v, text_normed[...], 0, 1).astype(BF16)

    def step_first(half, s):
        links.wait(*first(half, s))
        if s < 3:
            links.start(*first(half, s + 1))

    step_first(0, 0)
    step_first(1, 0)
    links.start(*rest(2, 0))
    step_first(0, 1)
    read_text()
    step_first(1, 1)
    links.start(*rest(1, 0))
    step_first(0, 2)
    step_first(0, 3)
    links.start(*rest(0, 0))
    project(0)

    gather_plan = {
        0: [(2, 0)], 1: [(1, 0)], 2: [(2, 1)], 3: [(0, 0)], 4: [(2, 2), (1, 1)], 5: [],
        6: [(0, 1), (1, 2)], 7: [(2, 3)],
    }

    def gather_point(t):
        for group, s in gather_plan[t]:
            links.wait(*rest(group, s))
            if s < 3:
                links.start(*rest(group, s + 1))

    row = lax.broadcasted_iota(jnp.int32, (128, ROWS), 0)
    one = jnp.where(row == 0, 1.0, 0.0).astype(BF16)

    def saved(t):
        return pltpu.make_async_copy(p_buf.at[t % 2], probs.at[t], local.at[t % 2])

    def second_half():
        step_first(1, 3)
        project(1)
        read_g.start()

    def mix(t):
        head = pl.ds(pl.multiple_of(t * 64, 64), 64)
        summed = jnp.concatenate([v_t[head, :], jnp.ones((16, KEYS), BF16)], axis=0)
        mixed = dot(summed, p_buf[t % 2])
        inv = 1.0 / mixed[64:65]
        att_t[head, :] = (mixed[0:64] * inv).astype(BF16)
        inverse[t] = inv

    @pl.loop(0, HEADS)
    def _(t):
        for k in range(HEADS):
            pl.when(t == k)(functools.partial(gather_point, k))
        pl.when(t == 0)(lambda: step_first(1, 2))
        pl.when(t == 2)(second_half)
        pl.when(t > 1)(lambda: saved(t - 2).wait())
        pl.when(t > 0)(lambda: mix(t - 1))
        i, h = t // 2, t % 2
        pair_q = q_t[pl.ds(pl.multiple_of(i * 128, 128), 128), :]
        mine = (row >= 64 * h) & (row < 64 * h + 64)
        q = jnp.where(mine, pair_q, jnp.zeros_like(pair_q))
        keys = jnp.concatenate([keyed[i], key_bias[...]], axis=1)
        scores = dot(keys, jnp.concatenate([q, one], axis=0))
        peak = jnp.max(scores, axis=0, keepdims=True)
        for first_key, end_key in KEY_PARTS:
            p_buf[h, first_key:end_key] = jnp.exp(scores[first_key:end_key] - peak).astype(BF16)
        pl.when(t < HEADS - 1)(lambda: saved(t).start())

    mix(HEADS - 1)
    read_g.wait()
    saved(HEADS - 2).wait()

    def fetched(t):
        return pltpu.make_async_copy(probs.at[t], p_buf.at[t % 2], local.at[t % 2])

    reducer = Reducer(
        "reduce", links, at, rest_all, (c_buf, ya_buf, xb_buf, xa_buf, yb_buf, z_sum, z_buf)
    )
    dense_order = (3, 2, 1, 0)
    groups = [(pl.ds(4, 4),), (pl.ds(0, 4),), (pl.ds(8, 1),)]

    def step_rest(group, stage):
        total = reducer.finish(stage, groups[group])
        if stage < 3:
            reducer.start(stage + 1, groups[group])
        else:
            red[groups[group]] = total

    def dense_unit(position):
        return w_rest[position].reshape(D, D)

    @pl.when(w >= 0)
    def _():
        gain, bias = vec_row(vec, 2 * D, D), vec_row(vec, 3 * D, D)
        tiles = [slice(k * ROWS // 2, (k + 1) * ROWS // 2) for k in range(2)]
        lows, outs = p_buf.at[0, :, 0:D], p_buf.at[0, :, D : 2 * D]
        normals, scales, backs, lives = [], [], [], []
        for k, rows in enumerate(tiles):
            index = lax.broadcasted_iota(jnp.int32, (ROWS // 2, 1), 0) + k * (ROWS // 2)
            live = jnp.zeros((ROWS // 2, 1), jnp.bool_)
            for v in range(VIEWS):
                live = live | ((index >= v * VIEW_ROWS) & (index < v * VIEW_ROWS + counts[0, v]))
            middle = x[rows].astype(F32) + dot(att_t[:, rows], dense_unit(8), 0, 0)
            normal, scale = normalize(middle)
            middle_buf[rows] = middle + vec_row(vec, 4 * D + FF, D)
            normals.append(normal)
            scales.append(scale)
            lows[rows] = (normal * gain + bias).astype(BF16)
            backs.append(jnp.zeros((ROWS // 2, D), F32))
            lives.append(live)
            outs[rows] = jnp.where(live, g_buf[rows].astype(F32), 0.0).astype(BF16)
        for turn, j in enumerate(dense_order):
            if turn == 1:
                links.wait(*rest(0, 2))
                links.start(*rest(0, 3))
                links.wait(*rest(1, 3))
            if turn == 2:
                links.wait(*rest(0, 3))
            w_up, w_down = dense_unit(2 * j), dense_unit(2 * j + 1)
            up_total, down_total, up_grad = 0.0, 0.0, 0.0
            for k, rows in enumerate(tiles):
                preact = dot(lows[rows], w_up) + vec_row(vec, 4 * D + j * D, D)
                phi = 0.5 + 0.5 * lax.erf(preact * 0.7071067811865476)
                active = (preact * phi).astype(BF16)
                slope = phi + preact * (jnp.exp(-0.5 * preact * preact) * 0.3989422804014327)
                middle_buf[rows] += dot(active, w_down)
                preact_back = (dot(outs[rows], w_down, 1, 1) * slope).astype(BF16)
                backs[k] = backs[k] + dot(preact_back, w_up, 1, 1)
                up_total = up_total + dot(lows[rows], preact_back, 0, 0)
                down_total = down_total + dot(active, outs[rows], 0, 0)
                up_grad = up_grad + jnp.sum(preact_back.astype(F32), axis=0, keepdims=True)
            rest_all[2 * j] = up_total.astype(BF16).reshape(*PIECES, D)
            rest_all[2 * j + 1] = down_total.astype(BF16).reshape(*PIECES, D)
            for r in range(4):
                v_own[16 + 4 * j + r : 17 + 4 * j + r, :] = up_grad[:, r * 128 : (r + 1) * 128]
            if turn == 1:
                reducer.start(0, groups[0])
            if turn > 1:
                step_rest(0, turn - 2)
            if turn == 3:
                reducer.start(0, groups[1])
        for k, rows in enumerate(tiles):
            g_buf[rows] = jnp.where(lives[k], middle_buf[rows], 0.0).astype(BF16)
        write_layer.start()
        out_total, gain_grad, bias_grad, down_grad = 0.0, 0.0, 0.0, 0.0
        for k, rows in enumerate(tiles):
            out_back = outs[rows].astype(F32)
            back = out_back + norm_back(backs[k], gain, normals[k], scales[k])
            middle_buf[rows] = back
            branch = back.astype(BF16)
            out_total = out_total + dot(att_t[:, rows], branch)
            back_rows = dot(dense_unit(8), branch, 1, 1).astype(BF16)
            product = back_rows.astype(F32) * att_t[:, rows].astype(F32)
            for h in range(HEADS):
                part = jnp.sum(product[h * 64 : (h + 1) * 64], axis=0, keepdims=True)
                delta[h, :, rows] = part * inverse[h, :, rows]
            att_t[:, rows] = back_rows
            gain_grad = gain_grad + jnp.sum(backs[k] * normals[k], axis=0, keepdims=True)
            bias_grad = bias_grad + jnp.sum(backs[k], axis=0, keepdims=True)
            down_grad = down_grad + jnp.sum(out_back, axis=0, keepdims=True)
        rest_all[8] = out_total.astype(BF16).reshape(*PIECES, D)
        for offset, piece in ((8, gain_grad), (12, bias_grad), (32, down_grad)):
            for r in range(4):
                v_own[offset + r : offset + r + 1, :] = piece[:, r * 128 : (r + 1) * 128]
        v_own[0:8, :] = jnp.zeros((8, 128), F32)

    fetched(HEADS - 2).start()
    back_t = att_t

    def chunk_core(p):
        return ("chunk", p, 0), lambda: [
            (first_all.at[p, :, :, :, :, 1 - c], first_c.at[p], (w, y * 2 + 1 - c))
        ]

    chip = z * 4 + sx * 2 + y

    def chunk_chips(p):
        return ("chunk", p, 1), lambda: [
            (first_all.at[p, :, cz, cx, cy, c], first_d.at[p, chip], peer)
            for cz, cx, cy, peer in chip_peers(at)
        ]

    def chunk_middle(p):
        links.wait(*chunk_core(p))
        own = (p, whole, whole, whole, whole, c)
        first_all[own] = add(first_all[own], first_c[p])
        links.start(*chunk_chips(p))
        first_d[p, chip] = first_all[p, :, z, sx, y, c]

    def chunk_end(p):
        links.wait(*chunk_chips(p))
        total = jnp.sum(first_d[p].astype(F32), axis=0).astype(BF16)
        red[9:12, :, p * 128 : (p + 1) * 128] = total

    staged = Reducer(
        "staged", links, at, first_all,
        (first_c.at[pl.ds(2, 2)], fa_buf, fb_buf, fc_buf, fd_buf, fz_sum, fz_buf),
        lambda head: (head[0] - 2, *head[1:]),
    )

    def step_chunk(p, stage):
        total = staged.finish(stage, (p, whole))
        if stage < 3:
            staged.start(stage + 1, (p, whole))
        else:
            red[9:12, :, p * 128 : (p + 1) * 128] = total

    wides = "wide", lambda: [(v_own, vw_buf.at[w], peer) for peer in wide_peers(at)]
    narrows = "narrow", lambda: [(v_sum, vn_buf.at[n], peer) for peer in narrow_peers(at)]

    def vector_start():
        vw_buf[w] = v_own[...]
        links.start(*wides)

    def vector_middle():
        links.wait(*wides)
        total = vw_buf[0]
        for k in range(1, 8):
            total = total + vw_buf[k]
        v_sum[...] = total
        vn_buf[n] = total
        links.start(*narrows)

    def reduce_point(t):
        for group, s in {
            0: [(0, 2), (1, 0)], 1: [(2, 0)], 2: [(1, 1)], 3: [(0, 3), (2, 1)], 4: [(1, 2)],
            5: [(2, 2)], 6: [], 7: [(1, 3), (2, 3)],
        }[t]:
            step_rest(group, s)
        if t == 0:
            reducer.start(0, groups[2])
            vector_start()
        if t == 3:
            vector_middle()
        for p, s in {
            3: [(3, 0)], 4: [(3, 1)], 5: [(3, 2), (2, 0)], 6: [(2, 1)], 7: [(3, 3), (2, 2)]
        }.get(t, []):
            step_chunk(p, s)
        if t == 7:
            chunk_middle(1)

    def start_chunk(p):
        if p > 1:
            staged.start(0, (p, whole))
        else:
            links.start(*chunk_core(p))

    lane = lax.broadcasted_iota(jnp.int32, (KEYS, 128), 1)
    ones = jnp.where(lane < 2, 1.0, 0.0).astype(BF16)

    @pl.loop(0, HEADS)
    def _(step):
        for k in range(HEADS):
            pl.when(step == k)(functools.partial(reduce_point, k))
        t = HEADS - 1 - step
        i, h = t // 2, t % 2
        pl.when(step > 0)(lambda: fetched(t).wait())
        pair = pl.ds(pl.multiple_of(i * 128, 128), 128)
        head = pl.ds(pl.multiple_of(t * 64, 64), 64)

        @pl.when(h == 1)
        def _():
            value_pair[...] = v_t[pair, :].astype(F32).T.astype(BF16)
            key_pair_t[...] = keyed[i].astype(F32).T.astype(BF16)

        inv = inverse[t]
        shift = delta[t]
        high = shift.astype(BF16).astype(F32)
        mine = (row >= 64 * h) & (row < 64 * h + 64)
        scaled = jnp.where(mine, back_t[pair, :].astype(F32) * inv, 0.0).astype(BF16)
        tail = jnp.where(row == 0, -high, jnp.where(row == 1, high - shift, 0.0)).astype(BF16)
        right = jnp.concatenate([scaled, tail], axis=0)
        value = jnp.concatenate([value_pair[...], ones], axis=1)
        key_head = key_pair_t[pl.ds(pl.multiple_of(h * 64, 64), 64), :]
        query_head = q_t[head, :]
        back_head = (back_t[head, :].astype(F32) * inv).astype(BF16)
        query_total = jnp.zeros((64, ROWS), F32)
        for first_key, end_key in KEY_PARTS:
            part = slice(first_key, end_key)
            low = p_buf[h, part]
            score_back = low * dot(value[part], right).astype(BF16)
            query_total = query_total + dot(key_head[:, part], score_back)
            key_back[head, part] = dot(query_head, score_back, 1, 1).astype(BF16)
            value_back[head, part] = dot(back_head, low, 1, 1).astype(BF16)
        query_back[head, :] = (query_total * 0.125).astype(BF16)
        pl.when(t > 1)(lambda: fetched(t - 2).start())

        @pl.when(h == 0)
        def _():
            part = dot(normed_t[:, 0:ROWS], query_back[pair, :], 1, 1).astype(BF16)
            first_all[i, 0] = part.reshape(*PIECES, 128)
            both = jnp.concatenate([key_back[pair, :], value_back[pair, :]], axis=0)
            part = dot(normed_t[...], both, 1, 1).astype(BF16)
            for u in range(2):
                first_all[i, 1 + u] = part[:, u * 128 : (u + 1) * 128].reshape(*PIECES, 128)

        for k in range(4):
            pl.when(step == 2 * k + 1)(functools.partial(start_chunk, 3 - k))

    @pl.when(w >= 0)
    def _():
        w_q, w_k, w_v = unit(0), unit(1), unit(2)
        normal, scale = normalize(text_buf[...].reshape(D, TEXT).astype(F32).T)
        text_back = dot(key_back[:, ROWS:KEYS], w_k, 0, 1) + dot(
            value_back[:, ROWS:KEYS], w_v, 0, 1
        )
        text_part[...] = (
            norm_back(text_back, gain_one, normal, scale).T.astype(BF16).reshape(8, 64, TEXT)
        )
        gain_grad = jnp.sum(text_back * normal, axis=0, keepdims=True)
        bias_grad = jnp.sum(text_back, axis=0, keepdims=True)
        text_sum[w] = text_part[w]
        text_parts = "parts", lambda: [
            (text_part.at[peer[0]], text_sum.at[w], peer) for peer in wide_peers(at)
        ]
        chunk_middle(0)
        links.start(*text_parts)
        step_chunk(2, 3)
        tile = ROWS // 2
        kept = []
        for t in range(2):
            rows = slice(t * tile, (t + 1) * tile)
            normal, scale = normalize(x[rows].astype(F32))
            projected = (
                dot(query_back[:, rows], w_q, 0, 1)
                + dot(key_back[:, rows], w_k, 0, 1)
                + dot(value_back[:, rows], w_v, 0, 1)
            )
            kept.append((rows, projected, normal, scale))
            gain_grad = gain_grad + jnp.sum(projected * normal, axis=0, keepdims=True)
            bias_grad = bias_grad + jnp.sum(projected, axis=0, keepdims=True)
        for r in range(4):
            l_own[r : r + 1, :] = gain_grad[:, r * 128 : (r + 1) * 128]
            l_own[4 + r : 5 + r, :] = bias_grad[:, r * 128 : (r + 1) * 128]
        late_wides = "late wide", lambda: [(l_own, lw_buf.at[w], peer) for peer in wide_peers(at)]
        late_narrows = "late narrow", lambda: [
            (l_sum, ln_buf.at[n], peer) for peer in narrow_peers(at)
        ]
        lw_buf[w] = l_own[...]
        links.start(*late_wides)
        for rows, projected, normal, scale in kept:
            middle_buf[rows] += norm_back(projected, gain_one, normal, scale)
        write_patch.start()
        links.wait(*narrows)
        vec_out[...] = (vn_buf[0] + vn_buf[1]) + (vn_buf[2] + vn_buf[3])
        owner, rank = unit_ranks(owners)
        spots = []
        for q in range(4):
            for s in range(SLOTS):
                spot = jnp.int32(0)
                for u in range(UNITS):
                    position = 9 + u if u < 3 else DENSE_PLACE[u - 3]
                    spot = spot + jnp.where((owner[u] == q) & (rank[u] == s), position, 0)
                spots.append((q, s, jnp.minimum(spot, UNITS - 1)))

        def grads(part, columns):
            return ("grads", part), lambda: [
                (s_buf.at[peer[1], :, :, columns], r_buf.at[n, :, :, columns], peer)
                for peer in narrow_peers(at)
            ]

        def send_grads(part, columns):
            for q, s, spot in spots:
                s_buf[q, s, :, columns] = red[spot, :, columns]
            links.start(*grads(part, columns))
            r_buf[n, :, :, columns] = s_buf[n, :, :, columns]

        others, last = slice(128, 512), slice(0, 128)
        chunk_end(1)
        send_grads(0, others)
        links.wait(*text_parts)
        text_out[...] = jnp.sum(text_sum[...].astype(F32), axis=0)
        chunk_end(0)
        send_grads(1, last)
        links.wait(*late_wides)
        total = lw_buf[0]
        for k in range(1, 8):
            total = total + lw_buf[k]
        l_sum[...] = total
        ln_buf[n] = total
        links.start(*late_narrows)
        links.wait(*grads(0, others))
        links.wait(*grads(1, last))
        for q in range(4):
            slot_grad[:, q * 16 : (q + 1) * 16, :] = r_buf[q]
        write_layer.wait()
        write_patch.wait()
        links.wait(*late_narrows)
        vec_out[0:8, :] = (ln_buf[0] + ln_buf[1]) + (ln_buf[2] + ln_buf[3])


def block(owners, counts, masters, text, x, vec, g):
    hbm = pl.BlockSpec(memory_space=pl.ANY)
    copies = 6 + 7 + 16 + 24 + 3 * 8 + 2 * 8 + 2 * 16 + 7 + 3 + 7 + 7 + 3 + 6
    bf = lambda *s: pltpu.VMEM(s, BF16)
    f32 = lambda *s: pltpu.VMEM(s, F32)
    rows = VEC // 128
    return pl.pallas_call(
        block_kernel,
        in_specs=[smem(), smem(), vmem(), vmem(), vmem(), vmem(), hbm],
        out_specs=[hbm, hbm, hbm, vmem(), vmem(), vmem()],
        out_shape=[
            jax.ShapeDtypeStruct((ROWS, D), F32),
            jax.ShapeDtypeStruct((ROWS, D), BF16),
            jax.ShapeDtypeStruct((HEADS - 1, KEYS, ROWS), BF16),
            jax.ShapeDtypeStruct((SLOTS, 64, D), BF16),
            jax.ShapeDtypeStruct((64, TEXT), F32),
            jax.ShapeDtypeStruct((rows, 128), F32),
        ],
        scratch_shapes=[
            bf(SLOTS, 4, 16, D),
            bf(4, SLOTS, 16, D // 2),
            bf(4, SLOTS, 16, D // 2),
            bf(3, *PIECES, D),
            bf(9, *PIECES, D),
            bf(4, 2, 64, TEXT),
            bf(D, ROWS),
            bf(4, KEYS, 128),
            bf(KEYS, 128),
            bf(D, KEYS),
            bf(D, KEYS),
            bf(TEXT, D),
            bf(D, ROWS),
            f32(HEADS, 1, ROWS),
            f32(HEADS, 1, ROWS),
            bf(2, KEYS, ROWS),
            bf(ROWS, D),
            f32(ROWS, D),
            bf(9, *PIECES, D),
            bf(9, 4, 2, 2, 16, D),
            bf(9, 2, 2, 16, D),
            bf(9, 2, 2, 16, D),
            bf(9, 2, 16, D),
            bf(9, 2, 16, D),
            bf(9, 4, 16, D),
            bf(3, 9, 16, D),
            bf(4, 3, *PIECES, 128),
            bf(4, 3, 4, 2, 2, 16, 128),
            bf(2, 16, 3, 16, 128),
            bf(2, 3, 2, 2, 16, 128),
            bf(2, 3, 2, 2, 16, 128),
            bf(2, 3, 2, 16, 128),
            bf(2, 3, 2, 16, 128),
            bf(2, 3, 4, 16, 128),
            bf(3, 2, 3, 16, 128),
            bf(UNITS, 16, D),
            bf(4, SLOTS, 16, D),
            bf(4, SLOTS, 16, D),
            bf(8, 64, TEXT),
            bf(8, 64, TEXT),
            f32(rows, 128),
            f32(8, rows, 128),
            f32(rows, 128),
            f32(4, rows, 128),
            f32(8, 128),
            f32(8, 8, 128),
            f32(8, 128),
            f32(4, 8, 128),
            bf(D, ROWS),
            bf(D, KEYS),
            bf(D, KEYS),
            bf(KEYS, 128),
            bf(128, KEYS),
            pltpu.SemaphoreType.DMA((copies,)),
            pltpu.SemaphoreType.DMA((copies,)),
            pltpu.SemaphoreType.DMA((5,)),
        ],
        compiler_params=pltpu.CompilerParams(
            collective_id=1, has_side_effects=True, vmem_limit_bytes=63 * 2**20
        ),
    )(owners, counts, masters, text, x, vec, g)


def gather(owners, masters, text_t):
    packed = lax.all_gather(masters.astype(BF16), "wide", axis=2, tiled=True)
    packed = lax.all_gather(packed, "narrow", axis=0, tiled=True)
    same = owners[:, None] == owners[None, :]
    ids = jnp.arange(UNITS)
    rank = jnp.sum((same & (ids[None, :] < ids[:, None])).astype(jnp.int32), axis=1)
    units = jnp.take(packed.reshape(-1, D, D), owners * SLOTS + rank, axis=0)
    rows = lax.all_gather(text_t, "wide", axis=1, tiled=True)[0]
    return units, jnp.pad(rows, ((0, 0), (0, TEXT - LANG)))


def live_column(counts, rows):
    index = lax.broadcasted_iota(jnp.int32, (VIEW_ROWS, 1), 0)
    return [(index < counts[0, v]) for v in range(rows // VIEW_ROWS)]


def forward_kernel(
    counts, x, text_t, vec, w, att_t, probs, inverse, q_t, keyed, v_t, normed, text_normed
):
    i = pl.program_id(0)

    @pl.when(i == 0)
    def _():
        gain, bias = vec_row(vec, 0, D), vec_row(vec, D, D)
        normed[...] = (normalize(x[...].astype(F32))[0] * gain + bias).astype(BF16)
        rows = text_t[...].astype(F32).T
        live_text = lax.broadcasted_iota(jnp.int32, (TEXT, 1), 0) < LANG
        text_normed[...] = jnp.where(
            live_text, normalize(rows)[0] * gain + bias, 0.0
        ).astype(BF16)
        q_t[...] = dot(w[0], normed[...], 0, 1).astype(BF16) * BF16(0.125)
        v_t[:, 0:ROWS] = dot(w[2], normed[...], 0, 1).astype(BF16)
        v_t[:, ROWS:KEYS] = dot(w[2], text_normed[...], 0, 1).astype(BF16)
        for p in range(4):
            pair = slice(p * 128, (p + 1) * 128)
            keyed[p, 0:ROWS, 0:128] = dot(normed[...], w[1, :, pair]).astype(BF16)
            keyed[p, ROWS:KEYS, 0:128] = dot(text_normed[...], w[1, :, pair]).astype(BF16)
            for v, live in enumerate(live_column(counts, ROWS)):
                keyed[p, v * VIEW_ROWS : (v + 1) * VIEW_ROWS, 128:256] = jnp.broadcast_to(
                    jnp.where(live, 0.0, NEG), (VIEW_ROWS, 128)
                ).astype(BF16)
            keyed[p, ROWS:KEYS, 128:256] = jnp.broadcast_to(
                jnp.where(live_text, 0.0, NEG), (TEXT, 128)
            ).astype(BF16)

    row = lax.broadcasted_iota(jnp.int32, (128, ROWS), 0)
    one = jnp.where(row == 0, 1.0, 0.0).astype(BF16)
    pair_q = q_t[pl.ds(pl.multiple_of(i * 128, 128), 128), :]
    for h in range(2):
        mine = (row >= 64 * h) & (row < 64 * h + 64)
        q = jnp.where(mine, pair_q, jnp.zeros_like(pair_q))
        scores = dot(keyed[i], jnp.concatenate([q, one], axis=0))
        peak = jnp.max(scores, axis=0, keepdims=True)
        e = jnp.exp(scores - peak)
        total = jnp.sum(e, axis=0, keepdims=True)
        low = e.astype(BF16)
        probs[h] = low
        mixed = dot(v_t[pl.ds(pl.multiple_of(i * 128 + h * 64, 64), 64), :], low)
        inv = 1.0 / total
        att_t[h * 64 : (h + 1) * 64, :] = (mixed * inv).astype(BF16)
        inverse[0, h : h + 1, :] = inv


def attention_forward(counts, x, text_t, vec, units):
    return pl.pallas_call(
        forward_kernel,
        grid=(4,),
        in_specs=[smem(), vmem(), vmem(), vmem(), pl.BlockSpec((3, D, D), lambda i: (0, 0, 0))],
        out_specs=[
            pl.BlockSpec((128, ROWS), lambda i: (i, 0)),
            pl.BlockSpec((2, KEYS, ROWS), lambda i: (i, 0, 0)),
            pl.BlockSpec((1, 2, ROWS), lambda i: (i, 0, 0)),
            pl.BlockSpec((D, ROWS), lambda i: (0, 0)),
            pl.BlockSpec((4, KEYS, 256), lambda i: (0, 0, 0)),
            pl.BlockSpec((D, KEYS), lambda i: (0, 0)),
        ],
        out_shape=[
            jax.ShapeDtypeStruct((D, ROWS), BF16),
            jax.ShapeDtypeStruct((HEADS, KEYS, ROWS), BF16),
            jax.ShapeDtypeStruct((4, 2, ROWS), F32),
            jax.ShapeDtypeStruct((D, ROWS), BF16),
            jax.ShapeDtypeStruct((4, KEYS, 256), BF16),
            jax.ShapeDtypeStruct((D, KEYS), BF16),
        ],
        scratch_shapes=[pltpu.VMEM((ROWS, D), BF16), pltpu.VMEM((TEXT, D), BF16)],
        compiler_params=pltpu.CompilerParams(vmem_limit_bytes=VMEM_LIMIT),
    )(counts, x, text_t, vec, units)


def dense_kernel(
    counts, att_t, x, g, vec, w,
    layer_out, middle_back, back_t, grads, gain_grad, bias_grad, up_grad, down_grad,
    total, *, tile
):
    i = pl.program_id(0)
    steps = pl.num_programs(0)
    gain, bias = vec_row(vec, 2 * D, D), vec_row(vec, 3 * D, D)
    a = att_t[...]
    index = lax.broadcasted_iota(jnp.int32, (tile, 1), 0) + i * tile
    live = jnp.zeros((tile, 1), jnp.bool_)
    for v in range(VIEWS):
        live = live | ((index >= v * VIEW_ROWS) & (index < v * VIEW_ROWS + counts[0, v]))
    middle = x[...].astype(F32) + dot(a, w[0], 0, 0)
    normed, scale = normalize(middle)
    low = (normed * gain + bias).astype(BF16)
    out_back = jnp.where(live, g[...].astype(F32), 0.0)
    out_low = out_back.astype(BF16)

    @pl.when(i == 0)
    def _():
        total[...] = jnp.zeros_like(total)
        gain_grad[...] = jnp.zeros_like(gain_grad)
        bias_grad[...] = jnp.zeros_like(bias_grad)
        up_grad[...] = jnp.zeros_like(up_grad)
        down_grad[...] = jnp.zeros_like(down_grad)

    out = middle + vec_row(vec, 4 * D + FF, D)
    normed_back = jnp.zeros((tile, D), F32)
    for j in range(4):
        block = slice(j * D, (j + 1) * D)
        preact = dot(low, w[1 + j]) + vec_row(vec, 4 * D + j * D, D)
        phi = 0.5 + 0.5 * lax.erf(preact * 0.7071067811865476)
        active = (preact * phi).astype(BF16)
        slope = phi + preact * (jnp.exp(-0.5 * preact * preact) * 0.3989422804014327)
        out = out + dot(active, w[5 + j])
        preact_back = (dot(out_low, w[5 + j], 1, 1) * slope).astype(BF16)
        normed_back = normed_back + dot(preact_back, w[1 + j], 1, 1)
        total[1 + j] += dot(low, preact_back, 0, 0)
        total[5 + j] += dot(active, out_low, 0, 0)
        up_grad[:, block] += jnp.sum(preact_back.astype(F32), axis=0, keepdims=True)
    layer_out[...] = jnp.where(live, out, 0.0).astype(BF16)
    back = out_back + norm_back(normed_back, gain, normed, scale)
    middle_back[...] = back
    branch = back.astype(BF16)
    back_t[...] = dot(w[0], branch, 1, 1).astype(BF16)
    total[0] += dot(a, branch)
    gain_grad[...] += jnp.sum(normed_back * normed, axis=0, keepdims=True)
    bias_grad[...] += jnp.sum(normed_back, axis=0, keepdims=True)
    down_grad[...] += jnp.sum(out_back, axis=0, keepdims=True)

    @pl.when(i == steps - 1)
    def _():
        grads[...] = total[...].astype(BF16)


def dense(counts, att_t, x, g, vec, units, tile=640):
    rows = pl.BlockSpec((tile, D), lambda i: (i, 0))
    columns = pl.BlockSpec((D, tile), lambda i: (0, i))
    return pl.pallas_call(
        functools.partial(dense_kernel, tile=tile),
        grid=(ROWS // tile,),
        in_specs=[smem(), columns, rows, rows, vmem(), vmem()],
        out_specs=[
            rows,
            rows,
            columns,
            pl.BlockSpec((9, D, D), lambda i: (0, 0, 0)),
            pl.BlockSpec((1, D), lambda i: (0, 0)),
            pl.BlockSpec((1, D), lambda i: (0, 0)),
            pl.BlockSpec((1, FF), lambda i: (0, 0)),
            pl.BlockSpec((1, D), lambda i: (0, 0)),
        ],
        out_shape=[
            jax.ShapeDtypeStruct((ROWS, D), BF16),
            jax.ShapeDtypeStruct((ROWS, D), F32),
            jax.ShapeDtypeStruct((D, ROWS), BF16),
            jax.ShapeDtypeStruct((9, D, D), BF16),
            jax.ShapeDtypeStruct((1, D), F32),
            jax.ShapeDtypeStruct((1, D), F32),
            jax.ShapeDtypeStruct((1, FF), F32),
            jax.ShapeDtypeStruct((1, D), F32),
        ],
        scratch_shapes=[pltpu.VMEM((9, D, D), F32)],
        compiler_params=pltpu.CompilerParams(vmem_limit_bytes=VMEM_LIMIT),
    )(counts, att_t, x, g, vec, units)


def backward_kernel(probs, inverse, keyed, v_t, back_t, q_t, att_t, query_back, key_back, value_back):
    row = lax.broadcasted_iota(jnp.int32, (128, ROWS), 0)
    lane = lax.broadcasted_iota(jnp.int32, (KEYS, 128), 1)
    ones = jnp.where(lane < 2, 1.0, 0.0).astype(BF16)
    value = jnp.concatenate([v_t[...].astype(F32).T.astype(BF16), ones], axis=1)
    key_t = keyed[:, 0:128].astype(F32).T.astype(BF16)
    back = back_t[...].astype(F32)
    product = back * att_t[...].astype(F32)
    query = q_t[...].astype(F32)
    key_total = jnp.zeros((KEYS, 128), F32)
    value_total = jnp.zeros((KEYS, 128), F32)
    for h in range(2):
        half = slice(h * 64, (h + 1) * 64)
        inv = inverse[0, h : h + 1, :]
        delta = jnp.sum(product[half], axis=0, keepdims=True) * inv
        high = delta.astype(BF16).astype(F32)
        mine = (row >= 64 * h) & (row < 64 * h + 64)
        scaled = jnp.where(mine, back * inv, 0.0)
        tail = jnp.where(row == 0, -high, jnp.where(row == 1, high - delta, 0.0))
        right = jnp.concatenate([scaled.astype(BF16), tail.astype(BF16)], axis=0)
        low = probs[h]
        score_back = low * dot(value, right).astype(BF16)
        query_back[half, :] = (dot(key_t[half], score_back) * 0.125).astype(BF16)
        key_total += dot(score_back, jnp.where(mine, query, 0.0).T.astype(BF16))
        value_total += dot(low, scaled.T.astype(BF16))
    key_back[...] = key_total.astype(BF16)
    value_back[...] = value_total.astype(BF16)


def attention_backward(probs, inverse, keyed, v_t, back_t, q_t, att_t):
    return pl.pallas_call(
        backward_kernel,
        grid=(4,),
        in_specs=[
            pl.BlockSpec((2, KEYS, ROWS), lambda i: (i, 0, 0)),
            pl.BlockSpec((1, 2, ROWS), lambda i: (i, 0, 0)),
            pl.BlockSpec((None, KEYS, 256), lambda i: (i, 0, 0)),
            pl.BlockSpec((128, KEYS), lambda i: (i, 0)),
            pl.BlockSpec((128, ROWS), lambda i: (i, 0)),
            pl.BlockSpec((128, ROWS), lambda i: (i, 0)),
            pl.BlockSpec((128, ROWS), lambda i: (i, 0)),
        ],
        out_specs=[
            pl.BlockSpec((128, ROWS), lambda i: (i, 0)),
            pl.BlockSpec((KEYS, 128), lambda i: (0, i)),
            pl.BlockSpec((KEYS, 128), lambda i: (0, i)),
        ],
        out_shape=[
            jax.ShapeDtypeStruct((D, ROWS), BF16),
            jax.ShapeDtypeStruct((KEYS, D), BF16),
            jax.ShapeDtypeStruct((KEYS, D), BF16),
        ],
        compiler_params=pltpu.CompilerParams(vmem_limit_bytes=VMEM_LIMIT),
    )(probs, inverse, keyed, v_t, back_t, q_t, att_t)


def project_kernel(
    x, text_t, vec, w, middle_back, query_back, key_back, value_back, text_key, text_value,
    patch_grad, grads, gain_grad, bias_grad, text_grad_t, total
):
    i = pl.program_id(0)
    steps = pl.num_programs(0)
    gain, bias = vec_row(vec, 0, D), vec_row(vec, D, D)

    @pl.when(i == 0)
    def _():
        live = lax.broadcasted_iota(jnp.int32, (TEXT, 1), 0) < LANG
        normed, scale = normalize(text_t[...].astype(F32).T)
        low_t = jnp.where(live, normed * gain + bias, 0.0).T.astype(BF16)
        k, v = text_key[...], text_value[...]
        back = dot(k, w[1], 1, 1) + dot(v, w[2], 1, 1)
        text_grad_t[...] = norm_back(back, gain, normed, scale).T.astype(BF16)
        gain_grad[...] = jnp.sum(back * normed, axis=0, keepdims=True)
        bias_grad[...] = jnp.sum(back, axis=0, keepdims=True)
        total[0] = jnp.zeros((D, D), F32)
        total[1] = dot(low_t, k)
        total[2] = dot(low_t, v)

    normed, scale = normalize(x[...].astype(F32))
    low_t = (normed * gain + bias).T.astype(BF16)
    q, k, v = query_back[...], key_back[...], value_back[...]
    back = dot(q, w[0], 0, 1) + dot(k, w[1], 1, 1) + dot(v, w[2], 1, 1)
    patch_grad[...] = middle_back[...] + norm_back(back, gain, normed, scale)
    total[0] += dot(low_t, q, 1, 1)
    total[1] += dot(low_t, k)
    total[2] += dot(low_t, v)
    gain_grad[...] += jnp.sum(back * normed, axis=0, keepdims=True)
    bias_grad[...] += jnp.sum(back, axis=0, keepdims=True)

    @pl.when(i == steps - 1)
    def _():
        grads[...] = total[...].astype(BF16)


def project_back(x, text_t, vec, units, middle_back, query_back, key_back, value_back, tile=640):
    rows = pl.BlockSpec((tile, D), lambda i: (i, 0))
    text_rows = pl.BlockSpec((TEXT, D), lambda i: (ROWS // TEXT, 0))
    return pl.pallas_call(
        project_kernel,
        grid=(ROWS // tile,),
        in_specs=[
            rows,
            vmem(),
            vmem(),
            pl.BlockSpec((3, D, D), lambda i: (0, 0, 0)),
            rows,
            pl.BlockSpec((D, tile), lambda i: (0, i)),
            rows,
            rows,
            text_rows,
            text_rows,
        ],
        out_specs=[
            rows,
            pl.BlockSpec((3, D, D), lambda i: (0, 0, 0)),
            pl.BlockSpec((1, D), lambda i: (0, 0)),
            pl.BlockSpec((1, D), lambda i: (0, 0)),
            pl.BlockSpec((D, TEXT), lambda i: (0, 0)),
        ],
        out_shape=[
            jax.ShapeDtypeStruct((ROWS, D), F32),
            jax.ShapeDtypeStruct((3, D, D), BF16),
            jax.ShapeDtypeStruct((1, D), F32),
            jax.ShapeDtypeStruct((1, D), F32),
            jax.ShapeDtypeStruct((D, TEXT), BF16),
        ],
        scratch_shapes=[pltpu.VMEM((3, D, D), F32)],
        compiler_params=pltpu.CompilerParams(vmem_limit_bytes=VMEM_LIMIT),
    )(
        x, text_t, vec, units, middle_back, query_back, key_back, value_back, key_back, value_back
    )


def reduce_all(owners, rest, first, text, vecs):
    vec = lax.psum(jnp.concatenate(vecs, axis=1), ("wide", "narrow"))
    text_sum = lax.psum_scatter(text.astype(F32), "wide", scatter_dimension=0, tiled=True)
    all_units = jnp.concatenate([first, rest], axis=0).astype(F32)
    rows = lax.psum_scatter(all_units, "wide", scatter_dimension=1, tiled=True)
    same = owners[:, None] == owners[None, :]
    ids = jnp.arange(UNITS)
    rank = jnp.sum((same & (ids[None, :] < ids[:, None])).astype(jnp.int32), axis=1)
    pick = (owners[None, None, :] == jnp.arange(lax.axis_size("narrow"))[:, None, None]) & (
        rank[None, None, :] == jnp.arange(SLOTS)[None, :, None]
    )
    terms = jnp.einsum("nsu,urc->nsrc", pick.astype(F32), rows, precision=lax.Precision.HIGHEST)
    slots = lax.psum_scatter(terms, "narrow", scatter_dimension=0, tiled=True)
    return slots[0], text_sum, vec.reshape(VEC // 128, 128)


def adam(master, moment_one, moment_two, averaged, gradient, rate):
    moment_one = beta_one * moment_one + (1.0 - beta_one) * gradient
    moment_two = beta_two * moment_two + (1.0 - beta_two) * gradient * gradient
    mean_hat = moment_one / (1.0 - beta_one**STEP)
    second_hat = moment_two / (1.0 - beta_two**STEP)
    master = master - rate * (
        mean_hat / (jnp.sqrt(second_hat) + adam_eps) + weight_decay * master
    )
    averaged = average_keep * averaged + (1.0 - average_keep) * master
    return master, moment_one, moment_two, averaged


def unit_rates():
    blocks = FF // D
    fans = [2 * D // 3, 2 * D // 3, D, D // 64] + [D] * blocks + [FF] * blocks
    return [float(fan) ** -0.5 for fan in fans]


def update_kernel(
    owners, grad, masters, first, second, average, text_t, vec_grad, vec, vec_first, vec_second,
    vec_average, patch_in, layer_in,
    new_masters, new_first, new_second, new_average, new_copies, text_grad,
    vec_new_value, vec_new_first, vec_new_second, vec_new_average, patch_out, layer_out,
):
    s = pl.program_id(0)
    patch_out[...] = patch_in[...]
    layer_out[...] = layer_in[...]
    n = lax.axis_index("narrow")
    owner, rank = unit_ranks(owners)
    rate, filled = jnp.float32(0.0), jnp.int32(0)
    for u, value in enumerate(unit_rates()):
        match = (owner[u] == n) & (rank[u] == s)
        rate = rate + jnp.where(match, jnp.float32(value), jnp.float32(0.0))
        filled = filled + match.astype(jnp.int32)
    state = adam(masters[0, 0], first[0, 0], second[0, 0], average[0, 0], grad[0].astype(F32), rate)
    keep = jnp.broadcast_to(filled, state[0].shape) > 0
    state = [jnp.where(keep, part, 0.0) for part in state]
    for ref, part in zip((new_masters, new_first, new_second, new_average), state):
        ref[0, 0] = part
    new_copies[0, 0] = state[0].astype(BF16)

    @pl.when(s == 0)
    def _():
        text_grad[0] = text_t[:, 0:LANG]
        state = adam(
            vec[...], vec_first[...], vec_second[...], vec_average[...], vec_grad[...], vector_rate
        )
        for ref, part in zip(
            (vec_new_value, vec_new_first, vec_new_second, vec_new_average), state
        ):
            ref[...] = part


def update(
    owners, grad, masters, first, second, average, text_t, vec_grad, vec, v1, v2, va, patch, layer
):
    rows = masters.shape[2]
    state = jax.ShapeDtypeStruct(masters.shape, F32)
    vector = jax.ShapeDtypeStruct(vec.shape, F32)
    slot = pl.BlockSpec((1, 1, rows, D), lambda s: (0, s, 0, 0))
    vec_spec = pl.BlockSpec(vec.shape, lambda s: (0, 0))
    handed = pl.BlockSpec((ROWS // SLOTS, D), lambda s: (s, 0))
    return pl.pallas_call(
        update_kernel,
        grid=(SLOTS,),
        out_shape=[state] * 4
        + [
            jax.ShapeDtypeStruct(masters.shape, BF16),
            jax.ShapeDtypeStruct((1, text_t.shape[0], LANG), F32),
        ]
        + [vector] * 4
        + [jax.ShapeDtypeStruct(patch.shape, F32), jax.ShapeDtypeStruct(layer.shape, BF16)],
        in_specs=[smem(), pl.BlockSpec((1, rows, D), lambda s: (s, 0, 0))]
        + [slot] * 4
        + [pl.BlockSpec(text_t.shape, lambda s: (0, 0))]
        + [vec_spec] * 5
        + [handed] * 2,
        out_specs=[slot] * 5
        + [pl.BlockSpec((1, text_t.shape[0], LANG), lambda s: (0, 0, 0))]
        + [vec_spec] * 4
        + [handed] * 2,
        compiler_params=pltpu.CompilerParams(vmem_limit_bytes=VMEM_LIMIT),
    )(
        owners, grad, masters, first, second, average, text_t, vec_grad, vec, v1, v2, va, patch, layer
    )


def local(
    patches, text_tokens, view_counts, out_grad, owners, masters, first_moment, second_moment,
    average, vec_value, vec_first, vec_second, vec_average,
):
    vec, v1, v2, va = [
        part.reshape(VEC // 128, 128) for part in (vec_value, vec_first, vec_second, vec_average)
    ]
    text_in = jnp.swapaxes(text_tokens, 1, 2)
    if lax.axis_size("wide") == 8 and lax.axis_size("narrow") == 4:
        patch_grad, layer_out, _, slot_grad, text_sum, vec_grad = block(
            owners, view_counts, masters, text_in, patches, vec, out_grad
        )
    else:
        units, text_t = gather(owners, masters, text_in)
        att_t, probs, inverse, q_t, keyed, v_t = attention_forward(
            view_counts, patches, text_t, vec, units
        )
        layer_out, middle_back, back_t, rest, *vecs = dense(
            view_counts, att_t, patches, out_grad, vec, units[3:]
        )
        query_back, key_back, value_back = attention_backward(
            probs, inverse, keyed, v_t, back_t, q_t, att_t
        )
        patch_grad, first, gain_one, bias_one, text_part = project_back(
            patches, text_t, vec, units, middle_back, query_back, key_back, value_back
        )
        slot_grad, text_sum, vec_grad = reduce_all(
            owners, rest, first, text_part, (gain_one, bias_one, *vecs)
        )
    outs = update(
        owners, slot_grad, masters, first_moment, second_moment, average, text_sum, vec_grad, vec,
        v1, v2, va, patch_grad, layer_out,
    )
    new_masters, new_first, new_second, new_average, new_copies, text_grad = outs[:6]
    vectors = [part.reshape(VEC) for part in outs[6:10]]
    patch_grad, layer_out = outs[10:]
    return (
        layer_out, patch_grad, jnp.swapaxes(text_grad, 1, 2), new_masters, new_first, new_second,
        new_average, new_copies, *vectors,
    )


def solution(mesh):
    rows = P(("wide", "narrow"), None)
    state = P("narrow", None, "wide", None)
    text = P("narrow", None, "wide")
    in_specs = (rows, text, rows, rows, P(), state, state, state, state, P(), P(), P(), P())
    out_specs = (rows, rows, text, state, state, state, state, state, P(), P(), P(), P())
    return jax.shard_map(local, mesh=mesh, in_specs=in_specs, out_specs=out_specs, check_vma=False)
```

```python
import functools

import jax
import jax.numpy as jnp
from jax import lax
from jax.experimental import pallas as pl
from jax.experimental.pallas import tpu as pltpu
from jax.sharding import PartitionSpec as P

D = 512
HEADS = 8
FF = 2048
VIEWS = 5
VIEW_ROWS = 256
ROWS = VIEWS * VIEW_ROWS
LANG = 77
TEXT = 128
KEYS = ROWS + TEXT
STEP = 5
UNITS = 12
SLOTS = 4
VEC = 5 * D + FF
F32 = jnp.float32
BF16 = jnp.bfloat16
MESH = pl.DeviceIdType.MESH
NEG = -1e30

norm_eps = 1e-05
beta_one = 0.5
beta_two = 0.5
adam_eps = 1e-08
weight_decay = 0.1
average_keep = 0.75
vector_rate = 0.25
VMEM_LIMIT = 60 * 2**20


def dot(left, right, left_dim=1, right_dim=0):
    return lax.dot_general(
        left, right, (((left_dim,), (right_dim,)), ((), ())), preferred_element_type=F32
    )


def vmem():
    return pl.BlockSpec(memory_space=pltpu.VMEM)


def smem():
    return pl.BlockSpec(memory_space=pltpu.SMEM)


def vec_row(vec, start, size):
    first = start // 128
    return jnp.concatenate([vec[first + r : first + r + 1, :] for r in range(size // 128)], axis=1)


def unit_ranks(owners_ref):
    owner = [owners_ref[u] for u in range(UNITS)]
    rank = []
    for u in range(UNITS):
        total = jnp.int32(0)
        for v in range(u):
            total = total + (owner[v] == owner[u]).astype(jnp.int32)
        rank.append(jnp.minimum(total, SLOTS - 1))
    return owner, rank


def normalize(values):
    center = values - jnp.mean(values, axis=-1, keepdims=True)
    spread = jnp.mean(center * center, axis=-1, keepdims=True)
    scale = lax.rsqrt(spread + norm_eps)
    return center * scale, scale


def norm_back(grads, gain, normed, scale):
    e = grads * gain
    return scale * (
        e
        - jnp.mean(e, axis=-1, keepdims=True)
        - normed * jnp.mean(e * normed, axis=-1, keepdims=True)
    )


def place():
    w = lax.axis_index("wide")
    n = lax.axis_index("narrow")
    return w, n, w // 2, w % 2, n // 2, n % 2


def narrow_peers(at):
    w, n = at[:2]
    return [(w, lax.rem(n + k, 4)) for k in range(1, 4)]


def wide_peers(at):
    w, n = at[:2]
    return [(lax.rem(w + k, 8), n) for k in range(1, 8)]


def chip_peers(at):
    w, n, z, x, y, c = at
    peers = []
    for k in range(1, 16):
        chip = lax.rem(z * 4 + x * 2 + y + k, 16)
        cz, cx, cy = chip // 4, (chip // 2) % 2, chip % 2
        peers.append((cz, cx, cy, (cz * 2 + cx, cy * 2 + c)))
    return peers


def all_peers(at):
    w, n, z, x, y, c = at
    return narrow_peers(at) + wide_peers(at) + [
        (lax.rem(w + k, 8), (1 - y) * 2 + c) for k in range(1, 8)
    ]


def greet(peers):
    barrier = pltpu.get_barrier_semaphore()
    for peer in peers:
        pl.semaphore_signal(barrier, inc=1, device_id=peer, device_id_type=MESH)


def greeted(peers):
    pl.semaphore_wait(pltpu.get_barrier_semaphore(), len(peers))


class Links:
    def __init__(self, send, recv):
        self.send, self.recv, self.slots = send, recv, {}

    def copies(self, key, parts):
        made = []
        for k, (src, dst, device) in enumerate(parts()):
            slot = self.slots.setdefault((key, k), len(self.slots))
            made.append(
                pltpu.make_async_remote_copy(
                    src_ref=src,
                    dst_ref=dst,
                    send_sem=self.send.at[slot],
                    recv_sem=self.recv.at[slot],
                    device_id=device,
                    device_id_type=MESH,
                )
            )
        return made

    def start(self, key, parts):
        for copy in self.copies(key, parts):
            copy.start()

    def wait(self, key, parts):
        for copy in self.copies(key, parts):
            copy.wait()


def partners(w, n, z, x, y, c):
    to_z = [(lax.rem(z + k, 4) * 2 + x, n) for k in range(1, 4)]
    return to_z, (z * 2 + 1 - x, n), (w, (1 - y) * 2 + c), (w, y * 2 + 1 - c)


def spread(ref, head, stage, at, tail=()):
    w, n, z, x, y, c = at
    to_z, to_x, to_y, to_c = partners(*at)
    whole = slice(None)
    if stage == 0:
        parts = [((z, x, y, c), peer) for peer in to_z]
    elif stage == 1:
        parts = [((pl.ds(0, 2), x, y, c), to_x), ((pl.ds(2, 2), x, y, c), to_y)]
    elif stage == 2:
        parts = [((pl.ds(0, 2), whole, y, c), to_y), ((pl.ds(2, 2), x, whole, c), to_x)]
    else:
        parts = [((whole, whole, whole, c), to_c)]
    pieces = [(ref.at[(*head, *part, *tail)], peer) for part, peer in parts]
    return [(piece, piece, peer) for piece, peer in pieces]


def add(a, b):
    return a + b


class Reducer:
    def __init__(self, name, links, at, source, bufs, shift=None):
        self.name, self.links, self.at, self.source = name, links, at, source
        self.shift = shift or (lambda head: head)
        (self.c_buf, self.ya_buf, self.xb_buf, self.xa_buf, self.yb_buf, self.z_sum,
         self.z_buf) = bufs

    def start(self, stage, head):
        self.links.start(*self.copies(stage, head))

    def copies(self, stage, head):
        return (self.name, str(head), stage), lambda: self.parts(stage, head)

    def parts(self, stage, head):
        w, n, z, x, y, c = self.at
        to_z, to_x, to_y, to_c = partners(*self.at)
        whole, low, high = slice(None), pl.ds(0, 2), pl.ds(2, 2)
        source, buf = self.source, self.shift(head)
        if stage == 0:
            return [(source.at[(*head, whole, whole, whole, 1 - c)], self.c_buf.at[buf], to_c)]
        if stage == 1:
            return [
                (source.at[(*head, low, whole, 1 - y, c)], self.ya_buf.at[buf], to_y),
                (source.at[(*head, high, 1 - x, whole, c)], self.xb_buf.at[buf], to_x),
            ]
        if stage == 2:
            return [
                (source.at[(*head, low, 1 - x, y, c)], self.xa_buf.at[buf], to_x),
                (source.at[(*head, high, x, 1 - y, c)], self.yb_buf.at[buf], to_y),
            ]
        return [
            (self.z_sum.at[(*buf, lax.rem(z + k, 4))], self.z_buf.at[(k - 1, *buf)], to_z[k - 1])
            for k in range(1, 4)
        ]

    def finish(self, stage, head):
        w, n, z, x, y, c = self.at
        self.links.wait(*self.copies(stage, head))
        whole, low, high = slice(None), pl.ds(0, 2), pl.ds(2, 2)
        source, buf = self.source, self.shift(head)
        if stage == 0:
            own = (*head, whole, whole, whole, c)
            source[own] = add(source[own], self.c_buf[buf])
        elif stage == 1:
            a = (*head, low, whole, y, c)
            b = (*head, high, x, whole, c)
            source[a] = add(source[a], self.ya_buf[buf])
            source[b] = add(source[b], self.xb_buf[buf])
        elif stage == 2:
            self.z_sum[(*buf, low)] = add(source[(*head, low, x, y, c)], self.xa_buf[buf])
            self.z_sum[(*buf, high)] = add(source[(*head, high, x, y, c)], self.yb_buf[buf])
        else:
            total = self.z_sum[(*buf, z)].astype(F32)
            for k in range(3):
                total = total + self.z_buf[(k, *buf)].astype(F32)
            return total.astype(BF16)


PIECES = (4, 2, 2, 2, 16)
KEY_PARTS = ((0, 512), (512, 1024), (1024, 1408))
DENSE_PLACE = (8, 0, 2, 4, 6, 1, 3, 5, 7)


def block_kernel(
    owners, counts, masters, text, x, vec, g,
    patch_out, layer_out, probs, slot_grad, text_out, vec_out,
    send_buf, slot_0, slot_1, slot_2, slot_3, w_first, w_rest, text_buf, q_t, keyed, key_bias, v_t, normed_t,
    text_normed, att_t, inverse, delta, p_buf, g_buf, middle_buf,
    rest_all, c_buf, ya_buf, xb_buf, xa_buf, yb_buf, z_sum, z_buf,
    first_all, first_c, first_d, fa_buf, fb_buf, fc_buf, fd_buf, fz_sum, fz_buf, red, s_buf, r_buf, text_part, text_sum,
    v_own, vw_buf, v_sum, vn_buf, l_own, lw_buf, l_sum, ln_buf,
    query_back, key_back, value_back, value_pair, key_pair_t, send, recv, local
):
    at = place()
    w, n, z, sx, y, c = at
    links = Links(send, recv)
    whole = slice(None)
    peers = all_peers(at)
    gain_one, bias_one = vec_row(vec, 0, D), vec_row(vec, D, D)
    live_text = lax.broadcasted_iota(jnp.int32, (TEXT, 1), 0) < LANG
    read_g = pltpu.make_async_copy(g, g_buf, local.at[2])
    write_layer = pltpu.make_async_copy(g_buf, layer_out, local.at[3])
    write_patch = pltpu.make_async_copy(middle_buf, patch_out, local.at[4])

    greet(peers)
    send_buf[...] = masters[0].reshape(SLOTS, 4, 16, D).astype(BF16)
    text_buf[z, sx] = jnp.zeros((64, TEXT), BF16)
    text_buf[z, sx, :, 0:LANG] = text[0]
    greeted(peers)
    quarters = [slice(k * 128, (k + 1) * 128) for k in range(4)]
    slot_bufs = (slot_0, slot_1, slot_2, slot_3)

    def slots(k):
        return ("slots", k), lambda: [
            (send_buf.at[:, peer[1], :, quarters[k]], slot_bufs[k].at[n], peer)
            for peer in narrow_peers(at)
        ]

    for k in range(4):
        links.start(*slots(k))
    texts = "text", lambda: [
        (text_buf.at[z, sx], text_buf.at[z, sx], peer) for peer in wide_peers(at)
    ]
    links.start(*texts)
    for k in range(4):
        slot_bufs[k][n] = send_buf[:, n, :, quarters[k]]
    low = (normalize(x[...].astype(F32))[0] * gain_one + bias_one).astype(BF16)
    normed = g_buf
    normed[...] = low
    normed_t[:, 0:ROWS] = low.astype(F32).T.astype(BF16)
    owner, rank = unit_ranks(owners)
    def first(k, s):
        tail = (slice(None), quarters[k])
        return ("first", k, s), lambda: spread(w_first, (slice(None),), s, at, tail)

    for k in range(4):
        links.wait(*slots(k))
        for u in range(3):
            w_first[u, z, sx, y, c, :, quarters[k]] = slot_bufs[k][owner[u], rank[u]]
        links.start(*first(k, 0))

    def rest(group, s):
        return ("rest", group, s), lambda: spread(w_rest, (pl.ds(3 * group, 3),), s, at)

    for k, position in enumerate(DENSE_PLACE):
        for part in range(4):
            w_rest[position, z, sx, y, c, :, quarters[part]] = slot_bufs[part][
                owner[3 + k], rank[3 + k]
            ]
    for v, live in enumerate(live_column(counts, ROWS)):
        key_bias[v * VIEW_ROWS : (v + 1) * VIEW_ROWS, :] = jnp.broadcast_to(
            jnp.where(live, 0.0, NEG), (VIEW_ROWS, 128)
        ).astype(BF16)
    key_bias[ROWS:KEYS, :] = jnp.broadcast_to(
        jnp.where(live_text, 0.0, NEG), (TEXT, 128)
    ).astype(BF16)
    def read_text():
        links.wait(*texts)
        rows = text_buf[...].reshape(D, TEXT).astype(F32).T
        text_low = jnp.where(live_text, normalize(rows)[0] * gain_one + bias_one, 0.0)
        text_normed[...] = text_low.astype(BF16)
        normed_t[:, ROWS:KEYS] = text_low.T.astype(BF16)

    def unit(u):
        return w_first[u].reshape(D, D)

    def project(k):
        w_q, w_k, w_v = [w_first[u, :, :, :, :, :, quarters[k]].reshape(D, 128) for u in range(3)]
        keyed[k, 0:ROWS] = dot(normed[...], w_k).astype(BF16)
        keyed[k, ROWS:KEYS] = dot(text_normed[...], w_k).astype(BF16)
        q_t[quarters[k], :] = dot(w_q, normed[...], 0, 1).astype(BF16) * BF16(0.125)
        v_t[quarters[k], 0:ROWS] = dot(w_v, normed[...], 0, 1).astype(BF16)
        v_t[quarters[k], ROWS:KEYS] = dot(w_v, text_normed[...], 0, 1).astype(BF16)

    def step_first(k, s):
        links.wait(*first(k, s))
        if s < 3:
            links.start(*first(k, s + 1))
        else:
            project(k)

    step_first(0, 0)
    step_first(1, 0)
    step_first(0, 1)
    step_first(2, 0)
    step_first(3, 0)
    links.start(*rest(2, 0))
    read_text()
    step_first(0, 2)
    step_first(1, 1)
    links.start(*rest(1, 0))
    step_first(0, 3)
    links.start(*rest(0, 0))

    gather_plan = {
        0: [(2, 0)], 1: [(1, 0)], 2: [(2, 1)], 3: [(0, 0)], 4: [(2, 2), (1, 1)], 5: [],
        6: [(0, 1), (1, 2)], 7: [(2, 3)],
    }

    def gather_point(t):
        for group, s in gather_plan[t]:
            links.wait(*rest(group, s))
            if s < 3:
                links.start(*rest(group, s + 1))

    row = lax.broadcasted_iota(jnp.int32, (128, ROWS), 0)
    one = jnp.where(row == 0, 1.0, 0.0).astype(BF16)

    def saved(t):
        return pltpu.make_async_copy(p_buf.at[t % 2], probs.at[t], local.at[t % 2])

    first_plan = {
        0: [(1, 2), (2, 1)], 1: [(1, 3), (2, 2), (3, 1)], 2: [(3, 2)], 3: [(2, 3)], 4: [(3, 3)]
    }

    def first_point(t):
        for k, s in first_plan[t]:
            step_first(k, s)
        if t == 4:
            read_g.start()

    def mix(t):
        head = pl.ds(pl.multiple_of(t * 64, 64), 64)
        summed = jnp.concatenate([v_t[head, :], jnp.ones((16, KEYS), BF16)], axis=0)
        mixed = dot(summed, p_buf[t % 2])
        inv = 1.0 / mixed[64:65]
        att_t[head, :] = (mixed[0:64] * inv).astype(BF16)
        inverse[t] = inv

    @pl.loop(0, HEADS)
    def _(t):
        for k in range(HEADS):
            pl.when(t == k)(functools.partial(gather_point, k))
        for k in first_plan:
            pl.when(t == k)(functools.partial(first_point, k))
        pl.when(t > 1)(lambda: saved(t - 2).wait())
        pl.when(t > 0)(lambda: mix(t - 1))
        i, h = t // 2, t % 2
        pair_q = q_t[pl.ds(pl.multiple_of(i * 128, 128), 128), :]
        mine = (row >= 64 * h) & (row < 64 * h + 64)
        q = jnp.where(mine, pair_q, jnp.zeros_like(pair_q))
        keys = jnp.concatenate([keyed[i], key_bias[...]], axis=1)
        scores = dot(keys, jnp.concatenate([q, one], axis=0))
        peak = jnp.max(scores, axis=0, keepdims=True)
        for first_key, end_key in KEY_PARTS:
            p_buf[h, first_key:end_key] = jnp.exp(scores[first_key:end_key] - peak).astype(BF16)
        pl.when(t < HEADS - 1)(lambda: saved(t).start())

    mix(HEADS - 1)
    read_g.wait()
    saved(HEADS - 2).wait()

    def fetched(t):
        return pltpu.make_async_copy(probs.at[t], p_buf.at[t % 2], local.at[t % 2])

    reducer = Reducer(
        "reduce", links, at, rest_all, (c_buf, ya_buf, xb_buf, xa_buf, yb_buf, z_sum, z_buf)
    )
    dense_order = (3, 2, 1, 0)
    groups = [(pl.ds(4, 4),), (pl.ds(0, 4),), (pl.ds(8, 1),)]

    def step_rest(group, stage):
        total = reducer.finish(stage, groups[group])
        if stage < 3:
            reducer.start(stage + 1, groups[group])
        else:
            red[groups[group]] = total

    def dense_unit(position):
        return w_rest[position].reshape(D, D)

    @pl.when(w >= 0)
    def _():
        gain, bias = vec_row(vec, 2 * D, D), vec_row(vec, 3 * D, D)
        tiles = [slice(k * ROWS // 2, (k + 1) * ROWS // 2) for k in range(2)]
        lows, outs = p_buf.at[0, :, 0:D], p_buf.at[0, :, D : 2 * D]
        normals, scales, backs, lives = [], [], [], []
        for k, rows in enumerate(tiles):
            index = lax.broadcasted_iota(jnp.int32, (ROWS // 2, 1), 0) + k * (ROWS // 2)
            live = jnp.zeros((ROWS // 2, 1), jnp.bool_)
            for v in range(VIEWS):
                live = live | ((index >= v * VIEW_ROWS) & (index < v * VIEW_ROWS + counts[0, v]))
            middle = x[rows].astype(F32) + dot(att_t[:, rows], dense_unit(8), 0, 0)
            normal, scale = normalize(middle)
            middle_buf[rows] = middle + vec_row(vec, 4 * D + FF, D)
            normals.append(normal)
            scales.append(scale)
            lows[rows] = (normal * gain + bias).astype(BF16)
            backs.append(jnp.zeros((ROWS // 2, D), F32))
            lives.append(live)
            outs[rows] = jnp.where(live, g_buf[rows].astype(F32), 0.0).astype(BF16)
        for turn, j in enumerate(dense_order):
            if turn == 1:
                links.wait(*rest(0, 2))
                links.start(*rest(0, 3))
                links.wait(*rest(1, 3))
            if turn == 2:
                links.wait(*rest(0, 3))
            w_up, w_down = dense_unit(2 * j), dense_unit(2 * j + 1)
            up_total, down_total, up_grad = 0.0, 0.0, 0.0
            for k, rows in enumerate(tiles):
                preact = dot(lows[rows], w_up) + vec_row(vec, 4 * D + j * D, D)
                phi = 0.5 + 0.5 * lax.erf(preact * 0.7071067811865476)
                active = (preact * phi).astype(BF16)
                slope = phi + preact * (jnp.exp(-0.5 * preact * preact) * 0.3989422804014327)
                middle_buf[rows] += dot(active, w_down)
                preact_back = (dot(outs[rows], w_down, 1, 1) * slope).astype(BF16)
                backs[k] = backs[k] + dot(preact_back, w_up, 1, 1)
                up_total = up_total + dot(lows[rows], preact_back, 0, 0)
                down_total = down_total + dot(active, outs[rows], 0, 0)
                up_grad = up_grad + jnp.sum(preact_back.astype(F32), axis=0, keepdims=True)
            rest_all[2 * j] = up_total.astype(BF16).reshape(*PIECES, D)
            rest_all[2 * j + 1] = down_total.astype(BF16).reshape(*PIECES, D)
            for r in range(4):
                v_own[16 + 4 * j + r : 17 + 4 * j + r, :] = up_grad[:, r * 128 : (r + 1) * 128]
            if turn == 1:
                reducer.start(0, groups[0])
            if turn > 1:
                step_rest(0, turn - 2)
            if turn == 3:
                reducer.start(0, groups[1])
        for k, rows in enumerate(tiles):
            g_buf[rows] = jnp.where(lives[k], middle_buf[rows], 0.0).astype(BF16)
        write_layer.start()
        out_total, gain_grad, bias_grad, down_grad = 0.0, 0.0, 0.0, 0.0
        for k, rows in enumerate(tiles):
            out_back = outs[rows].astype(F32)
            back = out_back + norm_back(backs[k], gain, normals[k], scales[k])
            middle_buf[rows] = back
            branch = back.astype(BF16)
            out_total = out_total + dot(att_t[:, rows], branch)
            back_rows = dot(dense_unit(8), branch, 1, 1).astype(BF16)
            product = back_rows.astype(F32) * att_t[:, rows].astype(F32)
            for h in range(HEADS):
                part = jnp.sum(product[h * 64 : (h + 1) * 64], axis=0, keepdims=True)
                delta[h, :, rows] = part * inverse[h, :, rows]
            att_t[:, rows] = back_rows
            gain_grad = gain_grad + jnp.sum(backs[k] * normals[k], axis=0, keepdims=True)
            bias_grad = bias_grad + jnp.sum(backs[k], axis=0, keepdims=True)
            down_grad = down_grad + jnp.sum(out_back, axis=0, keepdims=True)
        rest_all[8] = out_total.astype(BF16).reshape(*PIECES, D)
        for offset, piece in ((8, gain_grad), (12, bias_grad), (32, down_grad)):
            for r in range(4):
                v_own[offset + r : offset + r + 1, :] = piece[:, r * 128 : (r + 1) * 128]
        v_own[0:8, :] = jnp.zeros((8, 128), F32)

    fetched(HEADS - 2).start()
    back_t = att_t

    def chunk_core(p):
        return ("chunk", p, 0), lambda: [
            (first_all.at[p, :, :, :, :, 1 - c], first_c.at[p], (w, y * 2 + 1 - c))
        ]

    chip = z * 4 + sx * 2 + y

    def chunk_chips(p):
        return ("chunk", p, 1), lambda: [
            (first_all.at[p, :, cz, cx, cy, c], first_d.at[p, chip], peer)
            for cz, cx, cy, peer in chip_peers(at)
        ]

    def chunk_middle(p):
        links.wait(*chunk_core(p))
        own = (p, whole, whole, whole, whole, c)
        first_all[own] = add(first_all[own], first_c[p])
        links.start(*chunk_chips(p))
        first_d[p, chip] = first_all[p, :, z, sx, y, c]

    def chunk_end(p):
        links.wait(*chunk_chips(p))
        total = jnp.sum(first_d[p].astype(F32), axis=0).astype(BF16)
        red[9:12, :, p * 128 : (p + 1) * 128] = total

    staged = Reducer(
        "staged", links, at, first_all,
        (first_c.at[pl.ds(2, 2)], fa_buf, fb_buf, fc_buf, fd_buf, fz_sum, fz_buf),
        lambda head: (head[0] - 2, *head[1:]),
    )

    def step_chunk(p, stage):
        total = staged.finish(stage, (p, whole))
        if stage < 3:
            staged.start(stage + 1, (p, whole))
        else:
            red[9:12, :, p * 128 : (p + 1) * 128] = total

    wides = "wide", lambda: [(v_own, vw_buf.at[w], peer) for peer in wide_peers(at)]
    narrows = "narrow", lambda: [(v_sum, vn_buf.at[n], peer) for peer in narrow_peers(at)]

    def vector_start():
        vw_buf[w] = v_own[...]
        links.start(*wides)

    def vector_middle():
        links.wait(*wides)
        total = vw_buf[0]
        for k in range(1, 8):
            total = total + vw_buf[k]
        v_sum[...] = total
        vn_buf[n] = total
        links.start(*narrows)

    def reduce_point(t):
        for group, s in {
            0: [(0, 2), (1, 0)], 1: [(2, 0)], 2: [(1, 1)], 3: [(0, 3), (2, 1)], 4: [(1, 2)],
            5: [(2, 2)], 6: [], 7: [(1, 3), (2, 3)],
        }[t]:
            step_rest(group, s)
        if t == 0:
            reducer.start(0, groups[2])
            vector_start()
        if t == 3:
            vector_middle()
        for p, s in {
            3: [(3, 0)], 4: [(3, 1)], 5: [(3, 2), (2, 0)], 6: [(2, 1)], 7: [(3, 3), (2, 2)]
        }.get(t, []):
            step_chunk(p, s)
        if t == 7:
            chunk_middle(1)

    def start_chunk(p):
        if p > 1:
            staged.start(0, (p, whole))
        else:
            links.start(*chunk_core(p))

    lane = lax.broadcasted_iota(jnp.int32, (KEYS, 128), 1)
    ones = jnp.where(lane < 2, 1.0, 0.0).astype(BF16)

    @pl.loop(0, HEADS)
    def _(step):
        for k in range(HEADS):
            pl.when(step == k)(functools.partial(reduce_point, k))
        t = HEADS - 1 - step
        i, h = t // 2, t % 2
        pl.when(step > 0)(lambda: fetched(t).wait())
        pair = pl.ds(pl.multiple_of(i * 128, 128), 128)
        head = pl.ds(pl.multiple_of(t * 64, 64), 64)

        @pl.when(h == 1)
        def _():
            value_pair[...] = v_t[pair, :].astype(F32).T.astype(BF16)
            key_pair_t[...] = keyed[i].astype(F32).T.astype(BF16)

        inv = inverse[t]
        shift = delta[t]
        high = shift.astype(BF16).astype(F32)
        mine = (row >= 64 * h) & (row < 64 * h + 64)
        scaled = jnp.where(mine, back_t[pair, :].astype(F32) * inv, 0.0).astype(BF16)
        tail = jnp.where(row == 0, -high, jnp.where(row == 1, high - shift, 0.0)).astype(BF16)
        right = jnp.concatenate([scaled, tail], axis=0)
        value = jnp.concatenate([value_pair[...], ones], axis=1)
        key_head = key_pair_t[pl.ds(pl.multiple_of(h * 64, 64), 64), :]
        query_head = q_t[head, :]
        back_head = (back_t[head, :].astype(F32) * inv).astype(BF16)
        query_total = jnp.zeros((64, ROWS), F32)
        for first_key, end_key in KEY_PARTS:
            part = slice(first_key, end_key)
            low = p_buf[h, part]
            score_back = low * dot(value[part], right).astype(BF16)
            query_total = query_total + dot(key_head[:, part], score_back)
            key_back[head, part] = dot(query_head, score_back, 1, 1).astype(BF16)
            value_back[head, part] = dot(back_head, low, 1, 1).astype(BF16)
        query_back[head, :] = (query_total * 0.125).astype(BF16)
        pl.when(t > 1)(lambda: fetched(t - 2).start())

        @pl.when(h == 0)
        def _():
            part = dot(normed_t[:, 0:ROWS], query_back[pair, :], 1, 1).astype(BF16)
            first_all[i, 0] = part.reshape(*PIECES, 128)
            both = jnp.concatenate([key_back[pair, :], value_back[pair, :]], axis=0)
            part = dot(normed_t[...], both, 1, 1).astype(BF16)
            for u in range(2):
                first_all[i, 1 + u] = part[:, u * 128 : (u + 1) * 128].reshape(*PIECES, 128)

        for k in range(4):
            pl.when(step == 2 * k + 1)(functools.partial(start_chunk, 3 - k))

    @pl.when(w >= 0)
    def _():
        w_q, w_k, w_v = unit(0), unit(1), unit(2)
        normal, scale = normalize(text_buf[...].reshape(D, TEXT).astype(F32).T)
        text_back = dot(key_back[:, ROWS:KEYS], w_k, 0, 1) + dot(
            value_back[:, ROWS:KEYS], w_v, 0, 1
        )
        text_part[...] = (
            norm_back(text_back, gain_one, normal, scale).T.astype(BF16).reshape(8, 64, TEXT)
        )
        gain_grad = jnp.sum(text_back * normal, axis=0, keepdims=True)
        bias_grad = jnp.sum(text_back, axis=0, keepdims=True)
        text_sum[w] = text_part[w]
        text_parts = "parts", lambda: [
            (text_part.at[peer[0]], text_sum.at[w], peer) for peer in wide_peers(at)
        ]
        chunk_middle(0)
        links.start(*text_parts)
        step_chunk(2, 3)
        tile = ROWS // 2
        kept = []
        for t in range(2):
            rows = slice(t * tile, (t + 1) * tile)
            normal, scale = normalize(x[rows].astype(F32))
            projected = (
                dot(query_back[:, rows], w_q, 0, 1)
                + dot(key_back[:, rows], w_k, 0, 1)
                + dot(value_back[:, rows], w_v, 0, 1)
            )
            kept.append((rows, projected, normal, scale))
            gain_grad = gain_grad + jnp.sum(projected * normal, axis=0, keepdims=True)
            bias_grad = bias_grad + jnp.sum(projected, axis=0, keepdims=True)
        for r in range(4):
            l_own[r : r + 1, :] = gain_grad[:, r * 128 : (r + 1) * 128]
            l_own[4 + r : 5 + r, :] = bias_grad[:, r * 128 : (r + 1) * 128]
        late_wides = "late wide", lambda: [(l_own, lw_buf.at[w], peer) for peer in wide_peers(at)]
        late_narrows = "late narrow", lambda: [
            (l_sum, ln_buf.at[n], peer) for peer in narrow_peers(at)
        ]
        lw_buf[w] = l_own[...]
        links.start(*late_wides)
        for rows, projected, normal, scale in kept:
            middle_buf[rows] += norm_back(projected, gain_one, normal, scale)
        write_patch.start()
        links.wait(*narrows)
        vec_out[...] = (vn_buf[0] + vn_buf[1]) + (vn_buf[2] + vn_buf[3])
        owner, rank = unit_ranks(owners)
        spots = []
        for q in range(4):
            for s in range(SLOTS):
                spot = jnp.int32(0)
                for u in range(UNITS):
                    position = 9 + u if u < 3 else DENSE_PLACE[u - 3]
                    spot = spot + jnp.where((owner[u] == q) & (rank[u] == s), position, 0)
                spots.append((q, s, jnp.minimum(spot, UNITS - 1)))

        def grads(part, columns):
            return ("grads", part), lambda: [
                (s_buf.at[peer[1], :, :, columns], r_buf.at[n, :, :, columns], peer)
                for peer in narrow_peers(at)
            ]

        def send_grads(part, columns):
            for q, s, spot in spots:
                s_buf[q, s, :, columns] = red[spot, :, columns]
            links.start(*grads(part, columns))
            r_buf[n, :, :, columns] = s_buf[n, :, :, columns]

        others, last = slice(128, 512), slice(0, 128)
        chunk_end(1)
        send_grads(0, others)
        links.wait(*text_parts)
        text_out[...] = jnp.sum(text_sum[...].astype(F32), axis=0)
        chunk_end(0)
        send_grads(1, last)
        links.wait(*late_wides)
        total = lw_buf[0]
        for k in range(1, 8):
            total = total + lw_buf[k]
        l_sum[...] = total
        ln_buf[n] = total
        links.start(*late_narrows)
        links.wait(*grads(0, others))
        links.wait(*grads(1, last))
        for q in range(4):
            slot_grad[:, q * 16 : (q + 1) * 16, :] = r_buf[q]
        write_layer.wait()
        write_patch.wait()
        links.wait(*late_narrows)
        vec_out[0:8, :] = (ln_buf[0] + ln_buf[1]) + (ln_buf[2] + ln_buf[3])


def block(owners, counts, masters, text, x, vec, g):
    hbm = pl.BlockSpec(memory_space=pl.ANY)
    copies = 12 + 7 + 32 + 24 + 3 * 8 + 2 * 8 + 2 * 16 + 7 + 3 + 7 + 7 + 3 + 6
    bf = lambda *s: pltpu.VMEM(s, BF16)
    f32 = lambda *s: pltpu.VMEM(s, F32)
    rows = VEC // 128
    return pl.pallas_call(
        block_kernel,
        in_specs=[smem(), smem(), vmem(), vmem(), vmem(), vmem(), hbm],
        out_specs=[hbm, hbm, hbm, vmem(), vmem(), vmem()],
        out_shape=[
            jax.ShapeDtypeStruct((ROWS, D), F32),
            jax.ShapeDtypeStruct((ROWS, D), BF16),
            jax.ShapeDtypeStruct((HEADS - 1, KEYS, ROWS), BF16),
            jax.ShapeDtypeStruct((SLOTS, 64, D), BF16),
            jax.ShapeDtypeStruct((64, TEXT), F32),
            jax.ShapeDtypeStruct((rows, 128), F32),
        ],
        scratch_shapes=[
            bf(SLOTS, 4, 16, D),
            bf(4, SLOTS, 16, 128),
            bf(4, SLOTS, 16, 128),
            bf(4, SLOTS, 16, 128),
            bf(4, SLOTS, 16, 128),
            bf(3, *PIECES, D),
            bf(9, *PIECES, D),
            bf(4, 2, 64, TEXT),
            bf(D, ROWS),
            bf(4, KEYS, 128),
            bf(KEYS, 128),
            bf(D, KEYS),
            bf(D, KEYS),
            bf(TEXT, D),
            bf(D, ROWS),
            f32(HEADS, 1, ROWS),
            f32(HEADS, 1, ROWS),
            bf(2, KEYS, ROWS),
            bf(ROWS, D),
            f32(ROWS, D),
            bf(9, *PIECES, D),
            bf(9, 4, 2, 2, 16, D),
            bf(9, 2, 2, 16, D),
            bf(9, 2, 2, 16, D),
            bf(9, 2, 16, D),
            bf(9, 2, 16, D),
            bf(9, 4, 16, D),
            bf(3, 9, 16, D),
            bf(4, 3, *PIECES, 128),
            bf(4, 3, 4, 2, 2, 16, 128),
            bf(2, 16, 3, 16, 128),
            bf(2, 3, 2, 2, 16, 128),
            bf(2, 3, 2, 2, 16, 128),
            bf(2, 3, 2, 16, 128),
            bf(2, 3, 2, 16, 128),
            bf(2, 3, 4, 16, 128),
            bf(3, 2, 3, 16, 128),
            bf(UNITS, 16, D),
            bf(4, SLOTS, 16, D),
            bf(4, SLOTS, 16, D),
            bf(8, 64, TEXT),
            bf(8, 64, TEXT),
            f32(rows, 128),
            f32(8, rows, 128),
            f32(rows, 128),
            f32(4, rows, 128),
            f32(8, 128),
            f32(8, 8, 128),
            f32(8, 128),
            f32(4, 8, 128),
            bf(D, ROWS),
            bf(D, KEYS),
            bf(D, KEYS),
            bf(KEYS, 128),
            bf(128, KEYS),
            pltpu.SemaphoreType.DMA((copies,)),
            pltpu.SemaphoreType.DMA((copies,)),
            pltpu.SemaphoreType.DMA((5,)),
        ],
        compiler_params=pltpu.CompilerParams(
            collective_id=1, has_side_effects=True, vmem_limit_bytes=63 * 2**20
        ),
    )(owners, counts, masters, text, x, vec, g)


def gather(owners, masters, text_t):
    packed = lax.all_gather(masters.astype(BF16), "wide", axis=2, tiled=True)
    packed = lax.all_gather(packed, "narrow", axis=0, tiled=True)
    same = owners[:, None] == owners[None, :]
    ids = jnp.arange(UNITS)
    rank = jnp.sum((same & (ids[None, :] < ids[:, None])).astype(jnp.int32), axis=1)
    units = jnp.take(packed.reshape(-1, D, D), owners * SLOTS + rank, axis=0)
    rows = lax.all_gather(text_t, "wide", axis=1, tiled=True)[0]
    return units, jnp.pad(rows, ((0, 0), (0, TEXT - LANG)))


def live_column(counts, rows):
    index = lax.broadcasted_iota(jnp.int32, (VIEW_ROWS, 1), 0)
    return [(index < counts[0, v]) for v in range(rows // VIEW_ROWS)]


def forward_kernel(
    counts, x, text_t, vec, w, att_t, probs, inverse, q_t, keyed, v_t, normed, text_normed
):
    i = pl.program_id(0)

    @pl.when(i == 0)
    def _():
        gain, bias = vec_row(vec, 0, D), vec_row(vec, D, D)
        normed[...] = (normalize(x[...].astype(F32))[0] * gain + bias).astype(BF16)
        rows = text_t[...].astype(F32).T
        live_text = lax.broadcasted_iota(jnp.int32, (TEXT, 1), 0) < LANG
        text_normed[...] = jnp.where(
            live_text, normalize(rows)[0] * gain + bias, 0.0
        ).astype(BF16)
        q_t[...] = dot(w[0], normed[...], 0, 1).astype(BF16) * BF16(0.125)
        v_t[:, 0:ROWS] = dot(w[2], normed[...], 0, 1).astype(BF16)
        v_t[:, ROWS:KEYS] = dot(w[2], text_normed[...], 0, 1).astype(BF16)
        for p in range(4):
            pair = slice(p * 128, (p + 1) * 128)
            keyed[p, 0:ROWS, 0:128] = dot(normed[...], w[1, :, pair]).astype(BF16)
            keyed[p, ROWS:KEYS, 0:128] = dot(text_normed[...], w[1, :, pair]).astype(BF16)
            for v, live in enumerate(live_column(counts, ROWS)):
                keyed[p, v * VIEW_ROWS : (v + 1) * VIEW_ROWS, 128:256] = jnp.broadcast_to(
                    jnp.where(live, 0.0, NEG), (VIEW_ROWS, 128)
                ).astype(BF16)
            keyed[p, ROWS:KEYS, 128:256] = jnp.broadcast_to(
                jnp.where(live_text, 0.0, NEG), (TEXT, 128)
            ).astype(BF16)

    row = lax.broadcasted_iota(jnp.int32, (128, ROWS), 0)
    one = jnp.where(row == 0, 1.0, 0.0).astype(BF16)
    pair_q = q_t[pl.ds(pl.multiple_of(i * 128, 128), 128), :]
    for h in range(2):
        mine = (row >= 64 * h) & (row < 64 * h + 64)
        q = jnp.where(mine, pair_q, jnp.zeros_like(pair_q))
        scores = dot(keyed[i], jnp.concatenate([q, one], axis=0))
        peak = jnp.max(scores, axis=0, keepdims=True)
        e = jnp.exp(scores - peak)
        total = jnp.sum(e, axis=0, keepdims=True)
        low = e.astype(BF16)
        probs[h] = low
        mixed = dot(v_t[pl.ds(pl.multiple_of(i * 128 + h * 64, 64), 64), :], low)
        inv = 1.0 / total
        att_t[h * 64 : (h + 1) * 64, :] = (mixed * inv).astype(BF16)
        inverse[0, h : h + 1, :] = inv


def attention_forward(counts, x, text_t, vec, units):
    return pl.pallas_call(
        forward_kernel,
        grid=(4,),
        in_specs=[smem(), vmem(), vmem(), vmem(), pl.BlockSpec((3, D, D), lambda i: (0, 0, 0))],
        out_specs=[
            pl.BlockSpec((128, ROWS), lambda i: (i, 0)),
            pl.BlockSpec((2, KEYS, ROWS), lambda i: (i, 0, 0)),
            pl.BlockSpec((1, 2, ROWS), lambda i: (i, 0, 0)),
            pl.BlockSpec((D, ROWS), lambda i: (0, 0)),
            pl.BlockSpec((4, KEYS, 256), lambda i: (0, 0, 0)),
            pl.BlockSpec((D, KEYS), lambda i: (0, 0)),
        ],
        out_shape=[
            jax.ShapeDtypeStruct((D, ROWS), BF16),
            jax.ShapeDtypeStruct((HEADS, KEYS, ROWS), BF16),
            jax.ShapeDtypeStruct((4, 2, ROWS), F32),
            jax.ShapeDtypeStruct((D, ROWS), BF16),
            jax.ShapeDtypeStruct((4, KEYS, 256), BF16),
            jax.ShapeDtypeStruct((D, KEYS), BF16),
        ],
        scratch_shapes=[pltpu.VMEM((ROWS, D), BF16), pltpu.VMEM((TEXT, D), BF16)],
        compiler_params=pltpu.CompilerParams(vmem_limit_bytes=VMEM_LIMIT),
    )(counts, x, text_t, vec, units)


def dense_kernel(
    counts, att_t, x, g, vec, w,
    layer_out, middle_back, back_t, grads, gain_grad, bias_grad, up_grad, down_grad,
    total, *, tile
):
    i = pl.program_id(0)
    steps = pl.num_programs(0)
    gain, bias = vec_row(vec, 2 * D, D), vec_row(vec, 3 * D, D)
    a = att_t[...]
    index = lax.broadcasted_iota(jnp.int32, (tile, 1), 0) + i * tile
    live = jnp.zeros((tile, 1), jnp.bool_)
    for v in range(VIEWS):
        live = live | ((index >= v * VIEW_ROWS) & (index < v * VIEW_ROWS + counts[0, v]))
    middle = x[...].astype(F32) + dot(a, w[0], 0, 0)
    normed, scale = normalize(middle)
    low = (normed * gain + bias).astype(BF16)
    out_back = jnp.where(live, g[...].astype(F32), 0.0)
    out_low = out_back.astype(BF16)

    @pl.when(i == 0)
    def _():
        total[...] = jnp.zeros_like(total)
        gain_grad[...] = jnp.zeros_like(gain_grad)
        bias_grad[...] = jnp.zeros_like(bias_grad)
        up_grad[...] = jnp.zeros_like(up_grad)
        down_grad[...] = jnp.zeros_like(down_grad)

    out = middle + vec_row(vec, 4 * D + FF, D)
    normed_back = jnp.zeros((tile, D), F32)
    for j in range(4):
        block = slice(j * D, (j + 1) * D)
        preact = dot(low, w[1 + j]) + vec_row(vec, 4 * D + j * D, D)
        phi = 0.5 + 0.5 * lax.erf(preact * 0.7071067811865476)
        active = (preact * phi).astype(BF16)
        slope = phi + preact * (jnp.exp(-0.5 * preact * preact) * 0.3989422804014327)
        out = out + dot(active, w[5 + j])
        preact_back = (dot(out_low, w[5 + j], 1, 1) * slope).astype(BF16)
        normed_back = normed_back + dot(preact_back, w[1 + j], 1, 1)
        total[1 + j] += dot(low, preact_back, 0, 0)
        total[5 + j] += dot(active, out_low, 0, 0)
        up_grad[:, block] += jnp.sum(preact_back.astype(F32), axis=0, keepdims=True)
    layer_out[...] = jnp.where(live, out, 0.0).astype(BF16)
    back = out_back + norm_back(normed_back, gain, normed, scale)
    middle_back[...] = back
    branch = back.astype(BF16)
    back_t[...] = dot(w[0], branch, 1, 1).astype(BF16)
    total[0] += dot(a, branch)
    gain_grad[...] += jnp.sum(normed_back * normed, axis=0, keepdims=True)
    bias_grad[...] += jnp.sum(normed_back, axis=0, keepdims=True)
    down_grad[...] += jnp.sum(out_back, axis=0, keepdims=True)

    @pl.when(i == steps - 1)
    def _():
        grads[...] = total[...].astype(BF16)


def dense(counts, att_t, x, g, vec, units, tile=640):
    rows = pl.BlockSpec((tile, D), lambda i: (i, 0))
    columns = pl.BlockSpec((D, tile), lambda i: (0, i))
    return pl.pallas_call(
        functools.partial(dense_kernel, tile=tile),
        grid=(ROWS // tile,),
        in_specs=[smem(), columns, rows, rows, vmem(), vmem()],
        out_specs=[
            rows,
            rows,
            columns,
            pl.BlockSpec((9, D, D), lambda i: (0, 0, 0)),
            pl.BlockSpec((1, D), lambda i: (0, 0)),
            pl.BlockSpec((1, D), lambda i: (0, 0)),
            pl.BlockSpec((1, FF), lambda i: (0, 0)),
            pl.BlockSpec((1, D), lambda i: (0, 0)),
        ],
        out_shape=[
            jax.ShapeDtypeStruct((ROWS, D), BF16),
            jax.ShapeDtypeStruct((ROWS, D), F32),
            jax.ShapeDtypeStruct((D, ROWS), BF16),
            jax.ShapeDtypeStruct((9, D, D), BF16),
            jax.ShapeDtypeStruct((1, D), F32),
            jax.ShapeDtypeStruct((1, D), F32),
            jax.ShapeDtypeStruct((1, FF), F32),
            jax.ShapeDtypeStruct((1, D), F32),
        ],
        scratch_shapes=[pltpu.VMEM((9, D, D), F32)],
        compiler_params=pltpu.CompilerParams(vmem_limit_bytes=VMEM_LIMIT),
    )(counts, att_t, x, g, vec, units)


def backward_kernel(probs, inverse, keyed, v_t, back_t, q_t, att_t, query_back, key_back, value_back):
    row = lax.broadcasted_iota(jnp.int32, (128, ROWS), 0)
    lane = lax.broadcasted_iota(jnp.int32, (KEYS, 128), 1)
    ones = jnp.where(lane < 2, 1.0, 0.0).astype(BF16)
    value = jnp.concatenate([v_t[...].astype(F32).T.astype(BF16), ones], axis=1)
    key_t = keyed[:, 0:128].astype(F32).T.astype(BF16)
    back = back_t[...].astype(F32)
    product = back * att_t[...].astype(F32)
    query = q_t[...].astype(F32)
    key_total = jnp.zeros((KEYS, 128), F32)
    value_total = jnp.zeros((KEYS, 128), F32)
    for h in range(2):
        half = slice(h * 64, (h + 1) * 64)
        inv = inverse[0, h : h + 1, :]
        delta = jnp.sum(product[half], axis=0, keepdims=True) * inv
        high = delta.astype(BF16).astype(F32)
        mine = (row >= 64 * h) & (row < 64 * h + 64)
        scaled = jnp.where(mine, back * inv, 0.0)
        tail = jnp.where(row == 0, -high, jnp.where(row == 1, high - delta, 0.0))
        right = jnp.concatenate([scaled.astype(BF16), tail.astype(BF16)], axis=0)
        low = probs[h]
        score_back = low * dot(value, right).astype(BF16)
        query_back[half, :] = (dot(key_t[half], score_back) * 0.125).astype(BF16)
        key_total += dot(score_back, jnp.where(mine, query, 0.0).T.astype(BF16))
        value_total += dot(low, scaled.T.astype(BF16))
    key_back[...] = key_total.astype(BF16)
    value_back[...] = value_total.astype(BF16)


def attention_backward(probs, inverse, keyed, v_t, back_t, q_t, att_t):
    return pl.pallas_call(
        backward_kernel,
        grid=(4,),
        in_specs=[
            pl.BlockSpec((2, KEYS, ROWS), lambda i: (i, 0, 0)),
            pl.BlockSpec((1, 2, ROWS), lambda i: (i, 0, 0)),
            pl.BlockSpec((None, KEYS, 256), lambda i: (i, 0, 0)),
            pl.BlockSpec((128, KEYS), lambda i: (i, 0)),
            pl.BlockSpec((128, ROWS), lambda i: (i, 0)),
            pl.BlockSpec((128, ROWS), lambda i: (i, 0)),
            pl.BlockSpec((128, ROWS), lambda i: (i, 0)),
        ],
        out_specs=[
            pl.BlockSpec((128, ROWS), lambda i: (i, 0)),
            pl.BlockSpec((KEYS, 128), lambda i: (0, i)),
            pl.BlockSpec((KEYS, 128), lambda i: (0, i)),
        ],
        out_shape=[
            jax.ShapeDtypeStruct((D, ROWS), BF16),
            jax.ShapeDtypeStruct((KEYS, D), BF16),
            jax.ShapeDtypeStruct((KEYS, D), BF16),
        ],
        compiler_params=pltpu.CompilerParams(vmem_limit_bytes=VMEM_LIMIT),
    )(probs, inverse, keyed, v_t, back_t, q_t, att_t)


def project_kernel(
    x, text_t, vec, w, middle_back, query_back, key_back, value_back, text_key, text_value,
    patch_grad, grads, gain_grad, bias_grad, text_grad_t, total
):
    i = pl.program_id(0)
    steps = pl.num_programs(0)
    gain, bias = vec_row(vec, 0, D), vec_row(vec, D, D)

    @pl.when(i == 0)
    def _():
        live = lax.broadcasted_iota(jnp.int32, (TEXT, 1), 0) < LANG
        normed, scale = normalize(text_t[...].astype(F32).T)
        low_t = jnp.where(live, normed * gain + bias, 0.0).T.astype(BF16)
        k, v = text_key[...], text_value[...]
        back = dot(k, w[1], 1, 1) + dot(v, w[2], 1, 1)
        text_grad_t[...] = norm_back(back, gain, normed, scale).T.astype(BF16)
        gain_grad[...] = jnp.sum(back * normed, axis=0, keepdims=True)
        bias_grad[...] = jnp.sum(back, axis=0, keepdims=True)
        total[0] = jnp.zeros((D, D), F32)
        total[1] = dot(low_t, k)
        total[2] = dot(low_t, v)

    normed, scale = normalize(x[...].astype(F32))
    low_t = (normed * gain + bias).T.astype(BF16)
    q, k, v = query_back[...], key_back[...], value_back[...]
    back = dot(q, w[0], 0, 1) + dot(k, w[1], 1, 1) + dot(v, w[2], 1, 1)
    patch_grad[...] = middle_back[...] + norm_back(back, gain, normed, scale)
    total[0] += dot(low_t, q, 1, 1)
    total[1] += dot(low_t, k)
    total[2] += dot(low_t, v)
    gain_grad[...] += jnp.sum(back * normed, axis=0, keepdims=True)
    bias_grad[...] += jnp.sum(back, axis=0, keepdims=True)

    @pl.when(i == steps - 1)
    def _():
        grads[...] = total[...].astype(BF16)


def project_back(x, text_t, vec, units, middle_back, query_back, key_back, value_back, tile=640):
    rows = pl.BlockSpec((tile, D), lambda i: (i, 0))
    text_rows = pl.BlockSpec((TEXT, D), lambda i: (ROWS // TEXT, 0))
    return pl.pallas_call(
        project_kernel,
        grid=(ROWS // tile,),
        in_specs=[
            rows,
            vmem(),
            vmem(),
            pl.BlockSpec((3, D, D), lambda i: (0, 0, 0)),
            rows,
            pl.BlockSpec((D, tile), lambda i: (0, i)),
            rows,
            rows,
            text_rows,
            text_rows,
        ],
        out_specs=[
            rows,
            pl.BlockSpec((3, D, D), lambda i: (0, 0, 0)),
            pl.BlockSpec((1, D), lambda i: (0, 0)),
            pl.BlockSpec((1, D), lambda i: (0, 0)),
            pl.BlockSpec((D, TEXT), lambda i: (0, 0)),
        ],
        out_shape=[
            jax.ShapeDtypeStruct((ROWS, D), F32),
            jax.ShapeDtypeStruct((3, D, D), BF16),
            jax.ShapeDtypeStruct((1, D), F32),
            jax.ShapeDtypeStruct((1, D), F32),
            jax.ShapeDtypeStruct((D, TEXT), BF16),
        ],
        scratch_shapes=[pltpu.VMEM((3, D, D), F32)],
        compiler_params=pltpu.CompilerParams(vmem_limit_bytes=VMEM_LIMIT),
    )(
        x, text_t, vec, units, middle_back, query_back, key_back, value_back, key_back, value_back
    )


def reduce_all(owners, rest, first, text, vecs):
    vec = lax.psum(jnp.concatenate(vecs, axis=1), ("wide", "narrow"))
    text_sum = lax.psum_scatter(text.astype(F32), "wide", scatter_dimension=0, tiled=True)
    all_units = jnp.concatenate([first, rest], axis=0).astype(F32)
    rows = lax.psum_scatter(all_units, "wide", scatter_dimension=1, tiled=True)
    same = owners[:, None] == owners[None, :]
    ids = jnp.arange(UNITS)
    rank = jnp.sum((same & (ids[None, :] < ids[:, None])).astype(jnp.int32), axis=1)
    pick = (owners[None, None, :] == jnp.arange(lax.axis_size("narrow"))[:, None, None]) & (
        rank[None, None, :] == jnp.arange(SLOTS)[None, :, None]
    )
    terms = jnp.einsum("nsu,urc->nsrc", pick.astype(F32), rows, precision=lax.Precision.HIGHEST)
    slots = lax.psum_scatter(terms, "narrow", scatter_dimension=0, tiled=True)
    return slots[0], text_sum, vec.reshape(VEC // 128, 128)


def adam(master, moment_one, moment_two, averaged, gradient, rate):
    moment_one = beta_one * moment_one + (1.0 - beta_one) * gradient
    moment_two = beta_two * moment_two + (1.0 - beta_two) * gradient * gradient
    mean_hat = moment_one / (1.0 - beta_one**STEP)
    second_hat = moment_two / (1.0 - beta_two**STEP)
    master = master - rate * (
        mean_hat / (jnp.sqrt(second_hat) + adam_eps) + weight_decay * master
    )
    averaged = average_keep * averaged + (1.0 - average_keep) * master
    return master, moment_one, moment_two, averaged


def unit_rates():
    blocks = FF // D
    fans = [2 * D // 3, 2 * D // 3, D, D // 64] + [D] * blocks + [FF] * blocks
    return [float(fan) ** -0.5 for fan in fans]


def update_kernel(
    owners, grad, masters, first, second, average, text_t, vec_grad, vec, vec_first, vec_second,
    vec_average, patch_in, layer_in,
    new_masters, new_first, new_second, new_average, new_copies, text_grad,
    vec_new_value, vec_new_first, vec_new_second, vec_new_average, patch_out, layer_out,
):
    s = pl.program_id(0)
    patch_out[...] = patch_in[...]
    layer_out[...] = layer_in[...]
    n = lax.axis_index("narrow")
    owner, rank = unit_ranks(owners)
    rate, filled = jnp.float32(0.0), jnp.int32(0)
    for u, value in enumerate(unit_rates()):
        match = (owner[u] == n) & (rank[u] == s)
        rate = rate + jnp.where(match, jnp.float32(value), jnp.float32(0.0))
        filled = filled + match.astype(jnp.int32)
    state = adam(masters[0, 0], first[0, 0], second[0, 0], average[0, 0], grad[0].astype(F32), rate)
    keep = jnp.broadcast_to(filled, state[0].shape) > 0
    state = [jnp.where(keep, part, 0.0) for part in state]
    for ref, part in zip((new_masters, new_first, new_second, new_average), state):
        ref[0, 0] = part
    new_copies[0, 0] = state[0].astype(BF16)

    @pl.when(s == 0)
    def _():
        text_grad[0] = text_t[:, 0:LANG]
        state = adam(
            vec[...], vec_first[...], vec_second[...], vec_average[...], vec_grad[...], vector_rate
        )
        for ref, part in zip(
            (vec_new_value, vec_new_first, vec_new_second, vec_new_average), state
        ):
            ref[...] = part


def update(
    owners, grad, masters, first, second, average, text_t, vec_grad, vec, v1, v2, va, patch, layer
):
    rows = masters.shape[2]
    state = jax.ShapeDtypeStruct(masters.shape, F32)
    vector = jax.ShapeDtypeStruct(vec.shape, F32)
    slot = pl.BlockSpec((1, 1, rows, D), lambda s: (0, s, 0, 0))
    vec_spec = pl.BlockSpec(vec.shape, lambda s: (0, 0))
    handed = pl.BlockSpec((ROWS // SLOTS, D), lambda s: (s, 0))
    return pl.pallas_call(
        update_kernel,
        grid=(SLOTS,),
        out_shape=[state] * 4
        + [
            jax.ShapeDtypeStruct(masters.shape, BF16),
            jax.ShapeDtypeStruct((1, text_t.shape[0], LANG), F32),
        ]
        + [vector] * 4
        + [jax.ShapeDtypeStruct(patch.shape, F32), jax.ShapeDtypeStruct(layer.shape, BF16)],
        in_specs=[smem(), pl.BlockSpec((1, rows, D), lambda s: (s, 0, 0))]
        + [slot] * 4
        + [pl.BlockSpec(text_t.shape, lambda s: (0, 0))]
        + [vec_spec] * 5
        + [handed] * 2,
        out_specs=[slot] * 5
        + [pl.BlockSpec((1, text_t.shape[0], LANG), lambda s: (0, 0, 0))]
        + [vec_spec] * 4
        + [handed] * 2,
        compiler_params=pltpu.CompilerParams(vmem_limit_bytes=VMEM_LIMIT),
    )(
        owners, grad, masters, first, second, average, text_t, vec_grad, vec, v1, v2, va, patch, layer
    )


def local(
    patches, text_tokens, view_counts, out_grad, owners, masters, first_moment, second_moment,
    average, vec_value, vec_first, vec_second, vec_average,
):
    vec, v1, v2, va = [
        part.reshape(VEC // 128, 128) for part in (vec_value, vec_first, vec_second, vec_average)
    ]
    text_in = jnp.swapaxes(text_tokens, 1, 2)
    if lax.axis_size("wide") == 8 and lax.axis_size("narrow") == 4:
        patch_grad, layer_out, _, slot_grad, text_sum, vec_grad = block(
            owners, view_counts, masters, text_in, patches, vec, out_grad
        )
    else:
        units, text_t = gather(owners, masters, text_in)
        att_t, probs, inverse, q_t, keyed, v_t = attention_forward(
            view_counts, patches, text_t, vec, units
        )
        layer_out, middle_back, back_t, rest, *vecs = dense(
            view_counts, att_t, patches, out_grad, vec, units[3:]
        )
        query_back, key_back, value_back = attention_backward(
            probs, inverse, keyed, v_t, back_t, q_t, att_t
        )
        patch_grad, first, gain_one, bias_one, text_part = project_back(
            patches, text_t, vec, units, middle_back, query_back, key_back, value_back
        )
        slot_grad, text_sum, vec_grad = reduce_all(
            owners, rest, first, text_part, (gain_one, bias_one, *vecs)
        )
    outs = update(
        owners, slot_grad, masters, first_moment, second_moment, average, text_sum, vec_grad, vec,
        v1, v2, va, patch_grad, layer_out,
    )
    new_masters, new_first, new_second, new_average, new_copies, text_grad = outs[:6]
    vectors = [part.reshape(VEC) for part in outs[6:10]]
    patch_grad, layer_out = outs[10:]
    return (
        layer_out, patch_grad, jnp.swapaxes(text_grad, 1, 2), new_masters, new_first, new_second,
        new_average, new_copies, *vectors,
    )


def solution(mesh):
    rows = P(("wide", "narrow"), None)
    state = P("narrow", None, "wide", None)
    text = P("narrow", None, "wide")
    in_specs = (rows, text, rows, rows, P(), state, state, state, state, P(), P(), P(), P())
    out_specs = (rows, rows, text, state, state, state, state, state, P(), P(), P(), P())
    return jax.shard_map(local, mesh=mesh, in_specs=in_specs, out_specs=out_specs, check_vma=False)
```
